32 devices in a mesh: grp: 2 (over y), sets: 16 (over z, x, core).
Axes of the slice: x: 2, y: 2, z: 4, core: 2. Of those that a mesh axis runs over, the one named last changes fastest.
Arguments:
- exposure_adjoint: bfloat16 [7680, 2048], P(('grp', 'sets')), parts along dimension 0, may hold values from -6 to 6
- positive_bits: int32 [512, 2048], P(('grp', 'sets')), parts along dimension 0, may hold values from 0 to 32704
- currencies: int32 [7680, 4], P(('grp', 'sets')), parts along dimension 0, may hold values from 0 to 39, all different within a row
- mix_count: int32 [7680], P(('grp', 'sets')), parts along dimension 0, may hold values from 1 to 4
- notional: float32 [7680, 4], P(('grp', 'sets')), parts along dimension 0, may hold values from -0.375 to 0.375
- fx_paths: float32 [80, 2048], P('grp', 'sets'), parts along dimension 0, may hold values from 0.5 to 2
- short_rates: float32 [80, 2048], P('grp', 'sets'), parts along dimension 0, may hold values from -0.05 to 0.25
- start_integral: float32 [80, 256], P('grp', 'sets'), parts along dimension 0, may hold values from 0 to 2
Outputs:
- fx_adjoint: float32 [80, 2048], P('grp', 'sets'), parts along dimension 0
- rate_adjoint: float32 [80, 2048], P('grp', 'sets'), parts along dimension 0
- notional_adjoint: float32 [7680, 4], P(('grp', 'sets')), parts along dimension 0
The draws below stay inside these ranges and needn't reach their ends.
There are 2 independent parts, one for each index of `grp`. The reference program is written for one: setup_inputs(seed, part) draws one part's arguments, and reference() takes and returns one part's arrays. A program takes and returns all parts, laid end to end along the dimension named above; each array names one. Nothing has to cross between parts.
Inputs may be any that keep to these rules, and one draw needn't show every extreme that they name: The 4 currencies of a set are distinct.
All inputs are finite; a program needn't handle non-finite values.
Results may differ from the reference program's by a relative error of at most 0.003.
Values may be sent and summed in bfloat16 or wider, within the bound.
No kernel may reach another device: no remote copies, remote signals or barrier semaphores. Data moves between devices by JAX's collectives and lax.ppermute only.
A program may use at most 128 MiB of HBM per device.

```python
import math
import jax
import jax.numpy as jnp
from jax import lax

CCY = 40
MIX = 4
DATES = 8
SETS_DEV = 240
SETS = 3840
PATHS = 256
N_SETS = 16


def plant(values, key, smallest, top_value):
    extent = values.shape
    index_at = [jax.random.randint(jax.random.fold_in(key, axis), (), 0, extent[axis]) for axis in range(len(extent))]
    values = values.at[tuple(index_at)].set(smallest)
    longest = extent.index(max(extent))
    index_at[longest] = (index_at[longest] + 1) % extent[longest]
    return values.at[tuple(index_at)].set(top_value)


def strengthened(drawn, own_key, source, target, blocks, factor):
    def block_of(axis_at):
        return (jnp.arange(drawn.shape[axis_at]) // (drawn.shape[axis_at] // blocks)).reshape((-1,) + (1,) * (drawn.ndim - 1 - axis_at))

    near = jax.random.permutation(own_key, blocks)[block_of(target)]
    far = (block_of(target) + blocks // 2) % blocks
    return jnp.where((block_of(source) == near) | (block_of(source) == far), factor * drawn, drawn)


def steps_of(key, shape, pieces, least, high):
    gain, own = 1.0, jax.random.fold_in(key, 6)
    for position, parts in pieces:
        heights = jnp.exp(jax.random.uniform(jax.random.fold_in(own, position), (parts,), jnp.float32, least / len(pieces), high / len(pieces)))
        gain = gain * jnp.repeat(heights, shape[position] // parts).reshape([-1 if axis == position else 1 for axis in range(len(shape))])
    return gain


def different_ones(stream_key, rows, count, top, lift):
    sequence = jax.random.permutation(jax.random.fold_in(stream_key, 1), count)
    pull = sequence
    for power in range(3):
        pull = pull * pull // count
    pull = pull * lift // count
    tickets = jax.random.randint(jax.random.fold_in(stream_key, 2), (rows, count), 0, 4096) + pull
    sure = jax.random.permutation(jax.random.fold_in(stream_key, 3), rows)[jnp.arange(count) % rows]
    tickets = jnp.where(jnp.arange(rows)[:, None] == sure[None, :], 1 << 14, tickets)
    score = tickets * count + jnp.arange(count)
    return lax.top_k(score.astype(jnp.int32), top)[1].astype(jnp.int32)


def normal_values(key, shape, width, reach, pieces=(), held_as=jnp.bfloat16):
    array = width * jax.random.normal(key, shape, jnp.float32)
    if pieces:
        array = array * steps_of(key, shape, pieces, -0.22, 0.18)
    return jnp.clip(array, -reach, reach).astype(held_as)


def gaussian_with(key, shape, scale, reach, split, heavy, kind=jnp.bfloat16):
    array = scale * jax.random.normal(key, shape, jnp.float32)
    if split:
        array = array * steps_of(key, shape, split, -0.22, 0.18)
    return jnp.clip(strengthened(array, jax.random.fold_in(key, 3), *heavy), -reach, reach).astype(kind)


def setup_inputs(seed: int = 0, part: int = 0) -> dict:
    keys = jax.random.split(jax.random.key(seed), 9)
    own_keys = jax.random.split(jax.random.fold_in(keys[8], part), 9)
    exposure_adjoint = gaussian_with(own_keys[0], (SETS, PATHS * DATES), 1.0, 6.0, ((0, 16),), (0, 1, 16, 2.0))
    positive_bits = plant(jax.random.randint(own_keys[1], (SETS // 15, PATHS * DATES), 0, 32705), jax.random.fold_in(own_keys[1], 1), 0, 32704).astype(jnp.int32)
    currencies = different_ones(own_keys[2], SETS, CCY, MIX, 1638)
    mix_count = plant(jax.random.randint(own_keys[3], (SETS,), 1, MIX + 1), jax.random.fold_in(own_keys[3], 1), 1, MIX).astype(jnp.int32)
    notional = normal_values(own_keys[4], (SETS, MIX), (SETS // 16) ** -0.5, 0.375, ((0, 16),), jnp.float32)
    fx_paths = jnp.clip(jnp.exp(math.log(2.0) - 1.3862944 * jax.random.uniform(own_keys[5], (CCY, PATHS * DATES), jnp.float32) ** steps_of(own_keys[5], (CCY, PATHS * DATES), ((1, 16),), -0.2, 0.2)), 0.5, 2.0)
    short_rates = jnp.clip(-0.05 + 0.3 * jax.random.uniform(own_keys[6], (CCY, PATHS * DATES), jnp.float32) ** steps_of(own_keys[6], (CCY, PATHS * DATES), ((1, 16),), -0.2, 0.2), -0.05, 0.25)
    start_integral = jnp.clip(2.0 * jax.random.uniform(own_keys[7], (CCY, PATHS), jnp.float32) ** steps_of(own_keys[7], (CCY, PATHS), ((1, 16),), -0.2, 0.2), 0.0, 2.0)
    return dict(exposure_adjoint=exposure_adjoint, positive_bits=positive_bits, currencies=currencies, mix_count=mix_count, notional=notional, fx_paths=fx_paths, short_rates=short_rates, start_integral=start_integral)


step_years = 0.25

def unpack(packed, exposure):
    shifts = jnp.arange(15, dtype=jnp.int32)
    flags = jnp.right_shift(packed[:, None, :], shifts[None, :, None]) & 1
    flags = flags.reshape(exposure.shape)
    return jnp.where(flags == 1, exposure, jnp.zeros((), jnp.bfloat16))

def reference(exposure_adjoint, positive_bits, currencies, mix_count, notional, fx_paths, short_rates, start_integral):
    columns = PATHS * DATES
    rates_cube = short_rates.reshape(CCY, PATHS, DATES)
    integral = start_integral[:, :, None] + step_years * jnp.cumsum(rates_cube, axis=2)
    discount = jnp.exp(-integral).reshape(CCY, columns)
    carried = (fx_paths * discount).astype(jnp.bfloat16)
    slot_index = jnp.arange(MIX, dtype=jnp.int32)
    active = slot_index[None, :] < mix_count[:, None]
    onehot = currencies[:, :, None] == jnp.arange(CCY, dtype=jnp.int32)[None, None, :]
    chosen = jnp.logical_and(active[:, :, None], onehot)
    mix_weights = lax.optimization_barrier(jnp.sum(jnp.where(chosen, notional[:, :, None], jnp.float32(0.0)), axis=1)).astype(jnp.bfloat16)
    exposure_blocks = exposure_adjoint.reshape(N_SETS, SETS_DEV, columns)
    packed_blocks = positive_bits.reshape(N_SETS, SETS_DEV // 15, columns)
    weight_blocks = mix_weights.reshape(N_SETS, SETS_DEV, CCY)

    def one_block(running, inputs):
        exposure, packed, weight = inputs
        masked = unpack(packed, exposure)
        running = running + jnp.dot(weight.T, masked, preferred_element_type=jnp.float32)
        projected = jnp.dot(masked, carried.T, preferred_element_type=jnp.float32)
        return (running, projected)
    aggregate, projected = lax.scan(one_block, jnp.zeros((CCY, columns), jnp.float32), (exposure_blocks, packed_blocks, weight_blocks))
    projected = projected.reshape(SETS, CCY)
    fx_adjoint = aggregate * discount
    sensitivity = (aggregate * fx_paths * discount).reshape(CCY, PATHS, DATES)
    tail_sums = jnp.flip(jnp.cumsum(jnp.flip(sensitivity, axis=2), axis=2), axis=2)
    rate_adjoint = (-step_years * tail_sums).reshape(CCY, columns)
    picked = lax.optimization_barrier(jnp.sum(jnp.where(chosen, projected[:, None, :], jnp.float32(0.0)), axis=2))
    notional_adjoint = picked * (1.0 / math.sqrt(PATHS * DATES))
    return (fx_adjoint, rate_adjoint, notional_adjoint)
```

```python
import math

import jax
import jax.numpy as jnp
from jax import lax
from jax.sharding import PartitionSpec as P

step_years = 0.25


def unpack(packed, exposure):
    shifts = jnp.arange(15, dtype=jnp.int32)
    flags = jnp.right_shift(packed[:, None, :], shifts[None, :, None]) & 1
    flags = flags.reshape(exposure.shape)
    return jnp.where(flags == 1, exposure, jnp.zeros((), jnp.bfloat16))


def body(
    exposure_adjoint,
    positive_bits,
    currencies,
    mix_count,
    notional,
    fx_paths,
    short_rates,
    start_integral,
):
    currency_count = fx_paths.shape[0]
    owned_columns = fx_paths.shape[1]
    owned_paths = start_integral.shape[1]
    dates_here = owned_columns // owned_paths
    all_columns = exposure_adjoint.shape[1]
    rates_cube = short_rates.reshape(currency_count, owned_paths, dates_here)
    integral = start_integral[:, :, None] + step_years * jnp.cumsum(rates_cube, axis=2)
    discount = jnp.exp(-integral).reshape(currency_count, owned_columns)
    carried = (fx_paths * discount).astype(jnp.bfloat16)
    slot_index = jnp.arange(currencies.shape[1], dtype=jnp.int32)
    active = slot_index[None, :] < mix_count[:, None]
    onehot = currencies[:, :, None] == jnp.arange(currency_count, dtype=jnp.int32)[None, None, :]
    chosen = jnp.logical_and(active[:, :, None], onehot)
    mix_weights = jnp.sum(jnp.where(chosen, notional[:, :, None], jnp.float32(0.0)), axis=1).astype(
        jnp.bfloat16
    )
    masked = unpack(positive_bits, exposure_adjoint)
    whole_term = lax.dot_general(
        mix_weights, masked, (((0,), (0,)), ((), ())), preferred_element_type=jnp.float32
    )
    peers = all_columns // owned_columns
    parts = whole_term.astype(jnp.bfloat16).reshape(currency_count, peers, owned_columns)
    outgoing = jnp.concatenate(
        [
            jnp.broadcast_to(carried[None], (peers, currency_count, owned_columns)),
            parts.transpose(1, 0, 2),
        ],
        axis=1,
    )
    arrived = lax.all_to_all(outgoing, "sets", 0, 0, tiled=True)
    carried_all = arrived[:, :currency_count]
    projected = lax.dot_general(
        masked,
        carried_all.transpose(1, 0, 2).reshape(currency_count, all_columns),
        (((1,), (1,)), ((), ())),
        preferred_element_type=jnp.float32,
    )
    aggregate = jnp.sum(arrived[:, currency_count:].astype(jnp.float32), axis=0)
    fx_adjoint = aggregate * discount
    sensitivity = (aggregate * fx_paths * discount).reshape(currency_count, owned_paths, dates_here)
    tail_sums = jnp.flip(jnp.cumsum(jnp.flip(sensitivity, axis=2), axis=2), axis=2)
    rate_adjoint = (-step_years * tail_sums).reshape(currency_count, owned_columns)
    picked = jnp.sum(jnp.where(chosen, projected[:, None, :], jnp.float32(0.0)), axis=2)
    notional_adjoint = picked * (1.0 / math.sqrt(all_columns))
    return (fx_adjoint, rate_adjoint, notional_adjoint)


def solution(mesh):
    in_specs = (
        P(("grp", "sets"), None),
        P(("grp", "sets"), None),
        P(("grp", "sets"), None),
        P(("grp", "sets")),
        P(("grp", "sets"), None),
        P("grp", "sets"),
        P("grp", "sets"),
        P("grp", "sets"),
    )
    out_specs = (P("grp", "sets"), P("grp", "sets"), P(("grp", "sets"), None))
    return jax.shard_map(body, mesh=mesh, in_specs=in_specs, out_specs=out_specs, check_vma=False)
```

```python
import functools
import math

import jax
import jax.numpy as jnp
from jax import lax
from jax.experimental import pallas as pl
from jax.experimental.pallas import tpu as pltpu
from jax.sharding import PartitionSpec as P

step_years = 0.25
bits_per_row = 15
lanes = 128
chunks = 8


def spread_paths(values, dates):
    paths, columns = values.shape[0], values.shape[0] * dates
    path_of = lax.broadcasted_iota(jnp.int32, (paths, columns), 1) // dates
    own = lax.broadcasted_iota(jnp.int32, (paths, columns), 0)
    return lax.dot_general(
        values,
        (path_of == own).astype(jnp.float32),
        (((0,), (0,)), ((), ())),
        precision=lax.Precision.HIGHEST,
        preferred_element_type=jnp.float32,
    )


def sums_to_date(values, dates):
    width = values.shape[1]
    date = lax.broadcasted_iota(jnp.int32, values.shape, 1) % dates
    step = 1
    while step < dates:
        values = values + jnp.where(date >= step, pltpu.roll(values, step, 1), 0.0)
        step *= 2
    return values


def sums_from_date(values, dates):
    width = values.shape[1]
    date = lax.broadcasted_iota(jnp.int32, values.shape, 1) % dates
    step = 1
    while step < dates:
        values = values + jnp.where(date < dates - step, pltpu.roll(values, width - step, 1), 0.0)
        step *= 2
    return values


def used_currencies(currencies, counts):
    slot = lax.broadcasted_iota(jnp.int32, currencies.shape, 0)
    return jnp.where(slot < counts, currencies, -1)


def local_kernel(
    dates,
    exposure_hbm,
    bits_hbm,
    currencies_ref,
    counts_ref,
    notional_ref,
    fx_ref,
    rates_ref,
    start_ref,
    outgoing_ref,
    masked_hbm,
    discount_ref,
    exposure,
    bits,
    masked,
    in_sems,
    bits_sems,
    out_sems,
):
    sets, columns = exposure.shape
    currency_count, owned = fx_ref.shape
    peers = columns // owned
    width = columns // chunks

    def exposure_copy(index):
        part = pl.ds(index * width, width)
        return pltpu.make_async_copy(
            exposure_hbm.at[:, part], exposure.at[:, part], in_sems.at[index]
        )

    def bits_copy(index):
        part = pl.ds(index * width, width)
        return pltpu.make_async_copy(bits_hbm.at[:, part], bits.at[:, part], bits_sems.at[index])

    def masked_copy(index):
        part = pl.ds(index * width, width)
        return pltpu.make_async_copy(masked.at[:, part], masked_hbm.at[:, part], out_sems.at[index])

    for index in range(chunks):
        bits_copy(index).start()
        exposure_copy(index).start()

    integral = spread_paths(start_ref[...], dates) + step_years * sums_to_date(rates_ref[...], dates)
    discount = jnp.exp(-integral)
    discount_ref[...] = discount
    carried = (fx_ref[...] * discount).astype(jnp.bfloat16)
    for peer in range(peers):
        outgoing_ref[peer, 0:currency_count, :] = carried

    used = used_currencies(currencies_ref[...], counts_ref[...])
    notional = notional_ref[...]
    currency = lax.broadcasted_iota(jnp.int32, (currency_count, sets), 0)
    weights = jnp.zeros((currency_count, sets), jnp.float32)
    for slot in range(used.shape[0]):
        weights = weights + jnp.where(
            currency == used[slot : slot + 1], notional[slot : slot + 1], 0.0
        )
    weights = weights.astype(jnp.bfloat16)

    row = lax.broadcasted_iota(jnp.int32, (8, lanes), 0)

    def flag_of(tile):
        shift = row + (8 * tile) % bits_per_row
        shift = jnp.where(shift >= bits_per_row, shift - bits_per_row, shift)
        return jnp.left_shift(jnp.int32(1), shift)

    def mask_columns(first, count):
        for pair in range(sets // 16):
            flags = [flag_of(2 * pair), flag_of(2 * pair + 1)]
            for block in range(count):
                part = pl.ds(first + block * lanes, lanes)
                values = exposure[16 * pair : 16 * pair + 16, part].astype(jnp.float32)
                kept = []
                for half in range(2):
                    top = 16 * pair + 8 * half
                    group = top // bits_per_row
                    left = bits_per_row * (group + 1) - top
                    packed = jnp.broadcast_to(bits[group : group + 1, part], (8, lanes))
                    if left < 8:
                        following = jnp.broadcast_to(bits[group + 1 : group + 2, part], (8, lanes))
                        packed = jnp.where(row < left, packed, following)
                    kept.append(
                        jnp.where(
                            (packed & flags[half]) != 0, values[8 * half : 8 * half + 8], 0.0
                        )
                    )
                masked[16 * pair : 16 * pair + 16, part] = jnp.concatenate(kept, axis=0).astype(
                    jnp.bfloat16
                )

    group_width = min(width, 256)

    for index in range(chunks):
        bits_copy(index).wait()
        exposure_copy(index).wait()

        def some_columns(step, _):
            first = index * width + step * group_width
            if not isinstance(first, int):
                first = pl.multiple_of(first, group_width)
            mask_columns(first, group_width // lanes)
            terms = jnp.dot(
                weights, masked[:, pl.ds(first, group_width)], preferred_element_type=jnp.float32
            ).astype(jnp.bfloat16)
            for block in range(group_width // owned):
                outgoing_ref[first // owned + block, currency_count:, :] = terms[
                    :, block * owned : (block + 1) * owned
                ]

        if width == group_width:
            some_columns(0, None)
        else:
            pl.loop(0, width // group_width)(lambda step: some_columns(step, None))
        masked_copy(index).start()
    for index in range(chunks):
        masked_copy(index).wait()


def final_kernel(
    dates,
    arrived_ref,
    masked_hbm,
    currencies_ref,
    counts_ref,
    fx_ref,
    discount_ref,
    fx_adjoint_ref,
    rate_adjoint_ref,
    notional_adjoint_ref,
    masked,
    in_sems,
):
    sets, columns = masked.shape
    currency_count, owned = fx_ref.shape
    peers = columns // owned
    width = columns // chunks

    def masked_copy(index):
        part = pl.ds(index * width, width)
        return pltpu.make_async_copy(masked_hbm.at[:, part], masked.at[:, part], in_sems.at[index])

    for index in range(chunks):
        masked_copy(index).start()

    aggregate = arrived_ref[0, currency_count:, :].astype(jnp.float32)
    for peer in range(1, peers):
        aggregate = aggregate + arrived_ref[peer, currency_count:, :].astype(jnp.float32)
    fx_adjoint = aggregate * discount_ref[...]
    fx_adjoint_ref[...] = fx_adjoint
    rate_adjoint_ref[...] = -step_years * sums_from_date(fx_adjoint * fx_ref[...], dates)

    projected = jnp.zeros((sets, currency_count), jnp.float32)
    for index in range(chunks):
        masked_copy(index).wait()
        per_chunk = width // owned
        carried = jnp.concatenate(
            [
                arrived_ref[index * per_chunk + block, 0:currency_count, :]
                for block in range(per_chunk)
            ],
            axis=1,
        )
        projected = projected + lax.dot_general(
            masked[:, index * width : (index + 1) * width],
            carried,
            (((1,), (1,)), ((), ())),
            preferred_element_type=jnp.float32,
        )
    projected = projected.T
    used = used_currencies(currencies_ref[...], counts_ref[...])
    currency = lax.broadcasted_iota(jnp.int32, (currency_count, sets), 0)
    for slot in range(used.shape[0]):
        picked = jnp.sum(
            jnp.where(currency == used[slot : slot + 1], projected, 0.0), axis=0, keepdims=True
        )
        notional_adjoint_ref[slot : slot + 1, :] = picked * (1.0 / math.sqrt(columns))


def body(
    exposure_adjoint,
    positive_bits,
    currencies,
    mix_count,
    notional,
    fx_paths,
    short_rates,
    start_integral,
):
    sets, columns = exposure_adjoint.shape
    currency_count, owned = fx_paths.shape
    dates = owned // start_integral.shape[1]
    peers = columns // owned
    slots = currencies.shape[1]
    in_vmem = pl.BlockSpec(memory_space=pltpu.VMEM)
    anywhere = pl.BlockSpec(memory_space=pl.ANY)
    slot_currencies = currencies.T
    counts = mix_count.reshape(1, sets)
    outgoing, masked, discount = pl.pallas_call(
        functools.partial(local_kernel, dates),
        out_shape=(
            jax.ShapeDtypeStruct((peers, 2 * currency_count, owned), jnp.bfloat16),
            jax.ShapeDtypeStruct((sets, columns), jnp.bfloat16),
            jax.ShapeDtypeStruct((currency_count, owned), jnp.float32),
        ),
        in_specs=[anywhere] * 2 + [in_vmem] * 6,
        out_specs=(in_vmem, anywhere, in_vmem),
        scratch_shapes=[
            pltpu.VMEM((sets, columns), jnp.bfloat16),
            pltpu.VMEM(positive_bits.shape, jnp.int32),
            pltpu.VMEM((sets, columns), jnp.bfloat16),
            pltpu.SemaphoreType.DMA((chunks,)),
            pltpu.SemaphoreType.DMA((chunks,)),
            pltpu.SemaphoreType.DMA((chunks,)),
        ],
        compiler_params=pltpu.CompilerParams(vmem_limit_bytes=32 * 2**20),
        name="local",
    )(
        exposure_adjoint,
        positive_bits,
        slot_currencies,
        counts,
        notional.T,
        fx_paths,
        short_rates,
        start_integral.T,
    )
    arrived = lax.all_to_all(outgoing, "sets", 0, 0, tiled=True)
    fx_adjoint, rate_adjoint, notional_adjoint = pl.pallas_call(
        functools.partial(final_kernel, dates),
        out_shape=(
            jax.ShapeDtypeStruct((currency_count, owned), jnp.float32),
            jax.ShapeDtypeStruct((currency_count, owned), jnp.float32),
            jax.ShapeDtypeStruct((slots, sets), jnp.float32),
        ),
        in_specs=[in_vmem, anywhere] + [in_vmem] * 4,
        out_specs=(in_vmem,) * 3,
        scratch_shapes=[
            pltpu.VMEM((sets, columns), jnp.bfloat16),
            pltpu.SemaphoreType.DMA((chunks,)),
        ],
        compiler_params=pltpu.CompilerParams(vmem_limit_bytes=32 * 2**20),
        name="final",
    )(arrived, masked, slot_currencies, counts, fx_paths, discount)
    return fx_adjoint, rate_adjoint, notional_adjoint.T


def solution(mesh):
    in_specs = (
        P(("grp", "sets"), None),
        P(("grp", "sets"), None),
        P(("grp", "sets"), None),
        P(("grp", "sets")),
        P(("grp", "sets"), None),
        P("grp", "sets"),
        P("grp", "sets"),
        P("grp", "sets"),
    )
    out_specs = (P("grp", "sets"), P("grp", "sets"), P(("grp", "sets"), None))
    return jax.shard_map(body, mesh=mesh, in_specs=in_specs, out_specs=out_specs, check_vma=False)
```

```python
import functools
import math

import jax
import jax.numpy as jnp
from jax import lax
from jax.experimental import pallas as pl
from jax.experimental.pallas import tpu as pltpu
from jax.sharding import PartitionSpec as P

step_years = 0.25
bits_per_row = 15
lanes = 128
chunks = 8


def spread_paths(values, dates):
    paths, columns = values.shape[0], values.shape[0] * dates
    path_of = lax.broadcasted_iota(jnp.int32, (paths, columns), 1) // dates
    own = lax.broadcasted_iota(jnp.int32, (paths, columns), 0)
    return lax.dot_general(
        values,
        (path_of == own).astype(jnp.float32),
        (((0,), (0,)), ((), ())),
        precision=lax.Precision.HIGHEST,
        preferred_element_type=jnp.float32,
    )


def sums_to_date(values, dates):
    width = values.shape[1]
    date = lax.broadcasted_iota(jnp.int32, values.shape, 1) % dates
    step = 1
    while step < dates:
        values = values + jnp.where(date >= step, pltpu.roll(values, step, 1), 0.0)
        step *= 2
    return values


def sums_from_date(values, dates):
    width = values.shape[1]
    date = lax.broadcasted_iota(jnp.int32, values.shape, 1) % dates
    step = 1
    while step < dates:
        values = values + jnp.where(date < dates - step, pltpu.roll(values, width - step, 1), 0.0)
        step *= 2
    return values


def used_currencies(currencies, counts):
    slot = lax.broadcasted_iota(jnp.int32, currencies.shape, 0)
    return jnp.where(slot < counts, currencies, -1)


def local_kernel(
    dates,
    exposure_hbm,
    bits_hbm,
    currencies_ref,
    counts_ref,
    notional_ref,
    fx_ref,
    rates_ref,
    start_ref,
    outgoing_ref,
    masked,
    discount_ref,
    exposure,
    bits,
    in_sems,
    bits_sems,
):
    sets, columns = exposure.shape
    currency_count, owned = fx_ref.shape
    peers = columns // owned
    width = columns // chunks

    def exposure_copy(index):
        part = pl.ds(index * width, width)
        return pltpu.make_async_copy(
            exposure_hbm.at[:, part], exposure.at[:, part], in_sems.at[index]
        )

    def bits_copy(index):
        part = pl.ds(index * width, width)
        return pltpu.make_async_copy(bits_hbm.at[:, part], bits.at[:, part], bits_sems.at[index])

    for index in range(chunks):
        bits_copy(index).start()
        exposure_copy(index).start()

    integral = spread_paths(start_ref[...], dates) + step_years * sums_to_date(rates_ref[...], dates)
    discount = jnp.exp(-integral)
    discount_ref[...] = discount
    carried = (fx_ref[...] * discount).astype(jnp.bfloat16)
    for peer in range(peers):
        outgoing_ref[peer, 0:currency_count, :] = carried

    used = used_currencies(currencies_ref[...], counts_ref[...])
    notional = notional_ref[...]
    currency = lax.broadcasted_iota(jnp.int32, (currency_count, sets), 0)
    weights = jnp.zeros((currency_count, sets), jnp.float32)
    for slot in range(used.shape[0]):
        weights = weights + jnp.where(
            currency == used[slot : slot + 1], notional[slot : slot + 1], 0.0
        )
    weights = weights.astype(jnp.bfloat16)

    row = lax.broadcasted_iota(jnp.int32, (8, lanes), 0)

    def flag_of(tile):
        shift = row + (8 * tile) % bits_per_row
        shift = jnp.where(shift >= bits_per_row, shift - bits_per_row, shift)
        return jnp.left_shift(jnp.int32(1), shift)

    def mask_columns(first, count):
        for pair in range(sets // 16):
            flags = [flag_of(2 * pair), flag_of(2 * pair + 1)]
            for block in range(count):
                part = pl.ds(first + block * lanes, lanes)
                values = exposure[16 * pair : 16 * pair + 16, part].astype(jnp.float32)
                kept = []
                for half in range(2):
                    top = 16 * pair + 8 * half
                    group = top // bits_per_row
                    left = bits_per_row * (group + 1) - top
                    packed = jnp.broadcast_to(bits[group : group + 1, part], (8, lanes))
                    if left < 8:
                        following = jnp.broadcast_to(bits[group + 1 : group + 2, part], (8, lanes))
                        packed = jnp.where(row < left, packed, following)
                    kept.append(
                        jnp.where(
                            (packed & flags[half]) != 0, values[8 * half : 8 * half + 8], 0.0
                        )
                    )
                masked[16 * pair : 16 * pair + 16, part] = jnp.concatenate(kept, axis=0).astype(
                    jnp.bfloat16
                )

    group_width = min(width, 256)

    for index in range(chunks):
        bits_copy(index).wait()
        exposure_copy(index).wait()

        def some_columns(step, _):
            first = index * width + step * group_width
            if not isinstance(first, int):
                first = pl.multiple_of(first, group_width)
            mask_columns(first, group_width // lanes)
            terms = jnp.dot(
                weights, masked[:, pl.ds(first, group_width)], preferred_element_type=jnp.float32
            ).astype(jnp.bfloat16)
            for block in range(group_width // owned):
                outgoing_ref[first // owned + block, currency_count:, :] = terms[
                    :, block * owned : (block + 1) * owned
                ]

        if width == group_width:
            some_columns(0, None)
        else:
            pl.loop(0, width // group_width)(lambda step: some_columns(step, None))


def final_kernel(
    dates,
    arrived_ref,
    masked,
    currencies_ref,
    counts_ref,
    fx_ref,
    discount_ref,
    fx_adjoint_ref,
    rate_adjoint_ref,
    notional_adjoint_ref,
):
    sets, columns = masked.shape
    currency_count, owned = fx_ref.shape
    peers = columns // owned
    width = columns // chunks

    aggregate = arrived_ref[0, currency_count:, :].astype(jnp.float32)
    for peer in range(1, peers):
        aggregate = aggregate + arrived_ref[peer, currency_count:, :].astype(jnp.float32)
    fx_adjoint = aggregate * discount_ref[...]
    fx_adjoint_ref[...] = fx_adjoint
    rate_adjoint_ref[...] = -step_years * sums_from_date(fx_adjoint * fx_ref[...], dates)

    projected = jnp.zeros((sets, currency_count), jnp.float32)
    for index in range(chunks):
        per_chunk = width // owned
        carried = jnp.concatenate(
            [
                arrived_ref[index * per_chunk + block, 0:currency_count, :]
                for block in range(per_chunk)
            ],
            axis=1,
        )
        projected = projected + lax.dot_general(
            masked[:, index * width : (index + 1) * width],
            carried,
            (((1,), (1,)), ((), ())),
            preferred_element_type=jnp.float32,
        )
    projected = projected.T
    used = used_currencies(currencies_ref[...], counts_ref[...])
    currency = lax.broadcasted_iota(jnp.int32, (currency_count, sets), 0)
    for slot in range(used.shape[0]):
        picked = jnp.sum(
            jnp.where(currency == used[slot : slot + 1], projected, 0.0), axis=0, keepdims=True
        )
        notional_adjoint_ref[slot : slot + 1, :] = picked * (1.0 / math.sqrt(columns))


def body(
    exposure_adjoint,
    positive_bits,
    currencies,
    mix_count,
    notional,
    fx_paths,
    short_rates,
    start_integral,
):
    sets, columns = exposure_adjoint.shape
    currency_count, owned = fx_paths.shape
    dates = owned // start_integral.shape[1]
    peers = columns // owned
    slots = currencies.shape[1]
    in_vmem = pl.BlockSpec(memory_space=pltpu.VMEM)
    anywhere = pl.BlockSpec(memory_space=pl.ANY)
    slot_currencies = currencies.T
    counts = mix_count.reshape(1, sets)
    outgoing, masked, discount = pl.pallas_call(
        functools.partial(local_kernel, dates),
        out_shape=(
            pltpu.VMEM((peers, 2 * currency_count, owned), jnp.bfloat16),
            pltpu.VMEM((sets, columns), jnp.bfloat16),
            jax.ShapeDtypeStruct((currency_count, owned), jnp.float32),
        ),
        in_specs=[anywhere] * 2 + [in_vmem] * 6,
        out_specs=(in_vmem,) * 3,
        scratch_shapes=[
            pltpu.VMEM((sets, columns), jnp.bfloat16),
            pltpu.VMEM(positive_bits.shape, jnp.int32),
            pltpu.SemaphoreType.DMA((chunks,)),
            pltpu.SemaphoreType.DMA((chunks,)),
        ],
        compiler_params=pltpu.CompilerParams(vmem_limit_bytes=32 * 2**20),
        name="local",
    )(
        *[
            pltpu.with_memory_space_constraint(value, pltpu.HBM)
            for value in (
                exposure_adjoint,
                positive_bits,
                slot_currencies,
                counts,
                notional.T,
                fx_paths,
                short_rates,
                start_integral.T,
            )
        ]
    )
    arrived = lax.all_to_all(outgoing, "sets", 0, 0, tiled=True)
    fx_adjoint, rate_adjoint, notional_adjoint = pl.pallas_call(
        functools.partial(final_kernel, dates),
        out_shape=(
            jax.ShapeDtypeStruct((currency_count, owned), jnp.float32),
            jax.ShapeDtypeStruct((currency_count, owned), jnp.float32),
            jax.ShapeDtypeStruct((slots, sets), jnp.float32),
        ),
        in_specs=[in_vmem] * 6,
        out_specs=(in_vmem,) * 3,
        compiler_params=pltpu.CompilerParams(vmem_limit_bytes=32 * 2**20),
        name="final",
    )(arrived, masked, slot_currencies, counts, fx_paths, discount)
    return fx_adjoint, rate_adjoint, notional_adjoint.T


def solution(mesh):
    in_specs = (
        P(("grp", "sets"), None),
        P(("grp", "sets"), None),
        P(("grp", "sets"), None),
        P(("grp", "sets")),
        P(("grp", "sets"), None),
        P("grp", "sets"),
        P("grp", "sets"),
        P("grp", "sets"),
    )
    out_specs = (P("grp", "sets"), P("grp", "sets"), P(("grp", "sets"), None))
    return jax.shard_map(body, mesh=mesh, in_specs=in_specs, out_specs=out_specs, check_vma=False)
```

```python
import functools
import math

import jax
import jax.numpy as jnp
from jax import lax
from jax.experimental import pallas as pl
from jax.experimental.pallas import tpu as pltpu
from jax.sharding import PartitionSpec as P

step_years = 0.25
bits_per_row = 15
lanes = 128
chunks = 8


def spread_paths(values, dates):
    paths, columns = values.shape[0], values.shape[0] * dates
    path_of = lax.broadcasted_iota(jnp.int32, (paths, columns), 1) // dates
    own = lax.broadcasted_iota(jnp.int32, (paths, columns), 0)
    return lax.dot_general(
        values,
        (path_of == own).astype(jnp.float32),
        (((0,), (0,)), ((), ())),
        precision=lax.Precision.HIGHEST,
        preferred_element_type=jnp.float32,
    )


def sums_to_date(values, dates):
    width = values.shape[1]
    date = lax.broadcasted_iota(jnp.int32, values.shape, 1) % dates
    step = 1
    while step < dates:
        values = values + jnp.where(date >= step, pltpu.roll(values, step, 1), 0.0)
        step *= 2
    return values


def sums_from_date(values, dates):
    width = values.shape[1]
    date = lax.broadcasted_iota(jnp.int32, values.shape, 1) % dates
    step = 1
    while step < dates:
        values = values + jnp.where(date < dates - step, pltpu.roll(values, width - step, 1), 0.0)
        step *= 2
    return values


def used_currencies(currencies, counts):
    slot = lax.broadcasted_iota(jnp.int32, currencies.shape, 0)
    return jnp.where(slot < counts, currencies, -1)


def carry_kernel(dates, fx_ref, rates_ref, start_ref, carried_ref, discount_ref):
    integral = spread_paths(start_ref[...], dates) + step_years * sums_to_date(rates_ref[...], dates)
    discount = jnp.exp(-integral)
    discount_ref[...] = discount
    carried_ref[...] = (fx_ref[...] * discount).astype(jnp.bfloat16)


def local_kernel(
    exposure_hbm,
    bits_hbm,
    currencies_ref,
    counts_ref,
    notional_ref,
    masked,
    terms_ref,
    used_ref,
    exposure,
    bits,
    in_sems,
    bits_sems,
):
    sets, columns = exposure.shape
    blocks, currency_count, owned = terms_ref.shape
    width = columns // chunks

    def exposure_copy(index):
        part = pl.ds(index * width, width)
        return pltpu.make_async_copy(
            exposure_hbm.at[:, part], exposure.at[:, part], in_sems.at[index]
        )

    def bits_copy(index):
        part = pl.ds(index * width, width)
        return pltpu.make_async_copy(bits_hbm.at[:, part], bits.at[:, part], bits_sems.at[index])

    for index in range(chunks):
        bits_copy(index).start()
        exposure_copy(index).start()

    used = used_currencies(currencies_ref[...], counts_ref[...])
    used_ref[...] = used
    notional = notional_ref[...]
    currency = lax.broadcasted_iota(jnp.int32, (currency_count, sets), 0)
    weights = jnp.zeros((currency_count, sets), jnp.float32)
    for slot in range(used.shape[0]):
        weights = weights + jnp.where(
            currency == used[slot : slot + 1], notional[slot : slot + 1], 0.0
        )
    weights = weights.astype(jnp.bfloat16)

    row = lax.broadcasted_iota(jnp.int32, (8, lanes), 0)

    def flag_of(tile):
        shift = row + (8 * tile) % bits_per_row
        shift = jnp.where(shift >= bits_per_row, shift - bits_per_row, shift)
        return jnp.left_shift(jnp.int32(1), shift)

    def mask_columns(first, count):
        for pair in range(sets // 16):
            flags = [flag_of(2 * pair), flag_of(2 * pair + 1)]
            for block in range(count):
                part = pl.ds(first + block * lanes, lanes)
                values = exposure[16 * pair : 16 * pair + 16, part].astype(jnp.float32)
                kept = []
                for half in range(2):
                    top = 16 * pair + 8 * half
                    group = top // bits_per_row
                    left = bits_per_row * (group + 1) - top
                    packed = jnp.broadcast_to(bits[group : group + 1, part], (8, lanes))
                    if left < 8:
                        following = jnp.broadcast_to(bits[group + 1 : group + 2, part], (8, lanes))
                        packed = jnp.where(row < left, packed, following)
                    kept.append(
                        jnp.where(
                            (packed & flags[half]) != 0, values[8 * half : 8 * half + 8], 0.0
                        )
                    )
                masked[16 * pair : 16 * pair + 16, part] = jnp.concatenate(kept, axis=0).astype(
                    jnp.bfloat16
                )

    group_width = min(width, 256)

    for index in range(chunks):
        bits_copy(index).wait()
        exposure_copy(index).wait()

        def some_columns(step):
            first = index * width + step * group_width
            if not isinstance(first, int):
                first = pl.multiple_of(first, group_width)
            mask_columns(first, group_width // lanes)
            terms = jnp.dot(
                weights, masked[:, pl.ds(first, group_width)], preferred_element_type=jnp.float32
            ).astype(jnp.bfloat16)
            for block in range(group_width // owned):
                terms_ref[first // owned + block] = terms[:, block * owned : (block + 1) * owned]

        if width == group_width:
            some_columns(0)
        else:
            pl.loop(0, width // group_width)(some_columns)


def packing_kernel(planes, near, *refs):
    carried_refs, terms_ref = refs[:planes], refs[planes]
    out_refs = refs[planes + 1 :]
    currency_count = terms_ref.shape[1]
    mine = lax.axis_index("sets") % near
    for offset, out_ref in enumerate(out_refs):
        for plane in range(planes):
            out_ref[plane, currency_count:, :] = terms_ref[plane * near + (mine ^ offset)]
            if offset:
                out_ref[plane, 0:currency_count, :] = carried_refs[plane][...]


def plane_kernel(planes, near, *refs):
    in_refs, out_refs, summed = refs[:near], refs[near:-1], refs[-1]
    currency_count = summed.shape[1]
    for plane in range(planes):
        total = in_refs[0][plane, currency_count:, :].astype(jnp.float32)
        for ref in in_refs[1:]:
            total = total + ref[plane, currency_count:, :].astype(jnp.float32)
        summed[plane] = total
    mine = lax.axis_index("sets") // near
    for offset, out_ref in enumerate(out_refs):
        out_ref[...] = summed[mine ^ offset]


def projection_kernel(planes, near, *refs):
    carried_refs, stacked_refs = refs[:planes], refs[planes : planes + near - 1]
    masked, used_ref, notional_adjoint_ref, carried = refs[planes + near - 1 :]
    sets, columns = masked.shape
    currency_count, owned = carried_refs[0].shape
    me = lax.axis_index("sets")
    for offset in range(near):
        for plane in range(planes):
            block = (
                stacked_refs[offset - 1][plane, 0:currency_count, :]
                if offset
                else carried_refs[plane][...]
            )
            source = me ^ (plane * near + offset)
            carried[:, pl.ds(pl.multiple_of(source * owned, owned), owned)] = block
    projected = lax.dot_general(
        masked[...], carried[...], (((1,), (1,)), ((), ())), preferred_element_type=jnp.float32
    ).T
    used = used_ref[...]
    currency = lax.broadcasted_iota(jnp.int32, (currency_count, sets), 0)
    for slot in range(used.shape[0]):
        picked = jnp.sum(
            jnp.where(currency == used[slot : slot + 1], projected, 0.0), axis=0, keepdims=True
        )
        notional_adjoint_ref[slot : slot + 1, :] = picked * (1.0 / math.sqrt(columns))


def final_kernel(dates, planes, *refs):
    part_refs, (fx_ref, discount_ref, fx_adjoint_ref, rate_adjoint_ref) = refs[:planes], refs[planes:]
    aggregate = part_refs[0][...]
    for ref in part_refs[1:]:
        aggregate = aggregate + ref[...]
    fx_adjoint = aggregate * discount_ref[...]
    fx_adjoint_ref[...] = fx_adjoint
    rate_adjoint_ref[...] = -step_years * sums_from_date(fx_adjoint * fx_ref[...], dates)


def body(
    exposure_adjoint,
    positive_bits,
    currencies,
    mix_count,
    notional,
    fx_paths,
    short_rates,
    start_integral,
):
    sets, columns = exposure_adjoint.shape
    currency_count, owned = fx_paths.shape
    dates = owned // start_integral.shape[1]
    peers = columns // owned
    slots = currencies.shape[1]
    near = 2 ** ((peers.bit_length() - 1) // 2)
    planes = peers // near
    in_vmem = pl.BlockSpec(memory_space=pltpu.VMEM)
    anywhere = pl.BlockSpec(memory_space=pl.ANY)
    params = pltpu.CompilerParams(vmem_limit_bytes=32 * 2**20)

    def in_hbm(value):
        return pltpu.with_memory_space_constraint(value, pltpu.HBM)

    def exchange(value, offset):
        return lax.ppermute(value, "sets", [(peer, peer ^ offset) for peer in range(peers)])

    block = (currency_count, owned)
    carried, discount = pl.pallas_call(
        functools.partial(carry_kernel, dates),
        out_shape=(pltpu.VMEM(block, jnp.bfloat16), pltpu.VMEM(block, jnp.float32)),
        in_specs=[in_vmem] * 3,
        out_specs=(in_vmem,) * 2,
        compiler_params=params,
        name="carry",
    )(in_hbm(fx_paths), in_hbm(short_rates), in_hbm(start_integral.T))
    along = [carried] + [exchange(carried, near * offset) for offset in range(1, planes)]
    masked, terms, used = pl.pallas_call(
        local_kernel,
        out_shape=(
            pltpu.VMEM((sets, columns), jnp.bfloat16),
            pltpu.VMEM((peers,) + block, jnp.bfloat16),
            pltpu.VMEM((slots, sets), jnp.int32),
        ),
        in_specs=[anywhere] * 2 + [in_vmem] * 3,
        out_specs=(in_vmem,) * 3,
        scratch_shapes=[
            pltpu.VMEM((sets, columns), jnp.bfloat16),
            pltpu.VMEM(positive_bits.shape, jnp.int32),
            pltpu.SemaphoreType.DMA((chunks,)),
            pltpu.SemaphoreType.DMA((chunks,)),
        ],
        compiler_params=params,
        name="local",
    )(
        in_hbm(exposure_adjoint),
        in_hbm(positive_bits),
        in_hbm(currencies.T),
        in_hbm(mix_count.reshape(1, sets)),
        in_hbm(notional.T),
    )
    outgoing = pl.pallas_call(
        functools.partial(packing_kernel, planes, near),
        out_shape=(pltpu.VMEM((planes, 2 * currency_count, owned), jnp.bfloat16),) * near,
        in_specs=[in_vmem] * (planes + 1),
        out_specs=(in_vmem,) * near,
        compiler_params=params,
        name="packing",
    )(*along, terms)
    arrived = [exchange(outgoing[offset], offset) for offset in range(1, near)]
    summed = pl.pallas_call(
        functools.partial(plane_kernel, planes, near),
        out_shape=(pltpu.VMEM(block, jnp.float32),) * planes,
        in_specs=[in_vmem] * near,
        out_specs=(in_vmem,) * planes,
        scratch_shapes=[pltpu.VMEM((planes,) + block, jnp.float32)],
        compiler_params=params,
        name="plane",
    )(outgoing[0], *arrived)
    parts = [summed[0]] + [exchange(summed[offset], near * offset) for offset in range(1, planes)]
    notional_adjoint = pl.pallas_call(
        functools.partial(projection_kernel, planes, near),
        out_shape=jax.ShapeDtypeStruct((slots, sets), jnp.float32),
        in_specs=[in_vmem] * (planes + near + 1),
        out_specs=in_vmem,
        scratch_shapes=[pltpu.VMEM((currency_count, columns), jnp.bfloat16)],
        compiler_params=params,
        name="projection",
    )(*along, *arrived, masked, used)
    fx_adjoint, rate_adjoint = pl.pallas_call(
        functools.partial(final_kernel, dates, planes),
        out_shape=(jax.ShapeDtypeStruct(block, jnp.float32),) * 2,
        in_specs=[in_vmem] * (planes + 2),
        out_specs=(in_vmem,) * 2,
        compiler_params=params,
        name="final",
    )(*parts, fx_paths, discount)
    return fx_adjoint, rate_adjoint, notional_adjoint.T


def solution(mesh):
    in_specs = (
        P(("grp", "sets"), None),
        P(("grp", "sets"), None),
        P(("grp", "sets"), None),
        P(("grp", "sets")),
        P(("grp", "sets"), None),
        P("grp", "sets"),
        P("grp", "sets"),
        P("grp", "sets"),
    )
    out_specs = (P("grp", "sets"), P("grp", "sets"), P(("grp", "sets"), None))
    return jax.shard_map(body, mesh=mesh, in_specs=in_specs, out_specs=out_specs, check_vma=False)
```

```python
import functools
import math

import jax
import jax.numpy as jnp
from jax import lax
from jax.experimental import pallas as pl
from jax.experimental.pallas import tpu as pltpu
from jax.sharding import PartitionSpec as P

step_years = 0.25
bits_per_row = 15
lanes = 128
chunks = 8


def spread_paths(values, dates):
    paths, columns = values.shape[0], values.shape[0] * dates
    path_of = lax.broadcasted_iota(jnp.int32, (paths, columns), 1) // dates
    own = lax.broadcasted_iota(jnp.int32, (paths, columns), 0)
    return lax.dot_general(
        values,
        (path_of == own).astype(jnp.float32),
        (((0,), (0,)), ((), ())),
        precision=lax.Precision.HIGHEST,
        preferred_element_type=jnp.float32,
    )


def sums_to_date(values, dates):
    width = values.shape[1]
    date = lax.broadcasted_iota(jnp.int32, values.shape, 1) % dates
    step = 1
    while step < dates:
        values = values + jnp.where(date >= step, pltpu.roll(values, step, 1), 0.0)
        step *= 2
    return values


def sums_from_date(values, dates):
    width = values.shape[1]
    date = lax.broadcasted_iota(jnp.int32, values.shape, 1) % dates
    step = 1
    while step < dates:
        values = values + jnp.where(date < dates - step, pltpu.roll(values, width - step, 1), 0.0)
        step *= 2
    return values


def used_currencies(currencies, counts):
    slot = lax.broadcasted_iota(jnp.int32, currencies.shape, 0)
    return jnp.where(slot < counts, currencies, -1)


def carry_kernel(dates, fx_ref, rates_ref, start_ref, carried_ref, discount_ref):
    integral = spread_paths(start_ref[...], dates) + step_years * sums_to_date(rates_ref[...], dates)
    discount = jnp.exp(-integral)
    discount_ref[...] = discount
    carried = (fx_ref[...] * discount).astype(jnp.bfloat16)
    for peer in range(carried_ref.shape[0]):
        carried_ref[peer] = carried


def local_kernel(
    exposure_hbm,
    bits_hbm,
    currencies_ref,
    counts_ref,
    notional_ref,
    masked,
    terms_ref,
    used_ref,
    exposure,
    bits,
    in_sems,
    bits_sems,
):
    sets, columns = exposure.shape
    blocks, currency_count, owned = terms_ref.shape
    width = columns // chunks

    def exposure_copy(index):
        part = pl.ds(index * width, width)
        return pltpu.make_async_copy(
            exposure_hbm.at[:, part], exposure.at[:, part], in_sems.at[index]
        )

    def bits_copy(index):
        part = pl.ds(index * width, width)
        return pltpu.make_async_copy(bits_hbm.at[:, part], bits.at[:, part], bits_sems.at[index])

    for index in range(chunks):
        bits_copy(index).start()
        exposure_copy(index).start()

    used = used_currencies(currencies_ref[...], counts_ref[...])
    used_ref[...] = used
    notional = notional_ref[...]
    currency = lax.broadcasted_iota(jnp.int32, (currency_count, sets), 0)
    weights = jnp.zeros((currency_count, sets), jnp.float32)
    for slot in range(used.shape[0]):
        weights = weights + jnp.where(
            currency == used[slot : slot + 1], notional[slot : slot + 1], 0.0
        )
    weights = weights.astype(jnp.bfloat16)

    row = lax.broadcasted_iota(jnp.int32, (8, lanes), 0)

    def flag_of(tile):
        shift = row + (8 * tile) % bits_per_row
        shift = jnp.where(shift >= bits_per_row, shift - bits_per_row, shift)
        return jnp.left_shift(jnp.int32(1), shift)

    def mask_columns(first, count):
        for pair in range(sets // 16):
            flags = [flag_of(2 * pair), flag_of(2 * pair + 1)]
            for block in range(count):
                part = pl.ds(first + block * lanes, lanes)
                values = exposure[16 * pair : 16 * pair + 16, part].astype(jnp.float32)
                kept = []
                for half in range(2):
                    top = 16 * pair + 8 * half
                    group = top // bits_per_row
                    left = bits_per_row * (group + 1) - top
                    packed = jnp.broadcast_to(bits[group : group + 1, part], (8, lanes))
                    if left < 8:
                        following = jnp.broadcast_to(bits[group + 1 : group + 2, part], (8, lanes))
                        packed = jnp.where(row < left, packed, following)
                    kept.append(
                        jnp.where(
                            (packed & flags[half]) != 0, values[8 * half : 8 * half + 8], 0.0
                        )
                    )
                masked[16 * pair : 16 * pair + 16, part] = jnp.concatenate(kept, axis=0).astype(
                    jnp.bfloat16
                )

    group_width = min(width, 256)

    for index in range(chunks):
        bits_copy(index).wait()
        exposure_copy(index).wait()

        def some_columns(step):
            first = index * width + step * group_width
            if not isinstance(first, int):
                first = pl.multiple_of(first, group_width)
            mask_columns(first, group_width // lanes)
            terms = jnp.dot(
                weights, masked[:, pl.ds(first, group_width)], preferred_element_type=jnp.float32
            ).astype(jnp.bfloat16)
            for block in range(group_width // owned):
                terms_ref[first // owned + block] = terms[:, block * owned : (block + 1) * owned]

        if width == group_width:
            some_columns(0)
        else:
            pl.loop(0, width // group_width)(some_columns)


def projection_kernel(carried_ref, masked, used_ref, notional_adjoint_ref):
    sets, columns = masked.shape
    blocks, currency_count, owned = carried_ref.shape
    width = columns // chunks
    projected = jnp.zeros((sets, currency_count), jnp.float32)
    for index in range(chunks):
        here = width // owned
        carried = jnp.concatenate([carried_ref[index * here + b] for b in range(here)], axis=1)
        projected = projected + lax.dot_general(
            masked[:, index * width : (index + 1) * width],
            carried,
            (((1,), (1,)), ((), ())),
            preferred_element_type=jnp.float32,
        )
    projected = projected.T
    used = used_ref[...]
    currency = lax.broadcasted_iota(jnp.int32, (currency_count, sets), 0)
    for slot in range(used.shape[0]):
        picked = jnp.sum(
            jnp.where(currency == used[slot : slot + 1], projected, 0.0), axis=0, keepdims=True
        )
        notional_adjoint_ref[slot : slot + 1, :] = picked * (1.0 / math.sqrt(columns))


def final_kernel(dates, parts_ref, fx_ref, discount_ref, fx_adjoint_ref, rate_adjoint_ref):
    aggregate = parts_ref[0].astype(jnp.float32)
    for peer in range(1, parts_ref.shape[0]):
        aggregate = aggregate + parts_ref[peer].astype(jnp.float32)
    fx_adjoint = aggregate * discount_ref[...]
    fx_adjoint_ref[...] = fx_adjoint
    rate_adjoint_ref[...] = -step_years * sums_from_date(fx_adjoint * fx_ref[...], dates)


def body(
    exposure_adjoint,
    positive_bits,
    currencies,
    mix_count,
    notional,
    fx_paths,
    short_rates,
    start_integral,
):
    sets, columns = exposure_adjoint.shape
    currency_count, owned = fx_paths.shape
    dates = owned // start_integral.shape[1]
    peers = columns // owned
    slots = currencies.shape[1]
    in_vmem = pl.BlockSpec(memory_space=pltpu.VMEM)
    anywhere = pl.BlockSpec(memory_space=pl.ANY)
    params = pltpu.CompilerParams(vmem_limit_bytes=32 * 2**20)

    def in_hbm(value):
        return pltpu.with_memory_space_constraint(value, pltpu.HBM)

    block = (currency_count, owned)
    carried, discount = pl.pallas_call(
        functools.partial(carry_kernel, dates),
        out_shape=(
            pltpu.VMEM((peers,) + block, jnp.bfloat16),
            pltpu.VMEM(block, jnp.float32),
        ),
        in_specs=[in_vmem] * 3,
        out_specs=(in_vmem,) * 2,
        compiler_params=params,
        name="carry",
    )(in_hbm(fx_paths), in_hbm(short_rates), in_hbm(start_integral.T))
    carried = lax.all_to_all(carried, "sets", 0, 0, tiled=True)
    masked, terms, used = pl.pallas_call(
        local_kernel,
        out_shape=(
            pltpu.VMEM((sets, columns), jnp.bfloat16),
            pltpu.VMEM((peers,) + block, jnp.bfloat16),
            pltpu.VMEM((slots, sets), jnp.int32),
        ),
        in_specs=[anywhere] * 2 + [in_vmem] * 3,
        out_specs=(in_vmem,) * 3,
        scratch_shapes=[
            pltpu.VMEM((sets, columns), jnp.bfloat16),
            pltpu.VMEM(positive_bits.shape, jnp.int32),
            pltpu.SemaphoreType.DMA((chunks,)),
            pltpu.SemaphoreType.DMA((chunks,)),
        ],
        compiler_params=params,
        name="local",
    )(
        in_hbm(exposure_adjoint),
        in_hbm(positive_bits),
        in_hbm(currencies.T),
        in_hbm(mix_count.reshape(1, sets)),
        in_hbm(notional.T),
    )
    parts = lax.all_to_all(terms, "sets", 0, 0, tiled=True)
    notional_adjoint = pl.pallas_call(
        projection_kernel,
        out_shape=jax.ShapeDtypeStruct((slots, sets), jnp.float32),
        in_specs=[in_vmem] * 3,
        out_specs=in_vmem,
        compiler_params=params,
        name="projection",
    )(carried, masked, used)
    fx_adjoint, rate_adjoint = pl.pallas_call(
        functools.partial(final_kernel, dates),
        out_shape=(jax.ShapeDtypeStruct(block, jnp.float32),) * 2,
        in_specs=[in_vmem] * 3,
        out_specs=(in_vmem,) * 2,
        compiler_params=params,
        name="final",
    )(parts, fx_paths, discount)
    return fx_adjoint, rate_adjoint, notional_adjoint.T


def solution(mesh):
    in_specs = (
        P(("grp", "sets"), None),
        P(("grp", "sets"), None),
        P(("grp", "sets"), None),
        P(("grp", "sets")),
        P(("grp", "sets"), None),
        P("grp", "sets"),
        P("grp", "sets"),
        P("grp", "sets"),
    )
    out_specs = (P("grp", "sets"), P("grp", "sets"), P(("grp", "sets"), None))
    return jax.shard_map(body, mesh=mesh, in_specs=in_specs, out_specs=out_specs, check_vma=False)
```

```python
import functools
import math

import jax
import jax.numpy as jnp
from jax import lax
from jax.experimental import pallas as pl
from jax.experimental.pallas import tpu as pltpu
from jax.sharding import PartitionSpec as P

step_years = 0.25
bits_per_row = 15
lanes = 128
chunks = 2


def spread_paths(values, dates):
    paths, columns = values.shape[0], values.shape[0] * dates
    path_of = lax.broadcasted_iota(jnp.int32, (paths, columns), 1) // dates
    own = lax.broadcasted_iota(jnp.int32, (paths, columns), 0)
    return lax.dot_general(
        values,
        (path_of == own).astype(jnp.float32),
        (((0,), (0,)), ((), ())),
        precision=lax.Precision.HIGHEST,
        preferred_element_type=jnp.float32,
    )


def sums_to_date(values, dates):
    width = values.shape[1]
    date = lax.broadcasted_iota(jnp.int32, values.shape, 1) % dates
    step = 1
    while step < dates:
        values = values + jnp.where(date >= step, pltpu.roll(values, step, 1), 0.0)
        step *= 2
    return values


def sums_from_date(values, dates):
    width = values.shape[1]
    date = lax.broadcasted_iota(jnp.int32, values.shape, 1) % dates
    step = 1
    while step < dates:
        values = values + jnp.where(date < dates - step, pltpu.roll(values, width - step, 1), 0.0)
        step *= 2
    return values


def used_currencies(currencies, counts):
    slot = lax.broadcasted_iota(jnp.int32, currencies.shape, 0)
    return jnp.where(slot < counts, currencies, -1)


def group_order(peers):
    first = max(peers - 2, 0)
    return [peer ^ first for peer in range(peers)]


def local_kernel(
    dates,
    exposure_hbm,
    bits_hbm,
    currencies_ref,
    counts_ref,
    notional_ref,
    fx_ref,
    rates_ref,
    start_ref,
    outgoing_ref,
    masked_ref,
    discount_ref,
    moved_ref,
    used_ref,
    exposure,
    bits,
    in_sems,
    bits_sems,
):
    sets, columns = exposure.shape
    currency_count, owned = fx_ref.shape
    peers = columns // owned
    width = columns // chunks
    place = group_order(peers)

    def exposure_copy(index):
        part = pl.ds(index * width, width)
        return pltpu.make_async_copy(
            exposure_hbm.at[:, part], exposure.at[:, part], in_sems.at[index]
        )

    def bits_copy(index):
        part = pl.ds(index * width, width)
        return pltpu.make_async_copy(bits_hbm.at[:, part], bits.at[:, part], bits_sems.at[index])

    for index in range(chunks):
        bits_copy(index).start()
        exposure_copy(index).start()

    used = used_currencies(currencies_ref[...], counts_ref[...])
    used_ref[...] = used
    notional = notional_ref[...]
    currency = lax.broadcasted_iota(jnp.int32, (currency_count, sets), 0)
    weights = jnp.zeros((currency_count, sets), jnp.float32)
    for slot in range(used.shape[0]):
        weights = weights + jnp.where(
            currency == used[slot : slot + 1], notional[slot : slot + 1], 0.0
        )
    weights = weights.astype(jnp.bfloat16)

    integral = spread_paths(start_ref[...], dates) + step_years * sums_to_date(rates_ref[...], dates)
    discount = jnp.exp(-integral)
    discount_ref[...] = discount
    moved = fx_ref[...] * discount
    moved_ref[...] = moved
    carried = moved.astype(jnp.bfloat16)
    for peer in range(peers):
        outgoing_ref[peer, 0:currency_count, :] = carried

    row = lax.broadcasted_iota(jnp.int32, (8, lanes), 0)

    def flag_of(tile):
        shift = row + (8 * tile) % bits_per_row
        shift = jnp.where(shift >= bits_per_row, shift - bits_per_row, shift)
        return jnp.left_shift(jnp.int32(1), shift)

    def masked_rows(pair, flags, part):
        values = exposure[16 * pair : 16 * pair + 16, part].astype(jnp.float32)
        kept = []
        for half in range(2):
            top = 16 * pair + 8 * half
            group = top // bits_per_row
            left = bits_per_row * (group + 1) - top
            packed = jnp.broadcast_to(bits[group : group + 1, part], (8, lanes))
            if left < 8:
                following = jnp.broadcast_to(bits[group + 1 : group + 2, part], (8, lanes))
                packed = jnp.where(row < left, packed, following)
            kept.append(
                jnp.where((packed & flags[half]) != 0, values[8 * half : 8 * half + 8], 0.0)
            )
        return jnp.concatenate(kept, axis=0).astype(jnp.bfloat16)

    group_width = min(width, 1024)
    dot_width = min(group_width, 256)

    for index in range(chunks):
        bits_copy(index).wait()
        exposure_copy(index).wait()

        def some_columns(step):
            first = index * width + step * group_width
            if not isinstance(first, int):
                first = pl.multiple_of(first, group_width)
            for pair in range(sets // 16):
                flags = [flag_of(2 * pair), flag_of(2 * pair + 1)]
                for block in range(group_width // lanes):
                    part = pl.ds(first + block * lanes, lanes)
                    masked_ref[16 * pair : 16 * pair + 16, part] = masked_rows(pair, flags, part)
            for dot in range(group_width // dot_width):
                terms = jnp.dot(
                    weights,
                    masked_ref[:, pl.ds(first + dot * dot_width, dot_width)],
                    preferred_element_type=jnp.float32,
                ).astype(jnp.bfloat16)
                for block in range(dot_width // owned):
                    peer = (first + dot * dot_width) // owned + block
                    where = place[peer] if isinstance(peer, int) else peer ^ place[0]
                    outgoing_ref[where, currency_count:, :] = terms[
                        :, block * owned : (block + 1) * owned
                    ]

        if width == group_width:
            some_columns(0)
        else:
            pl.loop(0, width // group_width)(some_columns)


def final_kernel(
    dates,
    arrived_ref,
    masked,
    used_ref,
    moved_ref,
    discount_ref,
    fx_adjoint_ref,
    rate_adjoint_ref,
    notional_adjoint_ref,
):
    sets, columns = masked.shape
    currency_count, owned = moved_ref.shape
    peers = columns // owned
    place = group_order(peers)

    aggregate = arrived_ref[0, currency_count:, :].astype(jnp.float32)
    for peer in range(1, peers):
        aggregate = aggregate + arrived_ref[peer, currency_count:, :].astype(jnp.float32)
    fx_adjoint_ref[...] = aggregate * discount_ref[...]
    rate_adjoint_ref[...] = -step_years * sums_from_date(aggregate * moved_ref[...], dates)

    width = min(columns, 2048)
    projected = jnp.zeros((sets, currency_count), jnp.float32)
    for index in range(columns // width):
        here = width // owned
        carried = jnp.concatenate(
            [
                arrived_ref[place[index * here + block], 0:currency_count, :]
                for block in range(here)
            ],
            axis=1,
        )
        projected = projected + lax.dot_general(
            masked[:, index * width : (index + 1) * width],
            carried,
            (((1,), (1,)), ((), ())),
            preferred_element_type=jnp.float32,
        )
    projected = projected.T
    used = used_ref[...]
    currency = lax.broadcasted_iota(jnp.int32, (currency_count, sets), 0)
    for slot in range(used.shape[0]):
        picked = jnp.sum(
            jnp.where(currency == used[slot : slot + 1], projected, 0.0), axis=0, keepdims=True
        )
        notional_adjoint_ref[slot : slot + 1, :] = picked * (1.0 / math.sqrt(columns))


def body(
    exposure_adjoint,
    positive_bits,
    currencies,
    mix_count,
    notional,
    fx_paths,
    short_rates,
    start_integral,
):
    sets, columns = exposure_adjoint.shape
    currency_count, owned = fx_paths.shape
    dates = owned // start_integral.shape[1]
    peers = columns // owned
    slots = currencies.shape[1]
    in_vmem = pl.BlockSpec(memory_space=pltpu.VMEM)
    anywhere = pl.BlockSpec(memory_space=pl.ANY)
    params = pltpu.CompilerParams(vmem_limit_bytes=32 * 2**20)
    block = (currency_count, owned)

    def in_hbm(value):
        return pltpu.with_memory_space_constraint(value, pltpu.HBM)

    outgoing, masked, discount, moved, used = pl.pallas_call(
        functools.partial(local_kernel, dates),
        out_shape=(
            pltpu.VMEM((peers, 2 * currency_count, owned), jnp.bfloat16),
            pltpu.VMEM((sets, columns), jnp.bfloat16),
            pltpu.VMEM(block, jnp.float32),
            pltpu.VMEM(block, jnp.float32),
            pltpu.VMEM((slots, sets), jnp.int32),
        ),
        in_specs=[anywhere] * 2 + [in_vmem] * 6,
        out_specs=(in_vmem,) * 5,
        scratch_shapes=[
            pltpu.VMEM((sets, columns), jnp.bfloat16),
            pltpu.VMEM(positive_bits.shape, jnp.int32),
            pltpu.SemaphoreType.DMA((chunks,)),
            pltpu.SemaphoreType.DMA((chunks,)),
        ],
        compiler_params=params,
        name="local",
    )(
        in_hbm(exposure_adjoint),
        in_hbm(positive_bits),
        in_hbm(currencies.T),
        in_hbm(mix_count.reshape(1, sets)),
        in_hbm(notional.T),
        in_hbm(fx_paths),
        in_hbm(short_rates),
        in_hbm(start_integral.T),
    )
    arrived = lax.all_to_all(
        outgoing, "sets", 0, 0, axis_index_groups=[group_order(peers)], tiled=True
    )
    fx_adjoint, rate_adjoint, notional_adjoint = pl.pallas_call(
        functools.partial(final_kernel, dates),
        out_shape=(
            jax.ShapeDtypeStruct(block, jnp.float32),
            jax.ShapeDtypeStruct(block, jnp.float32),
            jax.ShapeDtypeStruct((slots, sets), jnp.float32),
        ),
        in_specs=[in_vmem] * 5,
        out_specs=(in_vmem,) * 3,
        compiler_params=params,
        name="final",
    )(arrived, masked, used, moved, discount)
    return fx_adjoint, rate_adjoint, notional_adjoint.T


def solution(mesh):
    in_specs = (
        P(("grp", "sets"), None),
        P(("grp", "sets"), None),
        P(("grp", "sets"), None),
        P(("grp", "sets")),
        P(("grp", "sets"), None),
        P("grp", "sets"),
        P("grp", "sets"),
        P("grp", "sets"),
    )
    out_specs = (P("grp", "sets"), P("grp", "sets"), P(("grp", "sets"), None))
    return jax.shard_map(body, mesh=mesh, in_specs=in_specs, out_specs=out_specs, check_vma=False)
```

```python
import functools
import math

import jax
import jax.numpy as jnp
from jax import lax
from jax.experimental import pallas as pl
from jax.experimental.pallas import tpu as pltpu
from jax.sharding import PartitionSpec as P

step_years = 0.25
bits_per_row = 15
lanes = 128
chunks = 2


def spread_paths(values, dates):
    paths, columns = values.shape[0], values.shape[0] * dates
    path_of = lax.broadcasted_iota(jnp.int32, (paths, columns), 1) // dates
    own = lax.broadcasted_iota(jnp.int32, (paths, columns), 0)
    return lax.dot_general(
        values,
        (path_of == own).astype(jnp.float32),
        (((0,), (0,)), ((), ())),
        precision=lax.Precision.HIGHEST,
        preferred_element_type=jnp.float32,
    )


def sums_to_date(values, dates):
    width = values.shape[1]
    date = lax.broadcasted_iota(jnp.int32, values.shape, 1) % dates
    step = 1
    while step < dates:
        values = values + jnp.where(date >= step, pltpu.roll(values, step, 1), 0.0)
        step *= 2
    return values


def sums_from_date(values, dates):
    width = values.shape[1]
    date = lax.broadcasted_iota(jnp.int32, values.shape, 1) % dates
    step = 1
    while step < dates:
        values = values + jnp.where(date < dates - step, pltpu.roll(values, width - step, 1), 0.0)
        step *= 2
    return values


def used_currencies(currencies, counts):
    slot = lax.broadcasted_iota(jnp.int32, currencies.shape, 0)
    return jnp.where(slot < counts, currencies, -1)


def group_order(peers):
    near = min(4, peers)
    far = peers // near
    planes = []
    for step in range((far + 1) // 2):
        planes += [far - 1 - step, step]
    planes = planes[:far]
    return [plane * near + (index ^ (near // 2)) for index in range(near) for plane in planes]


def local_kernel(
    dates,
    exposure_hbm,
    bits_hbm,
    currencies_hbm,
    counts_hbm,
    notional_hbm,
    fx_hbm,
    rates_hbm,
    start_hbm,
    outgoing_ref,
    masked_ref,
    discount_ref,
    moved_ref,
    used_ref,
    exposure,
    bits,
    currencies_ref,
    counts_ref,
    notional_ref,
    fx_ref,
    rates_ref,
    start_ref,
    in_sems,
    bits_sems,
    small_sems,
):
    sets, columns = exposure.shape
    currency_count, owned = fx_ref.shape
    peers = columns // owned
    width = columns // chunks
    order = group_order(peers)
    place = [order.index(peer) for peer in range(peers)]

    def exposure_copy(index):
        part = pl.ds(index * width, width)
        return pltpu.make_async_copy(
            exposure_hbm.at[:, part], exposure.at[:, part], in_sems.at[index]
        )

    def bits_copy(index):
        part = pl.ds(index * width, width)
        return pltpu.make_async_copy(bits_hbm.at[:, part], bits.at[:, part], bits_sems.at[index])

    small_copies = [
        pltpu.make_async_copy(source, target, small_sems.at[index])
        for index, (source, target) in enumerate(
            [
                (rates_hbm, rates_ref),
                (start_hbm, start_ref),
                (fx_hbm, fx_ref),
                (currencies_hbm, currencies_ref),
                (counts_hbm, counts_ref),
                (notional_hbm, notional_ref),
            ]
        )
    ]
    for copy in small_copies:
        copy.start()
    for index in range(chunks):
        bits_copy(index).start()
        exposure_copy(index).start()
    for copy in small_copies:
        copy.wait()

    used = used_currencies(currencies_ref[...], counts_ref[...])
    used_ref[...] = used
    notional = notional_ref[...]
    currency = lax.broadcasted_iota(jnp.int32, (currency_count, sets), 0)
    weights = jnp.zeros((currency_count, sets), jnp.float32)
    for slot in range(used.shape[0]):
        weights = weights + jnp.where(
            currency == used[slot : slot + 1], notional[slot : slot + 1], 0.0
        )
    weights = weights.astype(jnp.bfloat16)

    integral = spread_paths(start_ref[...], dates) + step_years * sums_to_date(rates_ref[...], dates)
    discount = jnp.exp(-integral)
    discount_ref[...] = discount
    moved = fx_ref[...] * discount
    moved_ref[...] = moved
    carried = moved.astype(jnp.bfloat16)
    for peer in range(peers):
        outgoing_ref[peer, 0:currency_count, :] = carried

    row = lax.broadcasted_iota(jnp.int32, (8, lanes), 0)

    def flag_of(tile):
        shift = row + (8 * tile) % bits_per_row
        shift = jnp.where(shift >= bits_per_row, shift - bits_per_row, shift)
        return jnp.left_shift(jnp.int32(1), shift)

    def masked_rows(pair, flags, part):
        values = exposure[16 * pair : 16 * pair + 16, part].astype(jnp.float32)
        kept = []
        for half in range(2):
            top = 16 * pair + 8 * half
            group = top // bits_per_row
            left = bits_per_row * (group + 1) - top
            packed = jnp.broadcast_to(bits[group : group + 1, part], (8, lanes))
            if left < 8:
                following = jnp.broadcast_to(bits[group + 1 : group + 2, part], (8, lanes))
                packed = jnp.where(row < left, packed, following)
            kept.append(
                jnp.where((packed & flags[half]) != 0, values[8 * half : 8 * half + 8], 0.0)
            )
        return jnp.concatenate(kept, axis=0).astype(jnp.bfloat16)

    group_width = min(width, 1024)
    dot_width = min(group_width, 256)

    for index in range(chunks):
        bits_copy(index).wait()
        exposure_copy(index).wait()

        for first in range(index * width, (index + 1) * width, group_width):
            for pair in range(sets // 16):
                flags = [flag_of(2 * pair), flag_of(2 * pair + 1)]
                for block in range(group_width // lanes):
                    part = pl.ds(first + block * lanes, lanes)
                    masked_ref[16 * pair : 16 * pair + 16, part] = masked_rows(pair, flags, part)
            for dot in range(group_width // dot_width):
                terms = jnp.dot(
                    weights,
                    masked_ref[:, pl.ds(first + dot * dot_width, dot_width)],
                    preferred_element_type=jnp.float32,
                ).astype(jnp.bfloat16)
                for block in range(dot_width // owned):
                    peer = (first + dot * dot_width) // owned + block
                    outgoing_ref[place[peer], currency_count:, :] = terms[
                        :, block * owned : (block + 1) * owned
                    ]


def final_kernel(
    dates,
    arrived_ref,
    masked,
    used_ref,
    moved_ref,
    discount_ref,
    fx_adjoint_ref,
    rate_adjoint_ref,
    notional_adjoint_ref,
):
    sets, columns = masked.shape
    currency_count, owned = moved_ref.shape
    peers = columns // owned
    order = group_order(peers)
    place = [order.index(peer) for peer in range(peers)]

    aggregate = arrived_ref[0, currency_count:, :].astype(jnp.float32)
    for peer in range(1, peers):
        aggregate = aggregate + arrived_ref[peer, currency_count:, :].astype(jnp.float32)
    fx_adjoint_ref[...] = aggregate * discount_ref[...]
    rate_adjoint_ref[...] = -step_years * sums_from_date(aggregate * moved_ref[...], dates)

    width = min(columns, 2048)
    projected = jnp.zeros((sets, currency_count), jnp.float32)
    for index in range(columns // width):
        here = width // owned
        carried = jnp.concatenate(
            [
                arrived_ref[place[index * here + block], 0:currency_count, :]
                for block in range(here)
            ],
            axis=1,
        )
        projected = projected + lax.dot_general(
            masked[:, index * width : (index + 1) * width],
            carried,
            (((1,), (1,)), ((), ())),
            preferred_element_type=jnp.float32,
        )
    projected = projected.T
    used = used_ref[...]
    currency = lax.broadcasted_iota(jnp.int32, (currency_count, sets), 0)
    for slot in range(used.shape[0]):
        picked = jnp.sum(
            jnp.where(currency == used[slot : slot + 1], projected, 0.0), axis=0, keepdims=True
        )
        notional_adjoint_ref[slot : slot + 1, :] = picked * (1.0 / math.sqrt(columns))


def body(
    exposure_adjoint,
    positive_bits,
    currencies,
    mix_count,
    notional,
    fx_paths,
    short_rates,
    start_integral,
):
    sets, columns = exposure_adjoint.shape
    currency_count, owned = fx_paths.shape
    dates = owned // start_integral.shape[1]
    peers = columns // owned
    slots = currencies.shape[1]
    in_vmem = pl.BlockSpec(memory_space=pltpu.VMEM)
    anywhere = pl.BlockSpec(memory_space=pl.ANY)
    params = pltpu.CompilerParams(vmem_limit_bytes=32 * 2**20)
    block = (currency_count, owned)

    def in_hbm(value):
        return pltpu.with_memory_space_constraint(value, pltpu.HBM)

    outgoing, masked, discount, moved, used = pl.pallas_call(
        functools.partial(local_kernel, dates),
        out_shape=(
            pltpu.VMEM((peers, 2 * currency_count, owned), jnp.bfloat16),
            pltpu.VMEM((sets, columns), jnp.bfloat16),
            pltpu.VMEM(block, jnp.float32),
            pltpu.VMEM(block, jnp.float32),
            pltpu.VMEM((slots, sets), jnp.int32),
        ),
        in_specs=[anywhere] * 8,
        out_specs=(in_vmem,) * 5,
        scratch_shapes=[
            pltpu.VMEM((sets, columns), jnp.bfloat16),
            pltpu.VMEM(positive_bits.shape, jnp.int32),
            pltpu.VMEM((slots, sets), jnp.int32),
            pltpu.VMEM((1, sets), jnp.int32),
            pltpu.VMEM((slots, sets), jnp.float32),
            pltpu.VMEM(block, jnp.float32),
            pltpu.VMEM(block, jnp.float32),
            pltpu.VMEM((owned // dates, currency_count), jnp.float32),
            pltpu.SemaphoreType.DMA((chunks,)),
            pltpu.SemaphoreType.DMA((chunks,)),
            pltpu.SemaphoreType.DMA((6,)),
        ],
        compiler_params=params,
        name="local",
    )(
        in_hbm(exposure_adjoint),
        in_hbm(positive_bits),
        in_hbm(currencies.T),
        in_hbm(mix_count.reshape(1, sets)),
        in_hbm(notional.T),
        in_hbm(fx_paths),
        in_hbm(short_rates),
        in_hbm(start_integral.T),
    )
    arrived = lax.all_to_all(
        outgoing, "sets", 0, 0, axis_index_groups=[group_order(peers)], tiled=True
    )
    fx_adjoint, rate_adjoint, notional_adjoint = pl.pallas_call(
        functools.partial(final_kernel, dates),
        out_shape=(
            jax.ShapeDtypeStruct(block, jnp.float32),
            jax.ShapeDtypeStruct(block, jnp.float32),
            jax.ShapeDtypeStruct((slots, sets), jnp.float32),
        ),
        in_specs=[in_vmem] * 5,
        out_specs=(in_vmem,) * 3,
        compiler_params=params,
        name="final",
    )(arrived, masked, used, moved, discount)
    return fx_adjoint, rate_adjoint, notional_adjoint.T


def solution(mesh):
    in_specs = (
        P(("grp", "sets"), None),
        P(("grp", "sets"), None),
        P(("grp", "sets"), None),
        P(("grp", "sets")),
        P(("grp", "sets"), None),
        P("grp", "sets"),
        P("grp", "sets"),
        P("grp", "sets"),
    )
    out_specs = (P("grp", "sets"), P("grp", "sets"), P(("grp", "sets"), None))
    return jax.shard_map(body, mesh=mesh, in_specs=in_specs, out_specs=out_specs, check_vma=False)
```

```python
import functools
import math

import jax
import jax.numpy as jnp
from jax import lax
from jax.experimental import pallas as pl
from jax.experimental.pallas import tpu as pltpu
from jax.sharding import PartitionSpec as P

step_years = 0.25
bits_per_row = 15
lanes = 128
chunks = 2


def spread_paths(values, dates):
    paths, columns = values.shape[0], values.shape[0] * dates
    path_of = lax.broadcasted_iota(jnp.int32, (paths, columns), 1) // dates
    own = lax.broadcasted_iota(jnp.int32, (paths, columns), 0)
    return lax.dot_general(
        values,
        (path_of == own).astype(jnp.float32),
        (((0,), (0,)), ((), ())),
        precision=lax.Precision.HIGHEST,
        preferred_element_type=jnp.float32,
    )


def sums_to_date(values, dates):
    width = values.shape[1]
    date = lax.broadcasted_iota(jnp.int32, values.shape, 1) % dates
    step = 1
    while step < dates:
        values = values + jnp.where(date >= step, pltpu.roll(values, step, 1), 0.0)
        step *= 2
    return values


def sums_from_date(values, dates):
    width = values.shape[1]
    date = lax.broadcasted_iota(jnp.int32, values.shape, 1) % dates
    step = 1
    while step < dates:
        values = values + jnp.where(date < dates - step, pltpu.roll(values, width - step, 1), 0.0)
        step *= 2
    return values


def used_currencies(currencies, counts):
    slot = lax.broadcasted_iota(jnp.int32, currencies.shape, 0)
    return jnp.where(slot < counts, currencies, -1)


def group_order(chips):
    first = chips - 1
    return [chip ^ first for chip in range(chips)]


def sibling_columns(chip, owned, core):
    return pl.ds(pl.multiple_of((2 * chip + core) * owned, owned), owned)


def row_flags(tile):
    shift = lax.broadcasted_iota(jnp.int32, (8, lanes), 0) + (8 * tile) % bits_per_row
    shift = jnp.where(shift >= bits_per_row, shift - bits_per_row, shift)
    return jnp.left_shift(jnp.int32(1), shift)


def masked_rows(exposure, bits, pair, flags, part):
    row = lax.broadcasted_iota(jnp.int32, (8, lanes), 0)
    values = exposure[16 * pair : 16 * pair + 16, part].astype(jnp.float32)
    kept = []
    for half in range(2):
        top = 16 * pair + 8 * half
        group = top // bits_per_row
        left = bits_per_row * (group + 1) - top
        packed = jnp.broadcast_to(bits[group : group + 1, part], (8, lanes))
        if left < 8:
            following = jnp.broadcast_to(bits[group + 1 : group + 2, part], (8, lanes))
            packed = jnp.where(row < left, packed, following)
        kept.append(jnp.where((packed & flags[half]) != 0, values[8 * half : 8 * half + 8], 0.0))
    return jnp.concatenate(kept, axis=0).astype(jnp.bfloat16)


def half_of_columns(exposure, bits, weights, masked_ref, terms_ref, core, first, last):
    sets = exposure.shape[0]
    owned = terms_ref.shape[2]
    for pair in range(sets // 16):
        flags = [row_flags(2 * pair), row_flags(2 * pair + 1)]
        for chip in range(first, last):
            masked_ref[16 * pair : 16 * pair + 16, chip * owned : (chip + 1) * owned] = masked_rows(
                exposure, bits, pair, flags, sibling_columns(chip, owned, core)
            )
    for chip in range(first, last, 2):
        terms = jnp.dot(
            weights,
            masked_ref[:, chip * owned : (chip + 2) * owned],
            preferred_element_type=jnp.float32,
        ).astype(terms_ref.dtype)
        terms_ref[chip] = terms[:, :owned]
        terms_ref[chip + 1] = terms[:, owned:]


def first_kernel(
    dates,
    exposure_hbm,
    bits_hbm,
    currencies_hbm,
    counts_hbm,
    notional_hbm,
    fx_hbm,
    rates_hbm,
    start_hbm,
    handed_ref,
    masked_ref,
    exposure,
    bits,
    weights_ref,
    carried_ref,
    discount_ref,
    moved_ref,
    used_ref,
    currencies_ref,
    counts_ref,
    notional_ref,
    fx_ref,
    rates_ref,
    start_ref,
    in_sems,
    bits_sems,
    small_sems,
):
    sets, columns = exposure.shape
    currency_count, owned = fx_ref.shape
    chips = columns // (2 * owned)
    width = columns // chunks

    def exposure_copy(index):
        part = pl.ds(index * width, width)
        return pltpu.make_async_copy(
            exposure_hbm.at[:, part], exposure.at[:, part], in_sems.at[index]
        )

    def bits_copy(index):
        part = pl.ds(index * width, width)
        return pltpu.make_async_copy(bits_hbm.at[:, part], bits.at[:, part], bits_sems.at[index])

    small_copies = [
        pltpu.make_async_copy(source, target, small_sems.at[index])
        for index, (source, target) in enumerate(
            [
                (rates_hbm, rates_ref),
                (start_hbm, start_ref),
                (fx_hbm, fx_ref),
                (currencies_hbm, currencies_ref),
                (counts_hbm, counts_ref),
                (notional_hbm, notional_ref),
            ]
        )
    ]
    for copy in small_copies:
        copy.start()
    for index in range(chunks):
        bits_copy(index).start()
        exposure_copy(index).start()
    for copy in small_copies:
        copy.wait()

    used = used_currencies(currencies_ref[...], counts_ref[...])
    used_ref[...] = used
    notional = notional_ref[...]
    currency = lax.broadcasted_iota(jnp.int32, (currency_count, sets), 0)
    weights = jnp.zeros((currency_count, sets), jnp.float32)
    for slot in range(used.shape[0]):
        weights = weights + jnp.where(
            currency == used[slot : slot + 1], notional[slot : slot + 1], 0.0
        )
    weights = weights.astype(jnp.bfloat16)
    weights_ref[...] = weights

    integral = spread_paths(start_ref[...], dates) + step_years * sums_to_date(rates_ref[...], dates)
    discount = jnp.exp(-integral)
    discount_ref[...] = discount
    moved = fx_ref[...] * discount
    moved_ref[...] = moved
    carried = moved.astype(jnp.bfloat16)
    carried_ref[...] = carried
    handed_ref[chips] = carried

    other = 1 - lax.axis_index("sets") % 2
    for index in range(chunks):
        bits_copy(index).wait()
        exposure_copy(index).wait()
        here = chips // chunks
        half_of_columns(
            exposure,
            bits,
            weights,
            masked_ref,
            handed_ref,
            other,
            index * here,
            (index + 1) * here,
        )


def second_kernel(exposure, bits, weights_ref, masked_ref, terms_ref):
    half_of_columns(
        exposure,
        bits,
        weights_ref[...],
        masked_ref,
        terms_ref,
        lax.axis_index("sets") % 2,
        0,
        terms_ref.shape[0],
    )


def merging_kernel(given_ref, terms_ref, carried_ref, outgoing_ref):
    chips, currency_count, owned = terms_ref.shape
    order = group_order(chips)
    carried = carried_ref[...]
    sibling = given_ref[chips]
    for place in range(chips):
        outgoing_ref[place, 0:currency_count, :] = carried
        outgoing_ref[place, currency_count : 2 * currency_count, :] = sibling
        outgoing_ref[place, 2 * currency_count :, :] = (
            terms_ref[order[place]] + given_ref[order[place]].astype(jnp.float32)
        ).astype(jnp.bfloat16)


def final_kernel(
    dates,
    arrived_ref,
    masked_other,
    masked_own,
    used_ref,
    moved_ref,
    discount_ref,
    fx_adjoint_ref,
    rate_adjoint_ref,
    notional_adjoint_ref,
):
    sets, half = masked_own.shape
    currency_count, owned = moved_ref.shape
    chips = half // owned
    order = group_order(chips)
    place = [order.index(chip) for chip in range(chips)]

    aggregate = arrived_ref[0, 2 * currency_count :, :].astype(jnp.float32)
    for chip in range(1, chips):
        aggregate = aggregate + arrived_ref[chip, 2 * currency_count :, :].astype(jnp.float32)
    fx_adjoint_ref[...] = aggregate * discount_ref[...]
    rate_adjoint_ref[...] = -step_years * sums_from_date(aggregate * moved_ref[...], dates)

    width = min(half, 1024)
    projected = jnp.zeros((sets, currency_count), jnp.float32)
    for index in range(half // width):
        here = width // owned
        for masked, top in ((masked_own, 0), (masked_other, currency_count)):
            carried = jnp.concatenate(
                [
                    arrived_ref[place[index * here + block], top : top + currency_count, :]
                    for block in range(here)
                ],
                axis=1,
            )
            projected = projected + lax.dot_general(
                masked[:, index * width : (index + 1) * width],
                carried,
                (((1,), (1,)), ((), ())),
                preferred_element_type=jnp.float32,
            )
    projected = projected.T
    used = used_ref[...]
    currency = lax.broadcasted_iota(jnp.int32, (currency_count, sets), 0)
    for slot in range(used.shape[0]):
        picked = jnp.sum(
            jnp.where(currency == used[slot : slot + 1], projected, 0.0), axis=0, keepdims=True
        )
        notional_adjoint_ref[slot : slot + 1, :] = picked * (1.0 / math.sqrt(2 * half))


def body(
    exposure_adjoint,
    positive_bits,
    currencies,
    mix_count,
    notional,
    fx_paths,
    short_rates,
    start_integral,
):
    sets, columns = exposure_adjoint.shape
    currency_count, owned = fx_paths.shape
    dates = owned // start_integral.shape[1]
    peers = columns // owned
    chips = peers // 2
    slots = currencies.shape[1]
    in_vmem = pl.BlockSpec(memory_space=pltpu.VMEM)
    anywhere = pl.BlockSpec(memory_space=pl.ANY)
    params = pltpu.CompilerParams(vmem_limit_bytes=32 * 2**20)
    block = (currency_count, owned)

    def in_hbm(value):
        return pltpu.with_memory_space_constraint(value, pltpu.HBM)

    handed, masked_other, exposure, bits, weights, carried, discount, moved, used = pl.pallas_call(
        functools.partial(first_kernel, dates),
        out_shape=(
            pltpu.VMEM((chips + 1,) + block, jnp.bfloat16),
            pltpu.VMEM((sets, columns // 2), jnp.bfloat16),
            pltpu.VMEM((sets, columns), jnp.bfloat16),
            pltpu.VMEM(positive_bits.shape, jnp.int32),
            pltpu.VMEM((currency_count, sets), jnp.bfloat16),
            pltpu.VMEM(block, jnp.bfloat16),
            pltpu.VMEM(block, jnp.float32),
            pltpu.VMEM(block, jnp.float32),
            pltpu.VMEM((slots, sets), jnp.int32),
        ),
        in_specs=[anywhere] * 8,
        out_specs=(in_vmem,) * 9,
        scratch_shapes=[
            pltpu.VMEM((slots, sets), jnp.int32),
            pltpu.VMEM((1, sets), jnp.int32),
            pltpu.VMEM((slots, sets), jnp.float32),
            pltpu.VMEM(block, jnp.float32),
            pltpu.VMEM(block, jnp.float32),
            pltpu.VMEM((owned // dates, currency_count), jnp.float32),
            pltpu.SemaphoreType.DMA((chunks,)),
            pltpu.SemaphoreType.DMA((chunks,)),
            pltpu.SemaphoreType.DMA((6,)),
        ],
        compiler_params=params,
        name="first",
    )(
        in_hbm(exposure_adjoint),
        in_hbm(positive_bits),
        in_hbm(currencies.T),
        in_hbm(mix_count.reshape(1, sets)),
        in_hbm(notional.T),
        in_hbm(fx_paths),
        in_hbm(short_rates),
        in_hbm(start_integral.T),
    )
    given = lax.ppermute(handed, "sets", [(peer, peer ^ 1) for peer in range(peers)])
    masked_own, terms = pl.pallas_call(
        second_kernel,
        out_shape=(
            pltpu.VMEM((sets, columns // 2), jnp.bfloat16),
            pltpu.VMEM((chips,) + block, jnp.float32),
        ),
        in_specs=[in_vmem] * 3,
        out_specs=(in_vmem,) * 2,
        compiler_params=params,
        name="second",
    )(exposure, bits, weights)
    outgoing = pl.pallas_call(
        merging_kernel,
        out_shape=pltpu.VMEM((chips, 3 * currency_count, owned), jnp.bfloat16),
        in_specs=[in_vmem] * 3,
        out_specs=in_vmem,
        compiler_params=params,
        name="merging",
    )(given, terms, carried)
    arrived = lax.all_to_all(
        outgoing,
        "sets",
        0,
        0,
        axis_index_groups=[[2 * chip + core for chip in group_order(chips)] for core in range(2)],
        tiled=True,
    )
    fx_adjoint, rate_adjoint, notional_adjoint = pl.pallas_call(
        functools.partial(final_kernel, dates),
        out_shape=(
            jax.ShapeDtypeStruct(block, jnp.float32),
            jax.ShapeDtypeStruct(block, jnp.float32),
            jax.ShapeDtypeStruct((slots, sets), jnp.float32),
        ),
        in_specs=[in_vmem] * 6,
        out_specs=(in_vmem,) * 3,
        compiler_params=params,
        name="final",
    )(arrived, masked_other, masked_own, used, moved, discount)
    return fx_adjoint, rate_adjoint, notional_adjoint.T


def solution(mesh):
    in_specs = (
        P(("grp", "sets"), None),
        P(("grp", "sets"), None),
        P(("grp", "sets"), None),
        P(("grp", "sets")),
        P(("grp", "sets"), None),
        P("grp", "sets"),
        P("grp", "sets"),
        P("grp", "sets"),
    )
    out_specs = (P("grp", "sets"), P("grp", "sets"), P(("grp", "sets"), None))
    return jax.shard_map(body, mesh=mesh, in_specs=in_specs, out_specs=out_specs, check_vma=False)
```

```python
import functools
import math

import jax
import jax.numpy as jnp
from jax import lax
from jax.experimental import pallas as pl
from jax.experimental.pallas import tpu as pltpu
from jax.sharding import PartitionSpec as P

step_years = 0.25
bits_per_row = 15
lanes = 128


def spread_paths(values, dates):
    paths, columns = values.shape[0], values.shape[0] * dates
    path_of = lax.broadcasted_iota(jnp.int32, (paths, columns), 1) // dates
    own = lax.broadcasted_iota(jnp.int32, (paths, columns), 0)
    return lax.dot_general(
        values,
        (path_of == own).astype(jnp.float32),
        (((0,), (0,)), ((), ())),
        precision=lax.Precision.HIGHEST,
        preferred_element_type=jnp.float32,
    )


def sums_to_date(values, dates):
    width = values.shape[1]
    date = lax.broadcasted_iota(jnp.int32, values.shape, 1) % dates
    step = 1
    while step < dates:
        values = values + jnp.where(date >= step, pltpu.roll(values, step, 1), 0.0)
        step *= 2
    return values


def sums_from_date(values, dates):
    width = values.shape[1]
    date = lax.broadcasted_iota(jnp.int32, values.shape, 1) % dates
    step = 1
    while step < dates:
        values = values + jnp.where(date < dates - step, pltpu.roll(values, width - step, 1), 0.0)
        step *= 2
    return values


def used_currencies(currencies, counts):
    slot = lax.broadcasted_iota(jnp.int32, currencies.shape, 0)
    return jnp.where(slot < counts, currencies, -1)


def group_order(chips):
    first = chips - 1
    return [chip ^ first for chip in range(chips)]


def sibling_columns(chip, owned, core):
    return pl.ds(pl.multiple_of((2 * chip + core) * owned, owned), owned)


def row_flags(tile):
    shift = lax.broadcasted_iota(jnp.int32, (8, lanes), 0) + (8 * tile) % bits_per_row
    shift = jnp.where(shift >= bits_per_row, shift - bits_per_row, shift)
    return jnp.left_shift(jnp.int32(1), shift)


def masked_rows(exposure, bits, pair, flags, part):
    row = lax.broadcasted_iota(jnp.int32, (8, lanes), 0)
    values = exposure[16 * pair : 16 * pair + 16, part].astype(jnp.float32)
    kept = []
    for half in range(2):
        top = 16 * pair + 8 * half
        group = top // bits_per_row
        left = bits_per_row * (group + 1) - top
        packed = jnp.broadcast_to(bits[group : group + 1, part], (8, lanes))
        if left < 8:
            following = jnp.broadcast_to(bits[group + 1 : group + 2, part], (8, lanes))
            packed = jnp.where(row < left, packed, following)
        kept.append(jnp.where((packed & flags[half]) != 0, values[8 * half : 8 * half + 8], 0.0))
    return jnp.concatenate(kept, axis=0).astype(jnp.bfloat16)


def half_of_columns(exposure, bits, weights, masked_ref, terms_ref, core, first, last):
    sets = exposure.shape[0]
    owned = terms_ref.shape[2]
    for pair in range(sets // 16):
        flags = [row_flags(2 * pair), row_flags(2 * pair + 1)]
        for chip in range(first, last):
            masked_ref[16 * pair : 16 * pair + 16, chip * owned : (chip + 1) * owned] = masked_rows(
                exposure, bits, pair, flags, sibling_columns(chip, owned, core)
            )
    for chip in range(first, last, 2):
        terms = jnp.dot(
            weights,
            masked_ref[:, chip * owned : (chip + 2) * owned],
            preferred_element_type=jnp.float32,
        ).astype(terms_ref.dtype)
        terms_ref[chip] = terms[:, :owned]
        terms_ref[chip + 1] = terms[:, owned:]


def first_kernel(
    exposure_hbm,
    bits_hbm,
    currencies_hbm,
    counts_hbm,
    notional_hbm,
    fx_hbm,
    rates_hbm,
    start_hbm,
    handed_ref,
    masked_ref,
    exposure,
    bits,
    weights_ref,
    used_ref,
    fx_ref,
    rates_ref,
    start_ref,
    currencies_ref,
    counts_ref,
    notional_ref,
    sems,
):
    sets = exposure.shape[0]
    chips, currency_count = handed_ref.shape[:2]
    copies = [
        pltpu.make_async_copy(source, target, sems.at[index])
        for index, (source, target) in enumerate(
            [
                (currencies_hbm, currencies_ref),
                (counts_hbm, counts_ref),
                (notional_hbm, notional_ref),
                (bits_hbm, bits),
                (exposure_hbm, exposure),
                (rates_hbm, rates_ref),
                (start_hbm, start_ref),
                (fx_hbm, fx_ref),
            ]
        )
    ]
    for copy in copies:
        copy.start()
    for copy in copies:
        copy.wait()

    used = used_currencies(currencies_ref[...], counts_ref[...])
    used_ref[...] = used
    notional = notional_ref[...]
    currency = lax.broadcasted_iota(jnp.int32, (currency_count, sets), 0)
    weights = jnp.zeros((currency_count, sets), jnp.float32)
    for slot in range(used.shape[0]):
        weights = weights + jnp.where(
            currency == used[slot : slot + 1], notional[slot : slot + 1], 0.0
        )
    weights = weights.astype(jnp.bfloat16)
    weights_ref[...] = weights
    other = 1 - lax.axis_index("sets") % 2
    half_of_columns(exposure, bits, weights, masked_ref, handed_ref, other, 0, chips)


def second_kernel(
    dates,
    exposure,
    bits,
    weights_ref,
    fx_ref,
    rates_ref,
    start_ref,
    masked_ref,
    terms_ref,
    carried_ref,
    discount_ref,
    moved_ref,
):
    integral = spread_paths(start_ref[...], dates) + step_years * sums_to_date(rates_ref[...], dates)
    discount = jnp.exp(-integral)
    discount_ref[...] = discount
    moved = fx_ref[...] * discount
    moved_ref[...] = moved
    carried_ref[...] = moved.astype(jnp.bfloat16)
    half_of_columns(
        exposure,
        bits,
        weights_ref[...],
        masked_ref,
        terms_ref,
        lax.axis_index("sets") % 2,
        0,
        terms_ref.shape[0],
    )


def merging_kernel(given_ref, terms_ref, carried_ref, outgoing_ref):
    chips, currency_count, owned = terms_ref.shape
    order = group_order(chips)
    carried = carried_ref[...]
    for place in range(chips):
        outgoing_ref[place, 0:currency_count, :] = carried
        outgoing_ref[place, currency_count:, :] = (
            terms_ref[order[place]] + given_ref[order[place]].astype(jnp.float32)
        ).astype(jnp.bfloat16)


def unpacking_kernel(arrived_ref, carried_ref):
    chips, currency_count, owned = carried_ref.shape
    order = group_order(chips)
    for place in range(chips):
        carried_ref[order[place]] = arrived_ref[place, 0:currency_count, :]


def projection(masked, carried_ref):
    sets, half = masked.shape
    chips, currency_count, owned = carried_ref.shape
    here = min(chips, 8)
    projected = jnp.zeros((sets, currency_count), jnp.float32)
    for first in range(0, chips, here):
        carried = jnp.concatenate([carried_ref[first + chip] for chip in range(here)], axis=1)
        projected = projected + lax.dot_general(
            masked[:, first * owned : (first + here) * owned],
            carried,
            (((1,), (1,)), ((), ())),
            preferred_element_type=jnp.float32,
        )
    return projected


def adjoint_kernel(
    dates,
    arrived_ref,
    carried_ref,
    masked_own,
    moved_ref,
    discount_ref,
    fx_adjoint_ref,
    rate_adjoint_ref,
    projected_ref,
):
    chips, currency_count, owned = carried_ref.shape
    aggregate = arrived_ref[0, currency_count:, :].astype(jnp.float32)
    for chip in range(1, chips):
        aggregate = aggregate + arrived_ref[chip, currency_count:, :].astype(jnp.float32)
    fx_adjoint_ref[...] = aggregate * discount_ref[...]
    rate_adjoint_ref[...] = -step_years * sums_from_date(aggregate * moved_ref[...], dates)
    projected_ref[...] = projection(masked_own, carried_ref)


def picking_kernel(carried_ref, masked_other, projected_ref, used_ref, notional_adjoint_ref):
    sets, half = masked_other.shape
    currency_count = carried_ref.shape[1]
    projected = (projected_ref[...] + projection(masked_other, carried_ref)).T
    used = used_ref[...]
    currency = lax.broadcasted_iota(jnp.int32, (currency_count, sets), 0)
    for slot in range(used.shape[0]):
        picked = jnp.sum(
            jnp.where(currency == used[slot : slot + 1], projected, 0.0), axis=0, keepdims=True
        )
        notional_adjoint_ref[slot : slot + 1, :] = picked * (1.0 / math.sqrt(2 * half))


def body(
    exposure_adjoint,
    positive_bits,
    currencies,
    mix_count,
    notional,
    fx_paths,
    short_rates,
    start_integral,
):
    sets, columns = exposure_adjoint.shape
    currency_count, owned = fx_paths.shape
    dates = owned // start_integral.shape[1]
    peers = columns // owned
    chips = peers // 2
    slots = currencies.shape[1]
    in_vmem = pl.BlockSpec(memory_space=pltpu.VMEM)
    anywhere = pl.BlockSpec(memory_space=pl.ANY)
    params = pltpu.CompilerParams(vmem_limit_bytes=32 * 2**20)
    block = (currency_count, owned)

    def in_hbm(value):
        return pltpu.with_memory_space_constraint(value, pltpu.HBM)

    def swapped(value):
        return lax.ppermute(value, "sets", [(peer, peer ^ 1) for peer in range(peers)])

    handed, masked_other, exposure, bits, weights, used, fx, rates, start = pl.pallas_call(
        first_kernel,
        out_shape=(
            pltpu.VMEM((chips,) + block, jnp.bfloat16),
            pltpu.VMEM((sets, columns // 2), jnp.bfloat16),
            pltpu.VMEM((sets, columns), jnp.bfloat16),
            pltpu.VMEM(positive_bits.shape, jnp.int32),
            pltpu.VMEM((currency_count, sets), jnp.bfloat16),
            pltpu.VMEM((slots, sets), jnp.int32),
            pltpu.VMEM(block, jnp.float32),
            pltpu.VMEM(block, jnp.float32),
            pltpu.VMEM((owned // dates, currency_count), jnp.float32),
        ),
        in_specs=[anywhere] * 8,
        out_specs=(in_vmem,) * 9,
        scratch_shapes=[
            pltpu.VMEM((slots, sets), jnp.int32),
            pltpu.VMEM((1, sets), jnp.int32),
            pltpu.VMEM((slots, sets), jnp.float32),
            pltpu.SemaphoreType.DMA((8,)),
        ],
        compiler_params=params,
        name="first",
    )(
        in_hbm(exposure_adjoint),
        in_hbm(positive_bits),
        in_hbm(currencies.T),
        in_hbm(mix_count.reshape(1, sets)),
        in_hbm(notional.T),
        in_hbm(fx_paths),
        in_hbm(short_rates),
        in_hbm(start_integral.T),
    )
    given = swapped(handed)
    masked_own, terms, carried, discount, moved = pl.pallas_call(
        functools.partial(second_kernel, dates),
        out_shape=(
            pltpu.VMEM((sets, columns // 2), jnp.bfloat16),
            pltpu.VMEM((chips,) + block, jnp.float32),
            pltpu.VMEM(block, jnp.bfloat16),
            pltpu.VMEM(block, jnp.float32),
            pltpu.VMEM(block, jnp.float32),
        ),
        in_specs=[in_vmem] * 6,
        out_specs=(in_vmem,) * 5,
        compiler_params=params,
        name="second",
    )(exposure, bits, weights, fx, rates, start)
    outgoing = pl.pallas_call(
        merging_kernel,
        out_shape=pltpu.VMEM((chips, 2 * currency_count, owned), jnp.bfloat16),
        in_specs=[in_vmem] * 3,
        out_specs=in_vmem,
        compiler_params=params,
        name="merging",
    )(given, terms, carried)
    arrived = lax.all_to_all(
        outgoing,
        "sets",
        0,
        0,
        axis_index_groups=[[2 * chip + core for chip in group_order(chips)] for core in range(2)],
        tiled=True,
    )
    carried_own = pl.pallas_call(
        unpacking_kernel,
        out_shape=pltpu.VMEM((chips,) + block, jnp.bfloat16),
        in_specs=[in_vmem],
        out_specs=in_vmem,
        compiler_params=params,
        name="unpacking",
    )(arrived)
    carried_other = swapped(carried_own)
    fx_adjoint, rate_adjoint, projected = pl.pallas_call(
        functools.partial(adjoint_kernel, dates),
        out_shape=(
            jax.ShapeDtypeStruct(block, jnp.float32),
            jax.ShapeDtypeStruct(block, jnp.float32),
            pltpu.VMEM((sets, currency_count), jnp.float32),
        ),
        in_specs=[in_vmem] * 5,
        out_specs=(in_vmem,) * 3,
        compiler_params=params,
        name="adjoint",
    )(arrived, carried_own, masked_own, moved, discount)
    notional_adjoint = pl.pallas_call(
        picking_kernel,
        out_shape=jax.ShapeDtypeStruct((slots, sets), jnp.float32),
        in_specs=[in_vmem] * 4,
        out_specs=in_vmem,
        compiler_params=params,
        name="picking",
    )(carried_other, masked_other, projected, used)
    return fx_adjoint, rate_adjoint, notional_adjoint.T


def solution(mesh):
    in_specs = (
        P(("grp", "sets"), None),
        P(("grp", "sets"), None),
        P(("grp", "sets"), None),
        P(("grp", "sets")),
        P(("grp", "sets"), None),
        P("grp", "sets"),
        P("grp", "sets"),
        P("grp", "sets"),
    )
    out_specs = (P("grp", "sets"), P("grp", "sets"), P(("grp", "sets"), None))
    return jax.shard_map(body, mesh=mesh, in_specs=in_specs, out_specs=out_specs, check_vma=False)
```

```python
import functools
import math

import jax
import jax.numpy as jnp
from jax import lax
from jax.experimental import pallas as pl
from jax.experimental.pallas import tpu as pltpu
from jax.sharding import PartitionSpec as P

step_years = 0.25
bits_per_row = 15
lanes = 128


def spread_paths(values, dates):
    paths, columns = values.shape[0], values.shape[0] * dates
    path_of = lax.broadcasted_iota(jnp.int32, (paths, columns), 1) // dates
    own = lax.broadcasted_iota(jnp.int32, (paths, columns), 0)
    return lax.dot_general(
        values,
        (path_of == own).astype(jnp.float32),
        (((0,), (0,)), ((), ())),
        precision=lax.Precision.HIGHEST,
        preferred_element_type=jnp.float32,
    )


def sums_to_date(values, dates):
    width = values.shape[1]
    date = lax.broadcasted_iota(jnp.int32, values.shape, 1) % dates
    step = 1
    while step < dates:
        values = values + jnp.where(date >= step, pltpu.roll(values, step, 1), 0.0)
        step *= 2
    return values


def sums_from_date(values, dates):
    width = values.shape[1]
    date = lax.broadcasted_iota(jnp.int32, values.shape, 1) % dates
    step = 1
    while step < dates:
        values = values + jnp.where(date < dates - step, pltpu.roll(values, width - step, 1), 0.0)
        step *= 2
    return values


def used_currencies(currencies, counts):
    slot = lax.broadcasted_iota(jnp.int32, currencies.shape, 0)
    return jnp.where(slot < counts, currencies, -1)


def group_order(chips):
    middle = chips // 2
    return list(range(chips - 1, middle - 1, -1)) + list(range(middle))


def sibling_columns(chip, owned, core):
    return pl.ds(pl.multiple_of((2 * chip + core) * owned, owned), owned)


def row_flags(tile):
    shift = lax.broadcasted_iota(jnp.int32, (8, lanes), 0) + (8 * tile) % bits_per_row
    shift = jnp.where(shift >= bits_per_row, shift - bits_per_row, shift)
    return jnp.left_shift(jnp.int32(1), shift)


def masked_rows(exposure, bits, pair, flags, part):
    row = lax.broadcasted_iota(jnp.int32, (8, lanes), 0)
    values = exposure[16 * pair : 16 * pair + 16, part].astype(jnp.float32)
    kept = []
    for half in range(2):
        top = 16 * pair + 8 * half
        group = top // bits_per_row
        left = bits_per_row * (group + 1) - top
        packed = jnp.broadcast_to(bits[group : group + 1, part], (8, lanes))
        if left < 8:
            following = jnp.broadcast_to(bits[group + 1 : group + 2, part], (8, lanes))
            packed = jnp.where(row < left, packed, following)
        kept.append(jnp.where((packed & flags[half]) != 0, values[8 * half : 8 * half + 8], 0.0))
    return jnp.concatenate(kept, axis=0).astype(jnp.bfloat16)


def mask_rows(exposure, bits, masked_ref, core, owned, first, last):
    for pair in range(first // 16, last // 16):
        flags = [row_flags(2 * pair), row_flags(2 * pair + 1)]
        for chip in range(masked_ref.shape[1] // owned):
            masked_ref[16 * pair : 16 * pair + 16, chip * owned : (chip + 1) * owned] = masked_rows(
                exposure, bits, pair, flags, sibling_columns(chip, owned, core)
            )


def sum_sets(weights, masked_ref, terms_ref):
    owned = terms_ref.shape[2]
    for chip in range(0, terms_ref.shape[0], 2):
        terms = jnp.dot(
            weights,
            masked_ref[:, chip * owned : (chip + 2) * owned],
            preferred_element_type=jnp.float32,
        ).astype(terms_ref.dtype)
        terms_ref[chip] = terms[:, :owned]
        terms_ref[chip + 1] = terms[:, owned:]


def first_kernel(
    exposure_hbm,
    bits_hbm,
    currencies_hbm,
    counts_hbm,
    notional_hbm,
    fx_hbm,
    rates_hbm,
    start_hbm,
    handed_ref,
    masked_ref,
    exposure,
    bits,
    weights_ref,
    used_ref,
    fx_ref,
    rates_ref,
    start_ref,
    currencies_ref,
    counts_ref,
    notional_ref,
    sems,
    exposure_sems,
):
    sets = exposure.shape[0]
    chips, currency_count = handed_ref.shape[:2]
    parts = exposure_sems.shape[0]
    rows = sets // parts

    def exposure_copy(index):
        part = pl.ds(index * rows, rows)
        return pltpu.make_async_copy(
            exposure_hbm.at[part], exposure.at[part], exposure_sems.at[index]
        )

    copies = [
        pltpu.make_async_copy(source, target, sems.at[index])
        for index, (source, target) in enumerate(
            [
                (currencies_hbm, currencies_ref),
                (counts_hbm, counts_ref),
                (notional_hbm, notional_ref),
                (bits_hbm, bits),
                (rates_hbm, rates_ref),
                (start_hbm, start_ref),
                (fx_hbm, fx_ref),
            ]
        )
    ]
    for copy in copies[:4]:
        copy.start()
    for index in range(parts):
        exposure_copy(index).start()
    for copy in copies[4:]:
        copy.start()
    for copy in copies:
        copy.wait()

    used = used_currencies(currencies_ref[...], counts_ref[...])
    used_ref[...] = used
    notional = notional_ref[...]
    currency = lax.broadcasted_iota(jnp.int32, (currency_count, sets), 0)
    weights = jnp.zeros((currency_count, sets), jnp.float32)
    for slot in range(used.shape[0]):
        weights = weights + jnp.where(
            currency == used[slot : slot + 1], notional[slot : slot + 1], 0.0
        )
    weights = weights.astype(jnp.bfloat16)
    weights_ref[...] = weights
    other = 1 - lax.axis_index("sets") % 2
    for index in range(parts):
        exposure_copy(index).wait()
        mask_rows(
            exposure, bits, masked_ref, other, handed_ref.shape[2], index * rows, (index + 1) * rows
        )
    sum_sets(weights, masked_ref, handed_ref)


def second_kernel(
    dates,
    exposure,
    bits,
    weights_ref,
    fx_ref,
    rates_ref,
    start_ref,
    masked_ref,
    terms_ref,
    carried_ref,
    discount_ref,
    moved_ref,
):
    integral = spread_paths(start_ref[...], dates) + step_years * sums_to_date(rates_ref[...], dates)
    discount = jnp.exp(-integral)
    discount_ref[...] = discount
    moved = fx_ref[...] * discount
    moved_ref[...] = moved
    carried_ref[...] = moved.astype(jnp.bfloat16)
    own = lax.axis_index("sets") % 2
    mask_rows(exposure, bits, masked_ref, own, terms_ref.shape[2], 0, exposure.shape[0])
    sum_sets(weights_ref[...], masked_ref, terms_ref)


def merging_kernel(given_ref, terms_ref, carried_ref, outgoing_ref):
    chips, currency_count, owned = terms_ref.shape
    order = group_order(chips)
    carried = carried_ref[...]
    for place in range(chips):
        outgoing_ref[place, 0:currency_count, :] = carried
        outgoing_ref[place, currency_count:, :] = (
            terms_ref[order[place]] + given_ref[order[place]].astype(jnp.float32)
        ).astype(jnp.bfloat16)


def unpacking_kernel(arrived_ref, carried_ref):
    chips, currency_count, owned = carried_ref.shape
    order = group_order(chips)
    for place in range(chips):
        carried_ref[order[place]] = arrived_ref[place, 0:currency_count, :]


def projection(masked, carried_ref):
    sets, half = masked.shape
    chips, currency_count, owned = carried_ref.shape
    here = min(chips, 8)
    projected = jnp.zeros((currency_count, sets), jnp.float32)
    for first in range(0, chips, here):
        carried = jnp.concatenate([carried_ref[first + chip] for chip in range(here)], axis=1)
        projected = projected + lax.dot_general(
            carried,
            masked[:, first * owned : (first + here) * owned],
            (((1,), (1,)), ((), ())),
            preferred_element_type=jnp.float32,
        )
    return projected


def adjoint_kernel(
    dates,
    arrived_ref,
    carried_ref,
    masked_own,
    moved_ref,
    discount_ref,
    fx_adjoint_ref,
    rate_adjoint_ref,
    projected_ref,
):
    chips, currency_count, owned = carried_ref.shape
    aggregate = arrived_ref[0, currency_count:, :].astype(jnp.float32)
    for chip in range(1, chips):
        aggregate = aggregate + arrived_ref[chip, currency_count:, :].astype(jnp.float32)
    fx_adjoint_ref[...] = aggregate * discount_ref[...]
    rate_adjoint_ref[...] = -step_years * sums_from_date(aggregate * moved_ref[...], dates)
    projected_ref[...] = projection(masked_own, carried_ref)


def picking_kernel(carried_ref, masked_other, projected_ref, used_ref, notional_adjoint_ref):
    sets, half = masked_other.shape
    currency_count = carried_ref.shape[1]
    projected = projected_ref[...] + projection(masked_other, carried_ref)
    used = used_ref[...]
    currency = lax.broadcasted_iota(jnp.int32, (currency_count, sets), 0)
    for slot in range(used.shape[0]):
        picked = jnp.sum(
            jnp.where(currency == used[slot : slot + 1], projected, 0.0), axis=0, keepdims=True
        )
        notional_adjoint_ref[slot : slot + 1, :] = picked * (1.0 / math.sqrt(2 * half))


def body(
    exposure_adjoint,
    positive_bits,
    currencies,
    mix_count,
    notional,
    fx_paths,
    short_rates,
    start_integral,
):
    sets, columns = exposure_adjoint.shape
    currency_count, owned = fx_paths.shape
    dates = owned // start_integral.shape[1]
    peers = columns // owned
    chips = peers // 2
    slots = currencies.shape[1]
    in_vmem = pl.BlockSpec(memory_space=pltpu.VMEM)
    anywhere = pl.BlockSpec(memory_space=pl.ANY)
    params = pltpu.CompilerParams(vmem_limit_bytes=32 * 2**20)
    block = (currency_count, owned)

    def in_hbm(value):
        return pltpu.with_memory_space_constraint(value, pltpu.HBM)

    def swapped(value):
        return lax.ppermute(value, "sets", [(peer, peer ^ 1) for peer in range(peers)])

    handed, masked_other, exposure, bits, weights, used, fx, rates, start = pl.pallas_call(
        first_kernel,
        out_shape=(
            pltpu.VMEM((chips,) + block, jnp.bfloat16),
            pltpu.VMEM((sets, columns // 2), jnp.bfloat16),
            pltpu.VMEM((sets, columns), jnp.bfloat16),
            pltpu.VMEM(positive_bits.shape, jnp.int32),
            pltpu.VMEM((currency_count, sets), jnp.bfloat16),
            pltpu.VMEM((slots, sets), jnp.int32),
            pltpu.VMEM(block, jnp.float32),
            pltpu.VMEM(block, jnp.float32),
            pltpu.VMEM((owned // dates, currency_count), jnp.float32),
        ),
        in_specs=[anywhere] * 8,
        out_specs=(in_vmem,) * 9,
        scratch_shapes=[
            pltpu.VMEM((slots, sets), jnp.int32),
            pltpu.VMEM((1, sets), jnp.int32),
            pltpu.VMEM((slots, sets), jnp.float32),
            pltpu.SemaphoreType.DMA((7,)),
            pltpu.SemaphoreType.DMA((math.gcd(sets // 16, 5),)),
        ],
        compiler_params=params,
        name="first",
    )(
        in_hbm(exposure_adjoint),
        in_hbm(positive_bits),
        in_hbm(currencies.T),
        in_hbm(mix_count.reshape(1, sets)),
        in_hbm(notional.T),
        in_hbm(fx_paths),
        in_hbm(short_rates),
        in_hbm(start_integral.T),
    )
    given = swapped(handed)
    masked_own, terms, carried, discount, moved = pl.pallas_call(
        functools.partial(second_kernel, dates),
        out_shape=(
            pltpu.VMEM((sets, columns // 2), jnp.bfloat16),
            pltpu.VMEM((chips,) + block, jnp.float32),
            pltpu.VMEM(block, jnp.bfloat16),
            pltpu.VMEM(block, jnp.float32),
            pltpu.VMEM(block, jnp.float32),
        ),
        in_specs=[in_vmem] * 6,
        out_specs=(in_vmem,) * 5,
        compiler_params=params,
        name="second",
    )(exposure, bits, weights, fx, rates, start)
    outgoing = pl.pallas_call(
        merging_kernel,
        out_shape=pltpu.VMEM((chips, 2 * currency_count, owned), jnp.bfloat16),
        in_specs=[in_vmem] * 3,
        out_specs=in_vmem,
        compiler_params=params,
        name="merging",
    )(given, terms, carried)
    arrived = lax.all_to_all(
        outgoing,
        "sets",
        0,
        0,
        axis_index_groups=[[2 * chip + core for chip in group_order(chips)] for core in range(2)],
        tiled=True,
    )
    carried_own = pl.pallas_call(
        unpacking_kernel,
        out_shape=pltpu.VMEM((chips,) + block, jnp.bfloat16),
        in_specs=[in_vmem],
        out_specs=in_vmem,
        compiler_params=params,
        name="unpacking",
    )(arrived)
    carried_other = swapped(carried_own)
    fx_adjoint, rate_adjoint, projected = pl.pallas_call(
        functools.partial(adjoint_kernel, dates),
        out_shape=(
            jax.ShapeDtypeStruct(block, jnp.float32),
            jax.ShapeDtypeStruct(block, jnp.float32),
            pltpu.VMEM((currency_count, sets), jnp.float32),
        ),
        in_specs=[in_vmem] * 5,
        out_specs=(in_vmem,) * 3,
        compiler_params=params,
        name="adjoint",
    )(arrived, carried_own, masked_own, moved, discount)
    notional_adjoint = pl.pallas_call(
        picking_kernel,
        out_shape=jax.ShapeDtypeStruct((slots, sets), jnp.float32),
        in_specs=[in_vmem] * 4,
        out_specs=in_vmem,
        compiler_params=params,
        name="picking",
    )(carried_other, masked_other, projected, used)
    return fx_adjoint, rate_adjoint, notional_adjoint.T


def solution(mesh):
    in_specs = (
        P(("grp", "sets"), None),
        P(("grp", "sets"), None),
        P(("grp", "sets"), None),
        P(("grp", "sets")),
        P(("grp", "sets"), None),
        P("grp", "sets"),
        P("grp", "sets"),
        P("grp", "sets"),
    )
    out_specs = (P("grp", "sets"), P("grp", "sets"), P(("grp", "sets"), None))
    return jax.shard_map(body, mesh=mesh, in_specs=in_specs, out_specs=out_specs, check_vma=False)
```

```python
import functools
import math

import jax
import jax.numpy as jnp
from jax import lax
from jax.experimental import pallas as pl
from jax.experimental.pallas import tpu as pltpu
from jax.sharding import PartitionSpec as P

step_years = 0.25
bits_per_row = 15
lanes = 128


def spread_paths(values, dates):
    paths, columns = values.shape[0], values.shape[0] * dates
    path_of = lax.broadcasted_iota(jnp.int32, (paths, columns), 1) // dates
    own = lax.broadcasted_iota(jnp.int32, (paths, columns), 0)
    return lax.dot_general(
        values,
        (path_of == own).astype(jnp.float32),
        (((0,), (0,)), ((), ())),
        precision=lax.Precision.HIGHEST,
        preferred_element_type=jnp.float32,
    )


def sums_to_date(values, dates):
    width = values.shape[1]
    date = lax.broadcasted_iota(jnp.int32, values.shape, 1) % dates
    step = 1
    while step < dates:
        values = values + jnp.where(date >= step, pltpu.roll(values, step, 1), 0.0)
        step *= 2
    return values


def sums_from_date(values, dates):
    width = values.shape[1]
    date = lax.broadcasted_iota(jnp.int32, values.shape, 1) % dates
    step = 1
    while step < dates:
        values = values + jnp.where(date < dates - step, pltpu.roll(values, width - step, 1), 0.0)
        step *= 2
    return values


def used_currencies(currencies, counts):
    slot = lax.broadcasted_iota(jnp.int32, currencies.shape, 0)
    return jnp.where(slot < counts, currencies, -1)


def group_order(chips):
    middle = chips // 2
    return list(range(chips - 1, middle - 1, -1)) + list(range(middle))


def sibling_columns(chip, owned, core):
    return pl.ds(pl.multiple_of((2 * chip + core) * owned, owned), owned)


def row_flags(tile):
    shift = lax.broadcasted_iota(jnp.int32, (8, lanes), 0) + (8 * tile) % bits_per_row
    shift = jnp.where(shift >= bits_per_row, shift - bits_per_row, shift)
    return jnp.left_shift(jnp.int32(1), shift)


def masked_rows(exposure, bits, pair, flags, column, packed_columns):
    row = lax.broadcasted_iota(jnp.int32, (8, lanes), 0)
    values = exposure[16 * pair : 16 * pair + 16, column : column + lanes].astype(jnp.float32)
    kept = []
    for half in range(2):
        top = 16 * pair + 8 * half
        group = top // bits_per_row
        left = bits_per_row * (group + 1) - top
        packed = jnp.broadcast_to(bits[group : group + 1, packed_columns], (8, lanes))
        if left < 8:
            following = jnp.broadcast_to(bits[group + 1 : group + 2, packed_columns], (8, lanes))
            packed = jnp.where(row < left, packed, following)
        kept.append(jnp.where((packed & flags[half]) != 0, values[8 * half : 8 * half + 8], 0.0))
    return jnp.concatenate(kept, axis=0).astype(jnp.bfloat16)


def mask_blocks(exposure, bits, masked_ref, core, owned, blocks):
    for pair in range(masked_ref.shape[0] // 16):
        flags = [row_flags(2 * pair), row_flags(2 * pair + 1)]
        for chip in blocks:
            masked_ref[16 * pair : 16 * pair + 16, chip * owned : (chip + 1) * owned] = masked_rows(
                exposure, bits, pair, flags, chip * owned, sibling_columns(chip, owned, core)
            )


def sum_sets(weights, masked_ref, terms_ref):
    owned = terms_ref.shape[2]
    for chip in range(0, terms_ref.shape[0], 2):
        terms = jnp.dot(
            weights,
            masked_ref[:, chip * owned : (chip + 2) * owned],
            preferred_element_type=jnp.float32,
        ).astype(terms_ref.dtype)
        terms_ref[chip] = terms[:, :owned]
        terms_ref[chip + 1] = terms[:, owned:]


def first_kernel(
    exposure_hbm,
    bits_hbm,
    currencies_hbm,
    counts_hbm,
    notional_hbm,
    fx_hbm,
    rates_hbm,
    start_hbm,
    handed_ref,
    masked_ref,
    exposure_own,
    bits,
    weights_ref,
    used_ref,
    fx_ref,
    rates_ref,
    start_ref,
    exposure_other,
    currencies_ref,
    counts_ref,
    notional_ref,
    sems,
    own_sems,
    other_sems,
):
    sets = exposure_own.shape[0]
    chips, currency_count, owned = handed_ref.shape
    own = lax.axis_index("sets") % 2
    other = 1 - own

    def block_copy(chip, core, target, block_sems):
        return pltpu.make_async_copy(
            exposure_hbm.at[:, sibling_columns(chip, owned, core)],
            target.at[:, pl.ds(chip * owned, owned)],
            block_sems.at[chip],
        )

    copies = [
        pltpu.make_async_copy(source, target, sems.at[index])
        for index, (source, target) in enumerate(
            [
                (currencies_hbm, currencies_ref),
                (counts_hbm, counts_ref),
                (notional_hbm, notional_ref),
                (bits_hbm, bits),
                (rates_hbm, rates_ref),
                (start_hbm, start_ref),
                (fx_hbm, fx_ref),
            ]
        )
    ]
    for copy in copies[:4]:
        copy.start()
    for chip in range(chips):
        block_copy(chip, other, exposure_other, other_sems).start()
    for chip in range(chips):
        block_copy(chip, own, exposure_own, own_sems).start()
    for copy in copies[4:]:
        copy.start()
    for copy in copies[:4]:
        copy.wait()

    used = used_currencies(currencies_ref[...], counts_ref[...])
    used_ref[...] = used
    notional = notional_ref[...]
    currency = lax.broadcasted_iota(jnp.int32, (currency_count, sets), 0)
    weights = jnp.zeros((currency_count, sets), jnp.float32)
    for slot in range(used.shape[0]):
        weights = weights + jnp.where(
            currency == used[slot : slot + 1], notional[slot : slot + 1], 0.0
        )
    weights = weights.astype(jnp.bfloat16)
    weights_ref[...] = weights
    step = 2
    for first in range(0, chips, step):
        for chip in range(first, first + step):
            block_copy(chip, other, exposure_other, other_sems).wait()
        mask_blocks(
            exposure_other, bits, masked_ref, other, owned, range(first, first + step)
        )
    sum_sets(weights, masked_ref, handed_ref)
    for chip in range(chips):
        block_copy(chip, own, exposure_own, own_sems).wait()
    for copy in copies[4:]:
        copy.wait()


def second_kernel(
    dates,
    exposure,
    bits,
    weights_ref,
    fx_ref,
    rates_ref,
    start_ref,
    masked_ref,
    terms_ref,
    carried_ref,
    discount_ref,
    moved_ref,
):
    integral = spread_paths(start_ref[...], dates) + step_years * sums_to_date(rates_ref[...], dates)
    discount = jnp.exp(-integral)
    discount_ref[...] = discount
    moved = fx_ref[...] * discount
    moved_ref[...] = moved
    carried_ref[...] = moved.astype(jnp.bfloat16)
    own = lax.axis_index("sets") % 2
    chips, currency_count, owned = terms_ref.shape
    mask_blocks(exposure, bits, masked_ref, own, owned, range(chips))
    sum_sets(weights_ref[...], masked_ref, terms_ref)


def merging_kernel(given_ref, terms_ref, carried_ref, outgoing_ref):
    chips, currency_count, owned = terms_ref.shape
    order = group_order(chips)
    carried = carried_ref[...]
    for place in range(chips):
        outgoing_ref[place, 0:currency_count, :] = carried
        outgoing_ref[place, currency_count:, :] = (
            terms_ref[order[place]] + given_ref[order[place]].astype(jnp.float32)
        ).astype(jnp.bfloat16)


def unpacking_kernel(arrived_ref, carried_ref):
    chips, currency_count, owned = carried_ref.shape
    order = group_order(chips)
    for place in range(chips):
        carried_ref[order[place]] = arrived_ref[place, 0:currency_count, :]


def projection(masked, carried_ref):
    sets, half = masked.shape
    chips, currency_count, owned = carried_ref.shape
    here = min(chips, 8)
    projected = jnp.zeros((currency_count, sets), jnp.float32)
    for first in range(0, chips, here):
        carried = jnp.concatenate([carried_ref[first + chip] for chip in range(here)], axis=1)
        projected = projected + lax.dot_general(
            carried,
            masked[:, first * owned : (first + here) * owned],
            (((1,), (1,)), ((), ())),
            preferred_element_type=jnp.float32,
        )
    return projected


def adjoint_kernel(
    dates,
    arrived_ref,
    carried_ref,
    masked_own,
    moved_ref,
    discount_ref,
    fx_adjoint_ref,
    rate_adjoint_ref,
    projected_ref,
):
    chips, currency_count, owned = carried_ref.shape
    aggregate = arrived_ref[0, currency_count:, :].astype(jnp.float32)
    for chip in range(1, chips):
        aggregate = aggregate + arrived_ref[chip, currency_count:, :].astype(jnp.float32)
    fx_adjoint_ref[...] = aggregate * discount_ref[...]
    rate_adjoint_ref[...] = -step_years * sums_from_date(aggregate * moved_ref[...], dates)
    projected_ref[...] = projection(masked_own, carried_ref)


def picking_kernel(carried_ref, masked_other, projected_ref, used_ref, notional_adjoint_ref):
    sets, half = masked_other.shape
    currency_count = carried_ref.shape[1]
    projected = projected_ref[...] + projection(masked_other, carried_ref)
    used = used_ref[...]
    currency = lax.broadcasted_iota(jnp.int32, (currency_count, sets), 0)
    for slot in range(used.shape[0]):
        picked = jnp.sum(
            jnp.where(currency == used[slot : slot + 1], projected, 0.0), axis=0, keepdims=True
        )
        notional_adjoint_ref[slot : slot + 1, :] = picked * (1.0 / math.sqrt(2 * half))


def body(
    exposure_adjoint,
    positive_bits,
    currencies,
    mix_count,
    notional,
    fx_paths,
    short_rates,
    start_integral,
):
    sets, columns = exposure_adjoint.shape
    currency_count, owned = fx_paths.shape
    dates = owned // start_integral.shape[1]
    peers = columns // owned
    chips = peers // 2
    slots = currencies.shape[1]
    in_vmem = pl.BlockSpec(memory_space=pltpu.VMEM)
    anywhere = pl.BlockSpec(memory_space=pl.ANY)
    params = pltpu.CompilerParams(vmem_limit_bytes=32 * 2**20)
    block = (currency_count, owned)

    def in_hbm(value):
        return pltpu.with_memory_space_constraint(value, pltpu.HBM)

    def swapped(value):
        return lax.ppermute(value, "sets", [(peer, peer ^ 1) for peer in range(peers)])

    handed, masked_other, exposure, bits, weights, used, fx, rates, start = pl.pallas_call(
        first_kernel,
        out_shape=(
            pltpu.VMEM((chips,) + block, jnp.bfloat16),
            pltpu.VMEM((sets, columns // 2), jnp.bfloat16),
            pltpu.VMEM((sets, columns // 2), jnp.bfloat16),
            pltpu.VMEM(positive_bits.shape, jnp.int32),
            pltpu.VMEM((currency_count, sets), jnp.bfloat16),
            pltpu.VMEM((slots, sets), jnp.int32),
            pltpu.VMEM(block, jnp.float32),
            pltpu.VMEM(block, jnp.float32),
            pltpu.VMEM((owned // dates, currency_count), jnp.float32),
        ),
        in_specs=[anywhere] * 8,
        out_specs=(in_vmem,) * 9,
        scratch_shapes=[
            pltpu.VMEM((sets, columns // 2), jnp.bfloat16),
            pltpu.VMEM((slots, sets), jnp.int32),
            pltpu.VMEM((1, sets), jnp.int32),
            pltpu.VMEM((slots, sets), jnp.float32),
            pltpu.SemaphoreType.DMA((7,)),
            pltpu.SemaphoreType.DMA((chips,)),
            pltpu.SemaphoreType.DMA((chips,)),
        ],
        compiler_params=params,
        name="first",
    )(
        in_hbm(exposure_adjoint),
        in_hbm(positive_bits),
        in_hbm(currencies.T),
        in_hbm(mix_count.reshape(1, sets)),
        in_hbm(notional.T),
        in_hbm(fx_paths),
        in_hbm(short_rates),
        in_hbm(start_integral.T),
    )
    given = swapped(handed)
    masked_own, terms, carried, discount, moved = pl.pallas_call(
        functools.partial(second_kernel, dates),
        out_shape=(
            pltpu.VMEM((sets, columns // 2), jnp.bfloat16),
            pltpu.VMEM((chips,) + block, jnp.float32),
            pltpu.VMEM(block, jnp.bfloat16),
            pltpu.VMEM(block, jnp.float32),
            pltpu.VMEM(block, jnp.float32),
        ),
        in_specs=[in_vmem] * 6,
        out_specs=(in_vmem,) * 5,
        compiler_params=params,
        name="second",
    )(exposure, bits, weights, fx, rates, start)
    outgoing = pl.pallas_call(
        merging_kernel,
        out_shape=pltpu.VMEM((chips, 2 * currency_count, owned), jnp.bfloat16),
        in_specs=[in_vmem] * 3,
        out_specs=in_vmem,
        compiler_params=params,
        name="merging",
    )(given, terms, carried)
    arrived = lax.all_to_all(
        outgoing,
        "sets",
        0,
        0,
        axis_index_groups=[[2 * chip + core for chip in group_order(chips)] for core in range(2)],
        tiled=True,
    )
    carried_own = pl.pallas_call(
        unpacking_kernel,
        out_shape=pltpu.VMEM((chips,) + block, jnp.bfloat16),
        in_specs=[in_vmem],
        out_specs=in_vmem,
        compiler_params=params,
        name="unpacking",
    )(arrived)
    carried_other = swapped(carried_own)
    fx_adjoint, rate_adjoint, projected = pl.pallas_call(
        functools.partial(adjoint_kernel, dates),
        out_shape=(
            jax.ShapeDtypeStruct(block, jnp.float32),
            jax.ShapeDtypeStruct(block, jnp.float32),
            pltpu.VMEM((currency_count, sets), jnp.float32),
        ),
        in_specs=[in_vmem] * 5,
        out_specs=(in_vmem,) * 3,
        compiler_params=params,
        name="adjoint",
    )(arrived, carried_own, masked_own, moved, discount)
    notional_adjoint = pl.pallas_call(
        picking_kernel,
        out_shape=jax.ShapeDtypeStruct((slots, sets), jnp.float32),
        in_specs=[in_vmem] * 4,
        out_specs=in_vmem,
        compiler_params=params,
        name="picking",
    )(carried_other, masked_other, projected, used)
    return fx_adjoint, rate_adjoint, notional_adjoint.T


def solution(mesh):
    in_specs = (
        P(("grp", "sets"), None),
        P(("grp", "sets"), None),
        P(("grp", "sets"), None),
        P(("grp", "sets")),
        P(("grp", "sets"), None),
        P("grp", "sets"),
        P("grp", "sets"),
        P("grp", "sets"),
    )
    out_specs = (P("grp", "sets"), P("grp", "sets"), P(("grp", "sets"), None))
    return jax.shard_map(body, mesh=mesh, in_specs=in_specs, out_specs=out_specs, check_vma=False)
```

```python
import functools
import math

import jax
import jax.numpy as jnp
from jax import lax
from jax.experimental import pallas as pl
from jax.experimental.pallas import tpu as pltpu
from jax.sharding import PartitionSpec as P

step_years = 0.25
bits_per_row = 15
lanes = 128


def spread_paths(values, dates):
    paths, columns = values.shape[0], values.shape[0] * dates
    path_of = lax.broadcasted_iota(jnp.int32, (paths, columns), 1) // dates
    own = lax.broadcasted_iota(jnp.int32, (paths, columns), 0)
    return lax.dot_general(
        values,
        (path_of == own).astype(jnp.float32),
        (((0,), (0,)), ((), ())),
        precision=lax.Precision.HIGHEST,
        preferred_element_type=jnp.float32,
    )


def sums_to_date(values, dates):
    width = values.shape[1]
    date = lax.broadcasted_iota(jnp.int32, values.shape, 1) % dates
    step = 1
    while step < dates:
        values = values + jnp.where(date >= step, pltpu.roll(values, step, 1), 0.0)
        step *= 2
    return values


def sums_from_date(values, dates):
    width = values.shape[1]
    date = lax.broadcasted_iota(jnp.int32, values.shape, 1) % dates
    step = 1
    while step < dates:
        values = values + jnp.where(date < dates - step, pltpu.roll(values, width - step, 1), 0.0)
        step *= 2
    return values


def used_currencies(currencies, counts):
    slot = lax.broadcasted_iota(jnp.int32, currencies.shape, 0)
    return jnp.where(slot < counts, currencies, -1)


def group_order(chips):
    middle = chips // 2
    return list(range(chips - 1, middle - 1, -1)) + list(range(middle))


def sibling_columns(chip, owned, core):
    return pl.ds(pl.multiple_of((2 * chip + core) * owned, owned), owned)


def row_flags(tile):
    shift = lax.broadcasted_iota(jnp.int32, (8, lanes), 0) + (8 * tile) % bits_per_row
    shift = jnp.where(shift >= bits_per_row, shift - bits_per_row, shift)
    return jnp.left_shift(jnp.int32(1), shift)


def masked_rows(exposure, bits, pair, flags, column, packed_columns):
    row = lax.broadcasted_iota(jnp.int32, (8, lanes), 0)
    values = exposure[16 * pair : 16 * pair + 16, column : column + lanes].astype(jnp.float32)
    kept = []
    for half in range(2):
        top = 16 * pair + 8 * half
        group = top // bits_per_row
        left = bits_per_row * (group + 1) - top
        packed = jnp.broadcast_to(bits[group : group + 1, packed_columns], (8, lanes))
        if left < 8:
            following = jnp.broadcast_to(bits[group + 1 : group + 2, packed_columns], (8, lanes))
            packed = jnp.where(row < left, packed, following)
        kept.append(jnp.where((packed & flags[half]) != 0, values[8 * half : 8 * half + 8], 0.0))
    return jnp.concatenate(kept, axis=0).astype(jnp.bfloat16)


def mask_blocks(exposure, bits, masked_ref, core, owned, blocks):
    for pair in range(masked_ref.shape[0] // 16):
        flags = [row_flags(2 * pair), row_flags(2 * pair + 1)]
        for chip in blocks:
            masked_ref[16 * pair : 16 * pair + 16, chip * owned : (chip + 1) * owned] = masked_rows(
                exposure, bits, pair, flags, chip * owned, sibling_columns(chip, owned, core)
            )


def sum_sets(weights, masked_ref, terms_ref):
    owned = terms_ref.shape[2]
    for chip in range(0, terms_ref.shape[0], 2):
        terms = jnp.dot(
            weights,
            masked_ref[:, chip * owned : (chip + 2) * owned],
            preferred_element_type=jnp.float32,
        ).astype(terms_ref.dtype)
        terms_ref[chip] = terms[:, :owned]
        terms_ref[chip + 1] = terms[:, owned:]


def block_copies(exposure_hbm, exposure, sems, core, owned):
    return [
        pltpu.make_async_copy(
            exposure_hbm.at[:, sibling_columns(chip, owned, core)],
            exposure.at[:, pl.ds(chip * owned, owned)],
            sems.at[chip],
        )
        for chip in range(exposure.shape[1] // owned)
    ]


def first_kernel(
    exposure_hbm,
    bits_hbm,
    currencies_hbm,
    counts_hbm,
    notional_hbm,
    handed_ref,
    masked_ref,
    bits,
    weights_ref,
    used_ref,
    exposure,
    currencies_ref,
    counts_ref,
    notional_ref,
    sems,
    exposure_sems,
):
    sets = exposure.shape[0]
    chips, currency_count, owned = handed_ref.shape
    other = 1 - lax.axis_index("sets") % 2
    copies = [
        pltpu.make_async_copy(source, target, sems.at[index])
        for index, (source, target) in enumerate(
            [
                (currencies_hbm, currencies_ref),
                (counts_hbm, counts_ref),
                (notional_hbm, notional_ref),
                (bits_hbm, bits),
            ]
        )
    ]
    exposure_copies = block_copies(exposure_hbm, exposure, exposure_sems, other, owned)
    for copy in copies:
        copy.start()
    for copy in exposure_copies:
        copy.start()
    for copy in copies:
        copy.wait()

    used = used_currencies(currencies_ref[...], counts_ref[...])
    used_ref[...] = used
    notional = notional_ref[...]
    currency = lax.broadcasted_iota(jnp.int32, (currency_count, sets), 0)
    weights = jnp.zeros((currency_count, sets), jnp.float32)
    for slot in range(used.shape[0]):
        weights = weights + jnp.where(
            currency == used[slot : slot + 1], notional[slot : slot + 1], 0.0
        )
    weights = weights.astype(jnp.bfloat16)
    weights_ref[...] = weights
    step = 2
    for first in range(0, chips, step):
        for copy in exposure_copies[first : first + step]:
            copy.wait()
        mask_blocks(exposure, bits, masked_ref, other, owned, range(first, first + step))
    sum_sets(weights, masked_ref, handed_ref)


def second_kernel(
    dates,
    exposure_hbm,
    fx_hbm,
    rates_hbm,
    start_hbm,
    bits,
    weights_ref,
    masked_ref,
    terms_ref,
    carried_ref,
    discount_ref,
    moved_ref,
    exposure,
    fx_ref,
    rates_ref,
    start_ref,
    sems,
    exposure_sems,
):
    chips, currency_count, owned = terms_ref.shape
    own = lax.axis_index("sets") % 2
    copies = [
        pltpu.make_async_copy(source, target, sems.at[index])
        for index, (source, target) in enumerate(
            [(rates_hbm, rates_ref), (start_hbm, start_ref), (fx_hbm, fx_ref)]
        )
    ]
    exposure_copies = block_copies(exposure_hbm, exposure, exposure_sems, own, owned)
    for copy in copies + exposure_copies:
        copy.start()
    for copy in copies:
        copy.wait()
    integral = spread_paths(start_ref[...], dates) + step_years * sums_to_date(rates_ref[...], dates)
    discount = jnp.exp(-integral)
    discount_ref[...] = discount
    moved = fx_ref[...] * discount
    moved_ref[...] = moved
    carried_ref[...] = moved.astype(jnp.bfloat16)
    for copy in exposure_copies:
        copy.wait()
    mask_blocks(exposure, bits, masked_ref, own, owned, range(chips))
    sum_sets(weights_ref[...], masked_ref, terms_ref)


def merging_kernel(given_ref, terms_ref, carried_ref, outgoing_ref):
    chips, currency_count, owned = terms_ref.shape
    order = group_order(chips)
    carried = carried_ref[...]
    for place in range(chips):
        outgoing_ref[place, 0:currency_count, :] = carried
        outgoing_ref[place, currency_count:, :] = (
            terms_ref[order[place]] + given_ref[order[place]].astype(jnp.float32)
        ).astype(jnp.bfloat16)


def unpacking_kernel(arrived_ref, carried_ref):
    chips, currency_count, owned = carried_ref.shape
    order = group_order(chips)
    for place in range(chips):
        carried_ref[order[place]] = arrived_ref[place, 0:currency_count, :]


def projection(masked, carried_ref):
    sets, half = masked.shape
    chips, currency_count, owned = carried_ref.shape
    here = min(chips, 8)
    projected = jnp.zeros((currency_count, sets), jnp.float32)
    for first in range(0, chips, here):
        carried = jnp.concatenate([carried_ref[first + chip] for chip in range(here)], axis=1)
        projected = projected + lax.dot_general(
            carried,
            masked[:, first * owned : (first + here) * owned],
            (((1,), (1,)), ((), ())),
            preferred_element_type=jnp.float32,
        )
    return projected


def adjoint_kernel(
    dates,
    arrived_ref,
    carried_ref,
    masked_own,
    moved_ref,
    discount_ref,
    fx_adjoint_ref,
    rate_adjoint_ref,
    projected_ref,
):
    chips, currency_count, owned = carried_ref.shape
    aggregate = arrived_ref[0, currency_count:, :].astype(jnp.float32)
    for chip in range(1, chips):
        aggregate = aggregate + arrived_ref[chip, currency_count:, :].astype(jnp.float32)
    fx_adjoint_ref[...] = aggregate * discount_ref[...]
    rate_adjoint_ref[...] = -step_years * sums_from_date(aggregate * moved_ref[...], dates)
    projected_ref[...] = projection(masked_own, carried_ref)


def picking_kernel(carried_ref, masked_other, projected_ref, used_ref, notional_adjoint_ref):
    sets, half = masked_other.shape
    currency_count = carried_ref.shape[1]
    projected = projected_ref[...] + projection(masked_other, carried_ref)
    used = used_ref[...]
    currency = lax.broadcasted_iota(jnp.int32, (currency_count, sets), 0)
    for slot in range(used.shape[0]):
        picked = jnp.sum(
            jnp.where(currency == used[slot : slot + 1], projected, 0.0), axis=0, keepdims=True
        )
        notional_adjoint_ref[slot : slot + 1, :] = picked * (1.0 / math.sqrt(2 * half))


def body(
    exposure_adjoint,
    positive_bits,
    currencies,
    mix_count,
    notional,
    fx_paths,
    short_rates,
    start_integral,
):
    sets, columns = exposure_adjoint.shape
    currency_count, owned = fx_paths.shape
    dates = owned // start_integral.shape[1]
    peers = columns // owned
    chips = peers // 2
    slots = currencies.shape[1]
    in_vmem = pl.BlockSpec(memory_space=pltpu.VMEM)
    anywhere = pl.BlockSpec(memory_space=pl.ANY)
    params = pltpu.CompilerParams(vmem_limit_bytes=32 * 2**20)
    block = (currency_count, owned)

    def in_hbm(value):
        return pltpu.with_memory_space_constraint(value, pltpu.HBM)

    def swapped(value):
        return lax.ppermute(value, "sets", [(peer, peer ^ 1) for peer in range(peers)])

    exposure_adjoint = in_hbm(exposure_adjoint)
    handed, masked_other, bits, weights, used = pl.pallas_call(
        first_kernel,
        out_shape=(
            pltpu.VMEM((chips,) + block, jnp.bfloat16),
            pltpu.VMEM((sets, columns // 2), jnp.bfloat16),
            pltpu.VMEM(positive_bits.shape, jnp.int32),
            pltpu.VMEM((currency_count, sets), jnp.bfloat16),
            pltpu.VMEM((slots, sets), jnp.int32),
        ),
        in_specs=[anywhere] * 5,
        out_specs=(in_vmem,) * 5,
        scratch_shapes=[
            pltpu.VMEM((sets, columns // 2), jnp.bfloat16),
            pltpu.VMEM((slots, sets), jnp.int32),
            pltpu.VMEM((1, sets), jnp.int32),
            pltpu.VMEM((slots, sets), jnp.float32),
            pltpu.SemaphoreType.DMA((4,)),
            pltpu.SemaphoreType.DMA((chips,)),
        ],
        compiler_params=params,
        name="first",
    )(
        exposure_adjoint,
        in_hbm(positive_bits),
        in_hbm(currencies.T),
        in_hbm(mix_count.reshape(1, sets)),
        in_hbm(notional.T),
    )
    given = swapped(handed)
    masked_own, terms, carried, discount, moved = pl.pallas_call(
        functools.partial(second_kernel, dates),
        out_shape=(
            pltpu.VMEM((sets, columns // 2), jnp.bfloat16),
            pltpu.VMEM((chips,) + block, jnp.float32),
            pltpu.VMEM(block, jnp.bfloat16),
            pltpu.VMEM(block, jnp.float32),
            pltpu.VMEM(block, jnp.float32),
        ),
        in_specs=[anywhere] * 4 + [in_vmem] * 2,
        out_specs=(in_vmem,) * 5,
        scratch_shapes=[
            pltpu.VMEM((sets, columns // 2), jnp.bfloat16),
            pltpu.VMEM(block, jnp.float32),
            pltpu.VMEM(block, jnp.float32),
            pltpu.VMEM((owned // dates, currency_count), jnp.float32),
            pltpu.SemaphoreType.DMA((3,)),
            pltpu.SemaphoreType.DMA((chips,)),
        ],
        compiler_params=params,
        name="second",
    )(
        exposure_adjoint,
        in_hbm(fx_paths),
        in_hbm(short_rates),
        in_hbm(start_integral.T),
        bits,
        weights,
    )
    outgoing = pl.pallas_call(
        merging_kernel,
        out_shape=pltpu.VMEM((chips, 2 * currency_count, owned), jnp.bfloat16),
        in_specs=[in_vmem] * 3,
        out_specs=in_vmem,
        compiler_params=params,
        name="merging",
    )(given, terms, carried)
    arrived = lax.all_to_all(
        outgoing,
        "sets",
        0,
        0,
        axis_index_groups=[[2 * chip + core for chip in group_order(chips)] for core in range(2)],
        tiled=True,
    )
    carried_own = pl.pallas_call(
        unpacking_kernel,
        out_shape=pltpu.VMEM((chips,) + block, jnp.bfloat16),
        in_specs=[in_vmem],
        out_specs=in_vmem,
        compiler_params=params,
        name="unpacking",
    )(arrived)
    carried_other = swapped(carried_own)
    fx_adjoint, rate_adjoint, projected = pl.pallas_call(
        functools.partial(adjoint_kernel, dates),
        out_shape=(
            jax.ShapeDtypeStruct(block, jnp.float32),
            jax.ShapeDtypeStruct(block, jnp.float32),
            pltpu.VMEM((currency_count, sets), jnp.float32),
        ),
        in_specs=[in_vmem] * 5,
        out_specs=(in_vmem,) * 3,
        compiler_params=params,
        name="adjoint",
    )(arrived, carried_own, masked_own, moved, discount)
    notional_adjoint = pl.pallas_call(
        picking_kernel,
        out_shape=jax.ShapeDtypeStruct((slots, sets), jnp.float32),
        in_specs=[in_vmem] * 4,
        out_specs=in_vmem,
        compiler_params=params,
        name="picking",
    )(carried_other, masked_other, projected, used)
    return fx_adjoint, rate_adjoint, notional_adjoint.T


def solution(mesh):
    in_specs = (
        P(("grp", "sets"), None),
        P(("grp", "sets"), None),
        P(("grp", "sets"), None),
        P(("grp", "sets")),
        P(("grp", "sets"), None),
        P("grp", "sets"),
        P("grp", "sets"),
        P("grp", "sets"),
    )
    out_specs = (P("grp", "sets"), P("grp", "sets"), P(("grp", "sets"), None))
    return jax.shard_map(body, mesh=mesh, in_specs=in_specs, out_specs=out_specs, check_vma=False)
```

```python
import functools
import math

import jax
import jax.numpy as jnp
from jax import lax
from jax.experimental import pallas as pl
from jax.experimental.pallas import tpu as pltpu
from jax.sharding import PartitionSpec as P

step_years = 0.25
bits_per_row = 15
lanes = 128


def spread_paths(values, dates):
    paths, columns = values.shape[0], values.shape[0] * dates
    path_of = lax.broadcasted_iota(jnp.int32, (paths, columns), 1) // dates
    own = lax.broadcasted_iota(jnp.int32, (paths, columns), 0)
    return lax.dot_general(
        values,
        (path_of == own).astype(jnp.float32),
        (((0,), (0,)), ((), ())),
        precision=lax.Precision.HIGHEST,
        preferred_element_type=jnp.float32,
    )


def sums_to_date(values, dates):
    width = values.shape[1]
    date = lax.broadcasted_iota(jnp.int32, values.shape, 1) % dates
    step = 1
    while step < dates:
        values = values + jnp.where(date >= step, pltpu.roll(values, step, 1), 0.0)
        step *= 2
    return values


def sums_from_date(values, dates):
    width = values.shape[1]
    date = lax.broadcasted_iota(jnp.int32, values.shape, 1) % dates
    step = 1
    while step < dates:
        values = values + jnp.where(date < dates - step, pltpu.roll(values, width - step, 1), 0.0)
        step *= 2
    return values


def used_currencies(currencies, counts):
    slot = lax.broadcasted_iota(jnp.int32, currencies.shape, 0)
    return jnp.where(slot < counts, currencies, -1)


def group_order(chips):
    middle = chips // 2
    return list(range(chips - 1, middle - 1, -1)) + list(range(middle))


def sibling_columns(chip, owned, core):
    return pl.ds(pl.multiple_of((2 * chip + core) * owned, owned), owned)


def row_flags(tile):
    shift = lax.broadcasted_iota(jnp.int32, (8, lanes), 0) + (8 * tile) % bits_per_row
    shift = jnp.where(shift >= bits_per_row, shift - bits_per_row, shift)
    return jnp.left_shift(jnp.int32(1), shift)


def masked_rows(exposure, bits, pair, flags, part):
    row = lax.broadcasted_iota(jnp.int32, (8, lanes), 0)
    values = exposure[16 * pair : 16 * pair + 16, part].astype(jnp.float32)
    kept = []
    for half in range(2):
        top = 16 * pair + 8 * half
        group = top // bits_per_row
        left = bits_per_row * (group + 1) - top
        packed = jnp.broadcast_to(bits[group : group + 1, part], (8, lanes))
        if left < 8:
            following = jnp.broadcast_to(bits[group + 1 : group + 2, part], (8, lanes))
            packed = jnp.where(row < left, packed, following)
        kept.append(jnp.where((packed & flags[half]) != 0, values[8 * half : 8 * half + 8], 0.0))
    return jnp.concatenate(kept, axis=0).astype(jnp.bfloat16)


def mask_rows(exposure, bits, masked_ref, core, owned, first, last):
    for pair in range(first // 16, last // 16):
        flags = [row_flags(2 * pair), row_flags(2 * pair + 1)]
        for chip in range(masked_ref.shape[1] // owned):
            masked_ref[16 * pair : 16 * pair + 16, chip * owned : (chip + 1) * owned] = masked_rows(
                exposure, bits, pair, flags, sibling_columns(chip, owned, core)
            )


def sum_sets(weights, masked_ref, terms_ref):
    owned = terms_ref.shape[2]
    for chip in range(0, terms_ref.shape[0], 2):
        terms = jnp.dot(
            weights,
            masked_ref[:, chip * owned : (chip + 2) * owned],
            preferred_element_type=jnp.float32,
        ).astype(terms_ref.dtype)
        terms_ref[chip] = terms[:, :owned]
        terms_ref[chip + 1] = terms[:, owned:]


def first_kernel(
    exposure_hbm,
    bits_hbm,
    currencies_hbm,
    counts_hbm,
    notional_hbm,
    fx_hbm,
    rates_hbm,
    start_hbm,
    handed_ref,
    masked_ref,
    exposure,
    bits,
    weights_ref,
    used_ref,
    fx_ref,
    rates_ref,
    start_ref,
    currencies_ref,
    counts_ref,
    notional_ref,
    sems,
    exposure_sems,
):
    sets = exposure.shape[0]
    chips, currency_count = handed_ref.shape[:2]
    parts = exposure_sems.shape[0]
    rows = sets // parts

    def exposure_copy(index):
        part = pl.ds(index * rows, rows)
        return pltpu.make_async_copy(
            exposure_hbm.at[part], exposure.at[part], exposure_sems.at[index]
        )

    copies = [
        pltpu.make_async_copy(source, target, sems.at[index])
        for index, (source, target) in enumerate(
            [
                (currencies_hbm, currencies_ref),
                (counts_hbm, counts_ref),
                (notional_hbm, notional_ref),
                (bits_hbm, bits),
                (rates_hbm, rates_ref),
                (start_hbm, start_ref),
                (fx_hbm, fx_ref),
            ]
        )
    ]
    for copy in copies[:4]:
        copy.start()
    for index in range(parts):
        exposure_copy(index).start(priority=index % 2)
    for copy in copies[4:]:
        copy.start()
    for copy in copies:
        copy.wait()

    used = used_currencies(currencies_ref[...], counts_ref[...])
    used_ref[...] = used
    notional = notional_ref[...]
    currency = lax.broadcasted_iota(jnp.int32, (currency_count, sets), 0)
    weights = jnp.zeros((currency_count, sets), jnp.float32)
    for slot in range(used.shape[0]):
        weights = weights + jnp.where(
            currency == used[slot : slot + 1], notional[slot : slot + 1], 0.0
        )
    weights = weights.astype(jnp.bfloat16)
    weights_ref[...] = weights
    other = 1 - lax.axis_index("sets") % 2
    for index in range(parts):
        exposure_copy(index).wait()
        mask_rows(
            exposure, bits, masked_ref, other, handed_ref.shape[2], index * rows, (index + 1) * rows
        )
    sum_sets(weights, masked_ref, handed_ref)


def second_kernel(
    dates,
    exposure,
    bits,
    weights_ref,
    fx_ref,
    rates_ref,
    start_ref,
    masked_ref,
    terms_ref,
    carried_ref,
    discount_ref,
    moved_ref,
):
    integral = spread_paths(start_ref[...], dates) + step_years * sums_to_date(rates_ref[...], dates)
    discount = jnp.exp(-integral)
    discount_ref[...] = discount
    moved = fx_ref[...] * discount
    moved_ref[...] = moved
    carried_ref[...] = moved.astype(jnp.bfloat16)
    own = lax.axis_index("sets") % 2
    mask_rows(exposure, bits, masked_ref, own, terms_ref.shape[2], 0, exposure.shape[0])
    sum_sets(weights_ref[...], masked_ref, terms_ref)


def merging_kernel(given_ref, terms_ref, carried_ref, outgoing_ref):
    chips, currency_count, owned = terms_ref.shape
    order = group_order(chips)
    carried = carried_ref[...]
    for place in range(chips):
        outgoing_ref[place, 0:currency_count, :] = carried
        outgoing_ref[place, currency_count:, :] = (
            terms_ref[order[place]] + given_ref[order[place]].astype(jnp.float32)
        ).astype(jnp.bfloat16)


def unpacking_kernel(arrived_ref, turned_own, turned_other, carried_ref):
    chips, currency_count, owned = carried_ref.shape
    order = group_order(chips)
    for place in range(chips):
        carried_ref[order[place]] = arrived_ref[place, 0:currency_count, :]


def turning_kernel(masked_own, masked_other, turned_own, turned_other):
    for masked, turned in ((masked_own, turned_own), (masked_other, turned_other)):
        for column in range(0, masked.shape[1], lanes):
            turned[column : column + lanes, :] = masked[:, column : column + lanes].T


def projection(turned, carried_ref):
    half, sets = turned.shape
    chips, currency_count, owned = carried_ref.shape
    here = min(chips, 8)
    projected = jnp.zeros((currency_count, sets), jnp.float32)
    for first in range(0, chips, here):
        carried = jnp.concatenate([carried_ref[first + chip] for chip in range(here)], axis=1)
        projected = projected + jnp.dot(
            carried,
            turned[first * owned : (first + here) * owned, :],
            preferred_element_type=jnp.float32,
        )
    return projected


def adjoint_kernel(
    dates,
    arrived_ref,
    carried_ref,
    turned_own,
    moved_ref,
    discount_ref,
    fx_adjoint_ref,
    rate_adjoint_ref,
    projected_ref,
):
    chips, currency_count, owned = carried_ref.shape
    aggregate = arrived_ref[0, currency_count:, :].astype(jnp.float32)
    for chip in range(1, chips):
        aggregate = aggregate + arrived_ref[chip, currency_count:, :].astype(jnp.float32)
    fx_adjoint_ref[...] = aggregate * discount_ref[...]
    rate_adjoint_ref[...] = -step_years * sums_from_date(aggregate * moved_ref[...], dates)
    projected_ref[...] = projection(turned_own, carried_ref)


def picking_kernel(carried_ref, turned_other, projected_ref, used_ref, notional_adjoint_ref):
    half, sets = turned_other.shape
    currency_count = carried_ref.shape[1]
    projected = projected_ref[...] + projection(turned_other, carried_ref)
    used = used_ref[...]
    currency = lax.broadcasted_iota(jnp.int32, (currency_count, sets), 0)
    for slot in range(used.shape[0]):
        picked = jnp.sum(
            jnp.where(currency == used[slot : slot + 1], projected, 0.0), axis=0, keepdims=True
        )
        notional_adjoint_ref[slot : slot + 1, :] = picked * (1.0 / math.sqrt(2 * half))


def body(
    exposure_adjoint,
    positive_bits,
    currencies,
    mix_count,
    notional,
    fx_paths,
    short_rates,
    start_integral,
):
    sets, columns = exposure_adjoint.shape
    currency_count, owned = fx_paths.shape
    dates = owned // start_integral.shape[1]
    peers = columns // owned
    chips = peers // 2
    slots = currencies.shape[1]
    in_vmem = pl.BlockSpec(memory_space=pltpu.VMEM)
    anywhere = pl.BlockSpec(memory_space=pl.ANY)
    params = pltpu.CompilerParams(vmem_limit_bytes=32 * 2**20)
    block = (currency_count, owned)

    def in_hbm(value):
        return pltpu.with_memory_space_constraint(value, pltpu.HBM)

    def swapped(value):
        return lax.ppermute(value, "sets", [(peer, peer ^ 1) for peer in range(peers)])

    handed, masked_other, exposure, bits, weights, used, fx, rates, start = pl.pallas_call(
        first_kernel,
        out_shape=(
            pltpu.VMEM((chips,) + block, jnp.bfloat16),
            pltpu.VMEM((sets, columns // 2), jnp.bfloat16),
            pltpu.VMEM((sets, columns), jnp.bfloat16),
            pltpu.VMEM(positive_bits.shape, jnp.int32),
            pltpu.VMEM((currency_count, sets), jnp.bfloat16),
            pltpu.VMEM((slots, sets), jnp.int32),
            pltpu.VMEM(block, jnp.float32),
            pltpu.VMEM(block, jnp.float32),
            pltpu.VMEM((owned // dates, currency_count), jnp.float32),
        ),
        in_specs=[anywhere] * 8,
        out_specs=(in_vmem,) * 9,
        scratch_shapes=[
            pltpu.VMEM((slots, sets), jnp.int32),
            pltpu.VMEM((1, sets), jnp.int32),
            pltpu.VMEM((slots, sets), jnp.float32),
            pltpu.SemaphoreType.DMA((7,)),
            pltpu.SemaphoreType.DMA((math.gcd(sets // 16, 5),)),
        ],
        compiler_params=params,
        name="first",
    )(
        in_hbm(exposure_adjoint),
        in_hbm(positive_bits),
        in_hbm(currencies.T),
        in_hbm(mix_count.reshape(1, sets)),
        in_hbm(notional.T),
        in_hbm(fx_paths),
        in_hbm(short_rates),
        in_hbm(start_integral.T),
    )
    given = swapped(handed)
    masked_own, terms, carried, discount, moved = pl.pallas_call(
        functools.partial(second_kernel, dates),
        out_shape=(
            pltpu.VMEM((sets, columns // 2), jnp.bfloat16),
            pltpu.VMEM((chips,) + block, jnp.float32),
            pltpu.VMEM(block, jnp.bfloat16),
            pltpu.VMEM(block, jnp.float32),
            pltpu.VMEM(block, jnp.float32),
        ),
        in_specs=[in_vmem] * 6,
        out_specs=(in_vmem,) * 5,
        compiler_params=params,
        name="second",
    )(exposure, bits, weights, fx, rates, start)
    outgoing = pl.pallas_call(
        merging_kernel,
        out_shape=pltpu.VMEM((chips, 2 * currency_count, owned), jnp.bfloat16),
        in_specs=[in_vmem] * 3,
        out_specs=in_vmem,
        compiler_params=params,
        name="merging",
    )(given, terms, carried)
    arrived = lax.all_to_all(
        outgoing,
        "sets",
        0,
        0,
        axis_index_groups=[[2 * chip + core for chip in group_order(chips)] for core in range(2)],
        tiled=True,
    )
    turned_own, turned_other = pl.pallas_call(
        turning_kernel,
        out_shape=(pltpu.VMEM((columns // 2, sets), jnp.bfloat16),) * 2,
        in_specs=[in_vmem] * 2,
        out_specs=(in_vmem,) * 2,
        compiler_params=params,
        name="turning",
    )(masked_own, masked_other)
    carried_own = pl.pallas_call(
        unpacking_kernel,
        out_shape=pltpu.VMEM((chips,) + block, jnp.bfloat16),
        in_specs=[in_vmem, anywhere, anywhere],
        out_specs=in_vmem,
        compiler_params=params,
        name="unpacking",
    )(arrived, turned_own, turned_other)
    carried_other = swapped(carried_own)
    fx_adjoint, rate_adjoint, projected = pl.pallas_call(
        functools.partial(adjoint_kernel, dates),
        out_shape=(
            jax.ShapeDtypeStruct(block, jnp.float32),
            jax.ShapeDtypeStruct(block, jnp.float32),
            pltpu.VMEM((currency_count, sets), jnp.float32),
        ),
        in_specs=[in_vmem] * 5,
        out_specs=(in_vmem,) * 3,
        compiler_params=params,
        name="adjoint",
    )(arrived, carried_own, turned_own, moved, discount)
    notional_adjoint = pl.pallas_call(
        picking_kernel,
        out_shape=jax.ShapeDtypeStruct((slots, sets), jnp.float32),
        in_specs=[in_vmem] * 4,
        out_specs=in_vmem,
        compiler_params=params,
        name="picking",
    )(carried_other, turned_other, projected, used)
    return fx_adjoint, rate_adjoint, notional_adjoint.T


def solution(mesh):
    in_specs = (
        P(("grp", "sets"), None),
        P(("grp", "sets"), None),
        P(("grp", "sets"), None),
        P(("grp", "sets")),
        P(("grp", "sets"), None),
        P("grp", "sets"),
        P("grp", "sets"),
        P("grp", "sets"),
    )
    out_specs = (P("grp", "sets"), P("grp", "sets"), P(("grp", "sets"), None))
    return jax.shard_map(body, mesh=mesh, in_specs=in_specs, out_specs=out_specs, check_vma=False)
```

```python
import functools
import math

import jax
import jax.numpy as jnp
from jax import lax
from jax.experimental import pallas as pl
from jax.experimental.pallas import tpu as pltpu
from jax.sharding import PartitionSpec as P

step_years = 0.25
bits_per_row = 15
lanes = 128


def spread_paths(values, dates):
    paths, columns = values.shape[0], values.shape[0] * dates
    path_of = lax.broadcasted_iota(jnp.int32, (paths, columns), 1) // dates
    own = lax.broadcasted_iota(jnp.int32, (paths, columns), 0)
    return lax.dot_general(
        values,
        (path_of == own).astype(jnp.float32),
        (((0,), (0,)), ((), ())),
        precision=lax.Precision.HIGHEST,
        preferred_element_type=jnp.float32,
    )


def sums_to_date(values, dates):
    width = values.shape[1]
    date = lax.broadcasted_iota(jnp.int32, values.shape, 1) % dates
    step = 1
    while step < dates:
        values = values + jnp.where(date >= step, pltpu.roll(values, step, 1), 0.0)
        step *= 2
    return values


def sums_from_date(values, dates):
    width = values.shape[1]
    date = lax.broadcasted_iota(jnp.int32, values.shape, 1) % dates
    step = 1
    while step < dates:
        values = values + jnp.where(date < dates - step, pltpu.roll(values, width - step, 1), 0.0)
        step *= 2
    return values


def used_currencies(currencies, counts):
    slot = lax.broadcasted_iota(jnp.int32, currencies.shape, 0)
    return jnp.where(slot < counts, currencies, -1)


def group_order(chips):
    middle = chips // 2
    return list(range(middle, chips)) + list(range(middle))


def sibling_columns(chip, owned, core):
    return pl.ds(pl.multiple_of((2 * chip + core) * owned, owned), owned)


def row_flags(tile):
    shift = lax.broadcasted_iota(jnp.int32, (8, lanes), 0) + (8 * tile) % bits_per_row
    shift = jnp.where(shift >= bits_per_row, shift - bits_per_row, shift)
    return jnp.left_shift(jnp.int32(1), shift)


def masked_rows(exposure, bits, pair, flags, part):
    row = lax.broadcasted_iota(jnp.int32, (8, lanes), 0)
    values = exposure[16 * pair : 16 * pair + 16, part].astype(jnp.float32)
    kept = []
    for half in range(2):
        top = 16 * pair + 8 * half
        group = top // bits_per_row
        left = bits_per_row * (group + 1) - top
        packed = jnp.broadcast_to(bits[group : group + 1, part], (8, lanes))
        if left < 8:
            following = jnp.broadcast_to(bits[group + 1 : group + 2, part], (8, lanes))
            packed = jnp.where(row < left, packed, following)
        kept.append(jnp.where((packed & flags[half]) != 0, values[8 * half : 8 * half + 8], 0.0))
    return jnp.concatenate(kept, axis=0).astype(jnp.bfloat16)


def mask_rows(exposure, bits, masked_ref, core, owned, first, last):
    for pair in range(first // 16, last // 16):
        flags = [row_flags(2 * pair), row_flags(2 * pair + 1)]
        for chip in range(masked_ref.shape[1] // owned):
            masked_ref[16 * pair : 16 * pair + 16, chip * owned : (chip + 1) * owned] = masked_rows(
                exposure, bits, pair, flags, sibling_columns(chip, owned, core)
            )


def sum_sets(weights, masked_ref, terms_ref):
    owned = terms_ref.shape[2]
    for chip in range(0, terms_ref.shape[0], 2):
        terms = jnp.dot(
            weights,
            masked_ref[:, chip * owned : (chip + 2) * owned],
            preferred_element_type=jnp.float32,
        ).astype(terms_ref.dtype)
        terms_ref[chip] = terms[:, :owned]
        terms_ref[chip + 1] = terms[:, owned:]


def first_kernel(
    exposure_hbm,
    bits_hbm,
    currencies_hbm,
    counts_hbm,
    notional_hbm,
    fx_hbm,
    rates_hbm,
    start_hbm,
    handed_ref,
    masked_ref,
    exposure,
    bits,
    weights_ref,
    used_ref,
    fx_ref,
    rates_ref,
    start_ref,
    currencies_ref,
    counts_ref,
    notional_ref,
    sems,
    exposure_sems,
    bits_sems,
):
    sets = exposure.shape[0]
    chips, currency_count = handed_ref.shape[:2]
    parts = exposure_sems.shape[0]
    rows = sets // parts

    def exposure_copy(index):
        part = pl.ds(index * rows, rows)
        return pltpu.make_async_copy(
            exposure_hbm.at[part], exposure.at[part], exposure_sems.at[index]
        )

    bits_parts = bits_sems.shape[0]
    bits_width = bits.shape[1] // bits_parts

    def bits_copy(index):
        part = pl.ds(index * bits_width, bits_width)
        return pltpu.make_async_copy(bits_hbm.at[:, part], bits.at[:, part], bits_sems.at[index])

    copies = [
        pltpu.make_async_copy(source, target, sems.at[index])
        for index, (source, target) in enumerate(
            [
                (currencies_hbm, currencies_ref),
                (counts_hbm, counts_ref),
                (notional_hbm, notional_ref),
                (rates_hbm, rates_ref),
                (start_hbm, start_ref),
                (fx_hbm, fx_ref),
            ]
        )
    ]
    for index in range(bits_parts):
        bits_copy(index).start()
    for index in range(parts):
        exposure_copy(index).start()
    for copy in copies:
        copy.start()
    for index in range(bits_parts):
        bits_copy(index).wait()

    other = 1 - lax.axis_index("sets") % 2
    for index in range(parts):
        exposure_copy(index).wait()
        mask_rows(
            exposure, bits, masked_ref, other, handed_ref.shape[2], index * rows, (index + 1) * rows
        )

    for copy in copies:
        copy.wait()
    used = used_currencies(currencies_ref[...], counts_ref[...])
    used_ref[...] = used
    notional = notional_ref[...]
    currency = lax.broadcasted_iota(jnp.int32, (currency_count, sets), 0)
    weights = jnp.zeros((currency_count, sets), jnp.float32)
    for slot in range(used.shape[0]):
        weights = weights + jnp.where(
            currency == used[slot : slot + 1], notional[slot : slot + 1], 0.0
        )
    weights = weights.astype(jnp.bfloat16)
    weights_ref[...] = weights
    sum_sets(weights, masked_ref, handed_ref)


def second_kernel(
    dates,
    exposure,
    bits,
    weights_ref,
    fx_ref,
    rates_ref,
    start_ref,
    masked_ref,
    terms_ref,
    carried_ref,
    discount_ref,
    moved_ref,
):
    integral = spread_paths(start_ref[...], dates) + step_years * sums_to_date(rates_ref[...], dates)
    discount = jnp.exp(-integral)
    discount_ref[...] = discount
    moved = fx_ref[...] * discount
    moved_ref[...] = moved
    carried_ref[...] = moved.astype(jnp.bfloat16)
    own = lax.axis_index("sets") % 2
    mask_rows(exposure, bits, masked_ref, own, terms_ref.shape[2], 0, exposure.shape[0])
    sum_sets(weights_ref[...], masked_ref, terms_ref)


def merging_kernel(given_ref, terms_ref, carried_ref, outgoing_ref):
    chips, currency_count, owned = terms_ref.shape
    order = group_order(chips)
    carried = carried_ref[...]
    for place in range(chips):
        outgoing_ref[place, 0:currency_count, :] = carried
        outgoing_ref[place, currency_count:, :] = (
            terms_ref[order[place]] + given_ref[order[place]].astype(jnp.float32)
        ).astype(jnp.bfloat16)


def unpacking_kernel(arrived_ref, carried_ref):
    chips, currency_count, owned = carried_ref.shape
    order = group_order(chips)
    for place in range(chips):
        carried_ref[order[place]] = arrived_ref[place, 0:currency_count, :]


def projection(masked, carried_ref):
    sets, half = masked.shape
    chips, currency_count, owned = carried_ref.shape
    here = min(chips, 8)
    projected = jnp.zeros((currency_count, sets), jnp.float32)
    for first in range(0, chips, here):
        carried = jnp.concatenate([carried_ref[first + chip] for chip in range(here)], axis=1)
        projected = projected + lax.dot_general(
            carried,
            masked[:, first * owned : (first + here) * owned],
            (((1,), (1,)), ((), ())),
            preferred_element_type=jnp.float32,
        )
    return projected


def adjoint_kernel(
    dates,
    arrived_ref,
    carried_ref,
    masked_own,
    moved_ref,
    discount_ref,
    fx_adjoint_ref,
    rate_adjoint_ref,
    projected_ref,
):
    chips, currency_count, owned = carried_ref.shape
    aggregate = arrived_ref[0, currency_count:, :].astype(jnp.float32)
    for chip in range(1, chips):
        aggregate = aggregate + arrived_ref[chip, currency_count:, :].astype(jnp.float32)
    fx_adjoint_ref[...] = aggregate * discount_ref[...]
    rate_adjoint_ref[...] = -step_years * sums_from_date(aggregate * moved_ref[...], dates)
    projected_ref[...] = projection(masked_own, carried_ref)


def picking_kernel(carried_ref, masked_other, projected_ref, used_ref, notional_adjoint_ref):
    sets, half = masked_other.shape
    currency_count = carried_ref.shape[1]
    projected = projected_ref[...] + projection(masked_other, carried_ref)
    used = used_ref[...]
    currency = lax.broadcasted_iota(jnp.int32, (currency_count, sets), 0)
    for slot in range(used.shape[0]):
        picked = jnp.sum(
            jnp.where(currency == used[slot : slot + 1], projected, 0.0), axis=0, keepdims=True
        )
        notional_adjoint_ref[slot : slot + 1, :] = picked * (1.0 / math.sqrt(2 * half))


def body(
    exposure_adjoint,
    positive_bits,
    currencies,
    mix_count,
    notional,
    fx_paths,
    short_rates,
    start_integral,
):
    sets, columns = exposure_adjoint.shape
    currency_count, owned = fx_paths.shape
    dates = owned // start_integral.shape[1]
    peers = columns // owned
    chips = peers // 2
    slots = currencies.shape[1]
    in_vmem = pl.BlockSpec(memory_space=pltpu.VMEM)
    anywhere = pl.BlockSpec(memory_space=pl.ANY)
    params = pltpu.CompilerParams(vmem_limit_bytes=32 * 2**20)
    block = (currency_count, owned)

    def in_hbm(value):
        return pltpu.with_memory_space_constraint(value, pltpu.HBM)

    def swapped(value):
        return lax.ppermute(value, "sets", [(peer, peer ^ 1) for peer in range(peers)])

    handed, masked_other, exposure, bits, weights, used, fx, rates, start = pl.pallas_call(
        first_kernel,
        out_shape=(
            pltpu.VMEM((chips,) + block, jnp.bfloat16),
            pltpu.VMEM((sets, columns // 2), jnp.bfloat16),
            pltpu.VMEM((sets, columns), jnp.bfloat16),
            pltpu.VMEM(positive_bits.shape, jnp.int32),
            pltpu.VMEM((currency_count, sets), jnp.bfloat16),
            pltpu.VMEM((slots, sets), jnp.int32),
            pltpu.VMEM(block, jnp.float32),
            pltpu.VMEM(block, jnp.float32),
            pltpu.VMEM((owned // dates, currency_count), jnp.float32),
        ),
        in_specs=[anywhere] * 8,
        out_specs=(in_vmem,) * 9,
        scratch_shapes=[
            pltpu.VMEM((slots, sets), jnp.int32),
            pltpu.VMEM((1, sets), jnp.int32),
            pltpu.VMEM((slots, sets), jnp.float32),
            pltpu.SemaphoreType.DMA((6,)),
            pltpu.SemaphoreType.DMA((math.gcd(sets // 16, 5),)),
            pltpu.SemaphoreType.DMA((4,)),
        ],
        compiler_params=params,
        name="first",
    )(
        in_hbm(exposure_adjoint),
        in_hbm(positive_bits),
        in_hbm(currencies.T),
        in_hbm(mix_count.reshape(1, sets)),
        in_hbm(notional.T),
        in_hbm(fx_paths),
        in_hbm(short_rates),
        in_hbm(start_integral.T),
    )
    given = swapped(handed)
    masked_own, terms, carried, discount, moved = pl.pallas_call(
        functools.partial(second_kernel, dates),
        out_shape=(
            pltpu.VMEM((sets, columns // 2), jnp.bfloat16),
            pltpu.VMEM((chips,) + block, jnp.float32),
            pltpu.VMEM(block, jnp.bfloat16),
            pltpu.VMEM(block, jnp.float32),
            pltpu.VMEM(block, jnp.float32),
        ),
        in_specs=[in_vmem] * 6,
        out_specs=(in_vmem,) * 5,
        compiler_params=params,
        name="second",
    )(exposure, bits, weights, fx, rates, start)
    outgoing = pl.pallas_call(
        merging_kernel,
        out_shape=pltpu.VMEM((chips, 2 * currency_count, owned), jnp.bfloat16),
        in_specs=[in_vmem] * 3,
        out_specs=in_vmem,
        compiler_params=params,
        name="merging",
    )(given, terms, carried)
    arrived = lax.all_to_all(
        outgoing,
        "sets",
        0,
        0,
        axis_index_groups=[[2 * chip + core for chip in group_order(chips)] for core in range(2)],
        tiled=True,
    )
    carried_own = pl.pallas_call(
        unpacking_kernel,
        out_shape=pltpu.VMEM((chips,) + block, jnp.bfloat16),
        in_specs=[in_vmem],
        out_specs=in_vmem,
        compiler_params=params,
        name="unpacking",
    )(arrived)
    carried_other = swapped(carried_own)
    fx_adjoint, rate_adjoint, projected = pl.pallas_call(
        functools.partial(adjoint_kernel, dates),
        out_shape=(
            jax.ShapeDtypeStruct(block, jnp.float32),
            jax.ShapeDtypeStruct(block, jnp.float32),
            pltpu.VMEM((currency_count, sets), jnp.float32),
        ),
        in_specs=[in_vmem] * 5,
        out_specs=(in_vmem,) * 3,
        compiler_params=params,
        name="adjoint",
    )(arrived, carried_own, masked_own, moved, discount)
    notional_adjoint = pl.pallas_call(
        picking_kernel,
        out_shape=jax.ShapeDtypeStruct((slots, sets), jnp.float32),
        in_specs=[in_vmem] * 4,
        out_specs=in_vmem,
        compiler_params=params,
        name="picking",
    )(carried_other, masked_other, projected, used)
    return fx_adjoint, rate_adjoint, notional_adjoint.T


def solution(mesh):
    in_specs = (
        P(("grp", "sets"), None),
        P(("grp", "sets"), None),
        P(("grp", "sets"), None),
        P(("grp", "sets")),
        P(("grp", "sets"), None),
        P("grp", "sets"),
        P("grp", "sets"),
        P("grp", "sets"),
    )
    out_specs = (P("grp", "sets"), P("grp", "sets"), P(("grp", "sets"), None))
    return jax.shard_map(body, mesh=mesh, in_specs=in_specs, out_specs=out_specs, check_vma=False)
```

```python
import functools
import math

import jax
import jax.numpy as jnp
from jax import lax
from jax.experimental import pallas as pl
from jax.experimental.pallas import tpu as pltpu
from jax.sharding import PartitionSpec as P

step_years = 0.25
bits_per_row = 15
lanes = 128


def spread_paths(values, dates):
    paths, columns = values.shape[0], values.shape[0] * dates
    path_of = lax.broadcasted_iota(jnp.int32, (paths, columns), 1) // dates
    own = lax.broadcasted_iota(jnp.int32, (paths, columns), 0)
    return lax.dot_general(
        values,
        (path_of == own).astype(jnp.float32),
        (((0,), (0,)), ((), ())),
        precision=lax.Precision.HIGHEST,
        preferred_element_type=jnp.float32,
    )


def sums_to_date(values, dates):
    width = values.shape[1]
    date = lax.broadcasted_iota(jnp.int32, values.shape, 1) % dates
    step = 1
    while step < dates:
        values = values + jnp.where(date >= step, pltpu.roll(values, step, 1), 0.0)
        step *= 2
    return values


def sums_from_date(values, dates):
    width = values.shape[1]
    date = lax.broadcasted_iota(jnp.int32, values.shape, 1) % dates
    step = 1
    while step < dates:
        values = values + jnp.where(date < dates - step, pltpu.roll(values, width - step, 1), 0.0)
        step *= 2
    return values


def used_currencies(currencies, counts):
    slot = lax.broadcasted_iota(jnp.int32, currencies.shape, 0)
    return jnp.where(slot < counts, currencies, -1)


def group_order(chips):
    return list(range(chips - 1, -1, -1))


def sibling_columns(chip, owned, core):
    return pl.ds(pl.multiple_of((2 * chip + core) * owned, owned), owned)


def row_flags(tile):
    shift = lax.broadcasted_iota(jnp.int32, (8, lanes), 0) + (8 * tile) % bits_per_row
    shift = jnp.where(shift >= bits_per_row, shift - bits_per_row, shift)
    return jnp.left_shift(jnp.int32(1), shift)


def masked_rows(exposure, bits, pair, flags, part):
    row = lax.broadcasted_iota(jnp.int32, (8, lanes), 0)
    values = exposure[16 * pair : 16 * pair + 16, part].astype(jnp.float32)
    kept = []
    for half in range(2):
        top = 16 * pair + 8 * half
        group = top // bits_per_row
        left = bits_per_row * (group + 1) - top
        packed = jnp.broadcast_to(bits[group : group + 1, part], (8, lanes))
        if left < 8:
            following = jnp.broadcast_to(bits[group + 1 : group + 2, part], (8, lanes))
            packed = jnp.where(row < left, packed, following)
        kept.append(jnp.where((packed & flags[half]) != 0, values[8 * half : 8 * half + 8], 0.0))
    return jnp.concatenate(kept, axis=0).astype(jnp.bfloat16)


def mask_rows(exposure, bits, masked_ref, core, owned, first, last):
    for pair in range(first // 16, last // 16):
        flags = [row_flags(2 * pair), row_flags(2 * pair + 1)]
        for chip in range(masked_ref.shape[1] // owned):
            masked_ref[16 * pair : 16 * pair + 16, chip * owned : (chip + 1) * owned] = masked_rows(
                exposure, bits, pair, flags, sibling_columns(chip, owned, core)
            )


def sum_sets(weights, masked_ref, terms_ref):
    owned = terms_ref.shape[2]
    for chip in range(0, terms_ref.shape[0], 2):
        terms = jnp.dot(
            weights,
            masked_ref[:, chip * owned : (chip + 2) * owned],
            preferred_element_type=jnp.float32,
        ).astype(terms_ref.dtype)
        terms_ref[chip] = terms[:, :owned]
        terms_ref[chip + 1] = terms[:, owned:]


def first_kernel(
    exposure_hbm,
    bits_hbm,
    currencies_hbm,
    counts_hbm,
    notional_hbm,
    fx_hbm,
    rates_hbm,
    start_hbm,
    handed_ref,
    masked_ref,
    exposure,
    bits,
    weights_ref,
    used_ref,
    fx_ref,
    rates_ref,
    start_ref,
    currencies_ref,
    counts_ref,
    notional_ref,
    sems,
    exposure_sems,
    bits_sems,
):
    sets = exposure.shape[0]
    chips, currency_count = handed_ref.shape[:2]
    parts = exposure_sems.shape[0]
    rows = sets // parts

    def exposure_copy(index):
        part = pl.ds(index * rows, rows)
        return pltpu.make_async_copy(
            exposure_hbm.at[part], exposure.at[part], exposure_sems.at[index]
        )

    bits_parts = bits_sems.shape[0]
    bits_width = bits.shape[1] // bits_parts

    def bits_copy(index):
        part = pl.ds(index * bits_width, bits_width)
        return pltpu.make_async_copy(bits_hbm.at[:, part], bits.at[:, part], bits_sems.at[index])

    copies = [
        pltpu.make_async_copy(source, target, sems.at[index])
        for index, (source, target) in enumerate(
            [
                (currencies_hbm, currencies_ref),
                (counts_hbm, counts_ref),
                (notional_hbm, notional_ref),
                (rates_hbm, rates_ref),
                (start_hbm, start_ref),
                (fx_hbm, fx_ref),
            ]
        )
    ]
    for index in range(bits_parts):
        bits_copy(index).start()
    for index in range(parts):
        exposure_copy(index).start()
    for copy in copies:
        copy.start()
    for index in range(bits_parts):
        bits_copy(index).wait()

    other = 1 - lax.axis_index("sets") % 2
    for index in range(parts):
        exposure_copy(index).wait()
        mask_rows(
            exposure, bits, masked_ref, other, handed_ref.shape[2], index * rows, (index + 1) * rows
        )

    for copy in copies:
        copy.wait()
    used = used_currencies(currencies_ref[...], counts_ref[...])
    used_ref[...] = used
    notional = notional_ref[...]
    currency = lax.broadcasted_iota(jnp.int32, (currency_count, sets), 0)
    weights = jnp.zeros((currency_count, sets), jnp.float32)
    for slot in range(used.shape[0]):
        weights = weights + jnp.where(
            currency == used[slot : slot + 1], notional[slot : slot + 1], 0.0
        )
    weights = weights.astype(jnp.bfloat16)
    weights_ref[...] = weights
    sum_sets(weights, masked_ref, handed_ref)


def second_kernel(
    dates,
    exposure,
    bits,
    weights_ref,
    fx_ref,
    rates_ref,
    start_ref,
    masked_ref,
    terms_ref,
    carried_ref,
    discount_ref,
    moved_ref,
):
    integral = spread_paths(start_ref[...], dates) + step_years * sums_to_date(rates_ref[...], dates)
    discount = jnp.exp(-integral)
    discount_ref[...] = discount
    moved = fx_ref[...] * discount
    moved_ref[...] = moved
    carried_ref[...] = moved.astype(jnp.bfloat16)
    own = lax.axis_index("sets") % 2
    mask_rows(exposure, bits, masked_ref, own, terms_ref.shape[2], 0, exposure.shape[0])
    sum_sets(weights_ref[...], masked_ref, terms_ref)


def merging_kernel(given_ref, terms_ref, carried_ref, outgoing_ref):
    chips, currency_count, owned = terms_ref.shape
    near = chips // 2
    half = lax.axis_index("sets") // (2 * near)
    carried = carried_ref[...]
    for place, chip in enumerate(group_order(near)):
        outgoing_ref[place, 0:currency_count, :] = carried
        for part, chosen in enumerate((half, 1 - half)):
            index = chosen * near + chip
            rows = pl.ds((1 + part) * currency_count, currency_count)
            outgoing_ref[place, rows, :] = (
                terms_ref[index] + given_ref[index].astype(jnp.float32)
            ).astype(jnp.bfloat16)


def halfway_kernel(arrived_ref, crossing_ref, summed_ref):
    near = arrived_ref.shape[0]
    currency_count = summed_ref.shape[0]
    for place, chip in enumerate(group_order(near)):
        crossing_ref[chip] = arrived_ref[place, 0:currency_count, :]
    sums = []
    for part in range(2):
        rows = pl.ds((1 + part) * currency_count, currency_count)
        total = arrived_ref[0, rows, :].astype(jnp.float32)
        for place in range(1, near):
            total = total + arrived_ref[place, rows, :].astype(jnp.float32)
        sums.append(total)
    summed_ref[...] = sums[0]
    crossing_ref[near] = sums[1].astype(jnp.bfloat16)


def unpacking_kernel(crossing_ref, crossed_ref, carried_ref):
    near = crossing_ref.shape[0] - 1
    half = lax.axis_index("sets") // (2 * near)
    for chip in range(near):
        carried_ref[half * near + chip] = crossing_ref[chip]
        carried_ref[(1 - half) * near + chip] = crossed_ref[chip]


def projection(masked, carried_ref):
    sets, half = masked.shape
    chips, currency_count, owned = carried_ref.shape
    here = min(chips, 8)
    projected = jnp.zeros((currency_count, sets), jnp.float32)
    for first in range(0, chips, here):
        carried = jnp.concatenate([carried_ref[first + chip] for chip in range(here)], axis=1)
        projected = projected + lax.dot_general(
            carried,
            masked[:, first * owned : (first + here) * owned],
            (((1,), (1,)), ((), ())),
            preferred_element_type=jnp.float32,
        )
    return projected


def adjoint_kernel(
    dates,
    summed_ref,
    crossed_ref,
    carried_ref,
    masked_own,
    moved_ref,
    discount_ref,
    fx_adjoint_ref,
    rate_adjoint_ref,
    projected_ref,
):
    near = crossed_ref.shape[0] - 1
    aggregate = summed_ref[...] + crossed_ref[near].astype(jnp.float32)
    fx_adjoint_ref[...] = aggregate * discount_ref[...]
    rate_adjoint_ref[...] = -step_years * sums_from_date(aggregate * moved_ref[...], dates)
    projected_ref[...] = projection(masked_own, carried_ref)


def picking_kernel(carried_ref, masked_other, projected_ref, used_ref, notional_adjoint_ref):
    sets, half = masked_other.shape
    currency_count = carried_ref.shape[1]
    projected = projected_ref[...] + projection(masked_other, carried_ref)
    used = used_ref[...]
    currency = lax.broadcasted_iota(jnp.int32, (currency_count, sets), 0)
    for slot in range(used.shape[0]):
        picked = jnp.sum(
            jnp.where(currency == used[slot : slot + 1], projected, 0.0), axis=0, keepdims=True
        )
        notional_adjoint_ref[slot : slot + 1, :] = picked * (1.0 / math.sqrt(2 * half))


def body(
    exposure_adjoint,
    positive_bits,
    currencies,
    mix_count,
    notional,
    fx_paths,
    short_rates,
    start_integral,
):
    sets, columns = exposure_adjoint.shape
    currency_count, owned = fx_paths.shape
    dates = owned // start_integral.shape[1]
    peers = columns // owned
    chips = peers // 2
    near = chips // 2
    slots = currencies.shape[1]
    in_vmem = pl.BlockSpec(memory_space=pltpu.VMEM)
    anywhere = pl.BlockSpec(memory_space=pl.ANY)
    params = pltpu.CompilerParams(vmem_limit_bytes=32 * 2**20)
    block = (currency_count, owned)

    def in_hbm(value):
        return pltpu.with_memory_space_constraint(value, pltpu.HBM)

    def swapped(value, offset=1):
        return lax.ppermute(value, "sets", [(peer, peer ^ offset) for peer in range(peers)])

    handed, masked_other, exposure, bits, weights, used, fx, rates, start = pl.pallas_call(
        first_kernel,
        out_shape=(
            pltpu.VMEM((chips,) + block, jnp.bfloat16),
            pltpu.VMEM((sets, columns // 2), jnp.bfloat16),
            pltpu.VMEM((sets, columns), jnp.bfloat16),
            pltpu.VMEM(positive_bits.shape, jnp.int32),
            pltpu.VMEM((currency_count, sets), jnp.bfloat16),
            pltpu.VMEM((slots, sets), jnp.int32),
            pltpu.VMEM(block, jnp.float32),
            pltpu.VMEM(block, jnp.float32),
            pltpu.VMEM((owned // dates, currency_count), jnp.float32),
        ),
        in_specs=[anywhere] * 8,
        out_specs=(in_vmem,) * 9,
        scratch_shapes=[
            pltpu.VMEM((slots, sets), jnp.int32),
            pltpu.VMEM((1, sets), jnp.int32),
            pltpu.VMEM((slots, sets), jnp.float32),
            pltpu.SemaphoreType.DMA((6,)),
            pltpu.SemaphoreType.DMA((math.gcd(sets // 16, 5),)),
            pltpu.SemaphoreType.DMA((4,)),
        ],
        compiler_params=params,
        name="first",
    )(
        in_hbm(exposure_adjoint),
        in_hbm(positive_bits),
        in_hbm(currencies.T),
        in_hbm(mix_count.reshape(1, sets)),
        in_hbm(notional.T),
        in_hbm(fx_paths),
        in_hbm(short_rates),
        in_hbm(start_integral.T),
    )
    given = swapped(handed)
    masked_own, terms, carried, discount, moved = pl.pallas_call(
        functools.partial(second_kernel, dates),
        out_shape=(
            pltpu.VMEM((sets, columns // 2), jnp.bfloat16),
            pltpu.VMEM((chips,) + block, jnp.float32),
            pltpu.VMEM(block, jnp.bfloat16),
            pltpu.VMEM(block, jnp.float32),
            pltpu.VMEM(block, jnp.float32),
        ),
        in_specs=[in_vmem] * 6,
        out_specs=(in_vmem,) * 5,
        compiler_params=params,
        name="second",
    )(exposure, bits, weights, fx, rates, start)
    outgoing = pl.pallas_call(
        merging_kernel,
        out_shape=pltpu.VMEM((near, 3 * currency_count, owned), jnp.bfloat16),
        in_specs=[in_vmem] * 3,
        out_specs=in_vmem,
        compiler_params=params,
        name="merging",
    )(given, terms, carried)
    arrived = lax.all_to_all(
        outgoing,
        "sets",
        0,
        0,
        axis_index_groups=[
            [2 * (half * near + chip) + core for chip in group_order(near)]
            for half in range(2)
            for core in range(2)
        ],
        tiled=True,
    )
    crossing, summed = pl.pallas_call(
        halfway_kernel,
        out_shape=(
            pltpu.VMEM((near + 1,) + block, jnp.bfloat16),
            pltpu.VMEM(block, jnp.float32),
        ),
        in_specs=[in_vmem],
        out_specs=(in_vmem,) * 2,
        compiler_params=params,
        name="halfway",
    )(arrived)
    crossed = swapped(crossing, 2 * near)
    carried_own = pl.pallas_call(
        unpacking_kernel,
        out_shape=pltpu.VMEM((chips,) + block, jnp.bfloat16),
        in_specs=[in_vmem] * 2,
        out_specs=in_vmem,
        compiler_params=params,
        name="unpacking",
    )(crossing, crossed)
    carried_other = swapped(carried_own)
    fx_adjoint, rate_adjoint, projected = pl.pallas_call(
        functools.partial(adjoint_kernel, dates),
        out_shape=(
            jax.ShapeDtypeStruct(block, jnp.float32),
            jax.ShapeDtypeStruct(block, jnp.float32),
            pltpu.VMEM((currency_count, sets), jnp.float32),
        ),
        in_specs=[in_vmem] * 6,
        out_specs=(in_vmem,) * 3,
        compiler_params=params,
        name="adjoint",
    )(summed, crossed, carried_own, masked_own, moved, discount)
    notional_adjoint = pl.pallas_call(
        picking_kernel,
        out_shape=jax.ShapeDtypeStruct((slots, sets), jnp.float32),
        in_specs=[in_vmem] * 4,
        out_specs=in_vmem,
        compiler_params=params,
        name="picking",
    )(carried_other, masked_other, projected, used)
    return fx_adjoint, rate_adjoint, notional_adjoint.T


def solution(mesh):
    in_specs = (
        P(("grp", "sets"), None),
        P(("grp", "sets"), None),
        P(("grp", "sets"), None),
        P(("grp", "sets")),
        P(("grp", "sets"), None),
        P("grp", "sets"),
        P("grp", "sets"),
        P("grp", "sets"),
    )
    out_specs = (P("grp", "sets"), P("grp", "sets"), P(("grp", "sets"), None))
    return jax.shard_map(body, mesh=mesh, in_specs=in_specs, out_specs=out_specs, check_vma=False)
```

```python
import functools
import math

import jax
import jax.numpy as jnp
from jax import lax
from jax.experimental import pallas as pl
from jax.experimental.pallas import tpu as pltpu
from jax.sharding import PartitionSpec as P

step_years = 0.25
bits_per_row = 15
lanes = 128


def spread_paths(values, dates):
    paths, columns = values.shape[0], values.shape[0] * dates
    path_of = lax.broadcasted_iota(jnp.int32, (paths, columns), 1) // dates
    own = lax.broadcasted_iota(jnp.int32, (paths, columns), 0)
    return lax.dot_general(
        values,
        (path_of == own).astype(jnp.float32),
        (((0,), (0,)), ((), ())),
        precision=lax.Precision.HIGHEST,
        preferred_element_type=jnp.float32,
    )


def sums_to_date(values, dates):
    width = values.shape[1]
    date = lax.broadcasted_iota(jnp.int32, values.shape, 1) % dates
    step = 1
    while step < dates:
        values = values + jnp.where(date >= step, pltpu.roll(values, step, 1), 0.0)
        step *= 2
    return values


def sums_from_date(values, dates):
    width = values.shape[1]
    date = lax.broadcasted_iota(jnp.int32, values.shape, 1) % dates
    step = 1
    while step < dates:
        values = values + jnp.where(date < dates - step, pltpu.roll(values, width - step, 1), 0.0)
        step *= 2
    return values


def used_currencies(currencies, counts):
    slot = lax.broadcasted_iota(jnp.int32, currencies.shape, 0)
    return jnp.where(slot < counts, currencies, -1)


def group_order(chips):
    middle = chips // 2
    return list(range(middle, chips)) + list(range(middle))


def sibling_columns(chip, owned, core):
    return pl.ds(pl.multiple_of((2 * chip + core) * owned, owned), owned)


def row_flags(tile):
    shift = lax.broadcasted_iota(jnp.int32, (8, lanes), 0) + (8 * tile) % bits_per_row
    shift = jnp.where(shift >= bits_per_row, shift - bits_per_row, shift)
    return jnp.left_shift(jnp.int32(1), shift)


def masked_rows(exposure, bits, pair, flags, part):
    row = lax.broadcasted_iota(jnp.int32, (8, lanes), 0)
    values = exposure[16 * pair : 16 * pair + 16, part].astype(jnp.float32)
    kept = []
    for half in range(2):
        top = 16 * pair + 8 * half
        group = top // bits_per_row
        left = bits_per_row * (group + 1) - top
        packed = jnp.broadcast_to(bits[group : group + 1, part], (8, lanes))
        if left < 8:
            following = jnp.broadcast_to(bits[group + 1 : group + 2, part], (8, lanes))
            packed = jnp.where(row < left, packed, following)
        kept.append(jnp.where((packed & flags[half]) != 0, values[8 * half : 8 * half + 8], 0.0))
    return jnp.concatenate(kept, axis=0).astype(jnp.bfloat16)


def mask_rows(exposure, bits, masked_ref, core, owned, first, last):
    for pair in range(first // 16, last // 16):
        flags = [row_flags(2 * pair), row_flags(2 * pair + 1)]
        for chip in range(masked_ref.shape[1] // owned):
            masked_ref[16 * pair : 16 * pair + 16, chip * owned : (chip + 1) * owned] = masked_rows(
                exposure, bits, pair, flags, sibling_columns(chip, owned, core)
            )


def sum_sets(weights, masked_ref, terms_ref):
    owned = terms_ref.shape[2]
    for chip in range(0, terms_ref.shape[0], 2):
        terms = jnp.dot(
            weights,
            masked_ref[0 : weights.shape[1], chip * owned : (chip + 2) * owned],
            preferred_element_type=jnp.float32,
        ).astype(terms_ref.dtype)
        terms_ref[chip] = terms[:, :owned]
        terms_ref[chip + 1] = terms[:, owned:]


def first_kernel(
    exposure_hbm,
    bits_hbm,
    currencies_hbm,
    counts_hbm,
    notional_hbm,
    fx_hbm,
    rates_hbm,
    start_hbm,
    handed_ref,
    lent_ref,
    exposure,
    bits,
    weights_ref,
    used_ref,
    fx_ref,
    rates_ref,
    start_ref,
    currencies_ref,
    counts_ref,
    notional_ref,
    sems,
    exposure_sems,
    bits_sems,
):
    sets = exposure.shape[0]
    chips, currency_count = handed_ref.shape[:2]
    parts = exposure_sems.shape[0]
    rows = sets // parts

    def exposure_copy(index):
        part = pl.ds(index * rows, rows)
        return pltpu.make_async_copy(
            exposure_hbm.at[part], exposure.at[part], exposure_sems.at[index]
        )

    bits_parts = bits_sems.shape[0]
    bits_width = bits.shape[1] // bits_parts

    def bits_copy(index):
        part = pl.ds(index * bits_width, bits_width)
        return pltpu.make_async_copy(bits_hbm.at[:, part], bits.at[:, part], bits_sems.at[index])

    copies = [
        pltpu.make_async_copy(source, target, sems.at[index])
        for index, (source, target) in enumerate(
            [
                (currencies_hbm, currencies_ref),
                (counts_hbm, counts_ref),
                (notional_hbm, notional_ref),
                (rates_hbm, rates_ref),
                (start_hbm, start_ref),
                (fx_hbm, fx_ref),
            ]
        )
    ]
    for index in range(bits_parts):
        bits_copy(index).start()
    for index in range(parts):
        exposure_copy(index).start()
    for copy in copies:
        copy.start()
    for copy in copies:
        copy.wait()
    used = used_currencies(currencies_ref[...], counts_ref[...])
    used_ref[...] = used
    lent_ref[sets : sets + used.shape[0], 0:sets] = used.astype(jnp.float32).astype(jnp.bfloat16)
    notional = notional_ref[...]
    currency = lax.broadcasted_iota(jnp.int32, (currency_count, sets), 0)
    weights = jnp.zeros((currency_count, sets), jnp.float32)
    for slot in range(used.shape[0]):
        weights = weights + jnp.where(
            currency == used[slot : slot + 1], notional[slot : slot + 1], 0.0
        )
    weights = weights.astype(jnp.bfloat16)
    weights_ref[...] = weights
    for index in range(bits_parts):
        bits_copy(index).wait()

    other = 1 - lax.axis_index("sets") % 2
    for index in range(parts):
        exposure_copy(index).wait()
        mask_rows(
            exposure, bits, lent_ref, other, handed_ref.shape[2], index * rows, (index + 1) * rows
        )
    sum_sets(weights, lent_ref, handed_ref)


def second_kernel(
    dates,
    exposure,
    bits,
    weights_ref,
    fx_ref,
    rates_ref,
    start_ref,
    masked_ref,
    terms_ref,
    carried_ref,
    discount_ref,
    moved_ref,
):
    integral = spread_paths(start_ref[...], dates) + step_years * sums_to_date(rates_ref[...], dates)
    discount = jnp.exp(-integral)
    discount_ref[...] = discount
    moved = fx_ref[...] * discount
    moved_ref[...] = moved
    carried_ref[...] = moved.astype(jnp.bfloat16)
    own = lax.axis_index("sets") % 2
    mask_rows(exposure, bits, masked_ref, own, terms_ref.shape[2], 0, exposure.shape[0])
    sum_sets(weights_ref[...], masked_ref, terms_ref)


def merging_kernel(given_ref, terms_ref, carried_ref, outgoing_ref):
    chips, currency_count, owned = terms_ref.shape
    order = group_order(chips)
    carried = carried_ref[...]
    for place in range(chips):
        outgoing_ref[place, 0:currency_count, :] = carried
        outgoing_ref[place, currency_count:, :] = (
            terms_ref[order[place]] + given_ref[order[place]].astype(jnp.float32)
        ).astype(jnp.bfloat16)


def projecting_kernel(arrived_ref, masked_own, lent_ref, used_ref, own_ref, others_ref):
    sets, half = masked_own.shape
    chips, owned = arrived_ref.shape[0], arrived_ref.shape[2]
    currency_count = arrived_ref.shape[1] // 2
    slots = used_ref.shape[0]
    order = group_order(chips)
    place = [order.index(chip) for chip in range(chips)]
    here = min(chips, 8)
    currency = lax.broadcasted_iota(jnp.int32, (currency_count, sets), 0).astype(jnp.float32)
    used_own = used_ref[...].astype(jnp.float32)
    used_others = lent_ref[sets : sets + slots, 0:sets].astype(jnp.float32)
    for masked, used, picked_ref in (
        (lent_ref, used_others, others_ref),
        (masked_own, used_own, own_ref),
    ):
        projected = jnp.zeros((currency_count, sets), jnp.float32)
        for first in range(0, chips, here):
            carried = jnp.concatenate(
                [arrived_ref[place[first + chip], 0:currency_count, :] for chip in range(here)],
                axis=1,
            )
            projected = projected + lax.dot_general(
                carried,
                masked[0:sets, first * owned : (first + here) * owned],
                (((1,), (1,)), ((), ())),
                preferred_element_type=jnp.float32,
            )
        for slot in range(slots):
            picked_ref[slot : slot + 1, :] = jnp.sum(
                jnp.where(currency == used[slot : slot + 1], projected, 0.0), axis=0, keepdims=True
            )


def adjoint_kernel(
    dates, arrived_ref, moved_ref, discount_ref, fx_adjoint_ref, rate_adjoint_ref
):
    currency_count = moved_ref.shape[0]
    aggregate = arrived_ref[0, currency_count:, :].astype(jnp.float32)
    for chip in range(1, arrived_ref.shape[0]):
        aggregate = aggregate + arrived_ref[chip, currency_count:, :].astype(jnp.float32)
    fx_adjoint_ref[...] = aggregate * discount_ref[...]
    rate_adjoint_ref[...] = -step_years * sums_from_date(aggregate * moved_ref[...], dates)


def adding_kernel(columns, own_ref, given_ref, notional_adjoint_ref):
    notional_adjoint_ref[...] = (own_ref[...] + given_ref[...]) * (1.0 / math.sqrt(columns))


def body(
    exposure_adjoint,
    positive_bits,
    currencies,
    mix_count,
    notional,
    fx_paths,
    short_rates,
    start_integral,
):
    sets, columns = exposure_adjoint.shape
    currency_count, owned = fx_paths.shape
    dates = owned // start_integral.shape[1]
    peers = columns // owned
    chips = peers // 2
    slots = currencies.shape[1]
    in_vmem = pl.BlockSpec(memory_space=pltpu.VMEM)
    anywhere = pl.BlockSpec(memory_space=pl.ANY)
    params = pltpu.CompilerParams(vmem_limit_bytes=32 * 2**20)
    block = (currency_count, owned)

    def in_hbm(value):
        return pltpu.with_memory_space_constraint(value, pltpu.HBM)

    def swapped(value):
        return lax.ppermute(value, "sets", [(peer, peer ^ 1) for peer in range(peers)])

    handed, lent, exposure, bits, weights, used, fx, rates, start = pl.pallas_call(
        first_kernel,
        out_shape=(
            pltpu.VMEM((chips,) + block, jnp.bfloat16),
            pltpu.VMEM((sets + 16, columns // 2), jnp.bfloat16),
            pltpu.VMEM((sets, columns), jnp.bfloat16),
            pltpu.VMEM(positive_bits.shape, jnp.int32),
            pltpu.VMEM((currency_count, sets), jnp.bfloat16),
            pltpu.VMEM((slots, sets), jnp.int32),
            pltpu.VMEM(block, jnp.float32),
            pltpu.VMEM(block, jnp.float32),
            pltpu.VMEM((owned // dates, currency_count), jnp.float32),
        ),
        in_specs=[anywhere] * 8,
        out_specs=(in_vmem,) * 9,
        scratch_shapes=[
            pltpu.VMEM((slots, sets), jnp.int32),
            pltpu.VMEM((1, sets), jnp.int32),
            pltpu.VMEM((slots, sets), jnp.float32),
            pltpu.SemaphoreType.DMA((6,)),
            pltpu.SemaphoreType.DMA((math.gcd(sets // 16, 5),)),
            pltpu.SemaphoreType.DMA((4,)),
        ],
        compiler_params=params,
        name="first",
    )(
        in_hbm(exposure_adjoint),
        in_hbm(positive_bits),
        in_hbm(currencies.T),
        in_hbm(mix_count.reshape(1, sets)),
        in_hbm(notional.T),
        in_hbm(fx_paths),
        in_hbm(short_rates),
        in_hbm(start_integral.T),
    )
    given = swapped(handed)
    borrowed = swapped(lent)
    masked_own, terms, carried, discount, moved = pl.pallas_call(
        functools.partial(second_kernel, dates),
        out_shape=(
            pltpu.VMEM((sets, columns // 2), jnp.bfloat16),
            pltpu.VMEM((chips,) + block, jnp.float32),
            pltpu.VMEM(block, jnp.bfloat16),
            pltpu.VMEM(block, jnp.float32),
            pltpu.VMEM(block, jnp.float32),
        ),
        in_specs=[in_vmem] * 6,
        out_specs=(in_vmem,) * 5,
        compiler_params=params,
        name="second",
    )(exposure, bits, weights, fx, rates, start)
    outgoing = pl.pallas_call(
        merging_kernel,
        out_shape=pltpu.VMEM((chips, 2 * currency_count, owned), jnp.bfloat16),
        in_specs=[in_vmem] * 3,
        out_specs=in_vmem,
        compiler_params=params,
        name="merging",
    )(given, terms, carried)
    arrived = lax.all_to_all(
        outgoing,
        "sets",
        0,
        0,
        axis_index_groups=[[2 * chip + core for chip in group_order(chips)] for core in range(2)],
        tiled=True,
    )
    own_part, others_part = pl.pallas_call(
        projecting_kernel,
        out_shape=(pltpu.VMEM((slots, sets), jnp.float32),) * 2,
        in_specs=[in_vmem] * 4,
        out_specs=(in_vmem,) * 2,
        compiler_params=params,
        name="projecting",
    )(arrived, masked_own, borrowed, used)
    given_part = swapped(others_part)
    fx_adjoint, rate_adjoint = pl.pallas_call(
        functools.partial(adjoint_kernel, dates),
        out_shape=(jax.ShapeDtypeStruct(block, jnp.float32),) * 2,
        in_specs=[in_vmem] * 3,
        out_specs=(in_vmem,) * 2,
        compiler_params=params,
        name="adjoint",
    )(arrived, moved, discount)
    notional_adjoint = pl.pallas_call(
        functools.partial(adding_kernel, columns),
        out_shape=jax.ShapeDtypeStruct((slots, sets), jnp.float32),
        in_specs=[in_vmem] * 2,
        out_specs=in_vmem,
        compiler_params=params,
        name="adding",
    )(own_part, given_part)
    return fx_adjoint, rate_adjoint, notional_adjoint.T


def solution(mesh):
    in_specs = (
        P(("grp", "sets"), None),
        P(("grp", "sets"), None),
        P(("grp", "sets"), None),
        P(("grp", "sets")),
        P(("grp", "sets"), None),
        P("grp", "sets"),
        P("grp", "sets"),
        P("grp", "sets"),
    )
    out_specs = (P("grp", "sets"), P("grp", "sets"), P(("grp", "sets"), None))
    return jax.shard_map(body, mesh=mesh, in_specs=in_specs, out_specs=out_specs, check_vma=False)
```

```python
import functools
import math

import jax
import jax.numpy as jnp
from jax import lax
from jax.experimental import pallas as pl
from jax.experimental.pallas import tpu as pltpu
from jax.sharding import PartitionSpec as P

step_years = 0.25
bits_per_row = 15
lanes = 128


def spread_paths(values, dates):
    paths, columns = values.shape[0], values.shape[0] * dates
    path_of = lax.broadcasted_iota(jnp.int32, (paths, columns), 1) // dates
    own = lax.broadcasted_iota(jnp.int32, (paths, columns), 0)
    return lax.dot_general(
        values,
        (path_of == own).astype(jnp.float32),
        (((0,), (0,)), ((), ())),
        precision=lax.Precision.HIGHEST,
        preferred_element_type=jnp.float32,
    )


def sums_to_date(values, dates):
    width = values.shape[1]
    date = lax.broadcasted_iota(jnp.int32, values.shape, 1) % dates
    step = 1
    while step < dates:
        values = values + jnp.where(date >= step, pltpu.roll(values, step, 1), 0.0)
        step *= 2
    return values


def sums_from_date(values, dates):
    width = values.shape[1]
    date = lax.broadcasted_iota(jnp.int32, values.shape, 1) % dates
    step = 1
    while step < dates:
        values = values + jnp.where(date < dates - step, pltpu.roll(values, width - step, 1), 0.0)
        step *= 2
    return values


def used_currencies(currencies, counts):
    slot = lax.broadcasted_iota(jnp.int32, currencies.shape, 0)
    return jnp.where(slot < counts, currencies, -1)


def group_order(chips):
    middle = chips // 2
    far, near = list(range(middle, chips)), list(range(middle))
    cut = middle // 2
    return far[:cut] + near[:1] + far[cut:] + near[1:]


def sibling_columns(chip, owned, core):
    return pl.ds(pl.multiple_of((2 * chip + core) * owned, owned), owned)


def row_flags(tile):
    shift = lax.broadcasted_iota(jnp.int32, (8, lanes), 0) + (8 * tile) % bits_per_row
    shift = jnp.where(shift >= bits_per_row, shift - bits_per_row, shift)
    return jnp.left_shift(jnp.int32(1), shift)


def masked_rows(exposure, bits, pair, flags, part):
    row = lax.broadcasted_iota(jnp.int32, (8, lanes), 0)
    values = exposure[16 * pair : 16 * pair + 16, part].astype(jnp.float32)
    kept = []
    for half in range(2):
        top = 16 * pair + 8 * half
        group = top // bits_per_row
        left = bits_per_row * (group + 1) - top
        packed = jnp.broadcast_to(bits[group : group + 1, part], (8, lanes))
        if left < 8:
            following = jnp.broadcast_to(bits[group + 1 : group + 2, part], (8, lanes))
            packed = jnp.where(row < left, packed, following)
        kept.append(jnp.where((packed & flags[half]) != 0, values[8 * half : 8 * half + 8], 0.0))
    return jnp.concatenate(kept, axis=0).astype(jnp.bfloat16)


def mask_and_sum(exposure, bits, weights, masked_ref, terms_ref, core):
    sets = exposure.shape[0]
    owned = terms_ref.shape[2]
    for first in range(0, terms_ref.shape[0], 2):
        rows = []
        for pair in range(sets // 16):
            flags = [row_flags(2 * pair), row_flags(2 * pair + 1)]
            rows.append(
                jnp.concatenate(
                    [
                        masked_rows(
                            exposure, bits, pair, flags, sibling_columns(chip, owned, core)
                        )
                        for chip in (first, first + 1)
                    ],
                    axis=1,
                )
            )
        masked = jnp.concatenate(rows, axis=0)
        masked_ref[:, first * owned : (first + 2) * owned] = masked
        terms = jnp.dot(weights, masked, preferred_element_type=jnp.float32)
        terms = terms.astype(terms_ref.dtype)
        terms_ref[first] = terms[:, :owned]
        terms_ref[first + 1] = terms[:, owned:]


def first_kernel(
    exposure_hbm,
    bits_hbm,
    currencies_hbm,
    counts_hbm,
    notional_hbm,
    fx_hbm,
    rates_hbm,
    start_hbm,
    handed_ref,
    masked_ref,
    exposure,
    bits,
    weights_ref,
    used_ref,
    fx_ref,
    rates_ref,
    start_ref,
    currencies_ref,
    counts_ref,
    notional_ref,
    sems,
    exposure_sems,
    bits_sems,
):
    sets = exposure.shape[0]
    chips, currency_count = handed_ref.shape[:2]
    parts = exposure_sems.shape[0]
    rows = sets // parts

    def exposure_copy(index):
        part = pl.ds(index * rows, rows)
        return pltpu.make_async_copy(
            exposure_hbm.at[part], exposure.at[part], exposure_sems.at[index]
        )

    bits_parts = bits_sems.shape[0]
    bits_width = bits.shape[1] // bits_parts

    def bits_copy(index):
        part = pl.ds(index * bits_width, bits_width)
        return pltpu.make_async_copy(bits_hbm.at[:, part], bits.at[:, part], bits_sems.at[index])

    copies = [
        pltpu.make_async_copy(source, target, sems.at[index])
        for index, (source, target) in enumerate(
            [
                (currencies_hbm, currencies_ref),
                (counts_hbm, counts_ref),
                (notional_hbm, notional_ref),
                (rates_hbm, rates_ref),
                (start_hbm, start_ref),
                (fx_hbm, fx_ref),
            ]
        )
    ]
    for index in range(bits_parts):
        bits_copy(index).start()
    for index in range(parts):
        exposure_copy(index).start()
    for copy in copies:
        copy.start()
    for copy in copies:
        copy.wait()
    used = used_currencies(currencies_ref[...], counts_ref[...])
    used_ref[...] = used
    notional = notional_ref[...]
    currency = lax.broadcasted_iota(jnp.int32, (currency_count, sets), 0)
    weights = jnp.zeros((currency_count, sets), jnp.float32)
    for slot in range(used.shape[0]):
        weights = weights + jnp.where(
            currency == used[slot : slot + 1], notional[slot : slot + 1], 0.0
        )
    weights = weights.astype(jnp.bfloat16)
    weights_ref[...] = weights
    for index in range(bits_parts):
        bits_copy(index).wait()
    for index in range(parts):
        exposure_copy(index).wait()
    other = 1 - lax.axis_index("sets") % 2
    mask_and_sum(exposure, bits, weights, masked_ref, handed_ref, other)


def second_kernel(
    dates,
    exposure,
    bits,
    weights_ref,
    fx_ref,
    rates_ref,
    start_ref,
    masked_ref,
    terms_ref,
    carried_ref,
    discount_ref,
    moved_ref,
):
    integral = spread_paths(start_ref[...], dates) + step_years * sums_to_date(rates_ref[...], dates)
    discount = jnp.exp(-integral)
    discount_ref[...] = discount
    moved = fx_ref[...] * discount
    moved_ref[...] = moved
    carried_ref[...] = moved.astype(jnp.bfloat16)
    own = lax.axis_index("sets") % 2
    mask_and_sum(exposure, bits, weights_ref[...], masked_ref, terms_ref, own)


def merging_kernel(given_ref, terms_ref, carried_ref, outgoing_ref):
    chips, currency_count, owned = terms_ref.shape
    order = group_order(chips)
    carried = carried_ref[...]
    for place in range(chips):
        outgoing_ref[place, 0:currency_count, :] = carried
        outgoing_ref[place, currency_count:, :] = (
            terms_ref[order[place]] + given_ref[order[place]].astype(jnp.float32)
        ).astype(jnp.bfloat16)


def unpacking_kernel(arrived_ref, carried_ref):
    chips, currency_count, owned = carried_ref.shape
    order = group_order(chips)
    for place in range(chips):
        carried_ref[order[place]] = arrived_ref[place, 0:currency_count, :]


def projection(masked, carried_ref):
    sets, half = masked.shape
    chips, currency_count, owned = carried_ref.shape
    here = min(chips, 8)
    projected = jnp.zeros((currency_count, sets), jnp.float32)
    for first in range(0, chips, here):
        carried = jnp.concatenate([carried_ref[first + chip] for chip in range(here)], axis=1)
        projected = projected + lax.dot_general(
            carried,
            masked[:, first * owned : (first + here) * owned],
            (((1,), (1,)), ((), ())),
            preferred_element_type=jnp.float32,
        )
    return projected


def adjoint_kernel(
    dates,
    arrived_ref,
    carried_ref,
    masked_own,
    moved_ref,
    discount_ref,
    fx_adjoint_ref,
    rate_adjoint_ref,
    projected_ref,
):
    chips, currency_count, owned = carried_ref.shape
    aggregate = arrived_ref[0, currency_count:, :].astype(jnp.float32)
    for chip in range(1, chips):
        aggregate = aggregate + arrived_ref[chip, currency_count:, :].astype(jnp.float32)
    fx_adjoint_ref[...] = aggregate * discount_ref[...]
    rate_adjoint_ref[...] = -step_years * sums_from_date(aggregate * moved_ref[...], dates)
    projected_ref[...] = projection(masked_own, carried_ref)


def picking_kernel(carried_ref, masked_other, projected_ref, used_ref, notional_adjoint_ref):
    sets, half = masked_other.shape
    currency_count = carried_ref.shape[1]
    projected = projected_ref[...] + projection(masked_other, carried_ref)
    used = used_ref[...]
    currency = lax.broadcasted_iota(jnp.int32, (currency_count, sets), 0)
    for slot in range(used.shape[0]):
        picked = jnp.sum(
            jnp.where(currency == used[slot : slot + 1], projected, 0.0), axis=0, keepdims=True
        )
        notional_adjoint_ref[slot : slot + 1, :] = picked * (1.0 / math.sqrt(2 * half))


def body(
    exposure_adjoint,
    positive_bits,
    currencies,
    mix_count,
    notional,
    fx_paths,
    short_rates,
    start_integral,
):
    sets, columns = exposure_adjoint.shape
    currency_count, owned = fx_paths.shape
    dates = owned // start_integral.shape[1]
    peers = columns // owned
    chips = peers // 2
    slots = currencies.shape[1]
    in_vmem = pl.BlockSpec(memory_space=pltpu.VMEM)
    anywhere = pl.BlockSpec(memory_space=pl.ANY)
    params = pltpu.CompilerParams(vmem_limit_bytes=32 * 2**20)
    block = (currency_count, owned)

    def in_hbm(value):
        return pltpu.with_memory_space_constraint(value, pltpu.HBM)

    def swapped(value):
        return lax.ppermute(value, "sets", [(peer, peer ^ 1) for peer in range(peers)])

    handed, masked_other, exposure, bits, weights, used, fx, rates, start = pl.pallas_call(
        first_kernel,
        out_shape=(
            pltpu.VMEM((chips,) + block, jnp.bfloat16),
            pltpu.VMEM((sets, columns // 2), jnp.bfloat16),
            pltpu.VMEM((sets, columns), jnp.bfloat16),
            pltpu.VMEM(positive_bits.shape, jnp.int32),
            pltpu.VMEM((currency_count, sets), jnp.bfloat16),
            pltpu.VMEM((slots, sets), jnp.int32),
            pltpu.VMEM(block, jnp.float32),
            pltpu.VMEM(block, jnp.float32),
            pltpu.VMEM((owned // dates, currency_count), jnp.float32),
        ),
        in_specs=[anywhere] * 8,
        out_specs=(in_vmem,) * 9,
        scratch_shapes=[
            pltpu.VMEM((slots, sets), jnp.int32),
            pltpu.VMEM((1, sets), jnp.int32),
            pltpu.VMEM((slots, sets), jnp.float32),
            pltpu.SemaphoreType.DMA((6,)),
            pltpu.SemaphoreType.DMA((math.gcd(sets // 16, 5),)),
            pltpu.SemaphoreType.DMA((4,)),
        ],
        compiler_params=params,
        name="first",
    )(
        in_hbm(exposure_adjoint),
        in_hbm(positive_bits),
        in_hbm(currencies.T),
        in_hbm(mix_count.reshape(1, sets)),
        in_hbm(notional.T),
        in_hbm(fx_paths),
        in_hbm(short_rates),
        in_hbm(start_integral.T),
    )
    given = swapped(handed)
    masked_own, terms, carried, discount, moved = pl.pallas_call(
        functools.partial(second_kernel, dates),
        out_shape=(
            pltpu.VMEM((sets, columns // 2), jnp.bfloat16),
            pltpu.VMEM((chips,) + block, jnp.float32),
            pltpu.VMEM(block, jnp.bfloat16),
            pltpu.VMEM(block, jnp.float32),
            pltpu.VMEM(block, jnp.float32),
        ),
        in_specs=[in_vmem] * 6,
        out_specs=(in_vmem,) * 5,
        compiler_params=params,
        name="second",
    )(exposure, bits, weights, fx, rates, start)
    outgoing = pl.pallas_call(
        merging_kernel,
        out_shape=pltpu.VMEM((chips, 2 * currency_count, owned), jnp.bfloat16),
        in_specs=[in_vmem] * 3,
        out_specs=in_vmem,
        compiler_params=params,
        name="merging",
    )(given, terms, carried)
    arrived = lax.all_to_all(
        outgoing,
        "sets",
        0,
        0,
        axis_index_groups=[[2 * chip + core for chip in group_order(chips)] for core in range(2)],
        tiled=True,
    )
    carried_own = pl.pallas_call(
        unpacking_kernel,
        out_shape=pltpu.VMEM((chips,) + block, jnp.bfloat16),
        in_specs=[in_vmem],
        out_specs=in_vmem,
        compiler_params=params,
        name="unpacking",
    )(arrived)
    carried_other = swapped(carried_own)
    fx_adjoint, rate_adjoint, projected = pl.pallas_call(
        functools.partial(adjoint_kernel, dates),
        out_shape=(
            jax.ShapeDtypeStruct(block, jnp.float32),
            jax.ShapeDtypeStruct(block, jnp.float32),
            pltpu.VMEM((currency_count, sets), jnp.float32),
        ),
        in_specs=[in_vmem] * 5,
        out_specs=(in_vmem,) * 3,
        compiler_params=params,
        name="adjoint",
    )(arrived, carried_own, masked_own, moved, discount)
    notional_adjoint = pl.pallas_call(
        picking_kernel,
        out_shape=jax.ShapeDtypeStruct((slots, sets), jnp.float32),
        in_specs=[in_vmem] * 4,
        out_specs=in_vmem,
        compiler_params=params,
        name="picking",
    )(carried_other, masked_other, projected, used)
    return fx_adjoint, rate_adjoint, notional_adjoint.T


def solution(mesh):
    in_specs = (
        P(("grp", "sets"), None),
        P(("grp", "sets"), None),
        P(("grp", "sets"), None),
        P(("grp", "sets")),
        P(("grp", "sets"), None),
        P("grp", "sets"),
        P("grp", "sets"),
        P("grp", "sets"),
    )
    out_specs = (P("grp", "sets"), P("grp", "sets"), P(("grp", "sets"), None))
    return jax.shard_map(body, mesh=mesh, in_specs=in_specs, out_specs=out_specs, check_vma=False)
```

```python
import functools
import math

import jax
import jax.numpy as jnp
from jax import lax
from jax.experimental import pallas as pl
from jax.experimental.pallas import tpu as pltpu
from jax.sharding import PartitionSpec as P

step_years = 0.25
bits_per_row = 15
lanes = 128


def spread_paths(values, dates):
    paths, columns = values.shape[0], values.shape[0] * dates
    path_of = lax.broadcasted_iota(jnp.int32, (paths, columns), 1) // dates
    own = lax.broadcasted_iota(jnp.int32, (paths, columns), 0)
    return lax.dot_general(
        values,
        (path_of == own).astype(jnp.float32),
        (((0,), (0,)), ((), ())),
        precision=lax.Precision.HIGHEST,
        preferred_element_type=jnp.float32,
    )


def sums_to_date(values, dates):
    width = values.shape[1]
    date = lax.broadcasted_iota(jnp.int32, values.shape, 1) % dates
    step = 1
    while step < dates:
        values = values + jnp.where(date >= step, pltpu.roll(values, step, 1), 0.0)
        step *= 2
    return values


def sums_from_date(values, dates):
    width = values.shape[1]
    date = lax.broadcasted_iota(jnp.int32, values.shape, 1) % dates
    step = 1
    while step < dates:
        values = values + jnp.where(date < dates - step, pltpu.roll(values, width - step, 1), 0.0)
        step *= 2
    return values


def used_currencies(currencies, counts):
    slot = lax.broadcasted_iota(jnp.int32, currencies.shape, 0)
    return jnp.where(slot < counts, currencies, -1)


def group_order(chips):
    middle = chips // 2
    far, near = list(range(middle, chips)), list(range(middle))
    cut = middle // 2
    return far[:cut] + near[:1] + far[cut:] + near[1:]


def sibling_columns(chip, owned, core):
    return pl.ds(pl.multiple_of((2 * chip + core) * owned, owned), owned)


def row_flags(tile):
    shift = lax.broadcasted_iota(jnp.int32, (8, lanes), 0) + (8 * tile) % bits_per_row
    shift = jnp.where(shift >= bits_per_row, shift - bits_per_row, shift)
    return jnp.left_shift(jnp.int32(1), shift)


def masked_rows(exposure, bits, pair, flags, column, packed_columns):
    row = lax.broadcasted_iota(jnp.int32, (8, lanes), 0)
    values = exposure[16 * pair : 16 * pair + 16, column : column + lanes].astype(jnp.float32)
    kept = []
    for half in range(2):
        top = 16 * pair + 8 * half
        group = top // bits_per_row
        left = bits_per_row * (group + 1) - top
        packed = jnp.broadcast_to(bits[group : group + 1, packed_columns], (8, lanes))
        if left < 8:
            following = jnp.broadcast_to(bits[group + 1 : group + 2, packed_columns], (8, lanes))
            packed = jnp.where(row < left, packed, following)
        kept.append(jnp.where((packed & flags[half]) != 0, values[8 * half : 8 * half + 8], 0.0))
    return jnp.concatenate(kept, axis=0).astype(jnp.bfloat16)


def mask_and_sum(exposure, bits, weights, masked_ref, terms_ref, core):
    sets = exposure.shape[0]
    owned = terms_ref.shape[2]
    for first in range(0, terms_ref.shape[0], 2):
        rows = []
        for pair in range(sets // 16):
            flags = [row_flags(2 * pair), row_flags(2 * pair + 1)]
            rows.append(
                jnp.concatenate(
                    [
                        masked_rows(
                            exposure,
                            bits,
                            pair,
                            flags,
                            chip * owned,
                            sibling_columns(chip, owned, core),
                        )
                        for chip in (first, first + 1)
                    ],
                    axis=1,
                )
            )
        masked = jnp.concatenate(rows, axis=0)
        masked_ref[:, first * owned : (first + 2) * owned] = masked
        terms = jnp.dot(weights, masked, preferred_element_type=jnp.float32)
        terms = terms.astype(terms_ref.dtype)
        terms_ref[first] = terms[:, :owned]
        terms_ref[first + 1] = terms[:, owned:]


def block_copies(exposure_hbm, exposure, sems, core, owned):
    return [
        pltpu.make_async_copy(
            exposure_hbm.at[:, sibling_columns(chip, owned, core)],
            exposure.at[:, pl.ds(chip * owned, owned)],
            sems.at[chip],
        )
        for chip in range(exposure.shape[1] // owned)
    ]


def first_kernel(
    exposure_hbm,
    bits_hbm,
    currencies_hbm,
    counts_hbm,
    notional_hbm,
    handed_ref,
    masked_ref,
    bits,
    weights_ref,
    used_ref,
    exposure,
    currencies_ref,
    counts_ref,
    notional_ref,
    sems,
    exposure_sems,
    bits_sems,
):
    sets = exposure.shape[0]
    chips, currency_count, owned = handed_ref.shape
    other = 1 - lax.axis_index("sets") % 2
    bits_parts = bits_sems.shape[0]
    bits_width = bits.shape[1] // bits_parts

    def bits_copy(index):
        part = pl.ds(index * bits_width, bits_width)
        return pltpu.make_async_copy(bits_hbm.at[:, part], bits.at[:, part], bits_sems.at[index])

    copies = [
        pltpu.make_async_copy(source, target, sems.at[index])
        for index, (source, target) in enumerate(
            [
                (currencies_hbm, currencies_ref),
                (counts_hbm, counts_ref),
                (notional_hbm, notional_ref),
            ]
        )
    ]
    exposure_copies = block_copies(exposure_hbm, exposure, exposure_sems, other, owned)
    for copy in exposure_copies:
        copy.start()
    for index in range(bits_parts):
        bits_copy(index).start()
    for copy in copies:
        copy.start()
    for copy in copies:
        copy.wait()

    used = used_currencies(currencies_ref[...], counts_ref[...])
    used_ref[...] = used
    notional = notional_ref[...]
    currency = lax.broadcasted_iota(jnp.int32, (currency_count, sets), 0)
    weights = jnp.zeros((currency_count, sets), jnp.float32)
    for slot in range(used.shape[0]):
        weights = weights + jnp.where(
            currency == used[slot : slot + 1], notional[slot : slot + 1], 0.0
        )
    weights = weights.astype(jnp.bfloat16)
    weights_ref[...] = weights
    for index in range(bits_parts):
        bits_copy(index).wait()
    for copy in exposure_copies:
        copy.wait()
    mask_and_sum(exposure, bits, weights, masked_ref, handed_ref, other)


def second_kernel(
    dates,
    exposure_hbm,
    fx_hbm,
    rates_hbm,
    start_hbm,
    bits,
    weights_ref,
    masked_ref,
    terms_ref,
    carried_ref,
    discount_ref,
    moved_ref,
    exposure,
    fx_ref,
    rates_ref,
    start_ref,
    sems,
    exposure_sems,
):
    owned = terms_ref.shape[2]
    own = lax.axis_index("sets") % 2
    copies = [
        pltpu.make_async_copy(source, target, sems.at[index])
        for index, (source, target) in enumerate(
            [(rates_hbm, rates_ref), (start_hbm, start_ref), (fx_hbm, fx_ref)]
        )
    ]
    exposure_copies = block_copies(exposure_hbm, exposure, exposure_sems, own, owned)
    for copy in exposure_copies + copies:
        copy.start()
    for copy in copies:
        copy.wait()
    integral = spread_paths(start_ref[...], dates) + step_years * sums_to_date(rates_ref[...], dates)
    discount = jnp.exp(-integral)
    discount_ref[...] = discount
    moved = fx_ref[...] * discount
    moved_ref[...] = moved
    carried_ref[...] = moved.astype(jnp.bfloat16)
    for copy in exposure_copies:
        copy.wait()
    mask_and_sum(exposure, bits, weights_ref[...], masked_ref, terms_ref, own)


def merging_kernel(given_ref, terms_ref, carried_ref, outgoing_ref):
    chips, currency_count, owned = terms_ref.shape
    order = group_order(chips)
    carried = carried_ref[...]
    for place in range(chips):
        outgoing_ref[place, 0:currency_count, :] = carried
        outgoing_ref[place, currency_count:, :] = (
            terms_ref[order[place]] + given_ref[order[place]].astype(jnp.float32)
        ).astype(jnp.bfloat16)


def unpacking_kernel(arrived_ref, carried_ref):
    chips, currency_count, owned = carried_ref.shape
    order = group_order(chips)
    for place in range(chips):
        carried_ref[order[place]] = arrived_ref[place, 0:currency_count, :]


def projection(masked, carried_ref):
    sets, half = masked.shape
    chips, currency_count, owned = carried_ref.shape
    here = min(chips, 8)
    projected = jnp.zeros((currency_count, sets), jnp.float32)
    for first in range(0, chips, here):
        carried = jnp.concatenate([carried_ref[first + chip] for chip in range(here)], axis=1)
        projected = projected + lax.dot_general(
            carried,
            masked[:, first * owned : (first + here) * owned],
            (((1,), (1,)), ((), ())),
            preferred_element_type=jnp.float32,
        )
    return projected


def adjoint_kernel(
    dates,
    arrived_ref,
    carried_ref,
    masked_own,
    moved_ref,
    discount_ref,
    fx_adjoint_ref,
    rate_adjoint_ref,
    projected_ref,
):
    chips, currency_count, owned = carried_ref.shape
    aggregate = arrived_ref[0, currency_count:, :].astype(jnp.float32)
    for chip in range(1, chips):
        aggregate = aggregate + arrived_ref[chip, currency_count:, :].astype(jnp.float32)
    fx_adjoint_ref[...] = aggregate * discount_ref[...]
    rate_adjoint_ref[...] = -step_years * sums_from_date(aggregate * moved_ref[...], dates)
    projected_ref[...] = projection(masked_own, carried_ref)


def picking_kernel(carried_ref, masked_other, projected_ref, used_ref, notional_adjoint_ref):
    sets, half = masked_other.shape
    currency_count = carried_ref.shape[1]
    projected = projected_ref[...] + projection(masked_other, carried_ref)
    used = used_ref[...]
    currency = lax.broadcasted_iota(jnp.int32, (currency_count, sets), 0)
    for slot in range(used.shape[0]):
        picked = jnp.sum(
            jnp.where(currency == used[slot : slot + 1], projected, 0.0), axis=0, keepdims=True
        )
        notional_adjoint_ref[slot : slot + 1, :] = picked * (1.0 / math.sqrt(2 * half))


def body(
    exposure_adjoint,
    positive_bits,
    currencies,
    mix_count,
    notional,
    fx_paths,
    short_rates,
    start_integral,
):
    sets, columns = exposure_adjoint.shape
    currency_count, owned = fx_paths.shape
    dates = owned // start_integral.shape[1]
    peers = columns // owned
    chips = peers // 2
    slots = currencies.shape[1]
    in_vmem = pl.BlockSpec(memory_space=pltpu.VMEM)
    anywhere = pl.BlockSpec(memory_space=pl.ANY)
    params = pltpu.CompilerParams(vmem_limit_bytes=32 * 2**20)
    block = (currency_count, owned)

    def in_hbm(value):
        return pltpu.with_memory_space_constraint(value, pltpu.HBM)

    def swapped(value):
        return lax.ppermute(value, "sets", [(peer, peer ^ 1) for peer in range(peers)])

    exposure_adjoint = in_hbm(exposure_adjoint)
    handed, masked_other, bits, weights, used = pl.pallas_call(
        first_kernel,
        out_shape=(
            pltpu.VMEM((chips,) + block, jnp.bfloat16),
            pltpu.VMEM((sets, columns // 2), jnp.bfloat16),
            pltpu.VMEM(positive_bits.shape, jnp.int32),
            pltpu.VMEM((currency_count, sets), jnp.bfloat16),
            pltpu.VMEM((slots, sets), jnp.int32),
        ),
        in_specs=[anywhere] * 5,
        out_specs=(in_vmem,) * 5,
        scratch_shapes=[
            pltpu.VMEM((sets, columns // 2), jnp.bfloat16),
            pltpu.VMEM((slots, sets), jnp.int32),
            pltpu.VMEM((1, sets), jnp.int32),
            pltpu.VMEM((slots, sets), jnp.float32),
            pltpu.SemaphoreType.DMA((3,)),
            pltpu.SemaphoreType.DMA((chips,)),
            pltpu.SemaphoreType.DMA((4,)),
        ],
        compiler_params=params,
        name="first",
    )(
        exposure_adjoint,
        in_hbm(positive_bits),
        in_hbm(currencies.T),
        in_hbm(mix_count.reshape(1, sets)),
        in_hbm(notional.T),
    )
    given = swapped(handed)
    masked_own, terms, carried, discount, moved = pl.pallas_call(
        functools.partial(second_kernel, dates),
        out_shape=(
            pltpu.VMEM((sets, columns // 2), jnp.bfloat16),
            pltpu.VMEM((chips,) + block, jnp.float32),
            pltpu.VMEM(block, jnp.bfloat16),
            pltpu.VMEM(block, jnp.float32),
            pltpu.VMEM(block, jnp.float32),
        ),
        in_specs=[anywhere] * 4 + [in_vmem] * 2,
        out_specs=(in_vmem,) * 5,
        scratch_shapes=[
            pltpu.VMEM((sets, columns // 2), jnp.bfloat16),
            pltpu.VMEM(block, jnp.float32),
            pltpu.VMEM(block, jnp.float32),
            pltpu.VMEM((owned // dates, currency_count), jnp.float32),
            pltpu.SemaphoreType.DMA((3,)),
            pltpu.SemaphoreType.DMA((chips,)),
        ],
        compiler_params=params,
        name="second",
    )(
        exposure_adjoint,
        in_hbm(fx_paths),
        in_hbm(short_rates),
        in_hbm(start_integral.T),
        bits,
        weights,
    )
    outgoing = pl.pallas_call(
        merging_kernel,
        out_shape=pltpu.VMEM((chips, 2 * currency_count, owned), jnp.bfloat16),
        in_specs=[in_vmem] * 3,
        out_specs=in_vmem,
        compiler_params=params,
        name="merging",
    )(given, terms, carried)
    arrived = lax.all_to_all(
        outgoing,
        "sets",
        0,
        0,
        axis_index_groups=[[2 * chip + core for chip in group_order(chips)] for core in range(2)],
        tiled=True,
    )
    carried_own = pl.pallas_call(
        unpacking_kernel,
        out_shape=pltpu.VMEM((chips,) + block, jnp.bfloat16),
        in_specs=[in_vmem],
        out_specs=in_vmem,
        compiler_params=params,
        name="unpacking",
    )(arrived)
    carried_other = swapped(carried_own)
    fx_adjoint, rate_adjoint, projected = pl.pallas_call(
        functools.partial(adjoint_kernel, dates),
        out_shape=(
            jax.ShapeDtypeStruct(block, jnp.float32),
            jax.ShapeDtypeStruct(block, jnp.float32),
            pltpu.VMEM((currency_count, sets), jnp.float32),
        ),
        in_specs=[in_vmem] * 5,
        out_specs=(in_vmem,) * 3,
        compiler_params=params,
        name="adjoint",
    )(arrived, carried_own, masked_own, moved, discount)
    notional_adjoint = pl.pallas_call(
        picking_kernel,
        out_shape=jax.ShapeDtypeStruct((slots, sets), jnp.float32),
        in_specs=[in_vmem] * 4,
        out_specs=in_vmem,
        compiler_params=params,
        name="picking",
    )(carried_other, masked_other, projected, used)
    return fx_adjoint, rate_adjoint, notional_adjoint.T


def solution(mesh):
    in_specs = (
        P(("grp", "sets"), None),
        P(("grp", "sets"), None),
        P(("grp", "sets"), None),
        P(("grp", "sets")),
        P(("grp", "sets"), None),
        P("grp", "sets"),
        P("grp", "sets"),
        P("grp", "sets"),
    )
    out_specs = (P("grp", "sets"), P("grp", "sets"), P(("grp", "sets"), None))
    return jax.shard_map(body, mesh=mesh, in_specs=in_specs, out_specs=out_specs, check_vma=False)
```

```python
import functools
import math

import jax
import jax.numpy as jnp
from jax import lax
from jax.experimental import pallas as pl
from jax.experimental.pallas import tpu as pltpu
from jax.sharding import PartitionSpec as P

step_years = 0.25
bits_per_row = 15
lanes = 128


def spread_paths(values, dates):
    paths, columns = values.shape[0], values.shape[0] * dates
    path_of = lax.broadcasted_iota(jnp.int32, (paths, columns), 1) // dates
    own = lax.broadcasted_iota(jnp.int32, (paths, columns), 0)
    return lax.dot_general(
        values,
        (path_of == own).astype(jnp.float32),
        (((0,), (0,)), ((), ())),
        precision=lax.Precision.HIGHEST,
        preferred_element_type=jnp.float32,
    )


def sums_to_date(values, dates):
    width = values.shape[1]
    date = lax.broadcasted_iota(jnp.int32, values.shape, 1) % dates
    step = 1
    while step < dates:
        values = values + jnp.where(date >= step, pltpu.roll(values, step, 1), 0.0)
        step *= 2
    return values


def sums_from_date(values, dates):
    width = values.shape[1]
    date = lax.broadcasted_iota(jnp.int32, values.shape, 1) % dates
    step = 1
    while step < dates:
        values = values + jnp.where(date < dates - step, pltpu.roll(values, width - step, 1), 0.0)
        step *= 2
    return values


def used_currencies(currencies, counts):
    slot = lax.broadcasted_iota(jnp.int32, currencies.shape, 0)
    return jnp.where(slot < counts, currencies, -1)


def group_order(chips):
    middle = chips // 2
    far, near = list(range(middle, chips)), list(range(middle))
    cut = middle // 2
    return far[:cut] + near[:1] + far[cut:] + near[1:]


def sibling_columns(chip, owned, core):
    return pl.ds(pl.multiple_of((2 * chip + core) * owned, owned), owned)


def row_flags(tile):
    shift = lax.broadcasted_iota(jnp.int32, (8, lanes), 0) + (8 * tile) % bits_per_row
    shift = jnp.where(shift >= bits_per_row, shift - bits_per_row, shift)
    return jnp.left_shift(jnp.int32(1), shift)


def masked_rows(exposure, bits, pair, flags, part):
    row = lax.broadcasted_iota(jnp.int32, (8, lanes), 0)
    values = exposure[16 * pair : 16 * pair + 16, part].astype(jnp.float32)
    kept = []
    for half in range(2):
        top = 16 * pair + 8 * half
        group = top // bits_per_row
        left = bits_per_row * (group + 1) - top
        packed = jnp.broadcast_to(bits[group : group + 1, part], (8, lanes))
        if left < 8:
            following = jnp.broadcast_to(bits[group + 1 : group + 2, part], (8, lanes))
            packed = jnp.where(row < left, packed, following)
        kept.append(jnp.where((packed & flags[half]) != 0, values[8 * half : 8 * half + 8], 0.0))
    return jnp.concatenate(kept, axis=0).astype(jnp.bfloat16)


def mask_and_sum(exposure, bits, weights, masked_ref, terms_ref, core):
    sets = exposure.shape[0]
    owned = terms_ref.shape[2]
    for first in range(0, terms_ref.shape[0], 2):
        rows = []
        for pair in range(sets // 16):
            flags = [row_flags(2 * pair), row_flags(2 * pair + 1)]
            rows.append(
                jnp.concatenate(
                    [
                        masked_rows(
                            exposure, bits, pair, flags, sibling_columns(chip, owned, core)
                        )
                        for chip in (first, first + 1)
                    ],
                    axis=1,
                )
            )
        masked = jnp.concatenate(rows, axis=0)
        masked_ref[:, first * owned : (first + 2) * owned] = masked
        terms = jnp.dot(weights, masked, preferred_element_type=jnp.float32)
        terms = terms.astype(terms_ref.dtype)
        terms_ref[first] = terms[:, :owned]
        terms_ref[first + 1] = terms[:, owned:]


def first_kernel(
    exposure_hbm,
    bits_hbm,
    currencies_hbm,
    counts_hbm,
    notional_hbm,
    handed_ref,
    masked_ref,
    exposure,
    bits,
    weights_ref,
    used_ref,
    currencies_ref,
    counts_ref,
    notional_ref,
    sems,
):
    sets = exposure.shape[0]
    currency_count = handed_ref.shape[1]
    copies = [
        pltpu.make_async_copy(source, target, sems.at[index])
        for index, (source, target) in enumerate(
            [
                (exposure_hbm, exposure),
                (bits_hbm, bits),
                (currencies_hbm, currencies_ref),
                (counts_hbm, counts_ref),
                (notional_hbm, notional_ref),
            ]
        )
    ]
    for copy in copies:
        copy.start()
    for copy in copies[2:]:
        copy.wait()

    used = used_currencies(currencies_ref[...], counts_ref[...])
    used_ref[...] = used
    notional = notional_ref[...]
    currency = lax.broadcasted_iota(jnp.int32, (currency_count, sets), 0)
    weights = jnp.zeros((currency_count, sets), jnp.float32)
    for slot in range(used.shape[0]):
        weights = weights + jnp.where(
            currency == used[slot : slot + 1], notional[slot : slot + 1], 0.0
        )
    weights = weights.astype(jnp.bfloat16)
    weights_ref[...] = weights
    for copy in copies[:2]:
        copy.wait()
    other = 1 - lax.axis_index("sets") % 2
    mask_and_sum(exposure, bits, weights, masked_ref, handed_ref, other)


def second_kernel(
    dates,
    exposure,
    bits,
    weights_ref,
    fx_hbm,
    rates_hbm,
    start_hbm,
    masked_ref,
    terms_ref,
    carried_ref,
    discount_ref,
    moved_ref,
    fx_ref,
    rates_ref,
    start_ref,
    sems,
):
    copies = [
        pltpu.make_async_copy(source, target, sems.at[index])
        for index, (source, target) in enumerate(
            [(rates_hbm, rates_ref), (start_hbm, start_ref), (fx_hbm, fx_ref)]
        )
    ]
    for copy in copies:
        copy.start()
    own = lax.axis_index("sets") % 2
    mask_and_sum(exposure, bits, weights_ref[...], masked_ref, terms_ref, own)
    for copy in copies:
        copy.wait()
    integral = spread_paths(start_ref[...], dates) + step_years * sums_to_date(rates_ref[...], dates)
    discount = jnp.exp(-integral)
    discount_ref[...] = discount
    moved = fx_ref[...] * discount
    moved_ref[...] = moved
    carried_ref[...] = moved.astype(jnp.bfloat16)


def merging_kernel(given_ref, terms_ref, carried_ref, outgoing_ref):
    chips, currency_count, owned = terms_ref.shape
    order = group_order(chips)
    carried = carried_ref[...]
    for place in range(chips):
        outgoing_ref[place, 0:currency_count, :] = carried
        outgoing_ref[place, currency_count:, :] = (
            terms_ref[order[place]] + given_ref[order[place]].astype(jnp.float32)
        ).astype(jnp.bfloat16)


def unpacking_kernel(arrived_ref, carried_ref):
    chips, currency_count, owned = carried_ref.shape
    order = group_order(chips)
    for place in range(chips):
        carried_ref[order[place]] = arrived_ref[place, 0:currency_count, :]


def projection(masked, carried_ref):
    sets, half = masked.shape
    chips, currency_count, owned = carried_ref.shape
    here = min(chips, 8)
    projected = jnp.zeros((currency_count, sets), jnp.float32)
    for first in range(0, chips, here):
        carried = jnp.concatenate([carried_ref[first + chip] for chip in range(here)], axis=1)
        projected = projected + lax.dot_general(
            carried,
            masked[:, first * owned : (first + here) * owned],
            (((1,), (1,)), ((), ())),
            preferred_element_type=jnp.float32,
        )
    return projected


def adjoint_kernel(
    dates,
    arrived_ref,
    carried_ref,
    masked_own,
    moved_ref,
    discount_ref,
    fx_adjoint_ref,
    rate_adjoint_ref,
    projected_ref,
):
    chips, currency_count, owned = carried_ref.shape
    aggregate = arrived_ref[0, currency_count:, :].astype(jnp.float32)
    for chip in range(1, chips):
        aggregate = aggregate + arrived_ref[chip, currency_count:, :].astype(jnp.float32)
    fx_adjoint_ref[...] = aggregate * discount_ref[...]
    rate_adjoint_ref[...] = -step_years * sums_from_date(aggregate * moved_ref[...], dates)
    projected_ref[...] = projection(masked_own, carried_ref)


def picking_kernel(carried_ref, masked_other, projected_ref, used_ref, notional_adjoint_ref):
    sets, half = masked_other.shape
    currency_count = carried_ref.shape[1]
    projected = projected_ref[...] + projection(masked_other, carried_ref)
    used = used_ref[...]
    currency = lax.broadcasted_iota(jnp.int32, (currency_count, sets), 0)
    for slot in range(used.shape[0]):
        picked = jnp.sum(
            jnp.where(currency == used[slot : slot + 1], projected, 0.0), axis=0, keepdims=True
        )
        notional_adjoint_ref[slot : slot + 1, :] = picked * (1.0 / math.sqrt(2 * half))


def body(
    exposure_adjoint,
    positive_bits,
    currencies,
    mix_count,
    notional,
    fx_paths,
    short_rates,
    start_integral,
):
    sets, columns = exposure_adjoint.shape
    currency_count, owned = fx_paths.shape
    dates = owned // start_integral.shape[1]
    peers = columns // owned
    chips = peers // 2
    slots = currencies.shape[1]
    in_vmem = pl.BlockSpec(memory_space=pltpu.VMEM)
    anywhere = pl.BlockSpec(memory_space=pl.ANY)
    params = pltpu.CompilerParams(vmem_limit_bytes=32 * 2**20)
    block = (currency_count, owned)

    def in_hbm(value):
        return pltpu.with_memory_space_constraint(value, pltpu.HBM)

    def swapped(value):
        return lax.ppermute(value, "sets", [(peer, peer ^ 1) for peer in range(peers)])

    handed, masked_other, exposure, bits, weights, used = pl.pallas_call(
        first_kernel,
        out_shape=(
            pltpu.VMEM((chips,) + block, jnp.bfloat16),
            pltpu.VMEM((sets, columns // 2), jnp.bfloat16),
            pltpu.VMEM((sets, columns), jnp.bfloat16),
            pltpu.VMEM(positive_bits.shape, jnp.int32),
            pltpu.VMEM((currency_count, sets), jnp.bfloat16),
            pltpu.VMEM((slots, sets), jnp.int32),
        ),
        in_specs=[anywhere] * 5,
        out_specs=(in_vmem,) * 6,
        scratch_shapes=[
            pltpu.VMEM((slots, sets), jnp.int32),
            pltpu.VMEM((1, sets), jnp.int32),
            pltpu.VMEM((slots, sets), jnp.float32),
            pltpu.SemaphoreType.DMA((5,)),
        ],
        compiler_params=params,
        name="first",
    )(
        in_hbm(exposure_adjoint),
        in_hbm(positive_bits),
        in_hbm(currencies.T),
        in_hbm(mix_count.reshape(1, sets)),
        in_hbm(notional.T),
    )
    given = swapped(handed)
    masked_own, terms, carried, discount, moved = pl.pallas_call(
        functools.partial(second_kernel, dates),
        out_shape=(
            pltpu.VMEM((sets, columns // 2), jnp.bfloat16),
            pltpu.VMEM((chips,) + block, jnp.float32),
            pltpu.VMEM(block, jnp.bfloat16),
            pltpu.VMEM(block, jnp.float32),
            pltpu.VMEM(block, jnp.float32),
        ),
        in_specs=[in_vmem] * 3 + [anywhere] * 3,
        out_specs=(in_vmem,) * 5,
        scratch_shapes=[
            pltpu.VMEM(block, jnp.float32),
            pltpu.VMEM(block, jnp.float32),
            pltpu.VMEM((owned // dates, currency_count), jnp.float32),
            pltpu.SemaphoreType.DMA((3,)),
        ],
        compiler_params=params,
        name="second",
    )(
        exposure,
        bits,
        weights,
        in_hbm(fx_paths),
        in_hbm(short_rates),
        in_hbm(start_integral.T),
    )
    outgoing = pl.pallas_call(
        merging_kernel,
        out_shape=pltpu.VMEM((chips, 2 * currency_count, owned), jnp.bfloat16),
        in_specs=[in_vmem] * 3,
        out_specs=in_vmem,
        compiler_params=params,
        name="merging",
    )(given, terms, carried)
    arrived = lax.all_to_all(
        outgoing,
        "sets",
        0,
        0,
        axis_index_groups=[[2 * chip + core for chip in group_order(chips)] for core in range(2)],
        tiled=True,
    )
    carried_own = pl.pallas_call(
        unpacking_kernel,
        out_shape=pltpu.VMEM((chips,) + block, jnp.bfloat16),
        in_specs=[in_vmem],
        out_specs=in_vmem,
        compiler_params=params,
        name="unpacking",
    )(arrived)
    carried_other = swapped(carried_own)
    fx_adjoint, rate_adjoint, projected = pl.pallas_call(
        functools.partial(adjoint_kernel, dates),
        out_shape=(
            jax.ShapeDtypeStruct(block, jnp.float32),
            jax.ShapeDtypeStruct(block, jnp.float32),
            pltpu.VMEM((currency_count, sets), jnp.float32),
        ),
        in_specs=[in_vmem] * 5,
        out_specs=(in_vmem,) * 3,
        compiler_params=params,
        name="adjoint",
    )(arrived, carried_own, masked_own, moved, discount)
    notional_adjoint = pl.pallas_call(
        picking_kernel,
        out_shape=jax.ShapeDtypeStruct((slots, sets), jnp.float32),
        in_specs=[in_vmem] * 4,
        out_specs=in_vmem,
        compiler_params=params,
        name="picking",
    )(carried_other, masked_other, projected, used)
    return fx_adjoint, rate_adjoint, notional_adjoint.T


def solution(mesh):
    in_specs = (
        P(("grp", "sets"), None),
        P(("grp", "sets"), None),
        P(("grp", "sets"), None),
        P(("grp", "sets")),
        P(("grp", "sets"), None),
        P("grp", "sets"),
        P("grp", "sets"),
        P("grp", "sets"),
    )
    out_specs = (P("grp", "sets"), P("grp", "sets"), P(("grp", "sets"), None))
    return jax.shard_map(body, mesh=mesh, in_specs=in_specs, out_specs=out_specs, check_vma=False)
```

```python
import functools
import math

import jax
import jax.numpy as jnp
from jax import lax
from jax.experimental import pallas as pl
from jax.experimental.pallas import tpu as pltpu
from jax.sharding import PartitionSpec as P

step_years = 0.25
bits_per_row = 15
lanes = 128


def spread_paths(values, dates):
    paths, columns = values.shape[0], values.shape[0] * dates
    path_of = lax.broadcasted_iota(jnp.int32, (paths, columns), 1) // dates
    own = lax.broadcasted_iota(jnp.int32, (paths, columns), 0)
    return lax.dot_general(
        values,
        (path_of == own).astype(jnp.float32),
        (((0,), (0,)), ((), ())),
        precision=lax.Precision.HIGHEST,
        preferred_element_type=jnp.float32,
    )


def sums_to_date(values, dates):
    width = values.shape[1]
    date = lax.broadcasted_iota(jnp.int32, values.shape, 1) % dates
    step = 1
    while step < dates:
        values = values + jnp.where(date >= step, pltpu.roll(values, step, 1), 0.0)
        step *= 2
    return values


def sums_from_date(values, dates):
    width = values.shape[1]
    date = lax.broadcasted_iota(jnp.int32, values.shape, 1) % dates
    step = 1
    while step < dates:
        values = values + jnp.where(date < dates - step, pltpu.roll(values, width - step, 1), 0.0)
        step *= 2
    return values


def used_currencies(currencies, counts):
    slot = lax.broadcasted_iota(jnp.int32, currencies.shape, 0)
    return jnp.where(slot < counts, currencies, -1)


def group_order(chips):
    middle = chips // 2
    far, near = list(range(middle, chips)), list(range(middle))
    cut = middle // 2
    return far[:cut] + near[:1] + far[cut:] + near[1:]


def sibling_columns(chip, owned, core):
    return pl.ds(pl.multiple_of((2 * chip + core) * owned, owned), owned)


def row_flags(tile):
    shift = lax.broadcasted_iota(jnp.int32, (8, lanes), 0) + (8 * tile) % bits_per_row
    shift = jnp.where(shift >= bits_per_row, shift - bits_per_row, shift)
    return jnp.left_shift(jnp.int32(1), shift)


def masked_rows(exposure, bits, pair, flags, part):
    row = lax.broadcasted_iota(jnp.int32, (8, lanes), 0)
    values = exposure[16 * pair : 16 * pair + 16, part].astype(jnp.float32)
    kept = []
    for half in range(2):
        top = 16 * pair + 8 * half
        group = top // bits_per_row
        left = bits_per_row * (group + 1) - top
        packed = jnp.broadcast_to(bits[group : group + 1, part], (8, lanes))
        if left < 8:
            following = jnp.broadcast_to(bits[group + 1 : group + 2, part], (8, lanes))
            packed = jnp.where(row < left, packed, following)
        kept.append(jnp.where((packed & flags[half]) != 0, values[8 * half : 8 * half + 8], 0.0))
    return jnp.concatenate(kept, axis=0).astype(jnp.bfloat16)


def mask_and_sum(exposure, bits, weights, masked_ref, terms_ref, core):
    sets = exposure.shape[0]
    owned = terms_ref.shape[2]
    for first in range(0, terms_ref.shape[0], 2):
        rows = []
        for pair in range(sets // 16):
            flags = [row_flags(2 * pair), row_flags(2 * pair + 1)]
            rows.append(
                jnp.concatenate(
                    [
                        masked_rows(
                            exposure, bits, pair, flags, sibling_columns(chip, owned, core)
                        )
                        for chip in (first, first + 1)
                    ],
                    axis=1,
                )
            )
        masked = jnp.concatenate(rows, axis=0)
        masked_ref[:, first * owned : (first + 2) * owned] = masked
        terms = jnp.dot(weights, masked, preferred_element_type=jnp.float32)
        terms = terms.astype(terms_ref.dtype)
        terms_ref[first] = terms[:, :owned]
        terms_ref[first + 1] = terms[:, owned:]


def first_kernel(
    exposure_hbm,
    bits_hbm,
    currencies_hbm,
    counts_hbm,
    notional_hbm,
    fx_hbm,
    rates_hbm,
    start_hbm,
    handed_ref,
    masked_ref,
    exposure,
    bits,
    weights_ref,
    used_ref,
    fx_ref,
    rates_ref,
    start_ref,
    currencies_ref,
    counts_ref,
    notional_ref,
    sems,
):
    sets = exposure.shape[0]
    currency_count = handed_ref.shape[1]
    copies = [
        pltpu.make_async_copy(source, target, sems.at[index])
        for index, (source, target) in enumerate(
            [
                (exposure_hbm, exposure),
                (bits_hbm, bits),
                (currencies_hbm, currencies_ref),
                (counts_hbm, counts_ref),
                (notional_hbm, notional_ref),
                (fx_hbm, fx_ref),
                (rates_hbm, rates_ref),
                (start_hbm, start_ref),
            ]
        )
    ]
    for copy in copies:
        copy.start()
    for copy in copies[2:5]:
        copy.wait()

    used = used_currencies(currencies_ref[...], counts_ref[...])
    used_ref[...] = used
    notional = notional_ref[...]
    currency = lax.broadcasted_iota(jnp.int32, (currency_count, sets), 0)
    weights = jnp.zeros((currency_count, sets), jnp.float32)
    for slot in range(used.shape[0]):
        weights = weights + jnp.where(
            currency == used[slot : slot + 1], notional[slot : slot + 1], 0.0
        )
    weights = weights.astype(jnp.bfloat16)
    weights_ref[...] = weights
    for copy in copies[:2]:
        copy.wait()
    other = 1 - lax.axis_index("sets") % 2
    mask_and_sum(exposure, bits, weights, masked_ref, handed_ref, other)
    for copy in copies[5:]:
        copy.wait()


def second_kernel(
    dates,
    exposure,
    bits,
    weights_ref,
    fx_ref,
    rates_ref,
    start_ref,
    masked_ref,
    terms_ref,
    carried_ref,
    discount_ref,
    moved_ref,
):
    own = lax.axis_index("sets") % 2
    mask_and_sum(exposure, bits, weights_ref[...], masked_ref, terms_ref, own)
    integral = spread_paths(start_ref[...], dates) + step_years * sums_to_date(rates_ref[...], dates)
    discount = jnp.exp(-integral)
    discount_ref[...] = discount
    moved = fx_ref[...] * discount
    moved_ref[...] = moved
    carried_ref[...] = moved.astype(jnp.bfloat16)


def merging_kernel(given_ref, terms_ref, carried_ref, outgoing_ref):
    chips, currency_count, owned = terms_ref.shape
    order = group_order(chips)
    carried = carried_ref[...]
    for place in range(chips):
        outgoing_ref[place, 0:currency_count, :] = carried
        outgoing_ref[place, currency_count:, :] = (
            terms_ref[order[place]] + given_ref[order[place]].astype(jnp.float32)
        ).astype(jnp.bfloat16)


def unpacking_kernel(arrived_ref, carried_ref):
    chips, currency_count, owned = carried_ref.shape
    order = group_order(chips)
    for place in range(chips):
        carried_ref[order[place]] = arrived_ref[place, 0:currency_count, :]


def projection(masked, carried_ref):
    sets, half = masked.shape
    chips, currency_count, owned = carried_ref.shape
    here = min(chips, 8)
    projected = jnp.zeros((currency_count, sets), jnp.float32)
    for first in range(0, chips, here):
        carried = jnp.concatenate([carried_ref[first + chip] for chip in range(here)], axis=1)
        projected = projected + lax.dot_general(
            carried,
            masked[:, first * owned : (first + here) * owned],
            (((1,), (1,)), ((), ())),
            preferred_element_type=jnp.float32,
        )
    return projected


def adjoint_kernel(
    dates,
    arrived_ref,
    carried_ref,
    masked_own,
    moved_ref,
    discount_ref,
    fx_adjoint_ref,
    rate_adjoint_ref,
    projected_ref,
):
    chips, currency_count, owned = carried_ref.shape
    aggregate = arrived_ref[0, currency_count:, :].astype(jnp.float32)
    for chip in range(1, chips):
        aggregate = aggregate + arrived_ref[chip, currency_count:, :].astype(jnp.float32)
    fx_adjoint_ref[...] = aggregate * discount_ref[...]
    rate_adjoint_ref[...] = -step_years * sums_from_date(aggregate * moved_ref[...], dates)
    projected_ref[...] = projection(masked_own, carried_ref)


def picking_kernel(carried_ref, masked_other, projected_ref, used_ref, notional_adjoint_ref):
    sets, half = masked_other.shape
    currency_count = carried_ref.shape[1]
    projected = projected_ref[...] + projection(masked_other, carried_ref)
    used = used_ref[...]
    currency = lax.broadcasted_iota(jnp.int32, (currency_count, sets), 0)
    for slot in range(used.shape[0]):
        picked = jnp.sum(
            jnp.where(currency == used[slot : slot + 1], projected, 0.0), axis=0, keepdims=True
        )
        notional_adjoint_ref[slot : slot + 1, :] = picked * (1.0 / math.sqrt(2 * half))


def body(
    exposure_adjoint,
    positive_bits,
    currencies,
    mix_count,
    notional,
    fx_paths,
    short_rates,
    start_integral,
):
    sets, columns = exposure_adjoint.shape
    currency_count, owned = fx_paths.shape
    dates = owned // start_integral.shape[1]
    peers = columns // owned
    chips = peers // 2
    slots = currencies.shape[1]
    in_vmem = pl.BlockSpec(memory_space=pltpu.VMEM)
    anywhere = pl.BlockSpec(memory_space=pl.ANY)
    params = pltpu.CompilerParams(vmem_limit_bytes=32 * 2**20)
    block = (currency_count, owned)

    def in_hbm(value):
        return pltpu.with_memory_space_constraint(value, pltpu.HBM)

    def swapped(value):
        return lax.ppermute(value, "sets", [(peer, peer ^ 1) for peer in range(peers)])

    handed, masked_other, exposure, bits, weights, used, fx, rates, start = pl.pallas_call(
        first_kernel,
        out_shape=(
            pltpu.VMEM((chips,) + block, jnp.bfloat16),
            pltpu.VMEM((sets, columns // 2), jnp.bfloat16),
            pltpu.VMEM((sets, columns), jnp.bfloat16),
            pltpu.VMEM(positive_bits.shape, jnp.int32),
            pltpu.VMEM((currency_count, sets), jnp.bfloat16),
            pltpu.VMEM((slots, sets), jnp.int32),
            pltpu.VMEM(block, jnp.float32),
            pltpu.VMEM(block, jnp.float32),
            pltpu.VMEM((owned // dates, currency_count), jnp.float32),
        ),
        in_specs=[anywhere] * 8,
        out_specs=(in_vmem,) * 9,
        scratch_shapes=[
            pltpu.VMEM((slots, sets), jnp.int32),
            pltpu.VMEM((1, sets), jnp.int32),
            pltpu.VMEM((slots, sets), jnp.float32),
            pltpu.SemaphoreType.DMA((8,)),
        ],
        compiler_params=params,
        name="first",
    )(
        in_hbm(exposure_adjoint),
        in_hbm(positive_bits),
        in_hbm(currencies.T),
        in_hbm(mix_count.reshape(1, sets)),
        in_hbm(notional.T),
        in_hbm(fx_paths),
        in_hbm(short_rates),
        in_hbm(start_integral.T),
    )
    given = swapped(handed)
    masked_own, terms, carried, discount, moved = pl.pallas_call(
        functools.partial(second_kernel, dates),
        out_shape=(
            pltpu.VMEM((sets, columns // 2), jnp.bfloat16),
            pltpu.VMEM((chips,) + block, jnp.float32),
            pltpu.VMEM(block, jnp.bfloat16),
            pltpu.VMEM(block, jnp.float32),
            pltpu.VMEM(block, jnp.float32),
        ),
        in_specs=[in_vmem] * 6,
        out_specs=(in_vmem,) * 5,
        compiler_params=params,
        name="second",
    )(
        exposure,
        bits,
        weights,
        fx,
        rates,
        start,
    )
    outgoing = pl.pallas_call(
        merging_kernel,
        out_shape=pltpu.VMEM((chips, 2 * currency_count, owned), jnp.bfloat16),
        in_specs=[in_vmem] * 3,
        out_specs=in_vmem,
        compiler_params=params,
        name="merging",
    )(given, terms, carried)
    arrived = lax.all_to_all(
        outgoing,
        "sets",
        0,
        0,
        axis_index_groups=[[2 * chip + core for chip in group_order(chips)] for core in range(2)],
        tiled=True,
    )
    carried_own = pl.pallas_call(
        unpacking_kernel,
        out_shape=pltpu.VMEM((chips,) + block, jnp.bfloat16),
        in_specs=[in_vmem],
        out_specs=in_vmem,
        compiler_params=params,
        name="unpacking",
    )(arrived)
    carried_other = swapped(carried_own)
    fx_adjoint, rate_adjoint, projected = pl.pallas_call(
        functools.partial(adjoint_kernel, dates),
        out_shape=(
            jax.ShapeDtypeStruct(block, jnp.float32),
            jax.ShapeDtypeStruct(block, jnp.float32),
            pltpu.VMEM((currency_count, sets), jnp.float32),
        ),
        in_specs=[in_vmem] * 5,
        out_specs=(in_vmem,) * 3,
        compiler_params=params,
        name="adjoint",
    )(arrived, carried_own, masked_own, moved, discount)
    notional_adjoint = pl.pallas_call(
        picking_kernel,
        out_shape=jax.ShapeDtypeStruct((slots, sets), jnp.float32),
        in_specs=[in_vmem] * 4,
        out_specs=in_vmem,
        compiler_params=params,
        name="picking",
    )(carried_other, masked_other, projected, used)
    return fx_adjoint, rate_adjoint, notional_adjoint.T


def solution(mesh):
    in_specs = (
        P(("grp", "sets"), None),
        P(("grp", "sets"), None),
        P(("grp", "sets"), None),
        P(("grp", "sets")),
        P(("grp", "sets"), None),
        P("grp", "sets"),
        P("grp", "sets"),
        P("grp", "sets"),
    )
    out_specs = (P("grp", "sets"), P("grp", "sets"), P(("grp", "sets"), None))
    return jax.shard_map(body, mesh=mesh, in_specs=in_specs, out_specs=out_specs, check_vma=False)
```

```python
import functools
import math

import jax
import jax.numpy as jnp
from jax import lax
from jax.experimental import pallas as pl
from jax.experimental.pallas import tpu as pltpu
from jax.sharding import PartitionSpec as P

step_years = 0.25
bits_per_row = 15
lanes = 128


def spread_paths(values, dates):
    paths, columns = values.shape[0], values.shape[0] * dates
    path_of = lax.broadcasted_iota(jnp.int32, (paths, columns), 1) // dates
    own = lax.broadcasted_iota(jnp.int32, (paths, columns), 0)
    return lax.dot_general(
        values,
        (path_of == own).astype(jnp.float32),
        (((0,), (0,)), ((), ())),
        precision=lax.Precision.HIGHEST,
        preferred_element_type=jnp.float32,
    )


def sums_to_date(values, dates):
    width = values.shape[1]
    date = lax.broadcasted_iota(jnp.int32, values.shape, 1) % dates
    step = 1
    while step < dates:
        values = values + jnp.where(date >= step, pltpu.roll(values, step, 1), 0.0)
        step *= 2
    return values


def sums_from_date(values, dates):
    width = values.shape[1]
    date = lax.broadcasted_iota(jnp.int32, values.shape, 1) % dates
    step = 1
    while step < dates:
        values = values + jnp.where(date < dates - step, pltpu.roll(values, width - step, 1), 0.0)
        step *= 2
    return values


def used_currencies(currencies, counts):
    slot = lax.broadcasted_iota(jnp.int32, currencies.shape, 0)
    return jnp.where(slot < counts, currencies, -1)


def group_order(chips, core):
    middle = chips // 2
    far, near = list(range(middle, chips)), list(range(middle))
    if core:
        return far[::-1] + near
    cut = middle // 2
    return far[:cut] + near[:1] + far[cut:] + near[1:]


def chip_at(chips, place):
    even, odd = (group_order(chips, core)[place] for core in range(2))
    return jnp.where(lax.axis_index("sets") % 2 == 0, even, odd)


def sibling_columns(chip, owned, core):
    return pl.ds(pl.multiple_of((2 * chip + core) * owned, owned), owned)


def row_flags(tile):
    shift = lax.broadcasted_iota(jnp.int32, (8, lanes), 0) + (8 * tile) % bits_per_row
    shift = jnp.where(shift >= bits_per_row, shift - bits_per_row, shift)
    return jnp.left_shift(jnp.int32(1), shift)


def masked_rows(exposure, bits, pair, flags, part):
    row = lax.broadcasted_iota(jnp.int32, (8, lanes), 0)
    values = exposure[16 * pair : 16 * pair + 16, part].astype(jnp.float32)
    kept = []
    for half in range(2):
        top = 16 * pair + 8 * half
        group = top // bits_per_row
        left = bits_per_row * (group + 1) - top
        packed = jnp.broadcast_to(bits[group : group + 1, part], (8, lanes))
        if left < 8:
            following = jnp.broadcast_to(bits[group + 1 : group + 2, part], (8, lanes))
            packed = jnp.where(row < left, packed, following)
        kept.append(jnp.where((packed & flags[half]) != 0, values[8 * half : 8 * half + 8], 0.0))
    return jnp.concatenate(kept, axis=0).astype(jnp.bfloat16)


def mask_and_sum(exposure, bits, weights, masked_ref, terms_ref, core):
    sets = exposure.shape[0]
    owned = terms_ref.shape[2]
    for first in range(0, terms_ref.shape[0], 2):
        rows = []
        for pair in range(sets // 16):
            flags = [row_flags(2 * pair), row_flags(2 * pair + 1)]
            rows.append(
                jnp.concatenate(
                    [
                        masked_rows(
                            exposure, bits, pair, flags, sibling_columns(chip, owned, core)
                        )
                        for chip in (first, first + 1)
                    ],
                    axis=1,
                )
            )
        masked = jnp.concatenate(rows, axis=0)
        masked_ref[:, first * owned : (first + 2) * owned] = masked
        terms = jnp.dot(weights, masked, preferred_element_type=jnp.float32)
        terms = terms.astype(terms_ref.dtype)
        terms_ref[first] = terms[:, :owned]
        terms_ref[first + 1] = terms[:, owned:]


def first_kernel(
    exposure_hbm,
    bits_hbm,
    currencies_hbm,
    counts_hbm,
    notional_hbm,
    fx_hbm,
    rates_hbm,
    start_hbm,
    handed_ref,
    masked_ref,
    exposure,
    bits,
    weights_ref,
    used_ref,
    fx_ref,
    rates_ref,
    start_ref,
    currencies_ref,
    counts_ref,
    notional_ref,
    sems,
):
    sets = exposure.shape[0]
    currency_count = handed_ref.shape[1]
    copies = [
        pltpu.make_async_copy(source, target, sems.at[index])
        for index, (source, target) in enumerate(
            [
                (exposure_hbm, exposure),
                (bits_hbm, bits),
                (currencies_hbm, currencies_ref),
                (counts_hbm, counts_ref),
                (notional_hbm, notional_ref),
                (fx_hbm, fx_ref),
                (rates_hbm, rates_ref),
                (start_hbm, start_ref),
            ]
        )
    ]
    for copy in copies:
        copy.start()
    for copy in copies[2:5]:
        copy.wait()

    used = used_currencies(currencies_ref[...], counts_ref[...])
    used_ref[...] = used
    notional = notional_ref[...]
    currency = lax.broadcasted_iota(jnp.int32, (currency_count, sets), 0)
    weights = jnp.zeros((currency_count, sets), jnp.float32)
    for slot in range(used.shape[0]):
        weights = weights + jnp.where(
            currency == used[slot : slot + 1], notional[slot : slot + 1], 0.0
        )
    weights = weights.astype(jnp.bfloat16)
    weights_ref[...] = weights
    for copy in copies[:2]:
        copy.wait()
    other = 1 - lax.axis_index("sets") % 2
    mask_and_sum(exposure, bits, weights, masked_ref, handed_ref, other)
    for copy in copies[5:]:
        copy.wait()


def second_kernel(
    dates,
    exposure,
    bits,
    weights_ref,
    fx_ref,
    rates_ref,
    start_ref,
    masked_ref,
    terms_ref,
    carried_ref,
    discount_ref,
    moved_ref,
):
    own = lax.axis_index("sets") % 2
    mask_and_sum(exposure, bits, weights_ref[...], masked_ref, terms_ref, own)
    integral = spread_paths(start_ref[...], dates) + step_years * sums_to_date(rates_ref[...], dates)
    discount = jnp.exp(-integral)
    discount_ref[...] = discount
    moved = fx_ref[...] * discount
    moved_ref[...] = moved
    carried_ref[...] = moved.astype(jnp.bfloat16)


def merging_kernel(given_ref, terms_ref, carried_ref, outgoing_ref):
    chips, currency_count, owned = terms_ref.shape
    carried = carried_ref[...]
    for place in range(chips):
        chip = chip_at(chips, place)
        outgoing_ref[place, 0:currency_count, :] = carried
        outgoing_ref[place, currency_count:, :] = (
            terms_ref[chip] + given_ref[chip].astype(jnp.float32)
        ).astype(jnp.bfloat16)


def unpacking_kernel(arrived_ref, carried_ref):
    chips, currency_count, owned = carried_ref.shape
    for place in range(chips):
        carried_ref[chip_at(chips, place)] = arrived_ref[place, 0:currency_count, :]


def projection(masked, carried_ref):
    sets, half = masked.shape
    chips, currency_count, owned = carried_ref.shape
    here = min(chips, 8)
    projected = jnp.zeros((currency_count, sets), jnp.float32)
    for first in range(0, chips, here):
        carried = jnp.concatenate([carried_ref[first + chip] for chip in range(here)], axis=1)
        projected = projected + lax.dot_general(
            carried,
            masked[:, first * owned : (first + here) * owned],
            (((1,), (1,)), ((), ())),
            preferred_element_type=jnp.float32,
        )
    return projected


def adjoint_kernel(
    dates,
    arrived_ref,
    carried_ref,
    masked_own,
    moved_ref,
    discount_ref,
    fx_adjoint_ref,
    rate_adjoint_ref,
    projected_ref,
):
    chips, currency_count, owned = carried_ref.shape
    aggregate = arrived_ref[0, currency_count:, :].astype(jnp.float32)
    for chip in range(1, chips):
        aggregate = aggregate + arrived_ref[chip, currency_count:, :].astype(jnp.float32)
    fx_adjoint_ref[...] = aggregate * discount_ref[...]
    rate_adjoint_ref[...] = -step_years * sums_from_date(aggregate * moved_ref[...], dates)
    projected_ref[...] = projection(masked_own, carried_ref)


def picking_kernel(carried_ref, masked_other, projected_ref, used_ref, notional_adjoint_ref):
    sets, half = masked_other.shape
    currency_count = carried_ref.shape[1]
    projected = projected_ref[...] + projection(masked_other, carried_ref)
    used = used_ref[...]
    currency = lax.broadcasted_iota(jnp.int32, (currency_count, sets), 0)
    for slot in range(used.shape[0]):
        picked = jnp.sum(
            jnp.where(currency == used[slot : slot + 1], projected, 0.0), axis=0, keepdims=True
        )
        notional_adjoint_ref[slot : slot + 1, :] = picked * (1.0 / math.sqrt(2 * half))


def body(
    exposure_adjoint,
    positive_bits,
    currencies,
    mix_count,
    notional,
    fx_paths,
    short_rates,
    start_integral,
):
    sets, columns = exposure_adjoint.shape
    currency_count, owned = fx_paths.shape
    dates = owned // start_integral.shape[1]
    peers = columns // owned
    chips = peers // 2
    slots = currencies.shape[1]
    in_vmem = pl.BlockSpec(memory_space=pltpu.VMEM)
    anywhere = pl.BlockSpec(memory_space=pl.ANY)
    params = pltpu.CompilerParams(vmem_limit_bytes=32 * 2**20)
    block = (currency_count, owned)

    def in_hbm(value):
        return pltpu.with_memory_space_constraint(value, pltpu.HBM)

    def swapped(value):
        return lax.ppermute(value, "sets", [(peer, peer ^ 1) for peer in range(peers)])

    handed, masked_other, exposure, bits, weights, used, fx, rates, start = pl.pallas_call(
        first_kernel,
        out_shape=(
            pltpu.VMEM((chips,) + block, jnp.bfloat16),
            pltpu.VMEM((sets, columns // 2), jnp.bfloat16),
            pltpu.VMEM((sets, columns), jnp.bfloat16),
            pltpu.VMEM(positive_bits.shape, jnp.int32),
            pltpu.VMEM((currency_count, sets), jnp.bfloat16),
            pltpu.VMEM((slots, sets), jnp.int32),
            pltpu.VMEM(block, jnp.float32),
            pltpu.VMEM(block, jnp.float32),
            pltpu.VMEM((owned // dates, currency_count), jnp.float32),
        ),
        in_specs=[anywhere] * 8,
        out_specs=(in_vmem,) * 9,
        scratch_shapes=[
            pltpu.VMEM((slots, sets), jnp.int32),
            pltpu.VMEM((1, sets), jnp.int32),
            pltpu.VMEM((slots, sets), jnp.float32),
            pltpu.SemaphoreType.DMA((8,)),
        ],
        compiler_params=params,
        name="first",
    )(
        in_hbm(exposure_adjoint),
        in_hbm(positive_bits),
        in_hbm(currencies.T),
        in_hbm(mix_count.reshape(1, sets)),
        in_hbm(notional.T),
        in_hbm(fx_paths),
        in_hbm(short_rates),
        in_hbm(start_integral.T),
    )
    given = swapped(handed)
    masked_own, terms, carried, discount, moved = pl.pallas_call(
        functools.partial(second_kernel, dates),
        out_shape=(
            pltpu.VMEM((sets, columns // 2), jnp.bfloat16),
            pltpu.VMEM((chips,) + block, jnp.float32),
            pltpu.VMEM(block, jnp.bfloat16),
            pltpu.VMEM(block, jnp.float32),
            pltpu.VMEM(block, jnp.float32),
        ),
        in_specs=[in_vmem] * 6,
        out_specs=(in_vmem,) * 5,
        compiler_params=params,
        name="second",
    )(
        exposure,
        bits,
        weights,
        fx,
        rates,
        start,
    )
    outgoing = pl.pallas_call(
        merging_kernel,
        out_shape=pltpu.VMEM((chips, 2 * currency_count, owned), jnp.bfloat16),
        in_specs=[in_vmem] * 3,
        out_specs=in_vmem,
        compiler_params=params,
        name="merging",
    )(given, terms, carried)
    arrived = lax.all_to_all(
        outgoing,
        "sets",
        0,
        0,
        axis_index_groups=[
            [2 * chip + core for chip in group_order(chips, core)] for core in range(2)
        ],
        tiled=True,
    )
    carried_own = pl.pallas_call(
        unpacking_kernel,
        out_shape=pltpu.VMEM((chips,) + block, jnp.bfloat16),
        in_specs=[in_vmem],
        out_specs=in_vmem,
        compiler_params=params,
        name="unpacking",
    )(arrived)
    carried_other = swapped(carried_own)
    fx_adjoint, rate_adjoint, projected = pl.pallas_call(
        functools.partial(adjoint_kernel, dates),
        out_shape=(
            jax.ShapeDtypeStruct(block, jnp.float32),
            jax.ShapeDtypeStruct(block, jnp.float32),
            pltpu.VMEM((currency_count, sets), jnp.float32),
        ),
        in_specs=[in_vmem] * 5,
        out_specs=(in_vmem,) * 3,
        compiler_params=params,
        name="adjoint",
    )(arrived, carried_own, masked_own, moved, discount)
    notional_adjoint = pl.pallas_call(
        picking_kernel,
        out_shape=jax.ShapeDtypeStruct((slots, sets), jnp.float32),
        in_specs=[in_vmem] * 4,
        out_specs=in_vmem,
        compiler_params=params,
        name="picking",
    )(carried_other, masked_other, projected, used)
    return fx_adjoint, rate_adjoint, notional_adjoint.T


def solution(mesh):
    in_specs = (
        P(("grp", "sets"), None),
        P(("grp", "sets"), None),
        P(("grp", "sets"), None),
        P(("grp", "sets")),
        P(("grp", "sets"), None),
        P("grp", "sets"),
        P("grp", "sets"),
        P("grp", "sets"),
    )
    out_specs = (P("grp", "sets"), P("grp", "sets"), P(("grp", "sets"), None))
    return jax.shard_map(body, mesh=mesh, in_specs=in_specs, out_specs=out_specs, check_vma=False)
```

```python
import functools
import math

import jax
import jax.numpy as jnp
from jax import lax
from jax.experimental import pallas as pl
from jax.experimental.pallas import tpu as pltpu
from jax.sharding import PartitionSpec as P

step_years = 0.25
bits_per_row = 15
lanes = 128


def spread_paths(values, dates):
    paths, columns = values.shape[0], values.shape[0] * dates
    path_of = lax.broadcasted_iota(jnp.int32, (paths, columns), 1) // dates
    own = lax.broadcasted_iota(jnp.int32, (paths, columns), 0)
    return lax.dot_general(
        values,
        (path_of == own).astype(jnp.float32),
        (((0,), (0,)), ((), ())),
        precision=lax.Precision.HIGHEST,
        preferred_element_type=jnp.float32,
    )


def sums_to_date(values, dates):
    width = values.shape[1]
    date = lax.broadcasted_iota(jnp.int32, values.shape, 1) % dates
    step = 1
    while step < dates:
        values = values + jnp.where(date >= step, pltpu.roll(values, step, 1), 0.0)
        step *= 2
    return values


def sums_from_date(values, dates):
    width = values.shape[1]
    date = lax.broadcasted_iota(jnp.int32, values.shape, 1) % dates
    step = 1
    while step < dates:
        values = values + jnp.where(date < dates - step, pltpu.roll(values, width - step, 1), 0.0)
        step *= 2
    return values


def used_currencies(currencies, counts):
    slot = lax.broadcasted_iota(jnp.int32, currencies.shape, 0)
    return jnp.where(slot < counts, currencies, -1)


def group_order(chips):
    middle = chips // 2
    far, near = list(range(middle, chips)), list(range(middle))
    cut = middle // 2
    return far[:cut] + near[:1] + far[cut:] + near[1:]


def core_in(chips, chip, group):
    return 1 - group if chip >= chips // 2 else group


def own_group(chips):
    me = lax.axis_index("sets")
    return jnp.where(me >= chips, 1 - me % 2, me % 2)


def group_columns(chips, chip, owned, group):
    block = 2 * chip + core_in(chips, chip, group)
    return pl.ds(pl.multiple_of(block * owned, owned), owned)


def row_flags(tile):
    shift = lax.broadcasted_iota(jnp.int32, (8, lanes), 0) + (8 * tile) % bits_per_row
    shift = jnp.where(shift >= bits_per_row, shift - bits_per_row, shift)
    return jnp.left_shift(jnp.int32(1), shift)


def masked_rows(exposure, bits, pair, flags, part):
    row = lax.broadcasted_iota(jnp.int32, (8, lanes), 0)
    values = exposure[16 * pair : 16 * pair + 16, part].astype(jnp.float32)
    kept = []
    for half in range(2):
        top = 16 * pair + 8 * half
        group = top // bits_per_row
        left = bits_per_row * (group + 1) - top
        packed = jnp.broadcast_to(bits[group : group + 1, part], (8, lanes))
        if left < 8:
            following = jnp.broadcast_to(bits[group + 1 : group + 2, part], (8, lanes))
            packed = jnp.where(row < left, packed, following)
        kept.append(jnp.where((packed & flags[half]) != 0, values[8 * half : 8 * half + 8], 0.0))
    return jnp.concatenate(kept, axis=0).astype(jnp.bfloat16)


def mask_and_sum(exposure, bits, weights, masked_ref, terms_ref, group):
    sets = exposure.shape[0]
    chips, owned = terms_ref.shape[0], terms_ref.shape[2]
    for first in range(0, chips, 2):
        rows = []
        for pair in range(sets // 16):
            flags = [row_flags(2 * pair), row_flags(2 * pair + 1)]
            rows.append(
                jnp.concatenate(
                    [
                        masked_rows(
                            exposure, bits, pair, flags, group_columns(chips, chip, owned, group)
                        )
                        for chip in (first, first + 1)
                    ],
                    axis=1,
                )
            )
        masked = jnp.concatenate(rows, axis=0)
        masked_ref[:, first * owned : (first + 2) * owned] = masked
        terms = jnp.dot(weights, masked, preferred_element_type=jnp.float32)
        terms = terms.astype(terms_ref.dtype)
        terms_ref[first] = terms[:, :owned]
        terms_ref[first + 1] = terms[:, owned:]


def first_kernel(
    exposure_hbm,
    bits_hbm,
    currencies_hbm,
    counts_hbm,
    notional_hbm,
    fx_hbm,
    rates_hbm,
    start_hbm,
    handed_ref,
    masked_ref,
    exposure,
    bits,
    weights_ref,
    used_ref,
    fx_ref,
    rates_ref,
    start_ref,
    currencies_ref,
    counts_ref,
    notional_ref,
    sems,
):
    sets = exposure.shape[0]
    currency_count = handed_ref.shape[1]
    copies = [
        pltpu.make_async_copy(source, target, sems.at[index])
        for index, (source, target) in enumerate(
            [
                (exposure_hbm, exposure),
                (bits_hbm, bits),
                (currencies_hbm, currencies_ref),
                (counts_hbm, counts_ref),
                (notional_hbm, notional_ref),
                (fx_hbm, fx_ref),
                (rates_hbm, rates_ref),
                (start_hbm, start_ref),
            ]
        )
    ]
    for copy in copies:
        copy.start()
    for copy in copies[2:5]:
        copy.wait()

    used = used_currencies(currencies_ref[...], counts_ref[...])
    used_ref[...] = used
    notional = notional_ref[...]
    currency = lax.broadcasted_iota(jnp.int32, (currency_count, sets), 0)
    weights = jnp.zeros((currency_count, sets), jnp.float32)
    for slot in range(used.shape[0]):
        weights = weights + jnp.where(
            currency == used[slot : slot + 1], notional[slot : slot + 1], 0.0
        )
    weights = weights.astype(jnp.bfloat16)
    weights_ref[...] = weights
    for copy in copies[:2]:
        copy.wait()
    other = 1 - own_group(handed_ref.shape[0])
    mask_and_sum(exposure, bits, weights, masked_ref, handed_ref, other)
    for copy in copies[5:]:
        copy.wait()


def second_kernel(
    dates,
    exposure,
    bits,
    weights_ref,
    fx_ref,
    rates_ref,
    start_ref,
    masked_ref,
    terms_ref,
    carried_ref,
    discount_ref,
    moved_ref,
):
    own = own_group(terms_ref.shape[0])
    mask_and_sum(exposure, bits, weights_ref[...], masked_ref, terms_ref, own)
    integral = spread_paths(start_ref[...], dates) + step_years * sums_to_date(rates_ref[...], dates)
    discount = jnp.exp(-integral)
    discount_ref[...] = discount
    moved = fx_ref[...] * discount
    moved_ref[...] = moved
    carried_ref[...] = moved.astype(jnp.bfloat16)


def merging_kernel(given_ref, terms_ref, carried_ref, outgoing_ref):
    chips, currency_count, owned = terms_ref.shape
    order = group_order(chips)
    carried = carried_ref[...]
    for place in range(chips):
        outgoing_ref[place, 0:currency_count, :] = carried
        outgoing_ref[place, currency_count:, :] = (
            terms_ref[order[place]] + given_ref[order[place]].astype(jnp.float32)
        ).astype(jnp.bfloat16)


def unpacking_kernel(arrived_ref, carried_ref):
    chips, currency_count, owned = carried_ref.shape
    order = group_order(chips)
    for place in range(chips):
        carried_ref[order[place]] = arrived_ref[place, 0:currency_count, :]


def projection(masked, carried_ref):
    sets, half = masked.shape
    chips, currency_count, owned = carried_ref.shape
    here = min(chips, 8)
    projected = jnp.zeros((currency_count, sets), jnp.float32)
    for first in range(0, chips, here):
        carried = jnp.concatenate([carried_ref[first + chip] for chip in range(here)], axis=1)
        projected = projected + lax.dot_general(
            carried,
            masked[:, first * owned : (first + here) * owned],
            (((1,), (1,)), ((), ())),
            preferred_element_type=jnp.float32,
        )
    return projected


def adjoint_kernel(
    dates,
    arrived_ref,
    carried_ref,
    masked_own,
    moved_ref,
    discount_ref,
    fx_adjoint_ref,
    rate_adjoint_ref,
    projected_ref,
):
    chips, currency_count, owned = carried_ref.shape
    aggregate = arrived_ref[0, currency_count:, :].astype(jnp.float32)
    for chip in range(1, chips):
        aggregate = aggregate + arrived_ref[chip, currency_count:, :].astype(jnp.float32)
    fx_adjoint_ref[...] = aggregate * discount_ref[...]
    rate_adjoint_ref[...] = -step_years * sums_from_date(aggregate * moved_ref[...], dates)
    projected_ref[...] = projection(masked_own, carried_ref)


def picking_kernel(carried_ref, masked_other, projected_ref, used_ref, notional_adjoint_ref):
    sets, half = masked_other.shape
    currency_count = carried_ref.shape[1]
    projected = projected_ref[...] + projection(masked_other, carried_ref)
    used = used_ref[...]
    currency = lax.broadcasted_iota(jnp.int32, (currency_count, sets), 0)
    for slot in range(used.shape[0]):
        picked = jnp.sum(
            jnp.where(currency == used[slot : slot + 1], projected, 0.0), axis=0, keepdims=True
        )
        notional_adjoint_ref[slot : slot + 1, :] = picked * (1.0 / math.sqrt(2 * half))


def body(
    exposure_adjoint,
    positive_bits,
    currencies,
    mix_count,
    notional,
    fx_paths,
    short_rates,
    start_integral,
):
    sets, columns = exposure_adjoint.shape
    currency_count, owned = fx_paths.shape
    dates = owned // start_integral.shape[1]
    peers = columns // owned
    chips = peers // 2
    slots = currencies.shape[1]
    in_vmem = pl.BlockSpec(memory_space=pltpu.VMEM)
    anywhere = pl.BlockSpec(memory_space=pl.ANY)
    params = pltpu.CompilerParams(vmem_limit_bytes=32 * 2**20)
    block = (currency_count, owned)

    def in_hbm(value):
        return pltpu.with_memory_space_constraint(value, pltpu.HBM)

    def swapped(value):
        return lax.ppermute(value, "sets", [(peer, peer ^ 1) for peer in range(peers)])

    handed, masked_other, exposure, bits, weights, used, fx, rates, start = pl.pallas_call(
        first_kernel,
        out_shape=(
            pltpu.VMEM((chips,) + block, jnp.bfloat16),
            pltpu.VMEM((sets, columns // 2), jnp.bfloat16),
            pltpu.VMEM((sets, columns), jnp.bfloat16),
            pltpu.VMEM(positive_bits.shape, jnp.int32),
            pltpu.VMEM((currency_count, sets), jnp.bfloat16),
            pltpu.VMEM((slots, sets), jnp.int32),
            pltpu.VMEM(block, jnp.float32),
            pltpu.VMEM(block, jnp.float32),
            pltpu.VMEM((owned // dates, currency_count), jnp.float32),
        ),
        in_specs=[anywhere] * 8,
        out_specs=(in_vmem,) * 9,
        scratch_shapes=[
            pltpu.VMEM((slots, sets), jnp.int32),
            pltpu.VMEM((1, sets), jnp.int32),
            pltpu.VMEM((slots, sets), jnp.float32),
            pltpu.SemaphoreType.DMA((8,)),
        ],
        compiler_params=params,
        name="first",
    )(
        in_hbm(exposure_adjoint),
        in_hbm(positive_bits),
        in_hbm(currencies.T),
        in_hbm(mix_count.reshape(1, sets)),
        in_hbm(notional.T),
        in_hbm(fx_paths),
        in_hbm(short_rates),
        in_hbm(start_integral.T),
    )
    given = swapped(handed)
    masked_own, terms, carried, discount, moved = pl.pallas_call(
        functools.partial(second_kernel, dates),
        out_shape=(
            pltpu.VMEM((sets, columns // 2), jnp.bfloat16),
            pltpu.VMEM((chips,) + block, jnp.float32),
            pltpu.VMEM(block, jnp.bfloat16),
            pltpu.VMEM(block, jnp.float32),
            pltpu.VMEM(block, jnp.float32),
        ),
        in_specs=[in_vmem] * 6,
        out_specs=(in_vmem,) * 5,
        compiler_params=params,
        name="second",
    )(
        exposure,
        bits,
        weights,
        fx,
        rates,
        start,
    )
    outgoing = pl.pallas_call(
        merging_kernel,
        out_shape=pltpu.VMEM((chips, 2 * currency_count, owned), jnp.bfloat16),
        in_specs=[in_vmem] * 3,
        out_specs=in_vmem,
        compiler_params=params,
        name="merging",
    )(given, terms, carried)
    arrived = lax.all_to_all(
        outgoing,
        "sets",
        0,
        0,
        axis_index_groups=[
            [2 * chip + core_in(chips, chip, group) for chip in group_order(chips)]
            for group in range(2)
        ],
        tiled=True,
    )
    carried_own = pl.pallas_call(
        unpacking_kernel,
        out_shape=pltpu.VMEM((chips,) + block, jnp.bfloat16),
        in_specs=[in_vmem],
        out_specs=in_vmem,
        compiler_params=params,
        name="unpacking",
    )(arrived)
    carried_other = swapped(carried_own)
    fx_adjoint, rate_adjoint, projected = pl.pallas_call(
        functools.partial(adjoint_kernel, dates),
        out_shape=(
            jax.ShapeDtypeStruct(block, jnp.float32),
            jax.ShapeDtypeStruct(block, jnp.float32),
            pltpu.VMEM((currency_count, sets), jnp.float32),
        ),
        in_specs=[in_vmem] * 5,
        out_specs=(in_vmem,) * 3,
        compiler_params=params,
        name="adjoint",
    )(arrived, carried_own, masked_own, moved, discount)
    notional_adjoint = pl.pallas_call(
        picking_kernel,
        out_shape=jax.ShapeDtypeStruct((slots, sets), jnp.float32),
        in_specs=[in_vmem] * 4,
        out_specs=in_vmem,
        compiler_params=params,
        name="picking",
    )(carried_other, masked_other, projected, used)
    return fx_adjoint, rate_adjoint, notional_adjoint.T


def solution(mesh):
    in_specs = (
        P(("grp", "sets"), None),
        P(("grp", "sets"), None),
        P(("grp", "sets"), None),
        P(("grp", "sets")),
        P(("grp", "sets"), None),
        P("grp", "sets"),
        P("grp", "sets"),
        P("grp", "sets"),
    )
    out_specs = (P("grp", "sets"), P("grp", "sets"), P(("grp", "sets"), None))
    return jax.shard_map(body, mesh=mesh, in_specs=in_specs, out_specs=out_specs, check_vma=False)
```

```python
import functools
import math

import jax
import jax.numpy as jnp
from jax import lax
from jax.experimental import pallas as pl
from jax.experimental.pallas import tpu as pltpu
from jax.sharding import PartitionSpec as P

step_years = 0.25
bits_per_row = 15
lanes = 128


def spread_paths(values, dates):
    paths, columns = values.shape[0], values.shape[0] * dates
    path_of = lax.broadcasted_iota(jnp.int32, (paths, columns), 1) // dates
    own = lax.broadcasted_iota(jnp.int32, (paths, columns), 0)
    return lax.dot_general(
        values,
        (path_of == own).astype(jnp.float32),
        (((0,), (0,)), ((), ())),
        precision=lax.Precision.HIGHEST,
        preferred_element_type=jnp.float32,
    )


def sums_to_date(values, dates):
    width = values.shape[1]
    date = lax.broadcasted_iota(jnp.int32, values.shape, 1) % dates
    step = 1
    while step < dates:
        values = values + jnp.where(date >= step, pltpu.roll(values, step, 1), 0.0)
        step *= 2
    return values


def sums_from_date(values, dates):
    width = values.shape[1]
    date = lax.broadcasted_iota(jnp.int32, values.shape, 1) % dates
    step = 1
    while step < dates:
        values = values + jnp.where(date < dates - step, pltpu.roll(values, width - step, 1), 0.0)
        step *= 2
    return values


def used_currencies(currencies, counts):
    slot = lax.broadcasted_iota(jnp.int32, currencies.shape, 0)
    return jnp.where(slot < counts, currencies, -1)


def core_in(chip, group):
    return 1 - group if chip % 2 else group


def own_group():
    me = lax.axis_index("sets")
    return (me + me // 2) % 2


def group_order(chips, group):
    middle = chips // 2
    far, near = list(range(middle, chips)), list(range(middle))
    if group == 0 and middle % 2 == 0:
        far = [chip ^ 1 for chip in far]
    cut = middle // 2
    return far[:cut] + near[:1] + far[cut:] + near[1:]


def chip_at(chips, place):
    chosen = [group_order(chips, group)[place] for group in range(2)]
    return jnp.where(own_group() == 0, chosen[0], chosen[1])


def group_columns(chip, owned, group):
    block = 2 * chip + core_in(chip, group)
    return pl.ds(pl.multiple_of(block * owned, owned), owned)


def row_flags(tile):
    shift = lax.broadcasted_iota(jnp.int32, (8, lanes), 0) + (8 * tile) % bits_per_row
    shift = jnp.where(shift >= bits_per_row, shift - bits_per_row, shift)
    return jnp.left_shift(jnp.int32(1), shift)


def masked_rows(exposure, bits, pair, flags, part):
    row = lax.broadcasted_iota(jnp.int32, (8, lanes), 0)
    values = exposure[16 * pair : 16 * pair + 16, part].astype(jnp.float32)
    kept = []
    for half in range(2):
        top = 16 * pair + 8 * half
        group = top // bits_per_row
        left = bits_per_row * (group + 1) - top
        packed = jnp.broadcast_to(bits[group : group + 1, part], (8, lanes))
        if left < 8:
            following = jnp.broadcast_to(bits[group + 1 : group + 2, part], (8, lanes))
            packed = jnp.where(row < left, packed, following)
        kept.append(jnp.where((packed & flags[half]) != 0, values[8 * half : 8 * half + 8], 0.0))
    return jnp.concatenate(kept, axis=0).astype(jnp.bfloat16)


def mask_and_sum(exposure, bits, weights, masked_ref, terms_ref, group):
    sets = exposure.shape[0]
    chips, owned = terms_ref.shape[0], terms_ref.shape[2]
    for first in range(0, chips, 2):
        rows = []
        for pair in range(sets // 16):
            flags = [row_flags(2 * pair), row_flags(2 * pair + 1)]
            rows.append(
                jnp.concatenate(
                    [
                        masked_rows(
                            exposure, bits, pair, flags, group_columns(chip, owned, group)
                        )
                        for chip in (first, first + 1)
                    ],
                    axis=1,
                )
            )
        masked = jnp.concatenate(rows, axis=0)
        masked_ref[:, first * owned : (first + 2) * owned] = masked
        terms = jnp.dot(weights, masked, preferred_element_type=jnp.float32)
        terms = terms.astype(terms_ref.dtype)
        terms_ref[first] = terms[:, :owned]
        terms_ref[first + 1] = terms[:, owned:]


def first_kernel(
    exposure_hbm,
    bits_hbm,
    currencies_hbm,
    counts_hbm,
    notional_hbm,
    fx_hbm,
    rates_hbm,
    start_hbm,
    handed_ref,
    masked_ref,
    exposure,
    bits,
    weights_ref,
    used_ref,
    fx_ref,
    rates_ref,
    start_ref,
    currencies_ref,
    counts_ref,
    notional_ref,
    sems,
):
    sets = exposure.shape[0]
    currency_count = handed_ref.shape[1]
    copies = [
        pltpu.make_async_copy(source, target, sems.at[index])
        for index, (source, target) in enumerate(
            [
                (exposure_hbm, exposure),
                (bits_hbm, bits),
                (currencies_hbm, currencies_ref),
                (counts_hbm, counts_ref),
                (notional_hbm, notional_ref),
                (fx_hbm, fx_ref),
                (rates_hbm, rates_ref),
                (start_hbm, start_ref),
            ]
        )
    ]
    for copy in copies:
        copy.start()
    for copy in copies[2:5]:
        copy.wait()

    used = used_currencies(currencies_ref[...], counts_ref[...])
    used_ref[...] = used
    notional = notional_ref[...]
    currency = lax.broadcasted_iota(jnp.int32, (currency_count, sets), 0)
    weights = jnp.zeros((currency_count, sets), jnp.float32)
    for slot in range(used.shape[0]):
        weights = weights + jnp.where(
            currency == used[slot : slot + 1], notional[slot : slot + 1], 0.0
        )
    weights = weights.astype(jnp.bfloat16)
    weights_ref[...] = weights
    for copy in copies[:2]:
        copy.wait()
    other = 1 - own_group()
    mask_and_sum(exposure, bits, weights, masked_ref, handed_ref, other)
    for copy in copies[5:]:
        copy.wait()


def second_kernel(
    dates,
    exposure,
    bits,
    weights_ref,
    fx_ref,
    rates_ref,
    start_ref,
    masked_ref,
    terms_ref,
    carried_ref,
    discount_ref,
    moved_ref,
):
    own = own_group()
    mask_and_sum(exposure, bits, weights_ref[...], masked_ref, terms_ref, own)
    integral = spread_paths(start_ref[...], dates) + step_years * sums_to_date(rates_ref[...], dates)
    discount = jnp.exp(-integral)
    discount_ref[...] = discount
    moved = fx_ref[...] * discount
    moved_ref[...] = moved
    carried_ref[...] = moved.astype(jnp.bfloat16)


def merging_kernel(given_ref, terms_ref, carried_ref, outgoing_ref):
    chips, currency_count, owned = terms_ref.shape
    carried = carried_ref[...]
    for place in range(chips):
        chip = chip_at(chips, place)
        outgoing_ref[place, 0:currency_count, :] = carried
        outgoing_ref[place, currency_count:, :] = (
            terms_ref[chip] + given_ref[chip].astype(jnp.float32)
        ).astype(jnp.bfloat16)


def unpacking_kernel(arrived_ref, carried_ref):
    chips, currency_count, owned = carried_ref.shape
    for place in range(chips):
        carried_ref[chip_at(chips, place)] = arrived_ref[place, 0:currency_count, :]


def projection(masked, carried_ref):
    sets, half = masked.shape
    chips, currency_count, owned = carried_ref.shape
    here = min(chips, 8)
    projected = jnp.zeros((currency_count, sets), jnp.float32)
    for first in range(0, chips, here):
        carried = jnp.concatenate([carried_ref[first + chip] for chip in range(here)], axis=1)
        projected = projected + lax.dot_general(
            carried,
            masked[:, first * owned : (first + here) * owned],
            (((1,), (1,)), ((), ())),
            preferred_element_type=jnp.float32,
        )
    return projected


def adjoint_kernel(
    dates,
    arrived_ref,
    carried_ref,
    masked_own,
    moved_ref,
    discount_ref,
    fx_adjoint_ref,
    rate_adjoint_ref,
    projected_ref,
):
    chips, currency_count, owned = carried_ref.shape
    aggregate = arrived_ref[0, currency_count:, :].astype(jnp.float32)
    for chip in range(1, chips):
        aggregate = aggregate + arrived_ref[chip, currency_count:, :].astype(jnp.float32)
    fx_adjoint_ref[...] = aggregate * discount_ref[...]
    rate_adjoint_ref[...] = -step_years * sums_from_date(aggregate * moved_ref[...], dates)
    projected_ref[...] = projection(masked_own, carried_ref)


def picking_kernel(carried_ref, masked_other, projected_ref, used_ref, notional_adjoint_ref):
    sets, half = masked_other.shape
    currency_count = carried_ref.shape[1]
    projected = projected_ref[...] + projection(masked_other, carried_ref)
    used = used_ref[...]
    currency = lax.broadcasted_iota(jnp.int32, (currency_count, sets), 0)
    for slot in range(used.shape[0]):
        picked = jnp.sum(
            jnp.where(currency == used[slot : slot + 1], projected, 0.0), axis=0, keepdims=True
        )
        notional_adjoint_ref[slot : slot + 1, :] = picked * (1.0 / math.sqrt(2 * half))


def body(
    exposure_adjoint,
    positive_bits,
    currencies,
    mix_count,
    notional,
    fx_paths,
    short_rates,
    start_integral,
):
    sets, columns = exposure_adjoint.shape
    currency_count, owned = fx_paths.shape
    dates = owned // start_integral.shape[1]
    peers = columns // owned
    chips = peers // 2
    slots = currencies.shape[1]
    in_vmem = pl.BlockSpec(memory_space=pltpu.VMEM)
    anywhere = pl.BlockSpec(memory_space=pl.ANY)
    params = pltpu.CompilerParams(vmem_limit_bytes=32 * 2**20)
    block = (currency_count, owned)

    def in_hbm(value):
        return pltpu.with_memory_space_constraint(value, pltpu.HBM)

    def swapped(value):
        return lax.ppermute(value, "sets", [(peer, peer ^ 1) for peer in range(peers)])

    handed, masked_other, exposure, bits, weights, used, fx, rates, start = pl.pallas_call(
        first_kernel,
        out_shape=(
            pltpu.VMEM((chips,) + block, jnp.bfloat16),
            pltpu.VMEM((sets, columns // 2), jnp.bfloat16),
            pltpu.VMEM((sets, columns), jnp.bfloat16),
            pltpu.VMEM(positive_bits.shape, jnp.int32),
            pltpu.VMEM((currency_count, sets), jnp.bfloat16),
            pltpu.VMEM((slots, sets), jnp.int32),
            pltpu.VMEM(block, jnp.float32),
            pltpu.VMEM(block, jnp.float32),
            pltpu.VMEM((owned // dates, currency_count), jnp.float32),
        ),
        in_specs=[anywhere] * 8,
        out_specs=(in_vmem,) * 9,
        scratch_shapes=[
            pltpu.VMEM((slots, sets), jnp.int32),
            pltpu.VMEM((1, sets), jnp.int32),
            pltpu.VMEM((slots, sets), jnp.float32),
            pltpu.SemaphoreType.DMA((8,)),
        ],
        compiler_params=params,
        name="first",
    )(
        in_hbm(exposure_adjoint),
        in_hbm(positive_bits),
        in_hbm(currencies.T),
        in_hbm(mix_count.reshape(1, sets)),
        in_hbm(notional.T),
        in_hbm(fx_paths),
        in_hbm(short_rates),
        in_hbm(start_integral.T),
    )
    given = swapped(handed)
    masked_own, terms, carried, discount, moved = pl.pallas_call(
        functools.partial(second_kernel, dates),
        out_shape=(
            pltpu.VMEM((sets, columns // 2), jnp.bfloat16),
            pltpu.VMEM((chips,) + block, jnp.float32),
            pltpu.VMEM(block, jnp.bfloat16),
            pltpu.VMEM(block, jnp.float32),
            pltpu.VMEM(block, jnp.float32),
        ),
        in_specs=[in_vmem] * 6,
        out_specs=(in_vmem,) * 5,
        compiler_params=params,
        name="second",
    )(
        exposure,
        bits,
        weights,
        fx,
        rates,
        start,
    )
    outgoing = pl.pallas_call(
        merging_kernel,
        out_shape=pltpu.VMEM((chips, 2 * currency_count, owned), jnp.bfloat16),
        in_specs=[in_vmem] * 3,
        out_specs=in_vmem,
        compiler_params=params,
        name="merging",
    )(given, terms, carried)
    arrived = lax.all_to_all(
        outgoing,
        "sets",
        0,
        0,
        axis_index_groups=[
            [2 * chip + core_in(chip, group) for chip in group_order(chips, group)]
            for group in range(2)
        ],
        tiled=True,
    )
    carried_own = pl.pallas_call(
        unpacking_kernel,
        out_shape=pltpu.VMEM((chips,) + block, jnp.bfloat16),
        in_specs=[in_vmem],
        out_specs=in_vmem,
        compiler_params=params,
        name="unpacking",
    )(arrived)
    carried_other = swapped(carried_own)
    fx_adjoint, rate_adjoint, projected = pl.pallas_call(
        functools.partial(adjoint_kernel, dates),
        out_shape=(
            jax.ShapeDtypeStruct(block, jnp.float32),
            jax.ShapeDtypeStruct(block, jnp.float32),
            pltpu.VMEM((currency_count, sets), jnp.float32),
        ),
        in_specs=[in_vmem] * 5,
        out_specs=(in_vmem,) * 3,
        compiler_params=params,
        name="adjoint",
    )(arrived, carried_own, masked_own, moved, discount)
    notional_adjoint = pl.pallas_call(
        picking_kernel,
        out_shape=jax.ShapeDtypeStruct((slots, sets), jnp.float32),
        in_specs=[in_vmem] * 4,
        out_specs=in_vmem,
        compiler_params=params,
        name="picking",
    )(carried_other, masked_other, projected, used)
    return fx_adjoint, rate_adjoint, notional_adjoint.T


def solution(mesh):
    in_specs = (
        P(("grp", "sets"), None),
        P(("grp", "sets"), None),
        P(("grp", "sets"), None),
        P(("grp", "sets")),
        P(("grp", "sets"), None),
        P("grp", "sets"),
        P("grp", "sets"),
        P("grp", "sets"),
    )
    out_specs = (P("grp", "sets"), P("grp", "sets"), P(("grp", "sets"), None))
    return jax.shard_map(body, mesh=mesh, in_specs=in_specs, out_specs=out_specs, check_vma=False)
```

```python
import functools
import math

import jax
import jax.numpy as jnp
from jax import lax
from jax.experimental import pallas as pl
from jax.experimental.pallas import tpu as pltpu
from jax.sharding import PartitionSpec as P

step_years = 0.25
bits_per_row = 15
lanes = 128


def spread_paths(values, dates):
    paths, columns = values.shape[0], values.shape[0] * dates
    path_of = lax.broadcasted_iota(jnp.int32, (paths, columns), 1) // dates
    own = lax.broadcasted_iota(jnp.int32, (paths, columns), 0)
    return lax.dot_general(
        values,
        (path_of == own).astype(jnp.float32),
        (((0,), (0,)), ((), ())),
        precision=lax.Precision.HIGHEST,
        preferred_element_type=jnp.float32,
    )


def sums_to_date(values, dates):
    width = values.shape[1]
    date = lax.broadcasted_iota(jnp.int32, values.shape, 1) % dates
    step = 1
    while step < dates:
        values = values + jnp.where(date >= step, pltpu.roll(values, step, 1), 0.0)
        step *= 2
    return values


def sums_from_date(values, dates):
    width = values.shape[1]
    date = lax.broadcasted_iota(jnp.int32, values.shape, 1) % dates
    step = 1
    while step < dates:
        values = values + jnp.where(date < dates - step, pltpu.roll(values, width - step, 1), 0.0)
        step *= 2
    return values


def used_currencies(currencies, counts):
    slot = lax.broadcasted_iota(jnp.int32, currencies.shape, 0)
    return jnp.where(slot < counts, currencies, -1)


def core_in(chip, group):
    return 1 - group if chip % 2 else group


def own_group():
    me = lax.axis_index("sets")
    return (me + me // 2) % 2


def group_order(chips, group):
    middle = chips // 2
    far, near = list(range(middle, chips)), list(range(middle))
    if group == 0 and middle % 2 == 0:
        far = [chip ^ 1 for chip in far]
    cut = middle // 2
    return far[:cut] + near[:1] + far[cut:] + near[1:]


def chip_at(chips, place):
    chosen = [group_order(chips, group)[place] for group in range(2)]
    return jnp.where(own_group() == 0, chosen[0], chosen[1])


def group_columns(chip, owned, group):
    block = 2 * chip + core_in(chip, group)
    return pl.ds(pl.multiple_of(block * owned, owned), owned)


def row_flags(tile):
    shift = lax.broadcasted_iota(jnp.int32, (8, lanes), 0) + (8 * tile) % bits_per_row
    shift = jnp.where(shift >= bits_per_row, shift - bits_per_row, shift)
    return jnp.left_shift(jnp.int32(1), shift)


def masked_rows(exposure, bits, pair, flags, chip, part):
    row = lax.broadcasted_iota(jnp.int32, (8, lanes), 0)
    kept = []
    for half in range(2):
        values = exposure[chip % 2, 2 * pair + half, chip // 2].astype(jnp.float32)
        top = 16 * pair + 8 * half
        group = top // bits_per_row
        left = bits_per_row * (group + 1) - top
        packed = jnp.broadcast_to(bits[group : group + 1, part], (8, lanes))
        if left < 8:
            following = jnp.broadcast_to(bits[group + 1 : group + 2, part], (8, lanes))
            packed = jnp.where(row < left, packed, following)
        kept.append(jnp.where((packed & flags[half]) != 0, values, 0.0))
    return jnp.concatenate(kept, axis=0).astype(jnp.bfloat16)


def mask_and_sum(exposure, bits, weights, masked_ref, terms_ref, group):
    sets = 8 * exposure.shape[1]
    chips, owned = terms_ref.shape[0], terms_ref.shape[2]
    for first in range(0, chips, 2):
        rows = []
        for pair in range(sets // 16):
            flags = [row_flags(2 * pair), row_flags(2 * pair + 1)]
            rows.append(
                jnp.concatenate(
                    [
                        masked_rows(
                            exposure, bits, pair, flags, chip, group_columns(chip, owned, group)
                        )
                        for chip in (first, first + 1)
                    ],
                    axis=1,
                )
            )
        masked = jnp.concatenate(rows, axis=0)
        masked_ref[:, first * owned : (first + 2) * owned] = masked
        terms = jnp.dot(weights, masked, preferred_element_type=jnp.float32)
        terms = terms.astype(terms_ref.dtype)
        terms_ref[first] = terms[:, :owned]
        terms_ref[first + 1] = terms[:, owned:]


def first_kernel(
    exposure_hbm,
    bits_hbm,
    currencies_hbm,
    counts_hbm,
    notional_hbm,
    fx_hbm,
    rates_hbm,
    start_hbm,
    handed_ref,
    masked_ref,
    exposure_own,
    bits,
    weights_ref,
    used_ref,
    fx_ref,
    rates_ref,
    start_ref,
    currencies_ref,
    counts_ref,
    notional_ref,
    exposure_other,
    sems,
    tile_sems,
):
    sets = 8 * exposure_own.shape[1]
    own = own_group()
    other = 1 - own
    currency_count = handed_ref.shape[1]
    copies = [
        pltpu.make_async_copy(source, target, sems.at[index])
        for index, (source, target) in enumerate(
            [
                (bits_hbm, bits),
                (currencies_hbm, currencies_ref),
                (counts_hbm, counts_ref),
                (notional_hbm, notional_ref),
                (fx_hbm, fx_ref),
                (rates_hbm, rates_ref),
                (start_hbm, start_ref),
            ]
        )
    ]
    tile_copies = [
        [
            pltpu.make_async_copy(
                exposure_hbm.at[:, :, parity, core_in(parity, group)],
                target.at[parity],
                tile_sems.at[2 * index + parity],
            )
            for parity in range(2)
        ]
        for index, (group, target) in enumerate([(other, exposure_other), (own, exposure_own)])
    ]
    for copy in copies[:1] + tile_copies[0] + copies[1:4] + tile_copies[1] + copies[4:]:
        copy.start()
    for copy in copies[1:4]:
        copy.wait()

    used = used_currencies(currencies_ref[...], counts_ref[...])
    used_ref[...] = used
    notional = notional_ref[...]
    currency = lax.broadcasted_iota(jnp.int32, (currency_count, sets), 0)
    weights = jnp.zeros((currency_count, sets), jnp.float32)
    for slot in range(used.shape[0]):
        weights = weights + jnp.where(
            currency == used[slot : slot + 1], notional[slot : slot + 1], 0.0
        )
    weights = weights.astype(jnp.bfloat16)
    weights_ref[...] = weights
    for copy in copies[:1] + tile_copies[0]:
        copy.wait()
    mask_and_sum(exposure_other, bits, weights, masked_ref, handed_ref, other)
    for copy in tile_copies[1] + copies[4:]:
        copy.wait()


def second_kernel(
    dates,
    exposure,
    bits,
    weights_ref,
    fx_ref,
    rates_ref,
    start_ref,
    masked_ref,
    terms_ref,
    carried_ref,
    discount_ref,
    moved_ref,
):
    own = own_group()
    mask_and_sum(exposure, bits, weights_ref[...], masked_ref, terms_ref, own)
    integral = spread_paths(start_ref[...], dates) + step_years * sums_to_date(rates_ref[...], dates)
    discount = jnp.exp(-integral)
    discount_ref[...] = discount
    moved = fx_ref[...] * discount
    moved_ref[...] = moved
    carried_ref[...] = moved.astype(jnp.bfloat16)


def merging_kernel(given_ref, terms_ref, carried_ref, outgoing_ref):
    chips, currency_count, owned = terms_ref.shape
    carried = carried_ref[...]
    for place in range(chips):
        chip = chip_at(chips, place)
        outgoing_ref[place, 0:currency_count, :] = carried
        outgoing_ref[place, currency_count:, :] = (
            terms_ref[chip] + given_ref[chip].astype(jnp.float32)
        ).astype(jnp.bfloat16)


def unpacking_kernel(arrived_ref, carried_ref):
    chips, currency_count, owned = carried_ref.shape
    for place in range(chips):
        carried_ref[chip_at(chips, place)] = arrived_ref[place, 0:currency_count, :]


def projection(masked, carried_ref):
    sets, half = masked.shape
    chips, currency_count, owned = carried_ref.shape
    here = min(chips, 8)
    projected = jnp.zeros((currency_count, sets), jnp.float32)
    for first in range(0, chips, here):
        carried = jnp.concatenate([carried_ref[first + chip] for chip in range(here)], axis=1)
        projected = projected + lax.dot_general(
            carried,
            masked[:, first * owned : (first + here) * owned],
            (((1,), (1,)), ((), ())),
            preferred_element_type=jnp.float32,
        )
    return projected


def adjoint_kernel(
    dates,
    arrived_ref,
    carried_ref,
    masked_own,
    moved_ref,
    discount_ref,
    fx_adjoint_ref,
    rate_adjoint_ref,
    projected_ref,
):
    chips, currency_count, owned = carried_ref.shape
    aggregate = arrived_ref[0, currency_count:, :].astype(jnp.float32)
    for chip in range(1, chips):
        aggregate = aggregate + arrived_ref[chip, currency_count:, :].astype(jnp.float32)
    fx_adjoint_ref[...] = aggregate * discount_ref[...]
    rate_adjoint_ref[...] = -step_years * sums_from_date(aggregate * moved_ref[...], dates)
    projected_ref[...] = projection(masked_own, carried_ref)


def picking_kernel(carried_ref, masked_other, projected_ref, used_ref, notional_adjoint_ref):
    sets, half = masked_other.shape
    currency_count = carried_ref.shape[1]
    projected = projected_ref[...] + projection(masked_other, carried_ref)
    used = used_ref[...]
    currency = lax.broadcasted_iota(jnp.int32, (currency_count, sets), 0)
    for slot in range(used.shape[0]):
        picked = jnp.sum(
            jnp.where(currency == used[slot : slot + 1], projected, 0.0), axis=0, keepdims=True
        )
        notional_adjoint_ref[slot : slot + 1, :] = picked * (1.0 / math.sqrt(2 * half))


def body(
    exposure_adjoint,
    positive_bits,
    currencies,
    mix_count,
    notional,
    fx_paths,
    short_rates,
    start_integral,
):
    sets, columns = exposure_adjoint.shape
    currency_count, owned = fx_paths.shape
    dates = owned // start_integral.shape[1]
    peers = columns // owned
    chips = peers // 2
    slots = currencies.shape[1]
    in_vmem = pl.BlockSpec(memory_space=pltpu.VMEM)
    anywhere = pl.BlockSpec(memory_space=pl.ANY)
    params = pltpu.CompilerParams(vmem_limit_bytes=32 * 2**20)
    block = (currency_count, owned)

    def in_hbm(value):
        return pltpu.with_memory_space_constraint(value, pltpu.HBM)

    tiles = exposure_adjoint.reshape(sets // 8, 8, chips // 2, 2, 2, owned)
    tiles = tiles.transpose(0, 2, 3, 4, 1, 5)
    half_tiles = (2, sets // 8, chips // 2, 8, owned)

    def swapped(value):
        return lax.ppermute(value, "sets", [(peer, peer ^ 1) for peer in range(peers)])

    handed, masked_other, exposure, bits, weights, used, fx, rates, start = pl.pallas_call(
        first_kernel,
        out_shape=(
            pltpu.VMEM((chips,) + block, jnp.bfloat16),
            pltpu.VMEM((sets, columns // 2), jnp.bfloat16),
            pltpu.VMEM(half_tiles, jnp.bfloat16),
            pltpu.VMEM(positive_bits.shape, jnp.int32),
            pltpu.VMEM((currency_count, sets), jnp.bfloat16),
            pltpu.VMEM((slots, sets), jnp.int32),
            pltpu.VMEM(block, jnp.float32),
            pltpu.VMEM(block, jnp.float32),
            pltpu.VMEM((owned // dates, currency_count), jnp.float32),
        ),
        in_specs=[anywhere] * 8,
        out_specs=(in_vmem,) * 9,
        scratch_shapes=[
            pltpu.VMEM((slots, sets), jnp.int32),
            pltpu.VMEM((1, sets), jnp.int32),
            pltpu.VMEM((slots, sets), jnp.float32),
            pltpu.VMEM(half_tiles, jnp.bfloat16),
            pltpu.SemaphoreType.DMA((7,)),
            pltpu.SemaphoreType.DMA((4,)),
        ],
        compiler_params=params,
        name="first",
    )(
        in_hbm(tiles),
        in_hbm(positive_bits),
        in_hbm(currencies.T),
        in_hbm(mix_count.reshape(1, sets)),
        in_hbm(notional.T),
        in_hbm(fx_paths),
        in_hbm(short_rates),
        in_hbm(start_integral.T),
    )
    given = swapped(handed)
    masked_own, terms, carried, discount, moved = pl.pallas_call(
        functools.partial(second_kernel, dates),
        out_shape=(
            pltpu.VMEM((sets, columns // 2), jnp.bfloat16),
            pltpu.VMEM((chips,) + block, jnp.float32),
            pltpu.VMEM(block, jnp.bfloat16),
            pltpu.VMEM(block, jnp.float32),
            pltpu.VMEM(block, jnp.float32),
        ),
        in_specs=[in_vmem] * 6,
        out_specs=(in_vmem,) * 5,
        compiler_params=params,
        name="second",
    )(
        exposure,
        bits,
        weights,
        fx,
        rates,
        start,
    )
    outgoing = pl.pallas_call(
        merging_kernel,
        out_shape=pltpu.VMEM((chips, 2 * currency_count, owned), jnp.bfloat16),
        in_specs=[in_vmem] * 3,
        out_specs=in_vmem,
        compiler_params=params,
        name="merging",
    )(given, terms, carried)
    arrived = lax.all_to_all(
        outgoing,
        "sets",
        0,
        0,
        axis_index_groups=[
            [2 * chip + core_in(chip, group) for chip in group_order(chips, group)]
            for group in range(2)
        ],
        tiled=True,
    )
    carried_own = pl.pallas_call(
        unpacking_kernel,
        out_shape=pltpu.VMEM((chips,) + block, jnp.bfloat16),
        in_specs=[in_vmem],
        out_specs=in_vmem,
        compiler_params=params,
        name="unpacking",
    )(arrived)
    carried_other = swapped(carried_own)
    fx_adjoint, rate_adjoint, projected = pl.pallas_call(
        functools.partial(adjoint_kernel, dates),
        out_shape=(
            jax.ShapeDtypeStruct(block, jnp.float32),
            jax.ShapeDtypeStruct(block, jnp.float32),
            pltpu.VMEM((currency_count, sets), jnp.float32),
        ),
        in_specs=[in_vmem] * 5,
        out_specs=(in_vmem,) * 3,
        compiler_params=params,
        name="adjoint",
    )(arrived, carried_own, masked_own, moved, discount)
    notional_adjoint = pl.pallas_call(
        picking_kernel,
        out_shape=jax.ShapeDtypeStruct((slots, sets), jnp.float32),
        in_specs=[in_vmem] * 4,
        out_specs=in_vmem,
        compiler_params=params,
        name="picking",
    )(carried_other, masked_other, projected, used)
    return fx_adjoint, rate_adjoint, notional_adjoint.T


def solution(mesh):
    in_specs = (
        P(("grp", "sets"), None),
        P(("grp", "sets"), None),
        P(("grp", "sets"), None),
        P(("grp", "sets")),
        P(("grp", "sets"), None),
        P("grp", "sets"),
        P("grp", "sets"),
        P("grp", "sets"),
    )
    out_specs = (P("grp", "sets"), P("grp", "sets"), P(("grp", "sets"), None))
    return jax.shard_map(body, mesh=mesh, in_specs=in_specs, out_specs=out_specs, check_vma=False)
```

```python
import functools
import math

import jax
import jax.numpy as jnp
from jax import lax
from jax.experimental import pallas as pl
from jax.experimental.pallas import tpu as pltpu
from jax.sharding import PartitionSpec as P

step_years = 0.25
bits_per_row = 15
lanes = 128


def spread_paths(values, dates):
    paths, columns = values.shape[0], values.shape[0] * dates
    path_of = lax.broadcasted_iota(jnp.int32, (paths, columns), 1) // dates
    own = lax.broadcasted_iota(jnp.int32, (paths, columns), 0)
    return lax.dot_general(
        values,
        (path_of == own).astype(jnp.float32),
        (((0,), (0,)), ((), ())),
        precision=lax.Precision.HIGHEST,
        preferred_element_type=jnp.float32,
    )


def sums_to_date(values, dates):
    width = values.shape[1]
    date = lax.broadcasted_iota(jnp.int32, values.shape, 1) % dates
    step = 1
    while step < dates:
        values = values + jnp.where(date >= step, pltpu.roll(values, step, 1), 0.0)
        step *= 2
    return values


def sums_from_date(values, dates):
    width = values.shape[1]
    date = lax.broadcasted_iota(jnp.int32, values.shape, 1) % dates
    step = 1
    while step < dates:
        values = values + jnp.where(date < dates - step, pltpu.roll(values, width - step, 1), 0.0)
        step *= 2
    return values


def used_currencies(currencies, counts):
    slot = lax.broadcasted_iota(jnp.int32, currencies.shape, 0)
    return jnp.where(slot < counts, currencies, -1)


def core_in(chip, group):
    return 1 - group if (chip + chip // 2) % 2 else group


def own_group():
    me = lax.axis_index("sets")
    return (me + me // 2 + me // 4) % 2


def group_order(chips, group):
    middle = chips // 2
    far, near = list(range(middle, chips)), list(range(middle))
    if group == 0 and middle % 2 == 0:
        far = [chip ^ 1 for chip in far]
    cut = middle // 2
    return far[:cut] + near[:1] + far[cut:] + near[1:]


def chip_at(chips, place):
    chosen = [group_order(chips, group)[place] for group in range(2)]
    return jnp.where(own_group() == 0, chosen[0], chosen[1])


def group_columns(chip, owned, group):
    block = 2 * chip + core_in(chip, group)
    return pl.ds(pl.multiple_of(block * owned, owned), owned)


def row_flags(tile):
    shift = lax.broadcasted_iota(jnp.int32, (8, lanes), 0) + (8 * tile) % bits_per_row
    shift = jnp.where(shift >= bits_per_row, shift - bits_per_row, shift)
    return jnp.left_shift(jnp.int32(1), shift)


def masked_rows(exposure, bits, pair, flags, part):
    row = lax.broadcasted_iota(jnp.int32, (8, lanes), 0)
    values = exposure[16 * pair : 16 * pair + 16, part].astype(jnp.float32)
    kept = []
    for half in range(2):
        top = 16 * pair + 8 * half
        group = top // bits_per_row
        left = bits_per_row * (group + 1) - top
        packed = jnp.broadcast_to(bits[group : group + 1, part], (8, lanes))
        if left < 8:
            following = jnp.broadcast_to(bits[group + 1 : group + 2, part], (8, lanes))
            packed = jnp.where(row < left, packed, following)
        kept.append(jnp.where((packed & flags[half]) != 0, values[8 * half : 8 * half + 8], 0.0))
    return jnp.concatenate(kept, axis=0).astype(jnp.bfloat16)


def mask_and_sum(exposure, bits, weights, masked_ref, terms_ref, group):
    sets = exposure.shape[0]
    chips, owned = terms_ref.shape[0], terms_ref.shape[2]
    for first in range(0, chips, 2):
        rows = []
        for pair in range(sets // 16):
            flags = [row_flags(2 * pair), row_flags(2 * pair + 1)]
            rows.append(
                jnp.concatenate(
                    [
                        masked_rows(
                            exposure, bits, pair, flags, group_columns(chip, owned, group)
                        )
                        for chip in (first, first + 1)
                    ],
                    axis=1,
                )
            )
        masked = jnp.concatenate(rows, axis=0)
        masked_ref[:, first * owned : (first + 2) * owned] = masked
        terms = jnp.dot(weights, masked, preferred_element_type=jnp.float32)
        terms = terms.astype(terms_ref.dtype)
        terms_ref[first] = terms[:, :owned]
        terms_ref[first + 1] = terms[:, owned:]


def first_kernel(
    exposure_hbm,
    bits_hbm,
    currencies_hbm,
    counts_hbm,
    notional_hbm,
    fx_hbm,
    rates_hbm,
    start_hbm,
    handed_ref,
    masked_ref,
    exposure,
    bits,
    weights_ref,
    used_ref,
    fx_ref,
    rates_ref,
    start_ref,
    currencies_ref,
    counts_ref,
    notional_ref,
    sems,
):
    sets = exposure.shape[0]
    currency_count = handed_ref.shape[1]
    copies = [
        pltpu.make_async_copy(source, target, sems.at[index])
        for index, (source, target) in enumerate(
            [
                (exposure_hbm, exposure),
                (bits_hbm, bits),
                (currencies_hbm, currencies_ref),
                (counts_hbm, counts_ref),
                (notional_hbm, notional_ref),
                (fx_hbm, fx_ref),
                (rates_hbm, rates_ref),
                (start_hbm, start_ref),
            ]
        )
    ]
    for copy in copies:
        copy.start()
    for copy in copies[2:5]:
        copy.wait()

    used = used_currencies(currencies_ref[...], counts_ref[...])
    used_ref[...] = used
    notional = notional_ref[...]
    currency = lax.broadcasted_iota(jnp.int32, (currency_count, sets), 0)
    weights = jnp.zeros((currency_count, sets), jnp.float32)
    for slot in range(used.shape[0]):
        weights = weights + jnp.where(
            currency == used[slot : slot + 1], notional[slot : slot + 1], 0.0
        )
    weights = weights.astype(jnp.bfloat16)
    weights_ref[...] = weights
    for copy in copies[:2]:
        copy.wait()
    other = 1 - own_group()
    mask_and_sum(exposure, bits, weights, masked_ref, handed_ref, other)
    for copy in copies[5:]:
        copy.wait()


def second_kernel(
    dates,
    exposure,
    bits,
    weights_ref,
    fx_ref,
    rates_ref,
    start_ref,
    masked_other,
    masked_ref,
    terms_ref,
    carried_ref,
    discount_ref,
    moved_ref,
    turned_ref,
):
    own = own_group()
    mask_and_sum(exposure, bits, weights_ref[...], masked_ref, terms_ref, own)
    integral = spread_paths(start_ref[...], dates) + step_years * sums_to_date(rates_ref[...], dates)
    discount = jnp.exp(-integral)
    discount_ref[...] = discount
    moved = fx_ref[...] * discount
    moved_ref[...] = moved
    carried_ref[...] = moved.astype(jnp.bfloat16)
    for column in range(0, masked_other.shape[1], lanes):
        turned_ref[column : column + lanes, :] = masked_other[:, column : column + lanes].T


def merging_kernel(given_ref, terms_ref, carried_ref, outgoing_ref):
    chips, currency_count, owned = terms_ref.shape
    carried = carried_ref[...]
    for place in range(chips):
        chip = chip_at(chips, place)
        outgoing_ref[place, 0:currency_count, :] = carried
        outgoing_ref[place, currency_count:, :] = (
            terms_ref[chip] + given_ref[chip].astype(jnp.float32)
        ).astype(jnp.bfloat16)


def unpacking_kernel(arrived_ref, carried_ref):
    chips, currency_count, owned = carried_ref.shape
    for place in range(chips):
        carried_ref[chip_at(chips, place)] = arrived_ref[place, 0:currency_count, :]


def projection(masked, carried_ref):
    sets, half = masked.shape
    chips, currency_count, owned = carried_ref.shape
    here = min(chips, 8)
    projected = jnp.zeros((currency_count, sets), jnp.float32)
    for first in range(0, chips, here):
        carried = jnp.concatenate([carried_ref[first + chip] for chip in range(here)], axis=1)
        projected = projected + lax.dot_general(
            carried,
            masked[:, first * owned : (first + here) * owned],
            (((1,), (1,)), ((), ())),
            preferred_element_type=jnp.float32,
        )
    return projected


def adjoint_kernel(
    dates,
    arrived_ref,
    carried_ref,
    masked_own,
    moved_ref,
    discount_ref,
    fx_adjoint_ref,
    rate_adjoint_ref,
    projected_ref,
):
    chips, currency_count, owned = carried_ref.shape
    aggregate = arrived_ref[0, currency_count:, :].astype(jnp.float32)
    for chip in range(1, chips):
        aggregate = aggregate + arrived_ref[chip, currency_count:, :].astype(jnp.float32)
    fx_adjoint_ref[...] = aggregate * discount_ref[...]
    rate_adjoint_ref[...] = -step_years * sums_from_date(aggregate * moved_ref[...], dates)
    projected_ref[...] = projection(masked_own, carried_ref)


def picking_kernel(carried_ref, turned_ref, projected_ref, used_ref, notional_adjoint_ref):
    half, sets = turned_ref.shape
    currency_count = carried_ref.shape[1]
    chips, _, owned = carried_ref.shape
    here = min(chips, 8)
    projected = projected_ref[...]
    for first in range(0, chips, here):
        carried = jnp.concatenate([carried_ref[first + chip] for chip in range(here)], axis=1)
        projected = projected + jnp.dot(
            carried,
            turned_ref[first * owned : (first + here) * owned, :],
            preferred_element_type=jnp.float32,
        )
    used = used_ref[...]
    currency = lax.broadcasted_iota(jnp.int32, (currency_count, sets), 0)
    for slot in range(used.shape[0]):
        picked = jnp.sum(
            jnp.where(currency == used[slot : slot + 1], projected, 0.0), axis=0, keepdims=True
        )
        notional_adjoint_ref[slot : slot + 1, :] = picked * (1.0 / math.sqrt(2 * half))


def body(
    exposure_adjoint,
    positive_bits,
    currencies,
    mix_count,
    notional,
    fx_paths,
    short_rates,
    start_integral,
):
    sets, columns = exposure_adjoint.shape
    currency_count, owned = fx_paths.shape
    dates = owned // start_integral.shape[1]
    peers = columns // owned
    chips = peers // 2
    slots = currencies.shape[1]
    in_vmem = pl.BlockSpec(memory_space=pltpu.VMEM)
    anywhere = pl.BlockSpec(memory_space=pl.ANY)
    params = pltpu.CompilerParams(vmem_limit_bytes=32 * 2**20)
    block = (currency_count, owned)

    def in_hbm(value):
        return pltpu.with_memory_space_constraint(value, pltpu.HBM)

    def swapped(value):
        return lax.ppermute(value, "sets", [(peer, peer ^ 1) for peer in range(peers)])

    handed, masked_other, exposure, bits, weights, used, fx, rates, start = pl.pallas_call(
        first_kernel,
        out_shape=(
            pltpu.VMEM((chips,) + block, jnp.bfloat16),
            pltpu.VMEM((sets, columns // 2), jnp.bfloat16),
            pltpu.VMEM((sets, columns), jnp.bfloat16),
            pltpu.VMEM(positive_bits.shape, jnp.int32),
            pltpu.VMEM((currency_count, sets), jnp.bfloat16),
            pltpu.VMEM((slots, sets), jnp.int32),
            pltpu.VMEM(block, jnp.float32),
            pltpu.VMEM(block, jnp.float32),
            pltpu.VMEM((owned // dates, currency_count), jnp.float32),
        ),
        in_specs=[anywhere] * 8,
        out_specs=(in_vmem,) * 9,
        scratch_shapes=[
            pltpu.VMEM((slots, sets), jnp.int32),
            pltpu.VMEM((1, sets), jnp.int32),
            pltpu.VMEM((slots, sets), jnp.float32),
            pltpu.SemaphoreType.DMA((8,)),
        ],
        compiler_params=params,
        name="first",
    )(
        in_hbm(exposure_adjoint),
        in_hbm(positive_bits),
        in_hbm(currencies.T),
        in_hbm(mix_count.reshape(1, sets)),
        in_hbm(notional.T),
        in_hbm(fx_paths),
        in_hbm(short_rates),
        in_hbm(start_integral.T),
    )
    given = swapped(handed)
    masked_own, terms, carried, discount, moved, turned = pl.pallas_call(
        functools.partial(second_kernel, dates),
        out_shape=(
            pltpu.VMEM((sets, columns // 2), jnp.bfloat16),
            pltpu.VMEM((chips,) + block, jnp.float32),
            pltpu.VMEM(block, jnp.bfloat16),
            pltpu.VMEM(block, jnp.float32),
            pltpu.VMEM(block, jnp.float32),
            pltpu.VMEM((columns // 2, sets), jnp.bfloat16),
        ),
        in_specs=[in_vmem] * 7,
        out_specs=(in_vmem,) * 6,
        compiler_params=params,
        name="second",
    )(
        exposure,
        bits,
        weights,
        fx,
        rates,
        start,
        masked_other,
    )
    outgoing = pl.pallas_call(
        merging_kernel,
        out_shape=pltpu.VMEM((chips, 2 * currency_count, owned), jnp.bfloat16),
        in_specs=[in_vmem] * 3,
        out_specs=in_vmem,
        compiler_params=params,
        name="merging",
    )(given, terms, carried)
    arrived = lax.all_to_all(
        outgoing,
        "sets",
        0,
        0,
        axis_index_groups=[
            [2 * chip + core_in(chip, group) for chip in group_order(chips, group)]
            for group in range(2)
        ],
        tiled=True,
    )
    carried_own = pl.pallas_call(
        unpacking_kernel,
        out_shape=pltpu.VMEM((chips,) + block, jnp.bfloat16),
        in_specs=[in_vmem],
        out_specs=in_vmem,
        compiler_params=params,
        name="unpacking",
    )(arrived)
    carried_other = swapped(carried_own)
    fx_adjoint, rate_adjoint, projected = pl.pallas_call(
        functools.partial(adjoint_kernel, dates),
        out_shape=(
            jax.ShapeDtypeStruct(block, jnp.float32),
            jax.ShapeDtypeStruct(block, jnp.float32),
            pltpu.VMEM((currency_count, sets), jnp.float32),
        ),
        in_specs=[in_vmem] * 5,
        out_specs=(in_vmem,) * 3,
        compiler_params=params,
        name="adjoint",
    )(arrived, carried_own, masked_own, moved, discount)
    notional_adjoint = pl.pallas_call(
        picking_kernel,
        out_shape=jax.ShapeDtypeStruct((slots, sets), jnp.float32),
        in_specs=[in_vmem] * 4,
        out_specs=in_vmem,
        compiler_params=params,
        name="picking",
    )(carried_other, turned, projected, used)
    return fx_adjoint, rate_adjoint, notional_adjoint.T


def solution(mesh):
    in_specs = (
        P(("grp", "sets"), None),
        P(("grp", "sets"), None),
        P(("grp", "sets"), None),
        P(("grp", "sets")),
        P(("grp", "sets"), None),
        P("grp", "sets"),
        P("grp", "sets"),
        P("grp", "sets"),
    )
    out_specs = (P("grp", "sets"), P("grp", "sets"), P(("grp", "sets"), None))
    return jax.shard_map(body, mesh=mesh, in_specs=in_specs, out_specs=out_specs, check_vma=False)
```

```python
import functools
import math

import jax
import jax.numpy as jnp
from jax import lax
from jax.experimental import pallas as pl
from jax.experimental.pallas import tpu as pltpu
from jax.sharding import PartitionSpec as P

step_years = 0.25
bits_per_row = 15
lanes = 128


def spread_paths(values, dates):
    paths, columns = values.shape[0], values.shape[0] * dates
    path_of = lax.broadcasted_iota(jnp.int32, (paths, columns), 1) // dates
    own = lax.broadcasted_iota(jnp.int32, (paths, columns), 0)
    return lax.dot_general(
        values,
        (path_of == own).astype(jnp.float32),
        (((0,), (0,)), ((), ())),
        precision=lax.Precision.HIGHEST,
        preferred_element_type=jnp.float32,
    )


def sums_to_date(values, dates):
    width = values.shape[1]
    date = lax.broadcasted_iota(jnp.int32, values.shape, 1) % dates
    step = 1
    while step < dates:
        values = values + jnp.where(date >= step, pltpu.roll(values, step, 1), 0.0)
        step *= 2
    return values


def sums_from_date(values, dates):
    width = values.shape[1]
    date = lax.broadcasted_iota(jnp.int32, values.shape, 1) % dates
    step = 1
    while step < dates:
        values = values + jnp.where(date < dates - step, pltpu.roll(values, width - step, 1), 0.0)
        step *= 2
    return values


def used_currencies(currencies, counts):
    slot = lax.broadcasted_iota(jnp.int32, currencies.shape, 0)
    return jnp.where(slot < counts, currencies, -1)


def core_in(chip, group):
    return 1 - group if (chip + chip // 2) % 2 else group


def own_group():
    me = lax.axis_index("sets")
    return (me + me // 2 + me // 4) % 2


def group_order(chips, group):
    middle = chips // 2
    far, near = list(range(middle, chips)), list(range(middle))
    lead = [chip for chip in near[middle // 2 :] if core_in(chip, group)][:1]
    return lead + far + [chip for chip in near if chip not in lead]


def chip_at(chips, place):
    chosen = [group_order(chips, group)[place] for group in range(2)]
    return jnp.where(own_group() == 0, chosen[0], chosen[1])


def group_columns(chip, owned, group):
    block = 2 * chip + core_in(chip, group)
    return pl.ds(pl.multiple_of(block * owned, owned), owned)


def row_flags(tile):
    shift = lax.broadcasted_iota(jnp.int32, (8, lanes), 0) + (8 * tile) % bits_per_row
    shift = jnp.where(shift >= bits_per_row, shift - bits_per_row, shift)
    return jnp.left_shift(jnp.int32(1), shift)


def masked_rows(exposure, bits, pair, flags, part):
    row = lax.broadcasted_iota(jnp.int32, (8, lanes), 0)
    values = exposure[16 * pair : 16 * pair + 16, part].astype(jnp.float32)
    kept = []
    for half in range(2):
        top = 16 * pair + 8 * half
        group = top // bits_per_row
        left = bits_per_row * (group + 1) - top
        packed = jnp.broadcast_to(bits[group : group + 1, part], (8, lanes))
        if left < 8:
            following = jnp.broadcast_to(bits[group + 1 : group + 2, part], (8, lanes))
            packed = jnp.where(row < left, packed, following)
        kept.append(jnp.where((packed & flags[half]) != 0, values[8 * half : 8 * half + 8], 0.0))
    return jnp.concatenate(kept, axis=0).astype(jnp.bfloat16)


def mask_and_sum(exposure, bits, weights, masked_ref, terms_ref, group):
    sets = exposure.shape[0]
    chips, owned = terms_ref.shape[0], terms_ref.shape[2]
    for first in range(0, chips, 2):
        rows = []
        for pair in range(sets // 16):
            flags = [row_flags(2 * pair), row_flags(2 * pair + 1)]
            rows.append(
                jnp.concatenate(
                    [
                        masked_rows(
                            exposure, bits, pair, flags, group_columns(chip, owned, group)
                        )
                        for chip in (first, first + 1)
                    ],
                    axis=1,
                )
            )
        masked = jnp.concatenate(rows, axis=0)
        masked_ref[:, first * owned : (first + 2) * owned] = masked
        terms = jnp.dot(weights, masked, preferred_element_type=jnp.float32)
        terms = terms.astype(terms_ref.dtype)
        terms_ref[first] = terms[:, :owned]
        terms_ref[first + 1] = terms[:, owned:]


def first_kernel(
    exposure_hbm,
    bits_hbm,
    currencies_hbm,
    counts_hbm,
    notional_hbm,
    fx_hbm,
    rates_hbm,
    start_hbm,
    handed_ref,
    masked_ref,
    exposure,
    bits,
    weights_ref,
    used_ref,
    fx_ref,
    rates_ref,
    start_ref,
    currencies_ref,
    counts_ref,
    notional_ref,
    sems,
):
    sets = exposure.shape[0]
    currency_count = handed_ref.shape[1]
    copies = [
        pltpu.make_async_copy(source, target, sems.at[index])
        for index, (source, target) in enumerate(
            [
                (exposure_hbm, exposure),
                (bits_hbm, bits),
                (currencies_hbm, currencies_ref),
                (counts_hbm, counts_ref),
                (notional_hbm, notional_ref),
                (fx_hbm, fx_ref),
                (rates_hbm, rates_ref),
                (start_hbm, start_ref),
            ]
        )
    ]
    for copy in copies:
        copy.start()
    for copy in copies[2:5]:
        copy.wait()

    used = used_currencies(currencies_ref[...], counts_ref[...])
    used_ref[...] = used
    notional = notional_ref[...]
    currency = lax.broadcasted_iota(jnp.int32, (currency_count, sets), 0)
    weights = jnp.zeros((currency_count, sets), jnp.float32)
    for slot in range(used.shape[0]):
        weights = weights + jnp.where(
            currency == used[slot : slot + 1], notional[slot : slot + 1], 0.0
        )
    weights = weights.astype(jnp.bfloat16)
    weights_ref[...] = weights
    for copy in copies[:2]:
        copy.wait()
    other = 1 - own_group()
    mask_and_sum(exposure, bits, weights, masked_ref, handed_ref, other)
    for copy in copies[5:]:
        copy.wait()


def second_kernel(
    dates,
    exposure,
    bits,
    weights_ref,
    fx_ref,
    rates_ref,
    start_ref,
    masked_other,
    masked_ref,
    terms_ref,
    carried_ref,
    discount_ref,
    moved_ref,
    turned_ref,
):
    own = own_group()
    mask_and_sum(exposure, bits, weights_ref[...], masked_ref, terms_ref, own)
    integral = spread_paths(start_ref[...], dates) + step_years * sums_to_date(rates_ref[...], dates)
    discount = jnp.exp(-integral)
    discount_ref[...] = discount
    moved = fx_ref[...] * discount
    moved_ref[...] = moved
    carried_ref[...] = moved.astype(jnp.bfloat16)
    for column in range(0, masked_other.shape[1], lanes):
        turned_ref[column : column + lanes, :] = masked_other[:, column : column + lanes].T


def merging_kernel(given_ref, terms_ref, carried_ref, outgoing_ref):
    chips, currency_count, owned = terms_ref.shape
    carried = carried_ref[...]
    for place in range(chips):
        chip = chip_at(chips, place)
        outgoing_ref[place, 0:currency_count, :] = carried
        outgoing_ref[place, currency_count:, :] = (
            terms_ref[chip] + given_ref[chip].astype(jnp.float32)
        ).astype(jnp.bfloat16)


def unpacking_kernel(arrived_ref, carried_ref):
    chips, currency_count, owned = carried_ref.shape
    for place in range(chips):
        carried_ref[chip_at(chips, place)] = arrived_ref[place, 0:currency_count, :]


def projection(masked, carried_ref):
    sets, half = masked.shape
    chips, currency_count, owned = carried_ref.shape
    here = min(chips, 8)
    projected = jnp.zeros((currency_count, sets), jnp.float32)
    for first in range(0, chips, here):
        carried = jnp.concatenate([carried_ref[first + chip] for chip in range(here)], axis=1)
        projected = projected + lax.dot_general(
            carried,
            masked[:, first * owned : (first + here) * owned],
            (((1,), (1,)), ((), ())),
            preferred_element_type=jnp.float32,
        )
    return projected


def adjoint_kernel(
    dates,
    arrived_ref,
    carried_ref,
    masked_own,
    moved_ref,
    discount_ref,
    fx_adjoint_ref,
    rate_adjoint_ref,
    projected_ref,
):
    chips, currency_count, owned = carried_ref.shape
    aggregate = arrived_ref[0, currency_count:, :].astype(jnp.float32)
    for chip in range(1, chips):
        aggregate = aggregate + arrived_ref[chip, currency_count:, :].astype(jnp.float32)
    fx_adjoint_ref[...] = aggregate * discount_ref[...]
    rate_adjoint_ref[...] = -step_years * sums_from_date(aggregate * moved_ref[...], dates)
    projected_ref[...] = projection(masked_own, carried_ref)


def picking_kernel(carried_ref, turned_ref, projected_ref, used_ref, notional_adjoint_ref):
    half, sets = turned_ref.shape
    currency_count = carried_ref.shape[1]
    chips, _, owned = carried_ref.shape
    here = min(chips, 8)
    projected = projected_ref[...]
    for first in range(0, chips, here):
        carried = jnp.concatenate([carried_ref[first + chip] for chip in range(here)], axis=1)
        projected = projected + jnp.dot(
            carried,
            turned_ref[first * owned : (first + here) * owned, :],
            preferred_element_type=jnp.float32,
        )
    used = used_ref[...]
    currency = lax.broadcasted_iota(jnp.int32, (currency_count, sets), 0)
    for slot in range(used.shape[0]):
        picked = jnp.sum(
            jnp.where(currency == used[slot : slot + 1], projected, 0.0), axis=0, keepdims=True
        )
        notional_adjoint_ref[slot : slot + 1, :] = picked * (1.0 / math.sqrt(2 * half))


def body(
    exposure_adjoint,
    positive_bits,
    currencies,
    mix_count,
    notional,
    fx_paths,
    short_rates,
    start_integral,
):
    sets, columns = exposure_adjoint.shape
    currency_count, owned = fx_paths.shape
    dates = owned // start_integral.shape[1]
    peers = columns // owned
    chips = peers // 2
    slots = currencies.shape[1]
    in_vmem = pl.BlockSpec(memory_space=pltpu.VMEM)
    anywhere = pl.BlockSpec(memory_space=pl.ANY)
    params = pltpu.CompilerParams(vmem_limit_bytes=32 * 2**20)
    block = (currency_count, owned)

    def in_hbm(value):
        return pltpu.with_memory_space_constraint(value, pltpu.HBM)

    def swapped(value):
        return lax.ppermute(value, "sets", [(peer, peer ^ 1) for peer in range(peers)])

    handed, masked_other, exposure, bits, weights, used, fx, rates, start = pl.pallas_call(
        first_kernel,
        out_shape=(
            pltpu.VMEM((chips,) + block, jnp.bfloat16),
            pltpu.VMEM((sets, columns // 2), jnp.bfloat16),
            pltpu.VMEM((sets, columns), jnp.bfloat16),
            pltpu.VMEM(positive_bits.shape, jnp.int32),
            pltpu.VMEM((currency_count, sets), jnp.bfloat16),
            pltpu.VMEM((slots, sets), jnp.int32),
            pltpu.VMEM(block, jnp.float32),
            pltpu.VMEM(block, jnp.float32),
            pltpu.VMEM((owned // dates, currency_count), jnp.float32),
        ),
        in_specs=[anywhere] * 8,
        out_specs=(in_vmem,) * 9,
        scratch_shapes=[
            pltpu.VMEM((slots, sets), jnp.int32),
            pltpu.VMEM((1, sets), jnp.int32),
            pltpu.VMEM((slots, sets), jnp.float32),
            pltpu.SemaphoreType.DMA((8,)),
        ],
        compiler_params=params,
        name="first",
    )(
        in_hbm(exposure_adjoint),
        in_hbm(positive_bits),
        in_hbm(currencies.T),
        in_hbm(mix_count.reshape(1, sets)),
        in_hbm(notional.T),
        in_hbm(fx_paths),
        in_hbm(short_rates),
        in_hbm(start_integral.T),
    )
    given = swapped(handed)
    masked_own, terms, carried, discount, moved, turned = pl.pallas_call(
        functools.partial(second_kernel, dates),
        out_shape=(
            pltpu.VMEM((sets, columns // 2), jnp.bfloat16),
            pltpu.VMEM((chips,) + block, jnp.float32),
            pltpu.VMEM(block, jnp.bfloat16),
            pltpu.VMEM(block, jnp.float32),
            pltpu.VMEM(block, jnp.float32),
            pltpu.VMEM((columns // 2, sets), jnp.bfloat16),
        ),
        in_specs=[in_vmem] * 7,
        out_specs=(in_vmem,) * 6,
        compiler_params=params,
        name="second",
    )(
        exposure,
        bits,
        weights,
        fx,
        rates,
        start,
        masked_other,
    )
    outgoing = pl.pallas_call(
        merging_kernel,
        out_shape=pltpu.VMEM((chips, 2 * currency_count, owned), jnp.bfloat16),
        in_specs=[in_vmem] * 3,
        out_specs=in_vmem,
        compiler_params=params,
        name="merging",
    )(given, terms, carried)
    arrived = lax.all_to_all(
        outgoing,
        "sets",
        0,
        0,
        axis_index_groups=[
            [2 * chip + core_in(chip, group) for chip in group_order(chips, group)]
            for group in range(2)
        ],
        tiled=True,
    )
    carried_own = pl.pallas_call(
        unpacking_kernel,
        out_shape=pltpu.VMEM((chips,) + block, jnp.bfloat16),
        in_specs=[in_vmem],
        out_specs=in_vmem,
        compiler_params=params,
        name="unpacking",
    )(arrived)
    carried_other = swapped(carried_own)
    fx_adjoint, rate_adjoint, projected = pl.pallas_call(
        functools.partial(adjoint_kernel, dates),
        out_shape=(
            jax.ShapeDtypeStruct(block, jnp.float32),
            jax.ShapeDtypeStruct(block, jnp.float32),
            pltpu.VMEM((currency_count, sets), jnp.float32),
        ),
        in_specs=[in_vmem] * 5,
        out_specs=(in_vmem,) * 3,
        compiler_params=params,
        name="adjoint",
    )(arrived, carried_own, masked_own, moved, discount)
    notional_adjoint = pl.pallas_call(
        picking_kernel,
        out_shape=jax.ShapeDtypeStruct((slots, sets), jnp.float32),
        in_specs=[in_vmem] * 4,
        out_specs=in_vmem,
        compiler_params=params,
        name="picking",
    )(carried_other, turned, projected, used)
    return fx_adjoint, rate_adjoint, notional_adjoint.T


def solution(mesh):
    in_specs = (
        P(("grp", "sets"), None),
        P(("grp", "sets"), None),
        P(("grp", "sets"), None),
        P(("grp", "sets")),
        P(("grp", "sets"), None),
        P("grp", "sets"),
        P("grp", "sets"),
        P("grp", "sets"),
    )
    out_specs = (P("grp", "sets"), P("grp", "sets"), P(("grp", "sets"), None))
    return jax.shard_map(body, mesh=mesh, in_specs=in_specs, out_specs=out_specs, check_vma=False)
```

```python
import functools
import math

import jax
import jax.numpy as jnp
from jax import lax
from jax.experimental import pallas as pl
from jax.experimental.pallas import tpu as pltpu
from jax.sharding import PartitionSpec as P

step_years = 0.25
bits_per_row = 15
lanes = 128


def spread_paths(values, dates):
    paths, columns = values.shape[0], values.shape[0] * dates
    path_of = lax.broadcasted_iota(jnp.int32, (paths, columns), 1) // dates
    own = lax.broadcasted_iota(jnp.int32, (paths, columns), 0)
    return lax.dot_general(
        values,
        (path_of == own).astype(jnp.float32),
        (((0,), (0,)), ((), ())),
        precision=lax.Precision.HIGHEST,
        preferred_element_type=jnp.float32,
    )


def sums_to_date(values, dates):
    width = values.shape[1]
    date = lax.broadcasted_iota(jnp.int32, values.shape, 1) % dates
    step = 1
    while step < dates:
        values = values + jnp.where(date >= step, pltpu.roll(values, step, 1), 0.0)
        step *= 2
    return values


def sums_from_date(values, dates):
    width = values.shape[1]
    date = lax.broadcasted_iota(jnp.int32, values.shape, 1) % dates
    step = 1
    while step < dates:
        values = values + jnp.where(date < dates - step, pltpu.roll(values, width - step, 1), 0.0)
        step *= 2
    return values


def used_currencies(currencies, counts):
    slot = lax.broadcasted_iota(jnp.int32, currencies.shape, 0)
    return jnp.where(slot < counts, currencies, -1)


def core_in(chip, group):
    return 1 - group if (chip + chip // 2) % 2 else group


def own_group():
    me = lax.axis_index("sets")
    return (me + me // 2 + me // 4) % 2


def group_order(chips, group):
    middle = chips // 2
    far, near = list(range(chips - 1, middle - 1, -1)), list(range(middle))
    if group == 0 and middle % 2 == 0:
        far = [chip ^ 1 for chip in far]
    cut = middle // 2
    return far[:cut] + near[:1] + far[cut:] + near[1:]


def chip_at(chips, place):
    chosen = [group_order(chips, group)[place] for group in range(2)]
    return jnp.where(own_group() == 0, chosen[0], chosen[1])


def group_columns(chip, owned, group):
    block = 2 * chip + core_in(chip, group)
    return pl.ds(pl.multiple_of(block * owned, owned), owned)


def row_flags(tile):
    shift = lax.broadcasted_iota(jnp.int32, (8, lanes), 0) + (8 * tile) % bits_per_row
    shift = jnp.where(shift >= bits_per_row, shift - bits_per_row, shift)
    return jnp.left_shift(jnp.int32(1), shift)


def masked_rows(exposure, bits, pair, flags, part):
    row = lax.broadcasted_iota(jnp.int32, (8, lanes), 0)
    values = exposure[16 * pair : 16 * pair + 16, part].astype(jnp.float32)
    kept = []
    for half in range(2):
        top = 16 * pair + 8 * half
        group = top // bits_per_row
        left = bits_per_row * (group + 1) - top
        packed = jnp.broadcast_to(bits[group : group + 1, part], (8, lanes))
        if left < 8:
            following = jnp.broadcast_to(bits[group + 1 : group + 2, part], (8, lanes))
            packed = jnp.where(row < left, packed, following)
        kept.append(jnp.where((packed & flags[half]) != 0, values[8 * half : 8 * half + 8], 0.0))
    return jnp.concatenate(kept, axis=0).astype(jnp.bfloat16)


def mask_and_sum(exposure, bits, weights, masked_ref, terms_ref, group):
    sets = exposure.shape[0]
    chips, owned = terms_ref.shape[0], terms_ref.shape[2]
    for first in range(0, chips, 2):
        rows = []
        for pair in range(sets // 16):
            flags = [row_flags(2 * pair), row_flags(2 * pair + 1)]
            rows.append(
                jnp.concatenate(
                    [
                        masked_rows(
                            exposure, bits, pair, flags, group_columns(chip, owned, group)
                        )
                        for chip in (first, first + 1)
                    ],
                    axis=1,
                )
            )
        masked = jnp.concatenate(rows, axis=0)
        masked_ref[:, first * owned : (first + 2) * owned] = masked
        terms = jnp.dot(weights, masked, preferred_element_type=jnp.float32)
        terms = terms.astype(terms_ref.dtype)
        terms_ref[first] = terms[:, :owned]
        terms_ref[first + 1] = terms[:, owned:]


def first_kernel(
    exposure_hbm,
    bits_hbm,
    currencies_hbm,
    counts_hbm,
    notional_hbm,
    fx_hbm,
    rates_hbm,
    start_hbm,
    handed_ref,
    masked_ref,
    exposure,
    bits,
    weights_ref,
    used_ref,
    fx_ref,
    rates_ref,
    start_ref,
    currencies_ref,
    counts_ref,
    notional_ref,
    sems,
):
    sets = exposure.shape[0]
    currency_count = handed_ref.shape[1]
    copies = [
        pltpu.make_async_copy(source, target, sems.at[index])
        for index, (source, target) in enumerate(
            [
                (exposure_hbm, exposure),
                (bits_hbm, bits),
                (currencies_hbm, currencies_ref),
                (counts_hbm, counts_ref),
                (notional_hbm, notional_ref),
                (fx_hbm, fx_ref),
                (rates_hbm, rates_ref),
                (start_hbm, start_ref),
            ]
        )
    ]
    for copy in copies:
        copy.start()
    for copy in copies[2:5]:
        copy.wait()

    used = used_currencies(currencies_ref[...], counts_ref[...])
    used_ref[...] = used
    notional = notional_ref[...]
    currency = lax.broadcasted_iota(jnp.int32, (currency_count, sets), 0)
    weights = jnp.zeros((currency_count, sets), jnp.float32)
    for slot in range(used.shape[0]):
        weights = weights + jnp.where(
            currency == used[slot : slot + 1], notional[slot : slot + 1], 0.0
        )
    weights = weights.astype(jnp.bfloat16)
    weights_ref[...] = weights
    for copy in copies[:2]:
        copy.wait()
    other = 1 - own_group()
    mask_and_sum(exposure, bits, weights, masked_ref, handed_ref, other)
    for copy in copies[5:]:
        copy.wait()


def second_kernel(
    dates,
    exposure,
    bits,
    weights_ref,
    fx_ref,
    rates_ref,
    start_ref,
    masked_other,
    masked_ref,
    terms_ref,
    carried_ref,
    discount_ref,
    moved_ref,
    turned_ref,
):
    own = own_group()
    mask_and_sum(exposure, bits, weights_ref[...], masked_ref, terms_ref, own)
    integral = spread_paths(start_ref[...], dates) + step_years * sums_to_date(rates_ref[...], dates)
    discount = jnp.exp(-integral)
    discount_ref[...] = discount
    moved = fx_ref[...] * discount
    moved_ref[...] = moved
    carried_ref[...] = moved.astype(jnp.bfloat16)
    for column in range(0, masked_other.shape[1], lanes):
        turned_ref[column : column + lanes, :] = masked_other[:, column : column + lanes].T


def merging_kernel(given_ref, terms_ref, carried_ref, outgoing_ref):
    chips, currency_count, owned = terms_ref.shape
    carried = carried_ref[...]
    for place in range(chips):
        chip = chip_at(chips, place)
        outgoing_ref[place, 0:currency_count, :] = carried
        outgoing_ref[place, currency_count:, :] = (
            terms_ref[chip] + given_ref[chip].astype(jnp.float32)
        ).astype(jnp.bfloat16)


def unpacking_kernel(arrived_ref, carried_ref):
    chips, currency_count, owned = carried_ref.shape
    for place in range(chips):
        carried_ref[chip_at(chips, place)] = arrived_ref[place, 0:currency_count, :]


def projection(masked, carried_ref):
    sets, half = masked.shape
    chips, currency_count, owned = carried_ref.shape
    here = min(chips, 8)
    projected = jnp.zeros((currency_count, sets), jnp.float32)
    for first in range(0, chips, here):
        carried = jnp.concatenate([carried_ref[first + chip] for chip in range(here)], axis=1)
        projected = projected + lax.dot_general(
            carried,
            masked[:, first * owned : (first + here) * owned],
            (((1,), (1,)), ((), ())),
            preferred_element_type=jnp.float32,
        )
    return projected


def adjoint_kernel(
    dates,
    arrived_ref,
    carried_ref,
    masked_own,
    moved_ref,
    discount_ref,
    fx_adjoint_ref,
    rate_adjoint_ref,
    projected_ref,
):
    chips, currency_count, owned = carried_ref.shape
    aggregate = arrived_ref[0, currency_count:, :].astype(jnp.float32)
    for chip in range(1, chips):
        aggregate = aggregate + arrived_ref[chip, currency_count:, :].astype(jnp.float32)
    fx_adjoint_ref[...] = aggregate * discount_ref[...]
    rate_adjoint_ref[...] = -step_years * sums_from_date(aggregate * moved_ref[...], dates)
    projected_ref[...] = projection(masked_own, carried_ref)


def picking_kernel(carried_ref, turned_ref, projected_ref, used_ref, notional_adjoint_ref):
    half, sets = turned_ref.shape
    currency_count = carried_ref.shape[1]
    chips, _, owned = carried_ref.shape
    here = min(chips, 8)
    projected = projected_ref[...]
    for first in range(0, chips, here):
        carried = jnp.concatenate([carried_ref[first + chip] for chip in range(here)], axis=1)
        projected = projected + jnp.dot(
            carried,
            turned_ref[first * owned : (first + here) * owned, :],
            preferred_element_type=jnp.float32,
        )
    used = used_ref[...]
    currency = lax.broadcasted_iota(jnp.int32, (currency_count, sets), 0)
    for slot in range(used.shape[0]):
        picked = jnp.sum(
            jnp.where(currency == used[slot : slot + 1], projected, 0.0), axis=0, keepdims=True
        )
        notional_adjoint_ref[slot : slot + 1, :] = picked * (1.0 / math.sqrt(2 * half))


def body(
    exposure_adjoint,
    positive_bits,
    currencies,
    mix_count,
    notional,
    fx_paths,
    short_rates,
    start_integral,
):
    sets, columns = exposure_adjoint.shape
    currency_count, owned = fx_paths.shape
    dates = owned // start_integral.shape[1]
    peers = columns // owned
    chips = peers // 2
    slots = currencies.shape[1]
    in_vmem = pl.BlockSpec(memory_space=pltpu.VMEM)
    anywhere = pl.BlockSpec(memory_space=pl.ANY)
    params = pltpu.CompilerParams(vmem_limit_bytes=32 * 2**20)
    block = (currency_count, owned)

    def in_hbm(value):
        return pltpu.with_memory_space_constraint(value, pltpu.HBM)

    def swapped(value):
        return lax.ppermute(value, "sets", [(peer, peer ^ 1) for peer in range(peers)])

    handed, masked_other, exposure, bits, weights, used, fx, rates, start = pl.pallas_call(
        first_kernel,
        out_shape=(
            pltpu.VMEM((chips,) + block, jnp.bfloat16),
            pltpu.VMEM((sets, columns // 2), jnp.bfloat16),
            pltpu.VMEM((sets, columns), jnp.bfloat16),
            pltpu.VMEM(positive_bits.shape, jnp.int32),
            pltpu.VMEM((currency_count, sets), jnp.bfloat16),
            pltpu.VMEM((slots, sets), jnp.int32),
            pltpu.VMEM(block, jnp.float32),
            pltpu.VMEM(block, jnp.float32),
            pltpu.VMEM((owned // dates, currency_count), jnp.float32),
        ),
        in_specs=[anywhere] * 8,
        out_specs=(in_vmem,) * 9,
        scratch_shapes=[
            pltpu.VMEM((slots, sets), jnp.int32),
            pltpu.VMEM((1, sets), jnp.int32),
            pltpu.VMEM((slots, sets), jnp.float32),
            pltpu.SemaphoreType.DMA((8,)),
        ],
        compiler_params=params,
        name="first",
    )(
        in_hbm(exposure_adjoint),
        in_hbm(positive_bits),
        in_hbm(currencies.T),
        in_hbm(mix_count.reshape(1, sets)),
        in_hbm(notional.T),
        in_hbm(fx_paths),
        in_hbm(short_rates),
        in_hbm(start_integral.T),
    )
    given = swapped(handed)
    masked_own, terms, carried, discount, moved, turned = pl.pallas_call(
        functools.partial(second_kernel, dates),
        out_shape=(
            pltpu.VMEM((sets, columns // 2), jnp.bfloat16),
            pltpu.VMEM((chips,) + block, jnp.float32),
            pltpu.VMEM(block, jnp.bfloat16),
            pltpu.VMEM(block, jnp.float32),
            pltpu.VMEM(block, jnp.float32),
            pltpu.VMEM((columns // 2, sets), jnp.bfloat16),
        ),
        in_specs=[in_vmem] * 7,
        out_specs=(in_vmem,) * 6,
        compiler_params=params,
        name="second",
    )(
        exposure,
        bits,
        weights,
        fx,
        rates,
        start,
        masked_other,
    )
    outgoing = pl.pallas_call(
        merging_kernel,
        out_shape=pltpu.VMEM((chips, 2 * currency_count, owned), jnp.bfloat16),
        in_specs=[in_vmem] * 3,
        out_specs=in_vmem,
        compiler_params=params,
        name="merging",
    )(given, terms, carried)
    arrived = lax.all_to_all(
        outgoing,
        "sets",
        0,
        0,
        axis_index_groups=[
            [2 * chip + core_in(chip, group) for chip in group_order(chips, group)]
            for group in range(2)
        ],
        tiled=True,
    )
    carried_own = pl.pallas_call(
        unpacking_kernel,
        out_shape=pltpu.VMEM((chips,) + block, jnp.bfloat16),
        in_specs=[in_vmem],
        out_specs=in_vmem,
        compiler_params=params,
        name="unpacking",
    )(arrived)
    carried_other = swapped(carried_own)
    fx_adjoint, rate_adjoint, projected = pl.pallas_call(
        functools.partial(adjoint_kernel, dates),
        out_shape=(
            jax.ShapeDtypeStruct(block, jnp.float32),
            jax.ShapeDtypeStruct(block, jnp.float32),
            pltpu.VMEM((currency_count, sets), jnp.float32),
        ),
        in_specs=[in_vmem] * 5,
        out_specs=(in_vmem,) * 3,
        compiler_params=params,
        name="adjoint",
    )(arrived, carried_own, masked_own, moved, discount)
    notional_adjoint = pl.pallas_call(
        picking_kernel,
        out_shape=jax.ShapeDtypeStruct((slots, sets), jnp.float32),
        in_specs=[in_vmem] * 4,
        out_specs=in_vmem,
        compiler_params=params,
        name="picking",
    )(carried_other, turned, projected, used)
    return fx_adjoint, rate_adjoint, notional_adjoint.T


def solution(mesh):
    in_specs = (
        P(("grp", "sets"), None),
        P(("grp", "sets"), None),
        P(("grp", "sets"), None),
        P(("grp", "sets")),
        P(("grp", "sets"), None),
        P("grp", "sets"),
        P("grp", "sets"),
        P("grp", "sets"),
    )
    out_specs = (P("grp", "sets"), P("grp", "sets"), P(("grp", "sets"), None))
    return jax.shard_map(body, mesh=mesh, in_specs=in_specs, out_specs=out_specs, check_vma=False)
```

```python
import functools
import math

import jax
import jax.numpy as jnp
from jax import lax
from jax.experimental import pallas as pl
from jax.experimental.pallas import tpu as pltpu
from jax.sharding import PartitionSpec as P

step_years = 0.25
bits_per_row = 15
lanes = 128


def spread_paths(values, dates):
    paths, columns = values.shape[0], values.shape[0] * dates
    path_of = lax.broadcasted_iota(jnp.int32, (paths, columns), 1) // dates
    own = lax.broadcasted_iota(jnp.int32, (paths, columns), 0)
    return lax.dot_general(
        values,
        (path_of == own).astype(jnp.float32),
        (((0,), (0,)), ((), ())),
        precision=lax.Precision.HIGHEST,
        preferred_element_type=jnp.float32,
    )


def sums_to_date(values, dates):
    width = values.shape[1]
    date = lax.broadcasted_iota(jnp.int32, values.shape, 1) % dates
    step = 1
    while step < dates:
        values = values + jnp.where(date >= step, pltpu.roll(values, step, 1), 0.0)
        step *= 2
    return values


def sums_from_date(values, dates):
    width = values.shape[1]
    date = lax.broadcasted_iota(jnp.int32, values.shape, 1) % dates
    step = 1
    while step < dates:
        values = values + jnp.where(date < dates - step, pltpu.roll(values, width - step, 1), 0.0)
        step *= 2
    return values


def used_currencies(currencies, counts):
    slot = lax.broadcasted_iota(jnp.int32, currencies.shape, 0)
    return jnp.where(slot < counts, currencies, -1)


def core_in(chip, group):
    return 1 - group if (chip + chip // 2) % 2 else group


def own_group():
    me = lax.axis_index("sets")
    return (me + me // 2 + me // 4) % 2


def group_order(chips, group):
    middle = chips // 2
    far, near = list(range(middle, chips)), list(range(middle))
    if group:
        far = far[::-1]
    elif middle % 2 == 0:
        far = [chip ^ 1 for chip in far]
    cut = middle // 2
    return far[:cut] + near[:1] + far[cut:] + near[1:]


def chip_at(chips, place):
    chosen = [group_order(chips, group)[place] for group in range(2)]
    return jnp.where(own_group() == 0, chosen[0], chosen[1])


def group_columns(chip, owned, group):
    block = 2 * chip + core_in(chip, group)
    return pl.ds(pl.multiple_of(block * owned, owned), owned)


def row_flags(tile):
    shift = lax.broadcasted_iota(jnp.int32, (8, lanes), 0) + (8 * tile) % bits_per_row
    shift = jnp.where(shift >= bits_per_row, shift - bits_per_row, shift)
    return jnp.left_shift(jnp.int32(1), shift)


def masked_rows(exposure, bits, pair, flags, part):
    row = lax.broadcasted_iota(jnp.int32, (8, lanes), 0)
    values = exposure[16 * pair : 16 * pair + 16, part].astype(jnp.float32)
    kept = []
    for half in range(2):
        top = 16 * pair + 8 * half
        group = top // bits_per_row
        left = bits_per_row * (group + 1) - top
        packed = jnp.broadcast_to(bits[group : group + 1, part], (8, lanes))
        if left < 8:
            following = jnp.broadcast_to(bits[group + 1 : group + 2, part], (8, lanes))
            packed = jnp.where(row < left, packed, following)
        kept.append(jnp.where((packed & flags[half]) != 0, values[8 * half : 8 * half + 8], 0.0))
    return jnp.concatenate(kept, axis=0).astype(jnp.bfloat16)


def mask_and_sum(exposure, bits, weights, masked_ref, terms_ref, group):
    sets = exposure.shape[0]
    chips, owned = terms_ref.shape[0], terms_ref.shape[2]
    for first in range(0, chips, 2):
        rows = []
        for pair in range(sets // 16):
            flags = [row_flags(2 * pair), row_flags(2 * pair + 1)]
            rows.append(
                jnp.concatenate(
                    [
                        masked_rows(
                            exposure, bits, pair, flags, group_columns(chip, owned, group)
                        )
                        for chip in (first, first + 1)
                    ],
                    axis=1,
                )
            )
        masked = jnp.concatenate(rows, axis=0)
        masked_ref[:, first * owned : (first + 2) * owned] = masked
        terms = jnp.dot(weights, masked, preferred_element_type=jnp.float32)
        terms = terms.astype(terms_ref.dtype)
        terms_ref[first] = terms[:, :owned]
        terms_ref[first + 1] = terms[:, owned:]


def first_kernel(
    exposure_hbm,
    bits_hbm,
    currencies_hbm,
    counts_hbm,
    notional_hbm,
    fx_hbm,
    rates_hbm,
    start_hbm,
    handed_ref,
    masked_ref,
    exposure,
    bits,
    weights_ref,
    used_ref,
    fx_ref,
    rates_ref,
    start_ref,
    currencies_ref,
    counts_ref,
    notional_ref,
    sems,
):
    sets = exposure.shape[0]
    currency_count = handed_ref.shape[1]
    copies = [
        pltpu.make_async_copy(source, target, sems.at[index])
        for index, (source, target) in enumerate(
            [
                (exposure_hbm, exposure),
                (bits_hbm, bits),
                (currencies_hbm, currencies_ref),
                (counts_hbm, counts_ref),
                (notional_hbm, notional_ref),
                (fx_hbm, fx_ref),
                (rates_hbm, rates_ref),
                (start_hbm, start_ref),
            ]
        )
    ]
    for copy in copies:
        copy.start()
    for copy in copies[2:5]:
        copy.wait()

    used = used_currencies(currencies_ref[...], counts_ref[...])
    used_ref[...] = used
    notional = notional_ref[...]
    currency = lax.broadcasted_iota(jnp.int32, (currency_count, sets), 0)
    weights = jnp.zeros((currency_count, sets), jnp.float32)
    for slot in range(used.shape[0]):
        weights = weights + jnp.where(
            currency == used[slot : slot + 1], notional[slot : slot + 1], 0.0
        )
    weights = weights.astype(jnp.bfloat16)
    weights_ref[...] = weights
    for copy in copies[:2]:
        copy.wait()
    other = 1 - own_group()
    mask_and_sum(exposure, bits, weights, masked_ref, handed_ref, other)
    for copy in copies[5:]:
        copy.wait()


def second_kernel(
    dates,
    exposure,
    bits,
    weights_ref,
    fx_ref,
    rates_ref,
    start_ref,
    masked_other,
    masked_ref,
    terms_ref,
    carried_ref,
    discount_ref,
    moved_ref,
    turned_ref,
):
    own = own_group()
    mask_and_sum(exposure, bits, weights_ref[...], masked_ref, terms_ref, own)
    integral = spread_paths(start_ref[...], dates) + step_years * sums_to_date(rates_ref[...], dates)
    discount = jnp.exp(-integral)
    discount_ref[...] = discount
    moved = fx_ref[...] * discount
    moved_ref[...] = moved
    carried_ref[...] = moved.astype(jnp.bfloat16)
    for column in range(0, masked_other.shape[1], lanes):
        turned_ref[column : column + lanes, :] = masked_other[:, column : column + lanes].T


def merging_kernel(given_ref, terms_ref, carried_ref, outgoing_ref):
    chips, currency_count, owned = terms_ref.shape
    carried = carried_ref[...]
    for place in range(chips):
        chip = chip_at(chips, place)
        outgoing_ref[place, 0:currency_count, :] = carried
        outgoing_ref[place, currency_count:, :] = (
            terms_ref[chip] + given_ref[chip].astype(jnp.float32)
        ).astype(jnp.bfloat16)


def unpacking_kernel(arrived_ref, carried_ref):
    chips, currency_count, owned = carried_ref.shape
    for place in range(chips):
        carried_ref[chip_at(chips, place)] = arrived_ref[place, 0:currency_count, :]


def projection(masked, carried_ref):
    sets, half = masked.shape
    chips, currency_count, owned = carried_ref.shape
    here = min(chips, 8)
    projected = jnp.zeros((currency_count, sets), jnp.float32)
    for first in range(0, chips, here):
        carried = jnp.concatenate([carried_ref[first + chip] for chip in range(here)], axis=1)
        projected = projected + lax.dot_general(
            carried,
            masked[:, first * owned : (first + here) * owned],
            (((1,), (1,)), ((), ())),
            preferred_element_type=jnp.float32,
        )
    return projected


def adjoint_kernel(
    dates,
    arrived_ref,
    carried_ref,
    masked_own,
    moved_ref,
    discount_ref,
    fx_adjoint_ref,
    rate_adjoint_ref,
    projected_ref,
):
    chips, currency_count, owned = carried_ref.shape
    aggregate = arrived_ref[0, currency_count:, :].astype(jnp.float32)
    for chip in range(1, chips):
        aggregate = aggregate + arrived_ref[chip, currency_count:, :].astype(jnp.float32)
    fx_adjoint_ref[...] = aggregate * discount_ref[...]
    rate_adjoint_ref[...] = -step_years * sums_from_date(aggregate * moved_ref[...], dates)
    projected_ref[...] = projection(masked_own, carried_ref)


def picking_kernel(carried_ref, turned_ref, projected_ref, used_ref, notional_adjoint_ref):
    half, sets = turned_ref.shape
    currency_count = carried_ref.shape[1]
    chips, _, owned = carried_ref.shape
    here = min(chips, 8)
    projected = projected_ref[...]
    for first in range(0, chips, here):
        carried = jnp.concatenate([carried_ref[first + chip] for chip in range(here)], axis=1)
        projected = projected + jnp.dot(
            carried,
            turned_ref[first * owned : (first + here) * owned, :],
            preferred_element_type=jnp.float32,
        )
    used = used_ref[...]
    currency = lax.broadcasted_iota(jnp.int32, (currency_count, sets), 0)
    for slot in range(used.shape[0]):
        picked = jnp.sum(
            jnp.where(currency == used[slot : slot + 1], projected, 0.0), axis=0, keepdims=True
        )
        notional_adjoint_ref[slot : slot + 1, :] = picked * (1.0 / math.sqrt(2 * half))


def body(
    exposure_adjoint,
    positive_bits,
    currencies,
    mix_count,
    notional,
    fx_paths,
    short_rates,
    start_integral,
):
    sets, columns = exposure_adjoint.shape
    currency_count, owned = fx_paths.shape
    dates = owned // start_integral.shape[1]
    peers = columns // owned
    chips = peers // 2
    slots = currencies.shape[1]
    in_vmem = pl.BlockSpec(memory_space=pltpu.VMEM)
    anywhere = pl.BlockSpec(memory_space=pl.ANY)
    params = pltpu.CompilerParams(vmem_limit_bytes=32 * 2**20)
    block = (currency_count, owned)

    def in_hbm(value):
        return pltpu.with_memory_space_constraint(value, pltpu.HBM)

    def swapped(value):
        return lax.ppermute(value, "sets", [(peer, peer ^ 1) for peer in range(peers)])

    handed, masked_other, exposure, bits, weights, used, fx, rates, start = pl.pallas_call(
        first_kernel,
        out_shape=(
            pltpu.VMEM((chips,) + block, jnp.bfloat16),
            pltpu.VMEM((sets, columns // 2), jnp.bfloat16),
            pltpu.VMEM((sets, columns), jnp.bfloat16),
            pltpu.VMEM(positive_bits.shape, jnp.int32),
            pltpu.VMEM((currency_count, sets), jnp.bfloat16),
            pltpu.VMEM((slots, sets), jnp.int32),
            pltpu.VMEM(block, jnp.float32),
            pltpu.VMEM(block, jnp.float32),
            pltpu.VMEM((owned // dates, currency_count), jnp.float32),
        ),
        in_specs=[anywhere] * 8,
        out_specs=(in_vmem,) * 9,
        scratch_shapes=[
            pltpu.VMEM((slots, sets), jnp.int32),
            pltpu.VMEM((1, sets), jnp.int32),
            pltpu.VMEM((slots, sets), jnp.float32),
            pltpu.SemaphoreType.DMA((8,)),
        ],
        compiler_params=params,
        name="first",
    )(
        in_hbm(exposure_adjoint),
        in_hbm(positive_bits),
        in_hbm(currencies.T),
        in_hbm(mix_count.reshape(1, sets)),
        in_hbm(notional.T),
        in_hbm(fx_paths),
        in_hbm(short_rates),
        in_hbm(start_integral.T),
    )
    given = swapped(handed)
    masked_own, terms, carried, discount, moved, turned = pl.pallas_call(
        functools.partial(second_kernel, dates),
        out_shape=(
            pltpu.VMEM((sets, columns // 2), jnp.bfloat16),
            pltpu.VMEM((chips,) + block, jnp.float32),
            pltpu.VMEM(block, jnp.bfloat16),
            pltpu.VMEM(block, jnp.float32),
            pltpu.VMEM(block, jnp.float32),
            pltpu.VMEM((columns // 2, sets), jnp.bfloat16),
        ),
        in_specs=[in_vmem] * 7,
        out_specs=(in_vmem,) * 6,
        compiler_params=params,
        name="second",
    )(
        exposure,
        bits,
        weights,
        fx,
        rates,
        start,
        masked_other,
    )
    outgoing = pl.pallas_call(
        merging_kernel,
        out_shape=pltpu.VMEM((chips, 2 * currency_count, owned), jnp.bfloat16),
        in_specs=[in_vmem] * 3,
        out_specs=in_vmem,
        compiler_params=params,
        name="merging",
    )(given, terms, carried)
    arrived = lax.all_to_all(
        outgoing,
        "sets",
        0,
        0,
        axis_index_groups=[
            [2 * chip + core_in(chip, group) for chip in group_order(chips, group)]
            for group in range(2)
        ],
        tiled=True,
    )
    carried_own = pl.pallas_call(
        unpacking_kernel,
        out_shape=pltpu.VMEM((chips,) + block, jnp.bfloat16),
        in_specs=[in_vmem],
        out_specs=in_vmem,
        compiler_params=params,
        name="unpacking",
    )(arrived)
    carried_other = swapped(carried_own)
    fx_adjoint, rate_adjoint, projected = pl.pallas_call(
        functools.partial(adjoint_kernel, dates),
        out_shape=(
            jax.ShapeDtypeStruct(block, jnp.float32),
            jax.ShapeDtypeStruct(block, jnp.float32),
            pltpu.VMEM((currency_count, sets), jnp.float32),
        ),
        in_specs=[in_vmem] * 5,
        out_specs=(in_vmem,) * 3,
        compiler_params=params,
        name="adjoint",
    )(arrived, carried_own, masked_own, moved, discount)
    notional_adjoint = pl.pallas_call(
        picking_kernel,
        out_shape=jax.ShapeDtypeStruct((slots, sets), jnp.float32),
        in_specs=[in_vmem] * 4,
        out_specs=in_vmem,
        compiler_params=params,
        name="picking",
    )(carried_other, turned, projected, used)
    return fx_adjoint, rate_adjoint, notional_adjoint.T


def solution(mesh):
    in_specs = (
        P(("grp", "sets"), None),
        P(("grp", "sets"), None),
        P(("grp", "sets"), None),
        P(("grp", "sets")),
        P(("grp", "sets"), None),
        P("grp", "sets"),
        P("grp", "sets"),
        P("grp", "sets"),
    )
    out_specs = (P("grp", "sets"), P("grp", "sets"), P(("grp", "sets"), None))
    return jax.shard_map(body, mesh=mesh, in_specs=in_specs, out_specs=out_specs, check_vma=False)
```

```python
import functools
import math

import jax
import jax.numpy as jnp
from jax import lax
from jax.experimental import pallas as pl
from jax.experimental.pallas import tpu as pltpu
from jax.sharding import PartitionSpec as P

step_years = 0.25
bits_per_row = 15
lanes = 128


def spread_paths(values, dates):
    paths, columns = values.shape[0], values.shape[0] * dates
    path_of = lax.broadcasted_iota(jnp.int32, (paths, columns), 1) // dates
    own = lax.broadcasted_iota(jnp.int32, (paths, columns), 0)
    return lax.dot_general(
        values,
        (path_of == own).astype(jnp.float32),
        (((0,), (0,)), ((), ())),
        precision=lax.Precision.HIGHEST,
        preferred_element_type=jnp.float32,
    )


def sums_to_date(values, dates):
    width = values.shape[1]
    date = lax.broadcasted_iota(jnp.int32, values.shape, 1) % dates
    step = 1
    while step < dates:
        values = values + jnp.where(date >= step, pltpu.roll(values, step, 1), 0.0)
        step *= 2
    return values


def sums_from_date(values, dates):
    width = values.shape[1]
    date = lax.broadcasted_iota(jnp.int32, values.shape, 1) % dates
    step = 1
    while step < dates:
        values = values + jnp.where(date < dates - step, pltpu.roll(values, width - step, 1), 0.0)
        step *= 2
    return values


def used_currencies(currencies, counts):
    slot = lax.broadcasted_iota(jnp.int32, currencies.shape, 0)
    return jnp.where(slot < counts, currencies, -1)


def core_in(chip, group):
    return 1 - group if (chip + chip // 2) % 2 else group


def own_group():
    me = lax.axis_index("sets")
    return (me + me // 2 + me // 4) % 2


def group_order(chips, group):
    middle = chips // 2
    far, near = list(range(middle, chips)), list(range(middle))
    if group == 0 and middle % 2 == 0:
        far = [chip ^ 1 for chip in far]
    cut = middle // 2
    return far[:cut] + near[:1] + far[cut:] + near[1:]


def chip_at(chips, place):
    chosen = [group_order(chips, group)[place] for group in range(2)]
    return jnp.where(own_group() == 0, chosen[0], chosen[1])


def group_columns(chip, owned, group):
    block = 2 * chip + core_in(chip, group)
    return pl.ds(pl.multiple_of(block * owned, owned), owned)


def row_flags(tile):
    shift = lax.broadcasted_iota(jnp.int32, (8, lanes), 0) + (8 * tile) % bits_per_row
    shift = jnp.where(shift >= bits_per_row, shift - bits_per_row, shift)
    return jnp.left_shift(jnp.int32(1), shift)


def masked_rows(exposure, bits, pair, flags, part):
    row = lax.broadcasted_iota(jnp.int32, (8, lanes), 0)
    values = exposure[16 * pair : 16 * pair + 16, part].astype(jnp.float32)
    kept = []
    for half in range(2):
        top = 16 * pair + 8 * half
        group = top // bits_per_row
        left = bits_per_row * (group + 1) - top
        packed = jnp.broadcast_to(bits[group : group + 1, part], (8, lanes))
        if left < 8:
            following = jnp.broadcast_to(bits[group + 1 : group + 2, part], (8, lanes))
            packed = jnp.where(row < left, packed, following)
        kept.append(jnp.where((packed & flags[half]) != 0, values[8 * half : 8 * half + 8], 0.0))
    return jnp.concatenate(kept, axis=0).astype(jnp.bfloat16)


def mask_and_sum(exposure, bits, weights, masked_ref, terms_ref, group, chips):
    sets = exposure.shape[0]
    owned = terms_ref.shape[2]
    for first in chips[::2]:
        rows = []
        for pair in range(sets // 16):
            flags = [row_flags(2 * pair), row_flags(2 * pair + 1)]
            rows.append(
                jnp.concatenate(
                    [
                        masked_rows(
                            exposure, bits, pair, flags, group_columns(chip, owned, group)
                        )
                        for chip in (first, first + 1)
                    ],
                    axis=1,
                )
            )
        masked = jnp.concatenate(rows, axis=0)
        masked_ref[:, first * owned : (first + 2) * owned] = masked
        terms = jnp.dot(weights, masked, preferred_element_type=jnp.float32)
        terms = terms.astype(terms_ref.dtype)
        terms_ref[first] = terms[:, :owned]
        terms_ref[first + 1] = terms[:, owned:]


def first_kernel(
    exposure_hbm,
    bits_hbm,
    currencies_hbm,
    counts_hbm,
    notional_hbm,
    fx_hbm,
    rates_hbm,
    start_hbm,
    handed_ref,
    masked_ref,
    exposure,
    bits,
    weights_ref,
    used_ref,
    fx_ref,
    rates_ref,
    start_ref,
    currencies_ref,
    counts_ref,
    notional_ref,
    sems,
):
    sets = exposure.shape[0]
    chips, currency_count = handed_ref.shape[:2]
    half = exposure.shape[1] // 2
    copies = [
        pltpu.make_async_copy(source, target, sems.at[index])
        for index, (source, target) in enumerate(
            [
                (exposure_hbm.at[:, :half], exposure.at[:, :half]),
                (exposure_hbm.at[:, half:], exposure.at[:, half:]),
                (bits_hbm, bits),
                (currencies_hbm, currencies_ref),
                (counts_hbm, counts_ref),
                (notional_hbm, notional_ref),
                (fx_hbm, fx_ref),
                (rates_hbm, rates_ref),
                (start_hbm, start_ref),
            ]
        )
    ]
    for copy in copies:
        copy.start()
    for copy in copies[3:6]:
        copy.wait()

    used = used_currencies(currencies_ref[...], counts_ref[...])
    used_ref[...] = used
    notional = notional_ref[...]
    currency = lax.broadcasted_iota(jnp.int32, (currency_count, sets), 0)
    weights = jnp.zeros((currency_count, sets), jnp.float32)
    for slot in range(used.shape[0]):
        weights = weights + jnp.where(
            currency == used[slot : slot + 1], notional[slot : slot + 1], 0.0
        )
    weights = weights.astype(jnp.bfloat16)
    weights_ref[...] = weights
    other = 1 - own_group()
    copies[2].wait()
    for index in range(2):
        copies[index].wait()
        part = range(index * chips // 2, (index + 1) * chips // 2)
        mask_and_sum(exposure, bits, weights, masked_ref, handed_ref, other, part)
    for copy in copies[6:]:
        copy.wait()


def second_kernel(
    dates,
    exposure,
    bits,
    weights_ref,
    fx_ref,
    rates_ref,
    start_ref,
    masked_other,
    masked_ref,
    terms_ref,
    carried_ref,
    discount_ref,
    moved_ref,
    turned_ref,
):
    own = own_group()
    mask_and_sum(
        exposure, bits, weights_ref[...], masked_ref, terms_ref, own, range(terms_ref.shape[0])
    )
    integral = spread_paths(start_ref[...], dates) + step_years * sums_to_date(rates_ref[...], dates)
    discount = jnp.exp(-integral)
    discount_ref[...] = discount
    moved = fx_ref[...] * discount
    moved_ref[...] = moved
    carried_ref[...] = moved.astype(jnp.bfloat16)
    for column in range(0, masked_other.shape[1], lanes):
        turned_ref[column : column + lanes, :] = masked_other[:, column : column + lanes].T


def merging_kernel(given_ref, terms_ref, carried_ref, outgoing_ref):
    chips, currency_count, owned = terms_ref.shape
    carried = carried_ref[...]
    for place in range(chips):
        chip = chip_at(chips, place)
        outgoing_ref[place, 0:currency_count, :] = carried
        outgoing_ref[place, currency_count:, :] = (
            terms_ref[chip] + given_ref[chip].astype(jnp.float32)
        ).astype(jnp.bfloat16)


def unpacking_kernel(arrived_ref, carried_ref):
    chips, currency_count, owned = carried_ref.shape
    for place in range(chips):
        carried_ref[chip_at(chips, place)] = arrived_ref[place, 0:currency_count, :]


def projection(masked, carried_ref):
    sets, half = masked.shape
    chips, currency_count, owned = carried_ref.shape
    here = min(chips, 8)
    projected = jnp.zeros((currency_count, sets), jnp.float32)
    for first in range(0, chips, here):
        carried = jnp.concatenate([carried_ref[first + chip] for chip in range(here)], axis=1)
        projected = projected + lax.dot_general(
            carried,
            masked[:, first * owned : (first + here) * owned],
            (((1,), (1,)), ((), ())),
            preferred_element_type=jnp.float32,
        )
    return projected


def adjoint_kernel(
    dates,
    arrived_ref,
    carried_ref,
    masked_own,
    moved_ref,
    discount_ref,
    fx_adjoint_ref,
    rate_adjoint_ref,
    projected_ref,
):
    chips, currency_count, owned = carried_ref.shape
    aggregate = arrived_ref[0, currency_count:, :].astype(jnp.float32)
    for chip in range(1, chips):
        aggregate = aggregate + arrived_ref[chip, currency_count:, :].astype(jnp.float32)
    fx_adjoint_ref[...] = aggregate * discount_ref[...]
    rate_adjoint_ref[...] = -step_years * sums_from_date(aggregate * moved_ref[...], dates)
    projected_ref[...] = projection(masked_own, carried_ref)


def picking_kernel(carried_ref, turned_ref, projected_ref, used_ref, notional_adjoint_ref):
    half, sets = turned_ref.shape
    currency_count = carried_ref.shape[1]
    chips, _, owned = carried_ref.shape
    here = min(chips, 8)
    projected = projected_ref[...]
    for first in range(0, chips, here):
        carried = jnp.concatenate([carried_ref[first + chip] for chip in range(here)], axis=1)
        projected = projected + jnp.dot(
            carried,
            turned_ref[first * owned : (first + here) * owned, :],
            preferred_element_type=jnp.float32,
        )
    used = used_ref[...]
    currency = lax.broadcasted_iota(jnp.int32, (currency_count, sets), 0)
    for slot in range(used.shape[0]):
        picked = jnp.sum(
            jnp.where(currency == used[slot : slot + 1], projected, 0.0), axis=0, keepdims=True
        )
        notional_adjoint_ref[slot : slot + 1, :] = picked * (1.0 / math.sqrt(2 * half))


def body(
    exposure_adjoint,
    positive_bits,
    currencies,
    mix_count,
    notional,
    fx_paths,
    short_rates,
    start_integral,
):
    sets, columns = exposure_adjoint.shape
    currency_count, owned = fx_paths.shape
    dates = owned // start_integral.shape[1]
    peers = columns // owned
    chips = peers // 2
    slots = currencies.shape[1]
    in_vmem = pl.BlockSpec(memory_space=pltpu.VMEM)
    anywhere = pl.BlockSpec(memory_space=pl.ANY)
    params = pltpu.CompilerParams(vmem_limit_bytes=32 * 2**20)
    block = (currency_count, owned)

    def in_hbm(value):
        return pltpu.with_memory_space_constraint(value, pltpu.HBM)

    def swapped(value):
        return lax.ppermute(value, "sets", [(peer, peer ^ 1) for peer in range(peers)])

    handed, masked_other, exposure, bits, weights, used, fx, rates, start = pl.pallas_call(
        first_kernel,
        out_shape=(
            pltpu.VMEM((chips,) + block, jnp.bfloat16),
            pltpu.VMEM((sets, columns // 2), jnp.bfloat16),
            pltpu.VMEM((sets, columns), jnp.bfloat16),
            pltpu.VMEM(positive_bits.shape, jnp.int32),
            pltpu.VMEM((currency_count, sets), jnp.bfloat16),
            pltpu.VMEM((slots, sets), jnp.int32),
            pltpu.VMEM(block, jnp.float32),
            pltpu.VMEM(block, jnp.float32),
            pltpu.VMEM((owned // dates, currency_count), jnp.float32),
        ),
        in_specs=[anywhere] * 8,
        out_specs=(in_vmem,) * 9,
        scratch_shapes=[
            pltpu.VMEM((slots, sets), jnp.int32),
            pltpu.VMEM((1, sets), jnp.int32),
            pltpu.VMEM((slots, sets), jnp.float32),
            pltpu.SemaphoreType.DMA((9,)),
        ],
        compiler_params=params,
        name="first",
    )(
        in_hbm(exposure_adjoint),
        in_hbm(positive_bits),
        in_hbm(currencies.T),
        in_hbm(mix_count.reshape(1, sets)),
        in_hbm(notional.T),
        in_hbm(fx_paths),
        in_hbm(short_rates),
        in_hbm(start_integral.T),
    )
    given = swapped(handed)
    masked_own, terms, carried, discount, moved, turned = pl.pallas_call(
        functools.partial(second_kernel, dates),
        out_shape=(
            pltpu.VMEM((sets, columns // 2), jnp.bfloat16),
            pltpu.VMEM((chips,) + block, jnp.float32),
            pltpu.VMEM(block, jnp.bfloat16),
            pltpu.VMEM(block, jnp.float32),
            pltpu.VMEM(block, jnp.float32),
            pltpu.VMEM((columns // 2, sets), jnp.bfloat16),
        ),
        in_specs=[in_vmem] * 7,
        out_specs=(in_vmem,) * 6,
        compiler_params=params,
        name="second",
    )(
        exposure,
        bits,
        weights,
        fx,
        rates,
        start,
        masked_other,
    )
    outgoing = pl.pallas_call(
        merging_kernel,
        out_shape=pltpu.VMEM((chips, 2 * currency_count, owned), jnp.bfloat16),
        in_specs=[in_vmem] * 3,
        out_specs=in_vmem,
        compiler_params=params,
        name="merging",
    )(given, terms, carried)
    arrived = lax.all_to_all(
        outgoing,
        "sets",
        0,
        0,
        axis_index_groups=[
            [2 * chip + core_in(chip, group) for chip in group_order(chips, group)]
            for group in range(2)
        ],
        tiled=True,
    )
    carried_own = pl.pallas_call(
        unpacking_kernel,
        out_shape=pltpu.VMEM((chips,) + block, jnp.bfloat16),
        in_specs=[in_vmem],
        out_specs=in_vmem,
        compiler_params=params,
        name="unpacking",
    )(arrived)
    carried_other = swapped(carried_own)
    fx_adjoint, rate_adjoint, projected = pl.pallas_call(
        functools.partial(adjoint_kernel, dates),
        out_shape=(
            jax.ShapeDtypeStruct(block, jnp.float32),
            jax.ShapeDtypeStruct(block, jnp.float32),
            pltpu.VMEM((currency_count, sets), jnp.float32),
        ),
        in_specs=[in_vmem] * 5,
        out_specs=(in_vmem,) * 3,
        compiler_params=params,
        name="adjoint",
    )(arrived, carried_own, masked_own, moved, discount)
    notional_adjoint = pl.pallas_call(
        picking_kernel,
        out_shape=jax.ShapeDtypeStruct((slots, sets), jnp.float32),
        in_specs=[in_vmem] * 4,
        out_specs=in_vmem,
        compiler_params=params,
        name="picking",
    )(carried_other, turned, projected, used)
    return fx_adjoint, rate_adjoint, notional_adjoint.T


def solution(mesh):
    in_specs = (
        P(("grp", "sets"), None),
        P(("grp", "sets"), None),
        P(("grp", "sets"), None),
        P(("grp", "sets")),
        P(("grp", "sets"), None),
        P("grp", "sets"),
        P("grp", "sets"),
        P("grp", "sets"),
    )
    out_specs = (P("grp", "sets"), P("grp", "sets"), P(("grp", "sets"), None))
    return jax.shard_map(body, mesh=mesh, in_specs=in_specs, out_specs=out_specs, check_vma=False)
```
